256 devices in a mesh: gx: 64 (over z, y, core), gy: 2 (over x_hi), gz: 2 (over x_lo).
Axes of the slice: x: 4 (x_hi: 2, x_lo: 2; x = x_hi * 2 + x_lo), y: 4, z: 8, core: 2. Of those that a mesh axis runs over, the one named last changes fastest.
Arguments:
- fields: float32 [2, 2, 1024, 2048], P(None, 'gz', 'gx', 'gy'), may hold values from -5.5 to 8
- kappa: float32 [2, 2, 1024, 2048], P(None, 'gz', 'gx', 'gy'), may hold values from 100 to 800000
- vertical: float32 [2, 2, 1024, 2048], P(None, 'gz', 'gx', 'gy'), may hold values from 0.03 to 0.4
Outputs:
- advanced: float32 [2, 2, 1024, 2048], P(None, 'gz', 'gx', 'gy')
The draws below stay inside these ranges and needn't reach their ends.
All inputs are finite; a program needn't handle non-finite values.
Results may differ from the reference program's by a relative error of at most 0.005.
Values sent between devices are 32-bit elements; how exact they have to be, the bound alone decides.
No kernel may reach another device: no remote copies, remote signals or barrier semaphores. Data moves between devices by JAX's collectives and lax.ppermute only.
A program may use at most 128 MiB of HBM per device.

```python
import math
import jax
import jax.numpy as jnp
from jax import lax

NX = 1024
NY = 2048
NZ = 2


def draw_fields(key, part):
    key = jax.random.fold_in(key, 5)
    jitter_key, level_key = jax.random.split(key, 2)
    extent = (2, NZ, NX, NY)
    jitter = jax.random.truncated_normal(jitter_key, -6.0, 6.0, extent, jnp.float32)
    offset = jax.random.uniform(level_key, (2, NZ, 1, 1), jnp.float32, 0.5, 2.0)
    return (jitter + offset).astype(jnp.float32)


def draw_kappa(key, part):
    key = jax.random.fold_in(key, 9)
    level_key, cell_key = jax.random.split(key, 2)
    extent = (2, NZ, NX, NY)
    levels = jax.random.uniform(level_key, (2, NZ, 8, 4), jnp.float32, 2.0, 5.3)
    levels = jnp.repeat(jnp.repeat(levels, NX // 8, axis=2), NY // 4, axis=3)
    factor = jnp.exp(jax.random.uniform(cell_key, extent, jnp.float32, 0.0, math.log(4.0)))
    return (jnp.power(10.0, levels) * factor).astype(jnp.float32)


def draw_vertical(key, part):
    key = jax.random.fold_in(key, 13)
    level_key, region_key, cell_key = jax.random.split(key, 3)
    extent = (2, NZ, NX, NY)
    levels = jax.random.uniform(level_key, (2, NZ, 1, 1), jnp.float32, 0.05, 0.25)
    regions = jax.random.uniform(region_key, (2, NZ, 8, 4), jnp.float32, 0.7, 1.3)
    regions = jnp.repeat(jnp.repeat(regions, NX // 8, axis=2), NY // 4, axis=3)
    rough = jax.random.uniform(cell_key, extent, jnp.float32, 0.9, 1.1)
    return (levels * regions * rough).astype(jnp.float32)


def setup_inputs(seed: int = 0) -> dict:
    streams_of = jax.random.split(jax.random.key(seed), 4)
    return {
        "fields": draw_fields(jax.random.fold_in(streams_of[3], 71), 0),
        "kappa": draw_kappa(jax.random.fold_in(streams_of[3], 71), 0),
        "vertical": draw_vertical(jax.random.fold_in(streams_of[3], 71), 0),
    }


def thomas(lower, middle, upper, right, axis):
    lower = jnp.moveaxis(lower, axis, 0)
    middle = jnp.moveaxis(middle, axis, 0)
    upper = jnp.moveaxis(upper, axis, 0)
    right = jnp.moveaxis(right, axis, 0)
    zeros = jnp.zeros(lower.shape[1:], lower.dtype)

    def forward(carry, row):
        upper_prev, value_prev = carry
        lower_row, middle_row, upper_row, right_row = row
        pivot = middle_row - lower_row * upper_prev
        upper_new = upper_row / pivot
        value_new = (right_row - lower_row * value_prev) / pivot
        return (upper_new, value_new), (upper_new, value_new)

    _, (uppers, values) = lax.scan(forward, (zeros, zeros), (lower, middle, upper, right))

    def backward(carry, row):
        upper_row, value_row = row
        result = value_row - upper_row * carry
        return result, result

    _, solved = lax.scan(backward, zeros, (uppers, values), reverse=True)
    return jnp.moveaxis(solved, 0, axis)


def reference(fields, kappa, vertical):
    padded = jnp.pad(kappa, ((0, 0), (0, 0), (1, 1), (1, 1)))
    west = (padded[:, :, :-2, 1:-1] + kappa) * 0.5
    east = (padded[:, :, 2:, 1:-1] + kappa) * 0.5
    south = (padded[:, :, 1:-1, :-2] + kappa) * 0.5
    north = (padded[:, :, 1:-1, 2:] + kappa) * 0.5
    field_planes = jnp.pad(fields, ((0, 0), (1, 1), (0, 0), (0, 0)))
    number_planes = jnp.pad(vertical, ((0, 0), (1, 1), (0, 0), (0, 0)))
    below = (number_planes[:, :-2] + vertical) * 0.5
    above = (number_planes[:, 2:] + vertical) * 0.5
    source = fields + above * (field_planes[:, 2:] - fields) - below * (fields - field_planes[:, :-2])
    section = thomas(-west, 1.0 + west + east, -east, source, 2)
    return thomas(-south, 1.0 + south + north, -north, section, 3)
```

```python
import functools

import jax
import jax.numpy as jnp
from jax import lax
from jax.experimental import pallas as pl
from jax.experimental.pallas import tpu as pltpu
from jax.sharding import PartitionSpec as P

F32 = jnp.float32
ROWS = 16
COLS = 1024
ALL = 2 * ROWS
VMEM = pl.BlockSpec(memory_space=pltpu.VMEM)
SMEM = pl.BlockSpec(memory_space=pltpu.SMEM)
X_STEPS = (1, 2, 4, 8)
Y_STEPS = (1, 2, 4, 8, 16, 32, 64, 128, 256, 512)
PARAMS = pltpu.CompilerParams(vmem_limit_bytes=40 * 1024 * 1024)


def shape(*dims):
    return jax.ShapeDtypeStruct(dims, F32)


def turn(x, k, axis):
    n = x.shape[axis]
    k = k % n
    unit = 128 if axis == 1 else 8
    if k == 0:
        return x
    if k % unit == 0:
        low = lax.slice_in_dim(x, n - k, n, axis=axis)
        high = lax.slice_in_dim(x, 0, n - k, axis=axis)
        return jnp.concatenate([low, high], axis=axis)
    return pltpu.roll(x, k, axis)


def reduce_matrix(low, excess, rights, steps, axis, keep):
    for index, k in enumerate(steps):
        high = turn(low, -k, axis)
        inverse = 1.0 / (low + high + excess)
        a = low * turn(inverse, k, axis)
        b = high * turn(inverse, -k, axis)
        keep(index, a, b)
        excess = excess + a * turn(excess, k, axis) + b * turn(excess, -k, axis)
        rights = [r + a * turn(r, k, axis) + b * turn(r, -k, axis) for r in rights]
        low = a * turn(low, k, axis)
    inverse = 1.0 / excess
    return inverse, [r * inverse for r in rights]


def reduce_right(right, steps, axis, load):
    for index, k in enumerate(steps):
        a, b = load(index)
        right = right + a * turn(right, k, axis) + b * turn(right, -k, axis)
    return right


def dense(row):
    return jnp.concatenate([row[:, 128 * i : 128 * (i + 1)] for i in range(8)], axis=0)


def natural(tile, rows):
    return jnp.concatenate(
        [jnp.broadcast_to(tile[i : i + 1, :], (rows, 128)) for i in range(8)], axis=1
    )


def factor_kernel(place, kappa, ax, bx, qx, h1, h2, ay, by, qy, hy, parts, edge):
    gy = place[0]
    half = 512
    rows = lax.broadcasted_iota(jnp.int32, (ROWS, half), 0)
    for f in range(2):
        mine = pl.ds(f * ROWS, ROWS)
        for c in range(COLS // half):
            cols = pl.ds(c * half, half)
            k = kappa[mine, cols]
            face = (k + turn(k, 1, 0)) * 0.5
            low = jnp.where((rows >= 2) & (rows <= 14), face, 0.0)
            first = jnp.where(rows == 1, face, 0.0)
            last = jnp.where(rows == 14, turn(face, -1, 0), 0.0)

            def keep(index, a, b, mine=mine, cols=cols):
                ax[index, mine, cols] = a
                bx[index, mine, cols] = b

            inverse, (one, two) = reduce_matrix(
                low, 1.0 + first + last, [first, last], X_STEPS, 0, keep
            )
            qx[mine, cols] = jnp.where((rows >= 1) & (rows <= 14), inverse, 0.0)
            one = jnp.where(rows == 0, 1.0, one)
            two = jnp.where(rows == ROWS - 1, 1.0, two)
            h1[mine, cols] = one
            h2[mine, cols] = two
            for n, row in enumerate(
                (
                    jnp.sum(first * two, axis=0, keepdims=True),
                    jnp.sum(one, axis=0, keepdims=True),
                    jnp.sum(two, axis=0, keepdims=True),
                )
            ):
                for i in range(half // 128):
                    parts[n, f, pl.ds(c * (half // 128) + i, 1), :] = row[:, 128 * i : 128 * (i + 1)]
    lanes = lax.broadcasted_iota(jnp.int32, (8, COLS), 1)
    wide = lax.broadcasted_iota(jnp.int32, (8, 128), 1)
    low_side = gy == 0
    terminal = lanes == jnp.where(low_side, COLS - 1, 0)
    cut = lanes == jnp.where(low_side, COLS - 1, 1)
    outer = lanes == jnp.where(low_side, 0, COLS - 1)
    beside = lanes == jnp.where(low_side, COLS - 2, 1)
    for g in range(ALL // 8):
        mine = pl.ds(g * 8, 8)
        k = kappa[mine, :]
        face = (k + turn(k, 1, 1)) * 0.5
        low = jnp.where((lanes == 0) | cut, 0.0, face)
        link = jnp.where(beside, jnp.where(low_side, turn(face, -1, 1), face), 0.0)
        ground = jnp.where(outer, 1.0 + 0.5 * k, 1.0)

        def keep(index, a, b, mine=mine):
            ay[index, mine, :] = a
            by[index, mine, :] = b

        inverse, (profile,) = reduce_matrix(low, ground + link, [link], Y_STEPS, 1, keep)
        qy[mine, :] = jnp.where(terminal, 0.0, inverse)
        profile = jnp.where(terminal, 1.0, profile)
        hy[mine, :] = profile
        total = jnp.sum(profile * ground, axis=1, keepdims=True)
        rim = jnp.sum(jnp.where(terminal, k, 0.0), axis=1, keepdims=True)
        edge[mine, :] = jnp.where(wide == 0, total, jnp.where(wide == 1, rim, 0.0))


def source_kernel(place, fields, fields_far, vertical, vertical_far, kappa, halo, h1, h2, parts, source, sums, message):
    gx = place[1]
    here = fields[...]
    v = vertical[...]
    s = here + (v + vertical_far[...]) * 0.5 * (fields_far[...] - here) - v * 0.5 * here
    source[...] = s
    for f in range(2):
        mine = slice(f * ROWS, (f + 1) * ROWS)
        first = dense(jnp.sum(h1[mine, :] * s[mine, :], axis=0, keepdims=True))
        last = dense(jnp.sum(h2[mine, :] * s[mine, :], axis=0, keepdims=True))
        west = (dense(kappa[f * ROWS : f * ROWS + 1, :]) + dense(halo[f : f + 1, :])) * 0.5
        east = dense(kappa[f * ROWS + ROWS - 1 : f * ROWS + ROWS, :]) * 0.5
        g, s_first, s_last = parts[0, f], parts[1, f], parts[2, f]
        inverse = 1.0 / (west + g + s_first)
        a = west * inverse
        b = g * inverse
        sums[0, f] = a
        sums[1, f] = b
        sums[2, f] = first * inverse
        element = (
            a * g,
            a * s_first,
            jnp.where(gx == 63, s_last + east, s_last) + b * s_first,
            a * first,
            last + b * first,
        )
        for n, value in enumerate(element):
            for j in range(4):
                message[2 * j + f, n] = value


def local_x_kernel(source, ax, bx, qx, out):
    half = 512
    for f in range(2):
        mine = pl.ds(f * ROWS, ROWS)
        for c in range(COLS // half):
            cols = pl.ds(c * half, half)
            r = source[mine, cols]
            r = reduce_right(r, X_STEPS, 0, lambda i: (ax[i, mine, cols], bx[i, mine, cols]))
            out[mine, cols] = r * qx[mine, cols]


def slab_kernel(got, message, chain):
    g, sl, sr, rl, rr = (got[0, n] for n in range(5))
    for k in range(7):
        g2, sl2, sr2, rl2, rr2 = (got[k + 1, n] for n in range(5))
        s = sr + sl2
        r = rr + rl2
        inverse = 1.0 / (g + g2 + s)
        a = g * inverse
        b = g2 * inverse
        chain[k, 0] = a
        chain[k, 1] = b
        chain[k, 2] = r * inverse
        sl = sl + a * s
        rl = rl + a * r
        sr = sr2 + b * s
        rr = rr2 + b * r
        g = a * g2
    for n, value in enumerate((g, sl, sr, rl, rr)):
        for j in range(8):
            message[j, n] = value


def ends_kernel(place, got, chain, mine, other):
    gx = place[1]
    slab = gx // 8
    seat = gx % 8
    zero = jnp.zeros((8, 128), F32)
    conduct = got[0, 0] + got[0, 2]
    right = got[0, 4]
    ratios, offsets = [], []
    for k in range(7):
        conduct = conduct + got[k + 1, 1]
        right = right + got[k + 1, 3]
        inverse = 1.0 / (conduct + got[k + 1, 0])
        f = got[k + 1, 0] * inverse
        ratios.append(f)
        offsets.append(right * inverse)
        conduct = got[k + 1, 2] + f * conduct
        right = got[k + 1, 4] + f * right
    value = right / conduct
    values = [value]
    for k in range(6, -1, -1):
        value = ratios[k] * value + offsets[k]
        values.append(value)
    values = [zero] + values[::-1]
    left, last = zero, zero
    for z in range(8):
        left = jnp.where(slab == z, values[z], left)
        last = jnp.where(slab == z, values[z + 1], last)
    nodes = [last]
    for k in range(6, -1, -1):
        nodes.append(chain[k, 0] * left + chain[k, 1] * nodes[-1] + chain[k, 2])
    nodes = [left] + nodes[::-1]
    even = seat % 2 == 0
    trio = [zero, zero, zero]
    for j in range(4):
        for n in range(3):
            trio[n] = jnp.where(seat // 2 == j, nodes[2 * j + n], trio[n])
    mine[0] = jnp.where(even, trio[0], trio[1])
    mine[1] = jnp.where(even, trio[1], trio[2])
    other[0] = jnp.where(even, trio[1], trio[0])
    other[1] = jnp.where(even, trio[2], trio[1])


def section_kernel(place, mine, other, sums, local, h1, h2, hy, edge, section, message):
    core = place[1] % 2
    wide = lax.broadcasted_iota(jnp.int32, (8, 128), 1)
    for f in range(2):
        left = jnp.where(core == f, mine[0], other[0])
        last = jnp.where(core == f, mine[1], other[1])
        first = sums[0, f] * left + sums[1, f] * last + sums[2, f]
        rows = slice(f * ROWS, (f + 1) * ROWS)
        s = local[rows, :] + h1[rows, :] * natural(first, ROWS) + h2[rows, :] * natural(last, ROWS)
        section[rows, :] = s
        total = jnp.sum(hy[rows, :] * s, axis=1, keepdims=True)
        for g in range(2):
            part = slice(f * ROWS + g * 8, f * ROWS + g * 8 + 8)
            message[part, :] = jnp.where(wide == 2, total[g * 8 : g * 8 + 8], edge[part, :])


def local_y_kernel(section, ay, by, qy, out):
    for g in range(ALL // 8):
        mine = pl.ds(g * 8, 8)
        r = section[mine, :]
        r = reduce_right(r, Y_STEPS, 1, lambda i: (ay[i, mine, :], by[i, mine, :]))
        out[mine, :] = r * qy[mine, :]


def output_kernel(message, far, local, hy, out):
    e, k, r = (message[:, n : n + 1] for n in range(3))
    e2, k2, r2 = (far[:, n : n + 1] for n in range(3))
    c = (k + k2) * 0.5
    value = ((e2 + c) * r + c * r2) / (e * e2 + c * (e + e2))
    out[...] = local[...] + hy[...] * value


def call(kernel, outs, specs, flops=0, size=0):
    return pl.pallas_call(
        kernel,
        out_shape=outs,
        in_specs=specs,
        out_specs=jax.tree.map(lambda _: VMEM, outs),
        compiler_params=PARAMS,
        cost_estimate=pl.CostEstimate(flops=flops, bytes_accessed=size, transcendentals=0),
    )


PLANE_GROUPS = [[8 * a + b for b in range(8)] for a in range(8)]
SLAB_GROUPS = [[8 * b + a for b in range(8)] for a in range(8)]


def local(fields, kappa, vertical):
    gx = lax.axis_index("gx")
    gy = lax.axis_index("gy")
    place = jnp.stack([gy, gx]).astype(jnp.int32)
    grid = (ALL, COLS)
    swap = [(0, 1), (1, 0)]
    fields_far = lax.ppermute(fields, "gz", swap)
    vertical_far = lax.ppermute(vertical, "gz", swap)
    halo = lax.ppermute(kappa[:, 0, ROWS - 1], "gx", [(i, i + 1) for i in range(63)])
    k = kappa.reshape(grid)
    full = shape(*grid)
    ax, bx, qx, h1, h2, ay, by, qy, hy, parts, edge = call(
        factor_kernel,
        (
            shape(4, *grid), shape(4, *grid), full, full, full,
            shape(10, *grid), shape(10, *grid), full, full,
            shape(3, 2, 8, 128), shape(ALL, 128),
        ),
        [SMEM, VMEM],
        flops=20_000_000,
        size=4_000_000,
    )(place, k)
    source, sums, message = call(
        source_kernel,
        (full, shape(3, 2, 8, 128), shape(8, 5, 8, 128)),
        [SMEM] + [VMEM] * 9,
    )(
        place, fields.reshape(grid), fields_far.reshape(grid), vertical.reshape(grid),
        vertical_far.reshape(grid), k, halo, h1, h2, parts,
    )
    got = lax.all_to_all(message, "gx", 0, 0, axis_index_groups=PLANE_GROUPS, tiled=True)
    local_x = call(local_x_kernel, full, [VMEM] * 4, flops=1_000_000, size=1_000_000)(source, ax, bx, qx)
    message, chain = call(
        slab_kernel, (shape(8, 5, 8, 128), shape(7, 3, 8, 128)), [VMEM]
    )(got)
    got = lax.all_to_all(message, "gx", 0, 0, axis_index_groups=SLAB_GROUPS, tiled=True)
    mine, other = call(
        ends_kernel, (shape(2, 8, 128), shape(2, 8, 128)), [SMEM, VMEM, VMEM]
    )(place, got, chain)
    other = lax.ppermute(other, "gx", [(i, i ^ 1) for i in range(64)])
    section, message = call(
        section_kernel, (full, shape(ALL, 128)), [SMEM] + [VMEM] * 8
    )(place, mine, other, sums, local_x, h1, h2, hy, edge)
    far = lax.ppermute(message, "gy", swap)
    local_y = call(local_y_kernel, full, [VMEM] * 4, flops=4_000_000, size=3_000_000)(section, ay, by, qy)
    out = call(output_kernel, full, [VMEM] * 4)(message, far, local_y, hy)
    return out.reshape(fields.shape)


def solution(mesh):
    spec = P(None, "gz", "gx", "gy")
    return jax.shard_map(
        local, mesh=mesh, in_specs=(spec, spec, spec), out_specs=spec, check_vma=False
    )
```

```python
import functools

import jax
import jax.numpy as jnp
from jax import lax
from jax.experimental import pallas as pl
from jax.experimental.pallas import tpu as pltpu
from jax.sharding import PartitionSpec as P

F32 = jnp.float32
ROWS = 16
COLS = 1024
ALL = 2 * ROWS
VMEM = pl.BlockSpec(memory_space=pltpu.VMEM)
HBM = pl.BlockSpec(memory_space=pltpu.HBM)
X_STEPS = (1, 2, 4, 8)
Y_STEPS = (1, 2, 4, 8, 16, 32, 64, 128, 256, 512)
PARAMS = pltpu.CompilerParams(vmem_limit_bytes=40 * 1024 * 1024)


def shape(*dims):
    return jax.ShapeDtypeStruct(dims, F32)


def turn(x, k, axis):
    n = x.shape[axis]
    k = k % n
    unit = 128 if axis == 1 else 8
    if k == 0:
        return x
    if k % unit == 0:
        low = lax.slice_in_dim(x, n - k, n, axis=axis)
        high = lax.slice_in_dim(x, 0, n - k, axis=axis)
        return jnp.concatenate([low, high], axis=axis)
    return pltpu.roll(x, k, axis)


def reduce_matrix(low, excess, rights, steps, axis, keep):
    for index, k in enumerate(steps):
        high = turn(low, -k, axis)
        inverse = 1.0 / (low + high + excess)
        a = low * turn(inverse, k, axis)
        b = high * turn(inverse, -k, axis)
        keep(index, a, b)
        excess = excess + a * turn(excess, k, axis) + b * turn(excess, -k, axis)
        rights = [r + a * turn(r, k, axis) + b * turn(r, -k, axis) for r in rights]
        low = a * turn(low, k, axis)
    inverse = 1.0 / excess
    return inverse, [r * inverse for r in rights]


def reduce_right(right, steps, axis, load):
    for index, k in enumerate(steps):
        a, b = load(index)
        right = right + a * turn(right, k, axis) + b * turn(right, -k, axis)
    return right


def dense(row):
    return jnp.concatenate([row[:, 128 * i : 128 * (i + 1)] for i in range(8)], axis=0)


def natural(tile, rows):
    return jnp.concatenate(
        [jnp.broadcast_to(tile[i : i + 1, :], (rows, 128)) for i in range(8)], axis=1
    )


def factor_kernel(
    fields_arg, vertical_arg, kappa_arg,
    fields, vertical, kappa, ax, bx, qx, h1, h2, ay, by, qy, hy, parts, edge, done,
):
    pairs = ((kappa_arg, kappa), (fields_arg, fields), (vertical_arg, vertical))
    copies = [pltpu.make_async_copy(a, b, done.at[n]) for n, (a, b) in enumerate(pairs)]
    for copy in copies:
        copy.start()
    copies[0].wait()
    gy = lax.axis_index("gy")
    half = 512
    rows = lax.broadcasted_iota(jnp.int32, (ROWS, half), 0)
    for f in range(2):
        mine = pl.ds(f * ROWS, ROWS)
        for c in range(COLS // half):
            cols = pl.ds(c * half, half)
            k = kappa[mine, cols]
            face = (k + turn(k, 1, 0)) * 0.5
            low = jnp.where((rows >= 2) & (rows <= 14), face, 0.0)
            first = jnp.where(rows == 1, face, 0.0)
            last = jnp.where(rows == 14, turn(face, -1, 0), 0.0)

            def keep(index, a, b, mine=mine, cols=cols):
                ax[index, mine, cols] = a
                bx[index, mine, cols] = b

            inverse, (one, two) = reduce_matrix(
                low, 1.0 + first + last, [first, last], X_STEPS, 0, keep
            )
            qx[mine, cols] = jnp.where((rows >= 1) & (rows <= 14), inverse, 0.0)
            one = jnp.where(rows == 0, 1.0, one)
            two = jnp.where(rows == ROWS - 1, 1.0, two)
            h1[mine, cols] = one
            h2[mine, cols] = two
            for n, row in enumerate(
                (
                    jnp.sum(first * two, axis=0, keepdims=True),
                    jnp.sum(one, axis=0, keepdims=True),
                    jnp.sum(two, axis=0, keepdims=True),
                )
            ):
                for i in range(half // 128):
                    parts[n, f, pl.ds(c * (half // 128) + i, 1), :] = row[:, 128 * i : 128 * (i + 1)]
    lanes = lax.broadcasted_iota(jnp.int32, (8, COLS), 1)
    wide = lax.broadcasted_iota(jnp.int32, (8, 128), 1)
    low_side = gy == 0
    terminal = lanes == jnp.where(low_side, COLS - 1, 0)
    cut = lanes == jnp.where(low_side, COLS - 1, 1)
    outer = lanes == jnp.where(low_side, 0, COLS - 1)
    beside = lanes == jnp.where(low_side, COLS - 2, 1)
    for g in range(ALL // 8):
        mine = pl.ds(g * 8, 8)
        k = kappa[mine, :]
        face = (k + turn(k, 1, 1)) * 0.5
        low = jnp.where((lanes == 0) | cut, 0.0, face)
        link = jnp.where(beside, jnp.where(low_side, turn(face, -1, 1), face), 0.0)
        ground = jnp.where(outer, 1.0 + 0.5 * k, 1.0)

        def keep(index, a, b, mine=mine):
            ay[index, mine, :] = a
            by[index, mine, :] = b

        inverse, (profile,) = reduce_matrix(low, ground + link, [link], Y_STEPS, 1, keep)
        qy[mine, :] = jnp.where(terminal, 0.0, inverse)
        profile = jnp.where(terminal, 1.0, profile)
        hy[mine, :] = profile
        total = jnp.sum(profile * ground, axis=1, keepdims=True)
        rim = jnp.sum(jnp.where(terminal, k, 0.0), axis=1, keepdims=True)
        edge[mine, :] = jnp.where(wide == 0, total, jnp.where(wide == 1, rim, 0.0))
    copies[1].wait()
    copies[2].wait()


def source_kernel(fields, fields_far, vertical, vertical_far, kappa, halo, h1, h2, parts, source, sums, message):
    gx = lax.axis_index("gx")
    here = fields[...]
    v = vertical[...]
    s = here + (v + vertical_far[...]) * 0.5 * (fields_far[...] - here) - v * 0.5 * here
    source[...] = s
    for f in range(2):
        mine = slice(f * ROWS, (f + 1) * ROWS)
        first = dense(jnp.sum(h1[mine, :] * s[mine, :], axis=0, keepdims=True))
        last = dense(jnp.sum(h2[mine, :] * s[mine, :], axis=0, keepdims=True))
        west = (dense(kappa[f * ROWS : f * ROWS + 1, :]) + dense(halo[f * ROWS + ROWS - 1 : f * ROWS + ROWS, :])) * 0.5
        east = dense(kappa[f * ROWS + ROWS - 1 : f * ROWS + ROWS, :]) * 0.5
        g, s_first, s_last = parts[0, f], parts[1, f], parts[2, f]
        inverse = 1.0 / (west + g + s_first)
        a = west * inverse
        b = g * inverse
        sums[0, f] = a
        sums[1, f] = b
        sums[2, f] = first * inverse
        element = (
            a * g,
            a * s_first,
            jnp.where(gx == 63, s_last + east, s_last) + b * s_first,
            a * first,
            last + b * first,
        )
        for n, value in enumerate(element):
            for j in range(4):
                message[2 * j + f, n] = value


def local_x_kernel(source, ax, bx, qx, out):
    half = 512
    for f in range(2):
        mine = pl.ds(f * ROWS, ROWS)
        for c in range(COLS // half):
            cols = pl.ds(c * half, half)
            r = source[mine, cols]
            r = reduce_right(r, X_STEPS, 0, lambda i: (ax[i, mine, cols], bx[i, mine, cols]))
            out[mine, cols] = r * qx[mine, cols]


def slab_kernel(got, message, chain):
    g, sl, sr, rl, rr = (got[0, n] for n in range(5))
    for k in range(7):
        g2, sl2, sr2, rl2, rr2 = (got[k + 1, n] for n in range(5))
        s = sr + sl2
        r = rr + rl2
        inverse = 1.0 / (g + g2 + s)
        a = g * inverse
        b = g2 * inverse
        chain[k, 0] = a
        chain[k, 1] = b
        chain[k, 2] = r * inverse
        sl = sl + a * s
        rl = rl + a * r
        sr = sr2 + b * s
        rr = rr2 + b * r
        g = a * g2
    for n, value in enumerate((g, sl, sr, rl, rr)):
        for j in range(8):
            message[j, n] = value


def ends_kernel(got, chain, mine, other):
    gx = lax.axis_index("gx")
    slab = gx // 8
    seat = gx % 8
    zero = jnp.zeros((8, 128), F32)
    conduct = got[0, 0] + got[0, 2]
    right = got[0, 4]
    ratios, offsets = [], []
    for k in range(7):
        conduct = conduct + got[k + 1, 1]
        right = right + got[k + 1, 3]
        inverse = 1.0 / (conduct + got[k + 1, 0])
        f = got[k + 1, 0] * inverse
        ratios.append(f)
        offsets.append(right * inverse)
        conduct = got[k + 1, 2] + f * conduct
        right = got[k + 1, 4] + f * right
    value = right / conduct
    values = [value]
    for k in range(6, -1, -1):
        value = ratios[k] * value + offsets[k]
        values.append(value)
    values = [zero] + values[::-1]
    left, last = zero, zero
    for z in range(8):
        left = jnp.where(slab == z, values[z], left)
        last = jnp.where(slab == z, values[z + 1], last)
    nodes = [last]
    for k in range(6, -1, -1):
        nodes.append(chain[k, 0] * left + chain[k, 1] * nodes[-1] + chain[k, 2])
    nodes = [left] + nodes[::-1]
    even = seat % 2 == 0
    trio = [zero, zero, zero]
    for j in range(4):
        for n in range(3):
            trio[n] = jnp.where(seat // 2 == j, nodes[2 * j + n], trio[n])
    mine[0] = jnp.where(even, trio[0], trio[1])
    mine[1] = jnp.where(even, trio[1], trio[2])
    other[0] = jnp.where(even, trio[1], trio[0])
    other[1] = jnp.where(even, trio[2], trio[1])


def section_kernel(mine, other, sums, local, h1, h2, hy, edge, section, message):
    core = lax.axis_index("gx") % 2
    wide = lax.broadcasted_iota(jnp.int32, (8, 128), 1)
    for f in range(2):
        left = jnp.where(core == f, mine[0], other[0])
        last = jnp.where(core == f, mine[1], other[1])
        first = sums[0, f] * left + sums[1, f] * last + sums[2, f]
        rows = slice(f * ROWS, (f + 1) * ROWS)
        s = local[rows, :] + h1[rows, :] * natural(first, ROWS) + h2[rows, :] * natural(last, ROWS)
        section[rows, :] = s
        total = jnp.sum(hy[rows, :] * s, axis=1, keepdims=True)
        for g in range(2):
            part = slice(f * ROWS + g * 8, f * ROWS + g * 8 + 8)
            message[part, :] = jnp.where(wide == 2, total[g * 8 : g * 8 + 8], edge[part, :])


def local_y_kernel(section, ay, by, qy, out):
    for g in range(ALL // 8):
        mine = pl.ds(g * 8, 8)
        r = section[mine, :]
        r = reduce_right(r, Y_STEPS, 1, lambda i: (ay[i, mine, :], by[i, mine, :]))
        out[mine, :] = r * qy[mine, :]


def output_kernel(message, far, local, hy, out):
    e, k, r = (message[:, n : n + 1] for n in range(3))
    e2, k2, r2 = (far[:, n : n + 1] for n in range(3))
    c = (k + k2) * 0.5
    value = ((e2 + c) * r + c * r2) / (e * e2 + c * (e + e2))
    out[...] = local[...] + hy[...] * value


def call(kernel, outs, specs, flops=0, size=0, scratch=()):
    return pl.pallas_call(
        kernel,
        out_shape=outs,
        in_specs=specs,
        out_specs=jax.tree.map(lambda _: VMEM, outs),
        scratch_shapes=scratch,
        compiler_params=PARAMS,
        cost_estimate=pl.CostEstimate(flops=flops, bytes_accessed=size, transcendentals=0),
    )


PLANE_GROUPS = [[8 * a + b for b in range(8)] for a in range(8)]
SLAB_GROUPS = [[8 * b + a for b in range(8)] for a in range(8)]


def local(fields, kappa, vertical):
    grid = (ALL, COLS)
    swap = [(0, 1), (1, 0)]
    fields_far = lax.ppermute(fields, "gz", swap)
    vertical_far = lax.ppermute(vertical, "gz", swap)
    halo = lax.ppermute(kappa, "gx", [(i, i + 1) for i in range(63)])
    full = shape(*grid)
    fields_here, vertical_here, kappa_here, ax, bx, qx, h1, h2, ay, by, qy, hy, parts, edge = call(
        factor_kernel,
        (
            full, full, full,
            shape(4, *grid), shape(4, *grid), full, full, full,
            shape(10, *grid), shape(10, *grid), full, full,
            shape(3, 2, 8, 128), shape(ALL, 128),
        ),
        [HBM] * 3,
        flops=20_000_000,
        size=4_000_000,
        scratch=[pltpu.SemaphoreType.DMA((3,))],
    )(*(pltpu.with_memory_space_constraint(x.reshape(grid), pltpu.HBM) for x in (fields, vertical, kappa)))
    source, sums, message = call(
        source_kernel,
        (full, shape(3, 2, 8, 128), shape(8, 5, 8, 128)),
        [VMEM] * 9,
    )(
        fields_here, fields_far.reshape(grid), vertical_here, vertical_far.reshape(grid),
        kappa_here, halo.reshape(grid), h1, h2, parts,
    )
    got = lax.all_to_all(message, "gx", 0, 0, axis_index_groups=PLANE_GROUPS, tiled=True)
    local_x = call(local_x_kernel, full, [VMEM] * 4, flops=1_000_000, size=1_000_000)(source, ax, bx, qx)
    message, chain = call(
        slab_kernel, (shape(8, 5, 8, 128), shape(7, 3, 8, 128)), [VMEM]
    )(got)
    got = lax.all_to_all(message, "gx", 0, 0, axis_index_groups=SLAB_GROUPS, tiled=True)
    mine, other = call(
        ends_kernel, (shape(2, 8, 128), shape(2, 8, 128)), [VMEM, VMEM]
    )(got, chain)
    other = lax.ppermute(other, "gx", [(i, i ^ 1) for i in range(64)])
    section, message = call(
        section_kernel, (full, shape(ALL, 128)), [VMEM] * 8
    )(mine, other, sums, local_x, h1, h2, hy, edge)
    far = lax.ppermute(message, "gy", swap)
    local_y = call(local_y_kernel, full, [VMEM] * 4, flops=4_000_000, size=3_000_000)(section, ay, by, qy)
    out = call(output_kernel, full, [VMEM] * 4)(message, far, local_y, hy)
    return out.reshape(fields.shape)


def solution(mesh):
    spec = P(None, "gz", "gx", "gy")
    return jax.shard_map(
        local, mesh=mesh, in_specs=(spec, spec, spec), out_specs=spec, check_vma=False
    )
```

```python
import functools

import jax
import jax.numpy as jnp
from jax import lax
from jax.experimental import pallas as pl
from jax.experimental.pallas import tpu as pltpu
from jax.sharding import PartitionSpec as P

F32 = jnp.float32
ROWS = 16
COLS = 1024
ALL = 2 * ROWS
VMEM = pl.BlockSpec(memory_space=pltpu.VMEM)
HBM = pl.BlockSpec(memory_space=pltpu.HBM)
X_STEPS = (1, 2, 4, 8)
Y_STEPS = (1, 2, 4, 8, 16, 32, 64, 128, 256, 512)
PARAMS = pltpu.CompilerParams(vmem_limit_bytes=40 * 1024 * 1024)


def shape(*dims):
    return jax.ShapeDtypeStruct(dims, F32)


def turn(x, k, axis):
    n = x.shape[axis]
    k = k % n
    unit = 128 if axis == 1 else 8
    if k == 0:
        return x
    if k % unit == 0:
        low = lax.slice_in_dim(x, n - k, n, axis=axis)
        high = lax.slice_in_dim(x, 0, n - k, axis=axis)
        return jnp.concatenate([low, high], axis=axis)
    return pltpu.roll(x, k, axis)


def reduce_matrix(low, excess, rights, steps, axis, keep):
    for index, k in enumerate(steps):
        high = turn(low, -k, axis)
        inverse = 1.0 / (low + high + excess)
        a = low * turn(inverse, k, axis)
        b = high * turn(inverse, -k, axis)
        keep(index, a, b)
        excess = excess + a * turn(excess, k, axis) + b * turn(excess, -k, axis)
        rights = [r + a * turn(r, k, axis) + b * turn(r, -k, axis) for r in rights]
        low = a * turn(low, k, axis)
    inverse = 1.0 / excess
    return inverse, [r * inverse for r in rights]


def reduce_right(right, steps, axis, load):
    for index, k in enumerate(steps):
        a, b = load(index)
        right = right + a * turn(right, k, axis) + b * turn(right, -k, axis)
    return right


def dense(row):
    return jnp.concatenate([row[:, 128 * i : 128 * (i + 1)] for i in range(8)], axis=0)


def natural(tile, rows):
    return jnp.concatenate(
        [jnp.broadcast_to(tile[i : i + 1, :], (rows, 128)) for i in range(8)], axis=1
    )


def factor_x_kernel(
    fields_arg, vertical_arg, kappa_arg, fields, vertical, kappa, ax, bx, qx, h1, h2, parts, done
):
    pairs = ((kappa_arg, kappa), (fields_arg, fields), (vertical_arg, vertical))
    copies = [pltpu.make_async_copy(a, b, done.at[n]) for n, (a, b) in enumerate(pairs)]
    for copy in copies:
        copy.start()
    copies[0].wait()
    half = 512
    rows = lax.broadcasted_iota(jnp.int32, (ROWS, half), 0)
    for f in range(2):
        mine = pl.ds(f * ROWS, ROWS)
        for c in range(COLS // half):
            cols = pl.ds(c * half, half)
            k = kappa[mine, cols]
            face = (k + turn(k, 1, 0)) * 0.5
            low = jnp.where((rows >= 2) & (rows <= 14), face, 0.0)
            first = jnp.where(rows == 1, face, 0.0)
            last = jnp.where(rows == 14, turn(face, -1, 0), 0.0)

            def keep(index, a, b, mine=mine, cols=cols):
                ax[index, mine, cols] = a
                bx[index, mine, cols] = b

            inverse, (one, two) = reduce_matrix(
                low, 1.0 + first + last, [first, last], X_STEPS, 0, keep
            )
            qx[mine, cols] = jnp.where((rows >= 1) & (rows <= 14), inverse, 0.0)
            one = jnp.where(rows == 0, 1.0, one)
            two = jnp.where(rows == ROWS - 1, 1.0, two)
            h1[mine, cols] = one
            h2[mine, cols] = two
            for n, row in enumerate(
                (
                    jnp.sum(first * two, axis=0, keepdims=True),
                    jnp.sum(one, axis=0, keepdims=True),
                    jnp.sum(two, axis=0, keepdims=True),
                )
            ):
                for i in range(half // 128):
                    parts[n, f, pl.ds(c * (half // 128) + i, 1), :] = row[:, 128 * i : 128 * (i + 1)]
    copies[1].wait()
    copies[2].wait()


def factor_y_kernel(kappa, after, ay, by, qy, hy, edge):
    del after
    gy = lax.axis_index("gy")
    lanes = lax.broadcasted_iota(jnp.int32, (8, COLS), 1)
    wide = lax.broadcasted_iota(jnp.int32, (8, 128), 1)
    low_side = gy == 0
    terminal = lanes == jnp.where(low_side, COLS - 1, 0)
    cut = lanes == jnp.where(low_side, COLS - 1, 1)
    outer = lanes == jnp.where(low_side, 0, COLS - 1)
    beside = lanes == jnp.where(low_side, COLS - 2, 1)
    for g in range(ALL // 8):
        mine = pl.ds(g * 8, 8)
        k = kappa[mine, :]
        face = (k + turn(k, 1, 1)) * 0.5
        low = jnp.where((lanes == 0) | cut, 0.0, face)
        link = jnp.where(beside, jnp.where(low_side, turn(face, -1, 1), face), 0.0)
        ground = jnp.where(outer, 1.0 + 0.5 * k, 1.0)

        def keep(index, a, b, mine=mine):
            ay[index, mine, :] = a
            by[index, mine, :] = b

        inverse, (profile,) = reduce_matrix(low, ground + link, [link], Y_STEPS, 1, keep)
        qy[mine, :] = jnp.where(terminal, 0.0, inverse)
        profile = jnp.where(terminal, 1.0, profile)
        hy[mine, :] = profile
        total = jnp.sum(profile * ground, axis=1, keepdims=True)
        rim = jnp.sum(jnp.where(terminal, k, 0.0), axis=1, keepdims=True)
        edge[mine, :] = jnp.where(wide == 0, total, jnp.where(wide == 1, rim, 0.0))


def source_kernel(fields, fields_far, vertical, vertical_far, kappa, halo, h1, h2, parts, source, sums, keep, send):
    gx = lax.axis_index("gx")
    even = gx % 2 == 0
    elements = []
    here = fields[...]
    v = vertical[...]
    s = here + (v + vertical_far[...]) * 0.5 * (fields_far[...] - here) - v * 0.5 * here
    source[...] = s
    for f in range(2):
        mine = slice(f * ROWS, (f + 1) * ROWS)
        first = dense(jnp.sum(h1[mine, :] * s[mine, :], axis=0, keepdims=True))
        last = dense(jnp.sum(h2[mine, :] * s[mine, :], axis=0, keepdims=True))
        west = (dense(kappa[f * ROWS : f * ROWS + 1, :]) + dense(halo[f * ROWS + ROWS - 1 : f * ROWS + ROWS, :])) * 0.5
        east = dense(kappa[f * ROWS + ROWS - 1 : f * ROWS + ROWS, :]) * 0.5
        g, s_first, s_last = parts[0, f], parts[1, f], parts[2, f]
        inverse = 1.0 / (west + g + s_first)
        a = west * inverse
        b = g * inverse
        sums[0, f] = a
        sums[1, f] = b
        sums[2, f] = first * inverse
        element = (
            a * g,
            a * s_first,
            jnp.where(gx == 63, s_last + east, s_last) + b * s_first,
            a * first,
            last + b * first,
        )
        elements.append(element)
    for n, (one, two) in enumerate(zip(*elements)):
        keep[n] = jnp.where(even, one, two)
        send[n] = jnp.where(even, two, one)


def local_x_kernel(source, ax, bx, qx, out):
    half = 512
    for f in range(2):
        mine = pl.ds(f * ROWS, ROWS)
        for c in range(COLS // half):
            cols = pl.ds(c * half, half)
            r = source[mine, cols]
            r = reduce_right(r, X_STEPS, 0, lambda i: (ax[i, mine, cols], bx[i, mine, cols]))
            out[mine, cols] = r * qx[mine, cols]


def merge(one, two):
    g, sl, sr, rl, rr = one
    g2, sl2, sr2, rl2, rr2 = two
    s = sr + sl2
    r = rr + rl2
    inverse = 1.0 / (g + g2 + s)
    a = g * inverse
    b = g2 * inverse
    return (a * g2, sl + a * s, sr2 + b * s, rl + a * r, rr2 + b * r), (a, b, r * inverse)


def load(ref):
    return tuple(ref[n] for n in range(5))


def chip_kernel(keep, got, chip, middle):
    even = lax.axis_index("gx") % 2 == 0
    mine, other = load(keep), load(got)
    first = [jnp.where(even, m, o) for m, o in zip(mine, other)]
    second = [jnp.where(even, o, m) for m, o in zip(mine, other)]
    element, node = merge(first, second)
    for n, value in enumerate(element):
        chip[n] = value
    for n, value in enumerate(node):
        middle[n] = value


def slab_kernel(chip, far1, far2, far3, middle, after, message, nodes):
    del after
    y = lax.axis_index("gx") // 2 % 4
    arrived = [load(chip), load(far1), load(far2), load(far3)]
    chips = []
    for m in range(4):
        chosen = arrived[0]
        for shift in range(1, 4):
            here = (y + shift) % 4 == m
            chosen = [jnp.where(here, a, c) for a, c in zip(arrived[shift], chosen)]
        chips.append(chosen)
    element = chips[0]
    inner = []
    for m in range(1, 4):
        element, node = merge(element, chips[m])
        inner.append(node)
    for n, value in enumerate(element):
        for j in range(8):
            message[j, n] = value
    zero, one = jnp.zeros((8, 128), F32), jnp.ones((8, 128), F32)
    ends = [(zero, one, zero)]
    for a, b, c in inner[::-1]:
        a2, b2, c2 = ends[-1]
        ends.append((a + b * a2, b * b2, c + b * c2))
    ends.append((one, zero, zero))
    ends = ends[::-1]
    west, east = ends[0], ends[1]
    for m in range(1, 4):
        west = [jnp.where(y == m, e, w) for e, w in zip(ends[m], west)]
        east = [jnp.where(y == m, e, w) for e, w in zip(ends[m + 1], east)]
    a, b, c = load3(middle)
    half = [a * w + b * e for w, e in zip(west, east)]
    half[2] = half[2] + c
    for n, trio in enumerate((west, half, east)):
        for m in range(3):
            nodes[n, m] = trio[m]


def load3(ref):
    return tuple(ref[n] for n in range(3))


def ends_kernel(got, nodes, mine, other):
    gx = lax.axis_index("gx")
    slab = gx // 8
    even = gx % 2 == 0
    zero = jnp.zeros((8, 128), F32)
    conduct = got[0, 0] + got[0, 2]
    right = got[0, 4]
    ratios, offsets = [], []
    for k in range(7):
        conduct = conduct + got[k + 1, 1]
        right = right + got[k + 1, 3]
        inverse = 1.0 / (conduct + got[k + 1, 0])
        f = got[k + 1, 0] * inverse
        ratios.append(f)
        offsets.append(right * inverse)
        conduct = got[k + 1, 2] + f * conduct
        right = got[k + 1, 4] + f * right
    value = right / conduct
    values = [value]
    for k in range(6, -1, -1):
        value = ratios[k] * value + offsets[k]
        values.append(value)
    values = [zero] + values[::-1]
    left, last = zero, zero
    for z in range(8):
        left = jnp.where(slab == z, values[z], left)
        last = jnp.where(slab == z, values[z + 1], last)
    trio = [nodes[n, 0] * left + nodes[n, 1] * last + nodes[n, 2] for n in range(3)]
    mine[0] = jnp.where(even, trio[0], trio[1])
    mine[1] = jnp.where(even, trio[1], trio[2])
    other[0] = jnp.where(even, trio[1], trio[0])
    other[1] = jnp.where(even, trio[2], trio[1])


def section_kernel(mine, other, sums, local, h1, h2, hy, edge, section, message):
    core = lax.axis_index("gx") % 2
    wide = lax.broadcasted_iota(jnp.int32, (8, 128), 1)
    for f in range(2):
        left = jnp.where(core == f, mine[0], other[0])
        last = jnp.where(core == f, mine[1], other[1])
        first = sums[0, f] * left + sums[1, f] * last + sums[2, f]
        rows = slice(f * ROWS, (f + 1) * ROWS)
        s = local[rows, :] + h1[rows, :] * natural(first, ROWS) + h2[rows, :] * natural(last, ROWS)
        section[rows, :] = s
        total = jnp.sum(hy[rows, :] * s, axis=1, keepdims=True)
        for g in range(2):
            part = slice(f * ROWS + g * 8, f * ROWS + g * 8 + 8)
            message[part, :] = jnp.where(wide == 2, total[g * 8 : g * 8 + 8], edge[part, :])


def local_y_kernel(section, ay, by, qy, out):
    for g in range(ALL // 8):
        mine = pl.ds(g * 8, 8)
        r = section[mine, :]
        r = reduce_right(r, Y_STEPS, 1, lambda i: (ay[i, mine, :], by[i, mine, :]))
        out[mine, :] = r * qy[mine, :]


def output_kernel(message, far, local, hy, out):
    e, k, r = (message[:, n : n + 1] for n in range(3))
    e2, k2, r2 = (far[:, n : n + 1] for n in range(3))
    c = (k + k2) * 0.5
    value = ((e2 + c) * r + c * r2) / (e * e2 + c * (e + e2))
    out[...] = local[...] + hy[...] * value


def call(kernel, outs, specs, flops=0, size=0, scratch=()):
    return pl.pallas_call(
        kernel,
        out_shape=outs,
        in_specs=specs,
        out_specs=jax.tree.map(lambda _: VMEM, outs),
        scratch_shapes=scratch,
        compiler_params=PARAMS,
        cost_estimate=pl.CostEstimate(flops=flops, bytes_accessed=size, transcendentals=0),
    )


SLAB_GROUPS = [[8 * b + a for b in range(8)] for a in range(8)]
CORES = [(i, i ^ 1) for i in range(64)]


def chips_on(shift):
    return [(i // 8 * 8 + (i + 2 * shift) % 8, i) for i in range(64)]


def local(fields, kappa, vertical):
    grid = (ALL, COLS)
    swap = [(0, 1), (1, 0)]
    fields_far = lax.ppermute(fields, "gz", swap)
    vertical_far = lax.ppermute(vertical, "gz", swap)
    halo = lax.ppermute(kappa, "gx", [(i, i + 1) for i in range(63)])
    full = shape(*grid)
    half = shape(5, 8, 128)
    fields_here, vertical_here, kappa_here, ax, bx, qx, h1, h2, parts = call(
        factor_x_kernel,
        (full, full, full, shape(4, *grid), shape(4, *grid), full, full, full, shape(3, 2, 8, 128)),
        [HBM] * 3,
        flops=4_000_000,
        size=2_000_000,
        scratch=[pltpu.SemaphoreType.DMA((3,))],
    )(*(pltpu.with_memory_space_constraint(x.reshape(grid), pltpu.HBM) for x in (fields, vertical, kappa)))
    source, sums, keep, send = call(
        source_kernel, (full, shape(3, 2, 8, 128), half, half), [VMEM] * 9
    )(
        fields_here, fields_far.reshape(grid), vertical_here, vertical_far.reshape(grid),
        kappa_here, halo.reshape(grid), h1, h2, parts,
    )
    got = lax.ppermute(send, "gx", CORES)
    local_x = call(local_x_kernel, full, [VMEM] * 4, flops=1_000_000, size=1_000_000)(source, ax, bx, qx)
    chip, middle = call(chip_kernel, (half, shape(3, 8, 128)), [VMEM] * 2)(keep, got)
    far = [lax.ppermute(chip, "gx", chips_on(shift)) for shift in (2, 1, 3)]
    ay, by, qy, hy, edge = call(
        factor_y_kernel,
        (shape(10, *grid), shape(10, *grid), full, full, shape(ALL, 128)),
        [VMEM] * 2,
        flops=20_000_000,
        size=4_000_000,
    )(kappa_here, middle)
    message, nodes = call(
        slab_kernel, (shape(8, 5, 8, 128), shape(3, 3, 8, 128)), [VMEM] * 6
    )(chip, far[1], far[0], far[2], middle, edge)
    got = lax.all_to_all(message, "gx", 0, 0, axis_index_groups=SLAB_GROUPS, tiled=True)
    mine, other = call(
        ends_kernel, (shape(2, 8, 128), shape(2, 8, 128)), [VMEM, VMEM]
    )(got, nodes)
    other = lax.ppermute(other, "gx", CORES)
    section, message = call(
        section_kernel, (full, shape(ALL, 128)), [VMEM] * 8
    )(mine, other, sums, local_x, h1, h2, hy, edge)
    far = lax.ppermute(message, "gy", swap)
    local_y = call(local_y_kernel, full, [VMEM] * 4, flops=4_000_000, size=3_000_000)(section, ay, by, qy)
    out = call(output_kernel, full, [VMEM] * 4)(message, far, local_y, hy)
    return out.reshape(fields.shape)


def solution(mesh):
    spec = P(None, "gz", "gx", "gy")
    return jax.shard_map(
        local, mesh=mesh, in_specs=(spec, spec, spec), out_specs=spec, check_vma=False
    )
```

```python
import functools

import jax
import jax.numpy as jnp
from jax import lax
from jax.experimental import pallas as pl
from jax.experimental.pallas import tpu as pltpu
from jax.sharding import PartitionSpec as P

F32 = jnp.float32
ROWS = 16
COLS = 1024
ALL = 2 * ROWS
VMEM = pl.BlockSpec(memory_space=pltpu.VMEM)
HBM = pl.BlockSpec(memory_space=pltpu.HBM)
X_STEPS = (1, 2, 4, 8)
Y_STEPS = (1, 2, 4, 8, 16, 32, 64, 128, 256, 512)
PARAMS = pltpu.CompilerParams(vmem_limit_bytes=40 * 1024 * 1024)


def shape(*dims):
    return jax.ShapeDtypeStruct(dims, F32)


def turn(x, k, axis):
    n = x.shape[axis]
    k = k % n
    unit = 128 if axis == 1 else 8
    if k == 0:
        return x
    if k % unit == 0:
        low = lax.slice_in_dim(x, n - k, n, axis=axis)
        high = lax.slice_in_dim(x, 0, n - k, axis=axis)
        return jnp.concatenate([low, high], axis=axis)
    return pltpu.roll(x, k, axis)


def turn_lines(x, k):
    lanes = lax.broadcasted_iota(jnp.int32, (1, 128), 1)

    def blocks(pair, n):
        if n == 4:
            return pair[::-1]
        turned = [pltpu.roll(p, 32 * n % 128, 1) for p in pair]
        over = lanes < 32 * n if n > 0 else lanes >= 128 + 32 * n
        return [jnp.where(over, turned[1 - h], turned[h]) for h in range(2)]

    pair = [x[:128], x[128:]]
    size = abs(k)
    if size >= 128:
        pair = blocks(pair, 4 if size == 512 else k // 128)
    elif size >= 8:
        if k > 0:
            moved = blocks([p[128 - k :] for p in pair], 1)
            pair = [jnp.concatenate([m, p[: 128 - k]], axis=0) for m, p in zip(moved, pair)]
        else:
            moved = blocks([p[:size] for p in pair], -1)
            pair = [jnp.concatenate([p[size:], m], axis=0) for m, p in zip(moved, pair)]
    else:
        rows = lax.broadcasted_iota(jnp.int32, (8, 128), 0)
        turned = [pltpu.roll(p, k % 128, 0) for p in pair]
        if k > 0:
            ends = [t[:8] for t in turned]
            ends = [jnp.where(rows < k, m, e) for m, e in zip(blocks(ends, 1), ends)]
            pair = [jnp.concatenate([e, t[8:]], axis=0) for e, t in zip(ends, turned)]
        else:
            ends = [t[120:] for t in turned]
            ends = [jnp.where(rows >= 8 + k, m, e) for m, e in zip(blocks(ends, -1), ends)]
            pair = [jnp.concatenate([t[:120], e], axis=0) for e, t in zip(ends, turned)]
    return jnp.concatenate(pair, axis=0)


def stand(x):
    tiles = [x[:, 128 * j : 128 * (j + 1)] for j in range(8)]
    return jnp.concatenate(
        [jnp.concatenate(tiles[4 * h : 4 * h + 4], axis=0).T for h in range(2)], axis=0
    )


def lie(x):
    tiles = [x[128 * h : 128 * (h + 1)].T for h in range(2)]
    return jnp.concatenate(
        [tiles[h][ALL * b : ALL * (b + 1)] for h in range(2) for b in range(4)], axis=1
    )


def turn_rows(x, k):
    return turn(x, k, 0)


def reduce_matrix(low, excess, rights, steps, move, keep):
    for index, k in enumerate(steps):
        high = move(low, -k)
        inverse = 1.0 / (low + high + excess)
        up = high * inverse
        down = low * inverse
        keep(index, up, down)
        excess = excess + move(up * excess, k) + move(down * excess, -k)
        rights = [r + move(up * r, k) + move(down * r, -k) for r in rights]
        low = move(up * low, k)
    inverse = 1.0 / excess
    return inverse, [r * inverse for r in rights]


def reduce_right(right, steps, move, load):
    for index, k in enumerate(steps):
        up, down = load(index)
        right = right + move(up * right, k) + move(down * right, -k)
    return right


def dense(row):
    return jnp.concatenate([row[:, 128 * i : 128 * (i + 1)] for i in range(8)], axis=0)


def natural(tile, rows):
    return jnp.concatenate(
        [jnp.broadcast_to(tile[i : i + 1, :], (rows, 128)) for i in range(8)], axis=1
    )


def input_kernel(fields_arg, vertical_arg, kappa_arg, fields, vertical, kappa, rim, done):
    pairs = ((kappa_arg, kappa), (fields_arg, fields), (vertical_arg, vertical))
    copies = [pltpu.make_async_copy(a, b, done.at[n]) for n, (a, b) in enumerate(pairs)]
    for copy in copies:
        copy.start()
    copies[0].wait()
    for f in range(2):
        rim[f] = dense(kappa[f * ROWS + ROWS - 1 : f * ROWS + ROWS, :])
    copies[1].wait()
    copies[2].wait()


def factor_x_kernel(kappa, ax, bx, qx, h1, h2, parts):
    half = 512
    rows = lax.broadcasted_iota(jnp.int32, (ROWS, half), 0)
    for f in range(2):
        mine = pl.ds(f * ROWS, ROWS)
        for c in range(COLS // half):
            cols = pl.ds(c * half, half)
            k = kappa[mine, cols]
            face = (k + turn(k, 1, 0)) * 0.5
            low = jnp.where((rows >= 2) & (rows <= 14), face, 0.0)
            first = jnp.where(rows == 1, face, 0.0)
            last = jnp.where(rows == 14, turn(face, -1, 0), 0.0)

            def keep(index, a, b, mine=mine, cols=cols):
                ax[index, mine, cols] = a
                bx[index, mine, cols] = b

            inverse, (one, two) = reduce_matrix(
                low, 1.0 + first + last, [first, last], X_STEPS, turn_rows, keep
            )
            qx[mine, cols] = jnp.where((rows >= 1) & (rows <= 14), inverse, 0.0)
            one = jnp.where(rows == 0, 1.0, one)
            two = jnp.where(rows == ROWS - 1, 1.0, two)
            h1[mine, cols] = one
            h2[mine, cols] = two
            for n, row in enumerate(
                (
                    jnp.sum(first * two, axis=0, keepdims=True),
                    jnp.sum(one, axis=0, keepdims=True),
                    jnp.sum(two, axis=0, keepdims=True),
                )
            ):
                for i in range(half // 128):
                    parts[n, f, pl.ds(c * (half // 128) + i, 1), :] = row[:, 128 * i : 128 * (i + 1)]


def factor_y_kernel(kappa, ay, by, qy, hy, edge):
    gy = lax.axis_index("gy")
    low_side = gy == 0
    end = jnp.where(low_side, COLS - 1, 0)
    start = COLS - 1 - end
    beside = jnp.where(low_side, COLS - 2, 1)
    cut = jnp.where(low_side, COLS - 1, 1)
    k = stand(kappa[...])
    row = lax.broadcasted_iota(jnp.int32, (256, 128), 0)
    lane = lax.broadcasted_iota(jnp.int32, (256, 128), 1)
    y = row // 128 * 512 + lane // 32 * 128 + row % 128
    face = (k + turn_lines(k, 1)) * 0.5
    low = jnp.where((y == 0) | (y == cut), 0.0, face)
    link = jnp.where(y == beside, jnp.where(low_side, turn_lines(face, -1), face), 0.0)
    ground = jnp.where(y == start, 1.0 + 0.5 * k, 1.0)

    def keep(index, up, down):
        ay[index] = up
        by[index] = down

    inverse, (profile,) = reduce_matrix(low, ground + link, [link], Y_STEPS, turn_lines, keep)
    qy[...] = jnp.where(y == end, 0.0, inverse)
    profile = lie(jnp.where(y == end, 1.0, profile))
    hy[...] = profile
    k = kappa[...]
    column = lax.broadcasted_iota(jnp.int32, (ALL, COLS), 1)
    total = jnp.sum(profile * jnp.where(column == start, 1.0 + 0.5 * k, 1.0), axis=1, keepdims=True)
    rim = jnp.sum(jnp.where(column == end, k, 0.0), axis=1, keepdims=True)
    wide = lax.broadcasted_iota(jnp.int32, (ALL, 128), 1)
    edge[...] = jnp.where(wide == 0, total, jnp.where(wide == 1, rim, 0.0))


def source_kernel(fields, fields_far, vertical, vertical_far, kappa, halo, h1, h2, parts, after, source, sums, keep, send):
    del after
    gx = lax.axis_index("gx")
    even = gx % 2 == 0
    elements = []
    here = fields[...]
    v = vertical[...]
    s = here + (v + vertical_far[...]) * 0.5 * (fields_far[...] - here) - v * 0.5 * here
    source[...] = s
    for f in range(2):
        mine = slice(f * ROWS, (f + 1) * ROWS)
        first = dense(jnp.sum(h1[mine, :] * s[mine, :], axis=0, keepdims=True))
        last = dense(jnp.sum(h2[mine, :] * s[mine, :], axis=0, keepdims=True))
        west = (dense(kappa[f * ROWS : f * ROWS + 1, :]) + halo[f]) * 0.5
        east = dense(kappa[f * ROWS + ROWS - 1 : f * ROWS + ROWS, :]) * 0.5
        g, s_first, s_last = parts[0, f], parts[1, f], parts[2, f]
        inverse = 1.0 / (west + g + s_first)
        a = west * inverse
        b = g * inverse
        sums[0, f] = a
        sums[1, f] = b
        sums[2, f] = first * inverse
        element = (
            a * g,
            a * s_first,
            jnp.where(gx == 63, s_last + east, s_last) + b * s_first,
            a * first,
            last + b * first,
        )
        elements.append(element)
    for n, (one, two) in enumerate(zip(*elements)):
        keep[n] = jnp.where(even, one, two)
        send[n] = jnp.where(even, two, one)


def local_x_kernel(source, ax, bx, qx, out):
    half = 512
    for f in range(2):
        mine = pl.ds(f * ROWS, ROWS)
        for c in range(COLS // half):
            cols = pl.ds(c * half, half)
            r = source[mine, cols]
            r = reduce_right(r, X_STEPS, turn_rows, lambda i: (ax[i, mine, cols], bx[i, mine, cols]))
            out[mine, cols] = r * qx[mine, cols]


def merge(one, two):
    g, sl, sr, rl, rr = one
    g2, sl2, sr2, rl2, rr2 = two
    s = sr + sl2
    r = rr + rl2
    inverse = 1.0 / (g + g2 + s)
    a = g * inverse
    b = g2 * inverse
    return (a * g2, sl + a * s, sr2 + b * s, rl + a * r, rr2 + b * r), (a, b, r * inverse)


def load(ref):
    return tuple(ref[n] for n in range(5))


def chip_kernel(keep, got, chip, middle):
    even = lax.axis_index("gx") % 2 == 0
    mine, other = load(keep), load(got)
    first = [jnp.where(even, m, o) for m, o in zip(mine, other)]
    second = [jnp.where(even, o, m) for m, o in zip(mine, other)]
    element, node = merge(first, second)
    for n, value in enumerate(element):
        chip[n] = value
    for n, value in enumerate(node):
        middle[n] = value


def slab_kernel(chip, far1, far2, far3, middle, message, nodes):
    y = lax.axis_index("gx") // 2 % 4
    arrived = [load(chip), load(far1), load(far2), load(far3)]
    chips = []
    for m in range(4):
        chosen = arrived[0]
        for shift in range(1, 4):
            here = (y + shift) % 4 == m
            chosen = [jnp.where(here, a, c) for a, c in zip(arrived[shift], chosen)]
        chips.append(chosen)
    element = chips[0]
    inner = []
    for m in range(1, 4):
        element, node = merge(element, chips[m])
        inner.append(node)
    for n, value in enumerate(element):
        for j in range(8):
            message[j, n] = value
    zero, one = jnp.zeros((8, 128), F32), jnp.ones((8, 128), F32)
    ends = [(zero, one, zero)]
    for a, b, c in inner[::-1]:
        a2, b2, c2 = ends[-1]
        ends.append((a + b * a2, b * b2, c + b * c2))
    ends.append((one, zero, zero))
    ends = ends[::-1]
    west, east = ends[0], ends[1]
    for m in range(1, 4):
        west = [jnp.where(y == m, e, w) for e, w in zip(ends[m], west)]
        east = [jnp.where(y == m, e, w) for e, w in zip(ends[m + 1], east)]
    a, b, c = load3(middle)
    half = [a * w + b * e for w, e in zip(west, east)]
    half[2] = half[2] + c
    for n, trio in enumerate((west, half, east)):
        for m in range(3):
            nodes[n, m] = trio[m]


def load3(ref):
    return tuple(ref[n] for n in range(3))


def ends_kernel(got, nodes, mine, other):
    gx = lax.axis_index("gx")
    slab = gx // 8
    even = gx % 2 == 0
    zero = jnp.zeros((8, 128), F32)
    conduct = got[0, 0] + got[0, 2]
    right = got[0, 4]
    ratios, offsets = [], []
    for k in range(7):
        conduct = conduct + got[k + 1, 1]
        right = right + got[k + 1, 3]
        inverse = 1.0 / (conduct + got[k + 1, 0])
        f = got[k + 1, 0] * inverse
        ratios.append(f)
        offsets.append(right * inverse)
        conduct = got[k + 1, 2] + f * conduct
        right = got[k + 1, 4] + f * right
    value = right / conduct
    values = [value]
    for k in range(6, -1, -1):
        value = ratios[k] * value + offsets[k]
        values.append(value)
    values = [zero] + values[::-1]
    left, last = zero, zero
    for z in range(8):
        left = jnp.where(slab == z, values[z], left)
        last = jnp.where(slab == z, values[z + 1], last)
    trio = [nodes[n, 0] * left + nodes[n, 1] * last + nodes[n, 2] for n in range(3)]
    mine[0] = jnp.where(even, trio[0], trio[1])
    mine[1] = jnp.where(even, trio[1], trio[2])
    other[0] = jnp.where(even, trio[1], trio[0])
    other[1] = jnp.where(even, trio[2], trio[1])


def section_kernel(mine, other, sums, local, h1, h2, hy, edge, section, message):
    core = lax.axis_index("gx") % 2
    wide = lax.broadcasted_iota(jnp.int32, (8, 128), 1)
    for f in range(2):
        left = jnp.where(core == f, mine[0], other[0])
        last = jnp.where(core == f, mine[1], other[1])
        first = sums[0, f] * left + sums[1, f] * last + sums[2, f]
        rows = slice(f * ROWS, (f + 1) * ROWS)
        s = local[rows, :] + h1[rows, :] * natural(first, ROWS) + h2[rows, :] * natural(last, ROWS)
        section[rows, :] = s
        total = jnp.sum(hy[rows, :] * s, axis=1, keepdims=True)
        for g in range(2):
            part = slice(f * ROWS + g * 8, f * ROWS + g * 8 + 8)
            message[part, :] = jnp.where(wide == 2, total[g * 8 : g * 8 + 8], edge[part, :])


def local_y_kernel(section, ay, by, qy, out):
    r = stand(section[...])
    r = reduce_right(r, Y_STEPS, turn_lines, lambda i: (ay[i], by[i]))
    out[...] = lie(r * qy[...])


def output_kernel(message, far, local, hy, out):
    e, k, r = (message[:, n : n + 1] for n in range(3))
    e2, k2, r2 = (far[:, n : n + 1] for n in range(3))
    c = (k + k2) * 0.5
    value = ((e2 + c) * r + c * r2) / (e * e2 + c * (e + e2))
    out[...] = local[...] + hy[...] * value


def call(kernel, outs, specs, flops=0, size=0, scratch=()):
    return pl.pallas_call(
        kernel,
        out_shape=outs,
        in_specs=specs,
        out_specs=jax.tree.map(lambda _: VMEM, outs),
        scratch_shapes=scratch,
        compiler_params=PARAMS,
        cost_estimate=pl.CostEstimate(flops=flops, bytes_accessed=size, transcendentals=0),
    )


SLAB_GROUPS = [[8 * b + a for b in range(8)] for a in range(8)]
CORES = [(i, i ^ 1) for i in range(64)]


def chips_on(shift):
    return [(i // 8 * 8 + (i + 2 * shift) % 8, i) for i in range(64)]


def local(fields, kappa, vertical):
    grid = (ALL, COLS)
    swap = [(0, 1), (1, 0)]
    fields_far = lax.ppermute(fields, "gz", swap)
    vertical_far = lax.ppermute(vertical, "gz", swap)
    full = shape(*grid)
    half = shape(5, 8, 128)
    standing = shape(256, 128)
    fields_here, vertical_here, kappa_here, rim = call(
        input_kernel,
        (full, full, full, shape(2, 8, 128)),
        [HBM] * 3,
        flops=1_000_000,
        size=1_000_000,
        scratch=[pltpu.SemaphoreType.DMA((3,))],
    )(*(pltpu.with_memory_space_constraint(x.reshape(grid), pltpu.HBM) for x in (fields, vertical, kappa)))
    halo = lax.ppermute(rim, "gx", [(i, i + 1) for i in range(63)])
    ax, bx, qx, h1, h2, parts = call(
        factor_x_kernel,
        (shape(4, *grid), shape(4, *grid), full, full, full, shape(3, 2, 8, 128)),
        [VMEM],
        flops=4_000_000,
        size=2_000_000,
    )(kappa_here)
    ay, by, qy, hy, edge = call(
        factor_y_kernel,
        (shape(10, 256, 128), shape(10, 256, 128), standing, full, shape(ALL, 128)),
        [VMEM],
        flops=20_000_000,
        size=4_000_000,
    )(kappa_here)
    source, sums, keep, send = call(
        source_kernel, (full, shape(3, 2, 8, 128), half, half), [VMEM] * 10
    )(
        fields_here, fields_far.reshape(grid), vertical_here, vertical_far.reshape(grid),
        kappa_here, halo, h1, h2, parts, edge,
    )
    got = lax.ppermute(send, "gx", CORES)
    local_x = call(local_x_kernel, full, [VMEM] * 4, flops=1_000_000, size=1_000_000)(source, ax, bx, qx)
    chip, middle = call(chip_kernel, (half, shape(3, 8, 128)), [VMEM] * 2)(keep, got)
    far = [lax.ppermute(chip, "gx", chips_on(shift)) for shift in (2, 1, 3)]
    message, nodes = call(
        slab_kernel, (shape(8, 5, 8, 128), shape(3, 3, 8, 128)), [VMEM] * 5
    )(chip, far[1], far[0], far[2], middle)
    got = lax.all_to_all(message, "gx", 0, 0, axis_index_groups=SLAB_GROUPS, tiled=True)
    mine, other = call(
        ends_kernel, (shape(2, 8, 128), shape(2, 8, 128)), [VMEM, VMEM]
    )(got, nodes)
    other = lax.ppermute(other, "gx", CORES)
    section, message = call(
        section_kernel, (full, shape(ALL, 128)), [VMEM] * 8
    )(mine, other, sums, local_x, h1, h2, hy, edge)
    far = lax.ppermute(message, "gy", swap)
    local_y = call(local_y_kernel, full, [VMEM] * 4, flops=4_000_000, size=3_000_000)(section, ay, by, qy)
    out = call(output_kernel, full, [VMEM] * 4)(message, far, local_y, hy)
    return out.reshape(fields.shape)


def solution(mesh):
    spec = P(None, "gz", "gx", "gy")
    return jax.shard_map(
        local, mesh=mesh, in_specs=(spec, spec, spec), out_specs=spec, check_vma=False
    )
```

```python
import functools

import jax
import jax.numpy as jnp
from jax import lax
from jax.experimental import pallas as pl
from jax.experimental.pallas import tpu as pltpu
from jax.sharding import PartitionSpec as P

F32 = jnp.float32
ROWS = 16
COLS = 1024
ALL = 2 * ROWS
VMEM = pl.BlockSpec(memory_space=pltpu.VMEM)
HBM = pl.BlockSpec(memory_space=pltpu.HBM)
X_STEPS = (1, 2, 4, 8)
Y_STEPS = (1, 2, 4, 8, 16, 32, 64, 128, 256, 512)
PARAMS = pltpu.CompilerParams(vmem_limit_bytes=40 * 1024 * 1024)


def shape(*dims):
    return jax.ShapeDtypeStruct(dims, F32)


def turn(x, k, axis):
    n = x.shape[axis]
    k = k % n
    unit = 128 if axis == 1 else 8
    if k == 0:
        return x
    if k % unit == 0:
        low = lax.slice_in_dim(x, n - k, n, axis=axis)
        high = lax.slice_in_dim(x, 0, n - k, axis=axis)
        return jnp.concatenate([low, high], axis=axis)
    return pltpu.roll(x, k, axis)


def turn_lines(x, k):
    lanes = lax.broadcasted_iota(jnp.int32, (1, 128), 1)

    def blocks(pair, n):
        if n == 4:
            return pair[::-1]
        turned = [pltpu.roll(p, 32 * n % 128, 1) for p in pair]
        over = lanes < 32 * n if n > 0 else lanes >= 128 + 32 * n
        return [jnp.where(over, turned[1 - h], turned[h]) for h in range(2)]

    pair = [x[:128], x[128:]]
    size = abs(k)
    if size >= 128:
        pair = blocks(pair, 4 if size == 512 else k // 128)
    elif size >= 8:
        if k > 0:
            moved = blocks([p[128 - k :] for p in pair], 1)
            pair = [jnp.concatenate([m, p[: 128 - k]], axis=0) for m, p in zip(moved, pair)]
        else:
            moved = blocks([p[:size] for p in pair], -1)
            pair = [jnp.concatenate([p[size:], m], axis=0) for m, p in zip(moved, pair)]
    else:
        rows = lax.broadcasted_iota(jnp.int32, (8, 128), 0)
        turned = [pltpu.roll(p, k % 128, 0) for p in pair]
        if k > 0:
            ends = [t[:8] for t in turned]
            ends = [jnp.where(rows < k, m, e) for m, e in zip(blocks(ends, 1), ends)]
            pair = [jnp.concatenate([e, t[8:]], axis=0) for e, t in zip(ends, turned)]
        else:
            ends = [t[120:] for t in turned]
            ends = [jnp.where(rows >= 8 + k, m, e) for m, e in zip(blocks(ends, -1), ends)]
            pair = [jnp.concatenate([t[:120], e], axis=0) for e, t in zip(ends, turned)]
    return jnp.concatenate(pair, axis=0)


def stand(x):
    tiles = [x[:, 128 * j : 128 * (j + 1)] for j in range(8)]
    return jnp.concatenate(
        [jnp.concatenate(tiles[4 * h : 4 * h + 4], axis=0).T for h in range(2)], axis=0
    )


def lie(x):
    tiles = [x[128 * h : 128 * (h + 1)].T for h in range(2)]
    return jnp.concatenate(
        [tiles[h][ALL * b : ALL * (b + 1)] for h in range(2) for b in range(4)], axis=1
    )


def turn_rows(x, k):
    return turn(x, k, 0)


def reduce_matrix(low, excess, rights, steps, move, keep):
    for index, k in enumerate(steps):
        high = move(low, -k)
        inverse = 1.0 / (low + high + excess)
        up = high * inverse
        down = low * inverse
        keep(index, up, down)
        excess = excess + move(up * excess, k) + move(down * excess, -k)
        rights = [r + move(up * r, k) + move(down * r, -k) for r in rights]
        low = move(up * low, k)
    inverse = 1.0 / excess
    return inverse, [r * inverse for r in rights]


def reduce_right(right, steps, move, load):
    for index, k in enumerate(steps):
        up, down = load(index)
        right = right + move(up * right, k) + move(down * right, -k)
    return right


def dense(row):
    return jnp.concatenate([row[:, 128 * i : 128 * (i + 1)] for i in range(8)], axis=0)


def natural(tile, rows):
    return jnp.concatenate(
        [jnp.broadcast_to(tile[i : i + 1, :], (rows, 128)) for i in range(8)], axis=1
    )


def factor_x_kernel(
    fields_arg, vertical_arg, kappa_arg, fields, vertical, kappa, ax, bx, qx, h1, h2, parts, done
):
    pairs = ((kappa_arg, kappa), (fields_arg, fields), (vertical_arg, vertical))
    copies = [pltpu.make_async_copy(a, b, done.at[n]) for n, (a, b) in enumerate(pairs)]
    for copy in copies:
        copy.start()
    copies[0].wait()
    half = 512
    rows = lax.broadcasted_iota(jnp.int32, (ROWS, half), 0)
    for f in range(2):
        mine = pl.ds(f * ROWS, ROWS)
        for c in range(COLS // half):
            cols = pl.ds(c * half, half)
            k = kappa[mine, cols]
            face = (k + turn(k, 1, 0)) * 0.5
            low = jnp.where((rows >= 2) & (rows <= 14), face, 0.0)
            first = jnp.where(rows == 1, face, 0.0)
            last = jnp.where(rows == 14, turn(face, -1, 0), 0.0)

            def keep(index, a, b, mine=mine, cols=cols):
                ax[index, mine, cols] = a
                bx[index, mine, cols] = b

            inverse, (one, two) = reduce_matrix(
                low, 1.0 + first + last, [first, last], X_STEPS, turn_rows, keep
            )
            qx[mine, cols] = jnp.where((rows >= 1) & (rows <= 14), inverse, 0.0)
            one = jnp.where(rows == 0, 1.0, one)
            two = jnp.where(rows == ROWS - 1, 1.0, two)
            h1[mine, cols] = one
            h2[mine, cols] = two
            sums = (
                jnp.sum(first * two, axis=0, keepdims=True),
                jnp.sum(one, axis=0, keepdims=True),
                jnp.sum(two, axis=0, keepdims=True),
                k[:1],
                k[ROWS - 1 :],
            )
            for n, row in enumerate(sums):
                for i in range(half // 128):
                    parts[n, f, pl.ds(c * (half // 128) + i, 1), :] = row[:, 128 * i : 128 * (i + 1)]
    copies[1].wait()
    copies[2].wait()


def factor_y_kernel(kappa, ay, by, qy, hy, edge):
    gy = lax.axis_index("gy")
    low_side = gy == 0
    end = jnp.where(low_side, COLS - 1, 0)
    start = COLS - 1 - end
    beside = jnp.where(low_side, COLS - 2, 1)
    cut = jnp.where(low_side, COLS - 1, 1)
    k = stand(kappa[...])
    row = lax.broadcasted_iota(jnp.int32, (256, 128), 0)
    lane = lax.broadcasted_iota(jnp.int32, (256, 128), 1)
    y = row // 128 * 512 + lane // 32 * 128 + row % 128
    face = (k + turn_lines(k, 1)) * 0.5
    low = jnp.where((y == 0) | (y == cut), 0.0, face)
    link = jnp.where(y == beside, jnp.where(low_side, turn_lines(face, -1), face), 0.0)
    ground = jnp.where(y == start, 1.0 + 0.5 * k, 1.0)

    def keep(index, up, down):
        ay[index] = up
        by[index] = down

    inverse, (profile,) = reduce_matrix(low, ground + link, [link], Y_STEPS, turn_lines, keep)
    qy[...] = jnp.where(y == end, 0.0, inverse)
    profile = lie(jnp.where(y == end, 1.0, profile))
    hy[...] = profile
    k = kappa[...]
    column = lax.broadcasted_iota(jnp.int32, (ALL, COLS), 1)
    total = jnp.sum(profile * jnp.where(column == start, 1.0 + 0.5 * k, 1.0), axis=1, keepdims=True)
    rim = jnp.sum(jnp.where(column == end, k, 0.0), axis=1, keepdims=True)
    wide = lax.broadcasted_iota(jnp.int32, (ALL, 128), 1)
    edge[...] = jnp.where(wide == 0, total, jnp.where(wide == 1, rim, 0.0))


def source_kernel(fields, fields_far, vertical, vertical_far, h1, h2, parts, after, source, keep, send):
    del after
    even = lax.axis_index("gx") % 2 == 0
    here = fields[...]
    v = vertical[...]
    s = here + (v + vertical_far[...]) * 0.5 * (fields_far[...] - here) - v * 0.5 * here
    source[...] = s
    elements = []
    for f in range(2):
        mine = slice(f * ROWS, (f + 1) * ROWS)
        first = dense(jnp.sum(h1[mine, :] * s[mine, :], axis=0, keepdims=True))
        last = dense(jnp.sum(h2[mine, :] * s[mine, :], axis=0, keepdims=True))
        elements.append((parts[0, f], parts[1, f], parts[2, f], first, last, parts[3, f], parts[4, f]))
    for n, (one, two) in enumerate(zip(*elements)):
        keep[n] = jnp.where(even, one, two)
        send[n] = jnp.where(even, two, one)


def local_x_kernel(source, ax, bx, qx, out):
    half = 512
    for f in range(2):
        mine = pl.ds(f * ROWS, ROWS)
        for c in range(COLS // half):
            cols = pl.ds(c * half, half)
            r = source[mine, cols]
            r = reduce_right(r, X_STEPS, turn_rows, lambda i: (ax[i, mine, cols], bx[i, mine, cols]))
            out[mine, cols] = r * qx[mine, cols]


def merge(one, two):
    g, sl, sr, rl, rr = one
    g2, sl2, sr2, rl2, rr2 = two
    s = sr + sl2
    r = rr + rl2
    inverse = 1.0 / (g + g2 + s)
    a = g * inverse
    b = g2 * inverse
    return (a * g2, sl + a * s, sr2 + b * s, rl + a * r, rr2 + b * r), (a, b, r * inverse)


def behind(face, two):
    g, s, sr, r, rr = two
    inverse = 1.0 / (face + g + s)
    a = face * inverse
    b = g * inverse
    return (a * g, a * s, sr + b * s, a * r, rr + b * r), (a, b, r * inverse)


def load(ref):
    return tuple(ref[n] for n in range(7))


def within(node, left, right):
    a, b, c = node
    return (a * left[0] + b * right[0], a * left[1] + b * right[1], a * left[2] + b * right[2] + c)


def chip_kernel(keep, got, chip, middle):
    even = lax.axis_index("gx") % 2 == 0
    mine, other = load(keep), load(got)
    first = [jnp.where(even, m, o) for m, o in zip(mine, other)]
    second = [jnp.where(even, o, m) for m, o in zip(mine, other)]
    tail, start = behind((first[6] + second[5]) * 0.5, second[:5])
    element, end = merge(first[:5], tail)
    for n, value in enumerate((*element, first[5], second[6])):
        chip[n] = value
    for n, value in enumerate((*end, *start)):
        middle[n] = value


def slab_kernel(chip, far1, far2, far3, middle, message, nodes):
    y = lax.axis_index("gx") // 2 % 4
    arrived = [load(chip), load(far1), load(far2), load(far3)]
    chips = []
    for m in range(4):
        chosen = arrived[0]
        for shift in range(1, 4):
            here = (y + shift) % 4 == m
            chosen = [jnp.where(here, a, c) for a, c in zip(arrived[shift], chosen)]
        chips.append(chosen)
    element = chips[0][:5]
    inner, fronts = [], []
    for m in range(1, 4):
        tail, front = behind((chips[m - 1][6] + chips[m][5]) * 0.5, chips[m][:5])
        element, node = merge(element, tail)
        inner.append(node)
        fronts.append(front)
    for n, value in enumerate((*element, chips[0][5], chips[3][6])):
        for j in range(8):
            message[j, n] = value
    zero, one = jnp.zeros((8, 128), F32), jnp.ones((8, 128), F32)
    left = (one, zero, zero)
    lasts = [(zero, one, zero)]
    for node in inner[::-1]:
        lasts.append(within(node, left, lasts[-1]))
    lasts = lasts[::-1]
    firsts = [left] + [within(fronts[m - 1], lasts[m - 1], lasts[m]) for m in range(1, 4)]
    first, last = firsts[0], lasts[0]
    for m in range(1, 4):
        first = [jnp.where(y == m, new, old) for new, old in zip(firsts[m], first)]
        last = [jnp.where(y == m, new, old) for new, old in zip(lasts[m], last)]
    before = within(tuple(middle[n] for n in range(3)), first, last)
    second = within(tuple(middle[n] for n in range(3, 6)), before, last)
    for n, trio in enumerate((first, before, second, last)):
        for m in range(3):
            nodes[n, m] = trio[m]


def ends_kernel(got, nodes, mine, other):
    gx = lax.axis_index("gx")
    slab = gx // 8
    even = gx % 2 == 0
    zero = jnp.zeros((8, 128), F32)
    slabs, fronts = [], []
    for z in range(8):
        face = got[z, 5] * 0.5 if z == 0 else (got[z - 1, 6] + got[z, 5]) * 0.5
        tail, front = behind(face, tuple(got[z, n] for n in range(5)))
        slabs.append(tail)
        fronts.append(front)
    g, _, conduct, _, right = slabs[0]
    conduct = conduct + g
    ratios, offsets = [], []
    for z in range(1, 8):
        g, sl, sr, rl, rr = slabs[z]
        conduct = conduct + sl
        right = right + rl
        inverse = 1.0 / (conduct + g)
        f = g * inverse
        ratios.append(f)
        offsets.append(right * inverse)
        conduct = sr + f * conduct
        right = rr + f * right
    value = right / (conduct + got[7, 6] * 0.5)
    values = [value]
    for k in range(6, -1, -1):
        value = ratios[k] * value + offsets[k]
        values.append(value)
    values = [zero] + values[::-1]
    first, last = zero, zero
    for z in range(8):
        a, b, c = fronts[z]
        first = jnp.where(slab == z, a * values[z] + b * values[z + 1] + c, first)
        last = jnp.where(slab == z, values[z + 1], last)
    row = [nodes[n, 0] * first + nodes[n, 1] * last + nodes[n, 2] for n in range(4)]
    for n in range(2):
        mine[n] = jnp.where(even, row[n], row[n + 2])
        other[n] = jnp.where(even, row[n + 2], row[n])


def section_kernel(mine, other, local, h1, h2, hy, edge, section, message):
    core = lax.axis_index("gx") % 2
    wide = lax.broadcasted_iota(jnp.int32, (8, 128), 1)
    for f in range(2):
        first = jnp.where(core == f, mine[0], other[0])
        last = jnp.where(core == f, mine[1], other[1])
        rows = slice(f * ROWS, (f + 1) * ROWS)
        s = local[rows, :] + h1[rows, :] * natural(first, ROWS) + h2[rows, :] * natural(last, ROWS)
        section[rows, :] = s
        total = jnp.sum(hy[rows, :] * s, axis=1, keepdims=True)
        for g in range(2):
            part = slice(f * ROWS + g * 8, f * ROWS + g * 8 + 8)
            message[part, :] = jnp.where(wide == 2, total[g * 8 : g * 8 + 8], edge[part, :])


def local_y_kernel(section, ay, by, qy, out):
    r = stand(section[...])
    r = reduce_right(r, Y_STEPS, turn_lines, lambda i: (ay[i], by[i]))
    out[...] = lie(r * qy[...])


def output_kernel(message, far, local, hy, out):
    e, k, r = (message[:, n : n + 1] for n in range(3))
    e2, k2, r2 = (far[:, n : n + 1] for n in range(3))
    c = (k + k2) * 0.5
    value = ((e2 + c) * r + c * r2) / (e * e2 + c * (e + e2))
    out[...] = local[...] + hy[...] * value


def call(kernel, outs, specs, flops=0, size=0, scratch=()):
    return pl.pallas_call(
        kernel,
        out_shape=outs,
        in_specs=specs,
        out_specs=jax.tree.map(lambda _: VMEM, outs),
        scratch_shapes=scratch,
        compiler_params=PARAMS,
        cost_estimate=pl.CostEstimate(flops=flops, bytes_accessed=size, transcendentals=0),
    )


SLAB_GROUPS = [[8 * b + a for b in range(8)] for a in range(8)]
CORES = [(i, i ^ 1) for i in range(64)]


def chips_on(shift):
    return [(i // 8 * 8 + (i + 2 * shift) % 8, i) for i in range(64)]


def local(fields, kappa, vertical):
    grid = (ALL, COLS)
    swap = [(0, 1), (1, 0)]
    fields_far = lax.ppermute(fields, "gz", swap)
    vertical_far = lax.ppermute(vertical, "gz", swap)
    full = shape(*grid)
    half = shape(7, 8, 128)
    standing = shape(256, 128)
    fields_here, vertical_here, kappa_here, ax, bx, qx, h1, h2, parts = call(
        factor_x_kernel,
        (full, full, full, shape(4, *grid), shape(4, *grid), full, full, full, shape(5, 2, 8, 128)),
        [HBM] * 3,
        flops=4_000_000,
        size=2_000_000,
        scratch=[pltpu.SemaphoreType.DMA((3,))],
    )(*(pltpu.with_memory_space_constraint(x.reshape(grid), pltpu.HBM) for x in (fields, vertical, kappa)))
    ay, by, qy, hy, edge = call(
        factor_y_kernel,
        (shape(10, 256, 128), shape(10, 256, 128), standing, full, shape(ALL, 128)),
        [VMEM],
        flops=20_000_000,
        size=4_000_000,
    )(kappa_here)
    source, keep, send = call(source_kernel, (full, half, half), [VMEM] * 8)(
        fields_here, fields_far.reshape(grid), vertical_here, vertical_far.reshape(grid),
        h1, h2, parts, edge,
    )
    got = lax.ppermute(send, "gx", CORES)
    local_x = call(local_x_kernel, full, [VMEM] * 4, flops=1_000_000, size=1_000_000)(source, ax, bx, qx)
    chip, middle = call(chip_kernel, (half, shape(6, 8, 128)), [VMEM] * 2)(keep, got)
    far = [lax.ppermute(chip, "gx", chips_on(shift)) for shift in (2, 1, 3)]
    message, nodes = call(
        slab_kernel, (shape(8, 7, 8, 128), shape(4, 3, 8, 128)), [VMEM] * 5
    )(chip, far[1], far[0], far[2], middle)
    got = lax.all_to_all(message, "gx", 0, 0, axis_index_groups=SLAB_GROUPS, tiled=True)
    mine, other = call(
        ends_kernel, (shape(2, 8, 128), shape(2, 8, 128)), [VMEM, VMEM]
    )(got, nodes)
    other = lax.ppermute(other, "gx", CORES)
    section, message = call(
        section_kernel, (full, shape(ALL, 128)), [VMEM] * 7
    )(mine, other, local_x, h1, h2, hy, edge)
    far = lax.ppermute(message, "gy", swap)
    local_y = call(local_y_kernel, full, [VMEM] * 4, flops=4_000_000, size=3_000_000)(section, ay, by, qy)
    out = call(output_kernel, full, [VMEM] * 4)(message, far, local_y, hy)
    return out.reshape(fields.shape)


def solution(mesh):
    spec = P(None, "gz", "gx", "gy")
    return jax.shard_map(
        local, mesh=mesh, in_specs=(spec, spec, spec), out_specs=spec, check_vma=False
    )
```

```python
import functools

import jax
import jax.numpy as jnp
from jax import lax
from jax.experimental import pallas as pl
from jax.experimental.pallas import tpu as pltpu
from jax.sharding import PartitionSpec as P

F32 = jnp.float32
ROWS = 16
COLS = 1024
ALL = 2 * ROWS
VMEM = pl.BlockSpec(memory_space=pltpu.VMEM)
HBM = pl.BlockSpec(memory_space=pltpu.HBM)
X_STEPS = (1, 2, 4, 8)
Y_STEPS = (1, 2, 4, 8, 16, 32, 64, 128, 256, 512)
PARAMS = pltpu.CompilerParams(vmem_limit_bytes=40 * 1024 * 1024)


def shape(*dims):
    return jax.ShapeDtypeStruct(dims, F32)


def turn(x, k, axis):
    n = x.shape[axis]
    k = k % n
    unit = 128 if axis == 1 else 8
    if k == 0:
        return x
    if k % unit == 0:
        low = lax.slice_in_dim(x, n - k, n, axis=axis)
        high = lax.slice_in_dim(x, 0, n - k, axis=axis)
        return jnp.concatenate([low, high], axis=axis)
    return pltpu.roll(x, k, axis)


def turn_lines(x, k):
    lanes = lax.broadcasted_iota(jnp.int32, (1, 128), 1)

    def blocks(pair, n):
        if n == 4:
            return pair[::-1]
        turned = [pltpu.roll(p, 32 * n % 128, 1) for p in pair]
        over = lanes < 32 * n if n > 0 else lanes >= 128 + 32 * n
        return [jnp.where(over, turned[1 - h], turned[h]) for h in range(2)]

    pair = [x[:128], x[128:]]
    size = abs(k)
    if size >= 128:
        pair = blocks(pair, 4 if size == 512 else k // 128)
    elif size >= 8:
        if k > 0:
            moved = blocks([p[128 - k :] for p in pair], 1)
            pair = [jnp.concatenate([m, p[: 128 - k]], axis=0) for m, p in zip(moved, pair)]
        else:
            moved = blocks([p[:size] for p in pair], -1)
            pair = [jnp.concatenate([p[size:], m], axis=0) for m, p in zip(moved, pair)]
    else:
        rows = lax.broadcasted_iota(jnp.int32, (8, 128), 0)
        turned = [pltpu.roll(p, k % 128, 0) for p in pair]
        if k > 0:
            ends = [t[:8] for t in turned]
            ends = [jnp.where(rows < k, m, e) for m, e in zip(blocks(ends, 1), ends)]
            pair = [jnp.concatenate([e, t[8:]], axis=0) for e, t in zip(ends, turned)]
        else:
            ends = [t[120:] for t in turned]
            ends = [jnp.where(rows >= 8 + k, m, e) for m, e in zip(blocks(ends, -1), ends)]
            pair = [jnp.concatenate([t[:120], e], axis=0) for e, t in zip(ends, turned)]
    return jnp.concatenate(pair, axis=0)


def stand(x):
    tiles = [x[:, 128 * j : 128 * (j + 1)] for j in range(8)]
    return jnp.concatenate(
        [jnp.concatenate(tiles[4 * h : 4 * h + 4], axis=0).T for h in range(2)], axis=0
    )


def lie(x):
    tiles = [x[128 * h : 128 * (h + 1)].T for h in range(2)]
    return jnp.concatenate(
        [tiles[h][ALL * b : ALL * (b + 1)] for h in range(2) for b in range(4)], axis=1
    )


def turn_rows(x, k):
    return turn(x, k, 0)


def reduce_matrix(low, excess, rights, steps, move, keep):
    for index, k in enumerate(steps):
        high = move(low, -k)
        inverse = 1.0 / (low + high + excess)
        up = high * inverse
        down = low * inverse
        keep(index, up, down)
        excess = excess + move(up * excess, k) + move(down * excess, -k)
        rights = [r + move(up * r, k) + move(down * r, -k) for r in rights]
        low = move(up * low, k)
    inverse = 1.0 / excess
    return inverse, [r * inverse for r in rights]


def reduce_right(right, steps, move, load):
    for index, k in enumerate(steps):
        up, down = load(index)
        right = right + move(up * right, k) + move(down * right, -k)
    return right


def dense(row):
    return jnp.concatenate([row[:, 128 * i : 128 * (i + 1)] for i in range(8)], axis=0)


def natural(tile, rows):
    return jnp.concatenate(
        [jnp.broadcast_to(tile[i : i + 1, :], (rows, 128)) for i in range(8)], axis=1
    )


def factor_x_kernel(
    fields_arg, vertical_arg, kappa_arg, fields, vertical, kappa, ax, bx, qx, h1, h2, parts, done
):
    pairs = ((kappa_arg, kappa), (fields_arg, fields), (vertical_arg, vertical))
    copies = [pltpu.make_async_copy(a, b, done.at[n]) for n, (a, b) in enumerate(pairs)]
    for copy in copies:
        copy.start()
    copies[0].wait()
    half = 512
    rows = lax.broadcasted_iota(jnp.int32, (ROWS, half), 0)
    for f in range(2):
        mine = pl.ds(f * ROWS, ROWS)
        for c in range(COLS // half):
            cols = pl.ds(c * half, half)
            k = kappa[mine, cols]
            face = (k + turn(k, 1, 0)) * 0.5
            low = jnp.where((rows >= 2) & (rows <= 14), face, 0.0)
            first = jnp.where(rows == 1, face, 0.0)
            last = jnp.where(rows == 14, turn(face, -1, 0), 0.0)

            def keep(index, a, b, mine=mine, cols=cols):
                ax[index, mine, cols] = a
                bx[index, mine, cols] = b

            inverse, (one, two) = reduce_matrix(
                low, 1.0 + first + last, [first, last], X_STEPS, turn_rows, keep
            )
            qx[mine, cols] = jnp.where((rows >= 1) & (rows <= 14), inverse, 0.0)
            one = jnp.where(rows == 0, 1.0, one)
            two = jnp.where(rows == ROWS - 1, 1.0, two)
            h1[mine, cols] = one
            h2[mine, cols] = two
            sums = (
                jnp.sum(first * two, axis=0, keepdims=True),
                jnp.sum(one, axis=0, keepdims=True),
                jnp.sum(two, axis=0, keepdims=True),
                k[:1],
                k[ROWS - 1 :],
            )
            for n, row in enumerate(sums):
                for i in range(half // 128):
                    parts[n, f, pl.ds(c * (half // 128) + i, 1), :] = row[:, 128 * i : 128 * (i + 1)]
    copies[1].wait()
    copies[2].wait()


def factor_y_kernel(kappa, ay, by, qy, hy, edge):
    gy = lax.axis_index("gy")
    low_side = gy == 0
    end = jnp.where(low_side, COLS - 1, 0)
    start = COLS - 1 - end
    beside = jnp.where(low_side, COLS - 2, 1)
    cut = jnp.where(low_side, COLS - 1, 1)
    k = stand(kappa[...])
    row = lax.broadcasted_iota(jnp.int32, (256, 128), 0)
    lane = lax.broadcasted_iota(jnp.int32, (256, 128), 1)
    y = row // 128 * 512 + lane // 32 * 128 + row % 128
    face = (k + turn_lines(k, 1)) * 0.5
    low = jnp.where((y == 0) | (y == cut), 0.0, face)
    link = jnp.where(y == beside, jnp.where(low_side, turn_lines(face, -1), face), 0.0)
    ground = jnp.where(y == start, 1.0 + 0.5 * k, 1.0)

    def keep(index, up, down):
        ay[index] = up
        by[index] = down

    inverse, (profile,) = reduce_matrix(low, ground + link, [link], Y_STEPS, turn_lines, keep)
    qy[...] = jnp.where(y == end, 0.0, inverse)
    profile = lie(jnp.where(y == end, 1.0, profile))
    hy[...] = profile
    k = kappa[...]
    column = lax.broadcasted_iota(jnp.int32, (ALL, COLS), 1)
    total = jnp.sum(profile * jnp.where(column == start, 1.0 + 0.5 * k, 1.0), axis=1, keepdims=True)
    rim = jnp.sum(jnp.where(column == end, k, 0.0), axis=1, keepdims=True)
    wide = lax.broadcasted_iota(jnp.int32, (ALL, 128), 1)
    edge[...] = jnp.where(wide == 0, total, jnp.where(wide == 1, rim, 0.0))


def source_kernel(fields, fields_far, vertical, vertical_far, h1, h2, parts, after, source, keep, send):
    del after
    even = lax.axis_index("gx") % 2 == 0
    here = fields[...]
    v = vertical[...]
    s = here + (v + vertical_far[...]) * 0.5 * (fields_far[...] - here) - v * 0.5 * here
    source[...] = s
    elements = []
    for f in range(2):
        mine = slice(f * ROWS, (f + 1) * ROWS)
        first = dense(jnp.sum(h1[mine, :] * s[mine, :], axis=0, keepdims=True))
        last = dense(jnp.sum(h2[mine, :] * s[mine, :], axis=0, keepdims=True))
        elements.append((parts[0, f], parts[1, f], parts[2, f], first, last, parts[3, f], parts[4, f]))
    for n, (one, two) in enumerate(zip(*elements)):
        keep[n] = jnp.where(even, one, two)
        send[n] = jnp.where(even, two, one)


def local_x_kernel(source, ax, bx, qx, out):
    half = 512
    for f in range(2):
        mine = pl.ds(f * ROWS, ROWS)
        for c in range(COLS // half):
            cols = pl.ds(c * half, half)
            r = source[mine, cols]
            r = reduce_right(r, X_STEPS, turn_rows, lambda i: (ax[i, mine, cols], bx[i, mine, cols]))
            out[mine, cols] = r * qx[mine, cols]


def merge(one, two):
    g, sl, sr, rl, rr = one
    g2, sl2, sr2, rl2, rr2 = two
    s = sr + sl2
    r = rr + rl2
    inverse = 1.0 / (g + g2 + s)
    a = g * inverse
    b = g2 * inverse
    return (a * g2, sl + a * s, sr2 + b * s, rl + a * r, rr2 + b * r), (a, b, r * inverse)


def behind(face, two):
    g, s, sr, r, rr = two
    inverse = 1.0 / (face + g + s)
    a = face * inverse
    b = g * inverse
    return (a * g, a * s, sr + b * s, a * r, rr + b * r), (a, b, r * inverse)


def load(ref):
    return tuple(ref[n] for n in range(7))


def within(node, left, right):
    a, b, c = node
    return (a * left[0] + b * right[0], a * left[1] + b * right[1], a * left[2] + b * right[2] + c)


def join(mine, other, low):
    first = [jnp.where(low, m, o) for m, o in zip(mine, other)]
    second = [jnp.where(low, o, m) for m, o in zip(mine, other)]
    tail, start = behind((first[6] + second[5]) * 0.5, second[:5])
    element, end = merge(first[:5], tail)
    return (*element, first[5], second[6]), (*end, *start)


def join_kernel(bit, mine, other, both, rows):
    low = lax.axis_index("gx") // bit % 2 == 0
    element, nodes = join(load(mine), load(other), low)
    for n, value in enumerate(element):
        both[n] = value
    for n, value in enumerate(nodes):
        rows[n] = value


def slab_kernel(mine, other, pair_rows, chip_rows, message, nodes):
    gx = lax.axis_index("gx")
    low = gx // 4 % 2 == 0
    element, rows = join(load(mine), load(other), low)
    for n, value in enumerate(element):
        for j in range(8):
            message[j, n] = value
    zero, one = jnp.zeros((8, 128), F32), jnp.ones((8, 128), F32)
    ends = ((one, zero, zero), (zero, one, zero))
    parts = [rows, *(tuple(ref[n] for n in range(6)) for ref in (pair_rows, chip_rows))]
    for n, (rows, low) in enumerate(zip(parts, (low, gx // 2 % 2 == 0, None))):
        end = within(rows[:3], *ends)
        start = within(rows[3:], end, ends[1])
        if n == 2:
            for m, trio in enumerate((ends[0], end, start, ends[1])):
                for k in range(3):
                    nodes[m, k] = trio[k]
        else:
            ends = (
                [jnp.where(low, a, b) for a, b in zip(ends[0], start)],
                [jnp.where(low, a, b) for a, b in zip(end, ends[1])],
            )


def ends_kernel(got, nodes, mine, other):
    gx = lax.axis_index("gx")
    slab = gx // 8
    even = gx % 2 == 0
    zero = jnp.zeros((8, 128), F32)
    slabs, fronts = [], []
    for z in range(8):
        face = got[z, 5] * 0.5 if z == 0 else (got[z - 1, 6] + got[z, 5]) * 0.5
        tail, front = behind(face, tuple(got[z, n] for n in range(5)))
        slabs.append(tail)
        fronts.append(front)
    g, _, conduct, _, right = slabs[0]
    conduct = conduct + g
    ratios, offsets = [], []
    for z in range(1, 8):
        g, sl, sr, rl, rr = slabs[z]
        conduct = conduct + sl
        right = right + rl
        inverse = 1.0 / (conduct + g)
        f = g * inverse
        ratios.append(f)
        offsets.append(right * inverse)
        conduct = sr + f * conduct
        right = rr + f * right
    value = right / (conduct + got[7, 6] * 0.5)
    values = [value]
    for k in range(6, -1, -1):
        value = ratios[k] * value + offsets[k]
        values.append(value)
    values = [zero] + values[::-1]
    first, last = zero, zero
    for z in range(8):
        a, b, c = fronts[z]
        first = jnp.where(slab == z, a * values[z] + b * values[z + 1] + c, first)
        last = jnp.where(slab == z, values[z + 1], last)
    row = [nodes[n, 0] * first + nodes[n, 1] * last + nodes[n, 2] for n in range(4)]
    for n in range(2):
        mine[n] = jnp.where(even, row[n], row[n + 2])
        other[n] = jnp.where(even, row[n + 2], row[n])


def section_kernel(mine, other, local, h1, h2, hy, edge, section, message):
    core = lax.axis_index("gx") % 2
    wide = lax.broadcasted_iota(jnp.int32, (8, 128), 1)
    for f in range(2):
        first = jnp.where(core == f, mine[0], other[0])
        last = jnp.where(core == f, mine[1], other[1])
        rows = slice(f * ROWS, (f + 1) * ROWS)
        s = local[rows, :] + h1[rows, :] * natural(first, ROWS) + h2[rows, :] * natural(last, ROWS)
        section[rows, :] = s
        total = jnp.sum(hy[rows, :] * s, axis=1, keepdims=True)
        for g in range(2):
            part = slice(f * ROWS + g * 8, f * ROWS + g * 8 + 8)
            message[part, :] = jnp.where(wide == 2, total[g * 8 : g * 8 + 8], edge[part, :])


def local_y_kernel(section, ay, by, qy, out):
    r = stand(section[...])
    r = reduce_right(r, Y_STEPS, turn_lines, lambda i: (ay[i], by[i]))
    out[...] = lie(r * qy[...])


def output_kernel(message, far, local, hy, out):
    e, k, r = (message[:, n : n + 1] for n in range(3))
    e2, k2, r2 = (far[:, n : n + 1] for n in range(3))
    c = (k + k2) * 0.5
    value = ((e2 + c) * r + c * r2) / (e * e2 + c * (e + e2))
    out[...] = local[...] + hy[...] * value


def call(kernel, outs, specs, flops=0, size=0, scratch=()):
    return pl.pallas_call(
        kernel,
        out_shape=outs,
        in_specs=specs,
        out_specs=jax.tree.map(lambda _: VMEM, outs),
        scratch_shapes=scratch,
        compiler_params=PARAMS,
        cost_estimate=pl.CostEstimate(flops=flops, bytes_accessed=size, transcendentals=0),
    )


SLAB_GROUPS = [[8 * b + a for b in range(8)] for a in range(8)]
CORES = [(i, i ^ 1) for i in range(64)]


CHIPS = [(i, i ^ 2) for i in range(64)]
PAIRS = [(i, i ^ 6) for i in range(64)]


def local(fields, kappa, vertical):
    grid = (ALL, COLS)
    swap = [(0, 1), (1, 0)]
    fields_far = lax.ppermute(fields, "gz", swap)
    vertical_far = lax.ppermute(vertical, "gz", swap)
    full = shape(*grid)
    half = shape(7, 8, 128)
    standing = shape(256, 128)
    fields_here, vertical_here, kappa_here, ax, bx, qx, h1, h2, parts = call(
        factor_x_kernel,
        (full, full, full, shape(4, *grid), shape(4, *grid), full, full, full, shape(5, 2, 8, 128)),
        [HBM] * 3,
        flops=4_000_000,
        size=2_000_000,
        scratch=[pltpu.SemaphoreType.DMA((3,))],
    )(*(pltpu.with_memory_space_constraint(x.reshape(grid), pltpu.HBM) for x in (fields, vertical, kappa)))
    ay, by, qy, hy, edge = call(
        factor_y_kernel,
        (shape(10, 256, 128), shape(10, 256, 128), standing, full, shape(ALL, 128)),
        [VMEM],
        flops=20_000_000,
        size=4_000_000,
    )(kappa_here)
    source, keep, send = call(source_kernel, (full, half, half), [VMEM] * 8)(
        fields_here, fields_far.reshape(grid), vertical_here, vertical_far.reshape(grid),
        h1, h2, parts, edge,
    )
    got = lax.ppermute(send, "gx", CORES)
    local_x = call(local_x_kernel, full, [VMEM] * 4, flops=1_000_000, size=1_000_000)(source, ax, bx, qx)
    rows = shape(6, 8, 128)
    chip, chip_rows = call(functools.partial(join_kernel, 1), (half, rows), [VMEM] * 2)(keep, got)
    got = lax.ppermute(chip, "gx", CHIPS)
    pair, pair_rows = call(functools.partial(join_kernel, 2), (half, rows), [VMEM] * 2)(chip, got)
    got = lax.ppermute(pair, "gx", PAIRS)
    message, nodes = call(
        slab_kernel, (shape(8, 7, 8, 128), shape(4, 3, 8, 128)), [VMEM] * 4
    )(pair, got, pair_rows, chip_rows)
    got = lax.all_to_all(message, "gx", 0, 0, axis_index_groups=SLAB_GROUPS, tiled=True)
    mine, other = call(
        ends_kernel, (shape(2, 8, 128), shape(2, 8, 128)), [VMEM, VMEM]
    )(got, nodes)
    other = lax.ppermute(other, "gx", CORES)
    section, message = call(
        section_kernel, (full, shape(ALL, 128)), [VMEM] * 7
    )(mine, other, local_x, h1, h2, hy, edge)
    far = lax.ppermute(message, "gy", swap)
    local_y = call(local_y_kernel, full, [VMEM] * 4, flops=4_000_000, size=3_000_000)(section, ay, by, qy)
    out = call(output_kernel, full, [VMEM] * 4)(message, far, local_y, hy)
    return out.reshape(fields.shape)


def solution(mesh):
    spec = P(None, "gz", "gx", "gy")
    return jax.shard_map(
        local, mesh=mesh, in_specs=(spec, spec, spec), out_specs=spec, check_vma=False
    )
```

```python
import functools

import jax
import jax.numpy as jnp
from jax import lax
from jax.experimental import pallas as pl
from jax.experimental.pallas import tpu as pltpu
from jax.sharding import PartitionSpec as P

F32 = jnp.float32
ROWS = 16
COLS = 1024
ALL = 2 * ROWS
VMEM = pl.BlockSpec(memory_space=pltpu.VMEM)
HBM = pl.BlockSpec(memory_space=pltpu.HBM)
X_STEPS = (1, 2, 4, 8)
Y_STEPS = (1, 2, 4, 8, 16, 32, 64, 128, 256, 512)
PARAMS = pltpu.CompilerParams(vmem_limit_bytes=40 * 1024 * 1024)


def shape(*dims):
    return jax.ShapeDtypeStruct(dims, F32)


def turn(x, k, axis):
    n = x.shape[axis]
    k = k % n
    unit = 128 if axis == 1 else 8
    if k == 0:
        return x
    if k % unit == 0:
        low = lax.slice_in_dim(x, n - k, n, axis=axis)
        high = lax.slice_in_dim(x, 0, n - k, axis=axis)
        return jnp.concatenate([low, high], axis=axis)
    return pltpu.roll(x, k, axis)


def turn_lines(x, k):
    lanes = lax.broadcasted_iota(jnp.int32, (1, 128), 1)

    def blocks(pair, n):
        if n == 4:
            return pair[::-1]
        turned = [pltpu.roll(p, 32 * n % 128, 1) for p in pair]
        over = lanes < 32 * n if n > 0 else lanes >= 128 + 32 * n
        return [jnp.where(over, turned[1 - h], turned[h]) for h in range(2)]

    pair = [x[:128], x[128:]]
    size = abs(k)
    if size >= 128:
        pair = blocks(pair, 4 if size == 512 else k // 128)
    elif size >= 8:
        if k > 0:
            moved = blocks([p[128 - k :] for p in pair], 1)
            pair = [jnp.concatenate([m, p[: 128 - k]], axis=0) for m, p in zip(moved, pair)]
        else:
            moved = blocks([p[:size] for p in pair], -1)
            pair = [jnp.concatenate([p[size:], m], axis=0) for m, p in zip(moved, pair)]
    else:
        rows = lax.broadcasted_iota(jnp.int32, (8, 128), 0)
        turned = [pltpu.roll(p, k % 128, 0) for p in pair]
        if k > 0:
            ends = [t[:8] for t in turned]
            ends = [jnp.where(rows < k, m, e) for m, e in zip(blocks(ends, 1), ends)]
            pair = [jnp.concatenate([e, t[8:]], axis=0) for e, t in zip(ends, turned)]
        else:
            ends = [t[120:] for t in turned]
            ends = [jnp.where(rows >= 8 + k, m, e) for m, e in zip(blocks(ends, -1), ends)]
            pair = [jnp.concatenate([t[:120], e], axis=0) for e, t in zip(ends, turned)]
    return jnp.concatenate(pair, axis=0)


def stand(x):
    tiles = [x[:, 128 * j : 128 * (j + 1)] for j in range(8)]
    return jnp.concatenate(
        [jnp.concatenate(tiles[4 * h : 4 * h + 4], axis=0).T for h in range(2)], axis=0
    )


def lie(x):
    tiles = [x[128 * h : 128 * (h + 1)].T for h in range(2)]
    return jnp.concatenate(
        [tiles[h][ALL * b : ALL * (b + 1)] for h in range(2) for b in range(4)], axis=1
    )


def turn_rows(x, k):
    return turn(x, k, 0)


def reduce_matrix(low, excess, rights, steps, move, keep):
    for index, k in enumerate(steps):
        high = move(low, -k)
        inverse = 1.0 / (low + high + excess)
        up = high * inverse
        down = low * inverse
        keep(index, up, down)
        excess = excess + move(up * excess, k) + move(down * excess, -k)
        rights = [r + move(up * r, k) + move(down * r, -k) for r in rights]
        low = move(up * low, k)
    inverse = 1.0 / excess
    return inverse, [r * inverse for r in rights]


def reduce_right(right, steps, move, load):
    for index, k in enumerate(steps):
        up, down = load(index)
        right = right + move(up * right, k) + move(down * right, -k)
    return right


def dense(row):
    return jnp.concatenate([row[:, 128 * i : 128 * (i + 1)] for i in range(8)], axis=0)


def natural(tile, rows):
    return jnp.concatenate(
        [jnp.broadcast_to(tile[i : i + 1, :], (rows, 128)) for i in range(8)], axis=1
    )


def factor_x_kernel(
    fields_arg, vertical_arg, kappa_arg, fields, vertical, kappa, ax, bx, qx, h1, h2, parts, done
):
    pairs = ((kappa_arg, kappa), (fields_arg, fields), (vertical_arg, vertical))
    copies = [pltpu.make_async_copy(a, b, done.at[n]) for n, (a, b) in enumerate(pairs)]
    for copy in copies:
        copy.start()
    copies[0].wait()
    half = 512
    rows = lax.broadcasted_iota(jnp.int32, (ROWS, half), 0)
    for f in range(2):
        mine = pl.ds(f * ROWS, ROWS)
        for c in range(COLS // half):
            cols = pl.ds(c * half, half)
            k = kappa[mine, cols]
            face = (k + turn(k, 1, 0)) * 0.5
            low = jnp.where((rows >= 2) & (rows <= 14), face, 0.0)
            first = jnp.where(rows == 1, face, 0.0)
            last = jnp.where(rows == 14, turn(face, -1, 0), 0.0)

            def keep(index, a, b, mine=mine, cols=cols):
                ax[index, mine, cols] = a
                bx[index, mine, cols] = b

            inverse, (one, two) = reduce_matrix(
                low, 1.0 + first + last, [first, last], X_STEPS, turn_rows, keep
            )
            qx[mine, cols] = jnp.where((rows >= 1) & (rows <= 14), inverse, 0.0)
            one = jnp.where(rows == 0, 1.0, one)
            two = jnp.where(rows == ROWS - 1, 1.0, two)
            h1[mine, cols] = one
            h2[mine, cols] = two
            sums = (
                jnp.sum(first * two, axis=0, keepdims=True),
                jnp.sum(one, axis=0, keepdims=True),
                jnp.sum(two, axis=0, keepdims=True),
                k[:1],
                k[ROWS - 1 :],
            )
            for n, row in enumerate(sums):
                for i in range(half // 128):
                    parts[n, f, pl.ds(c * (half // 128) + i, 1), :] = row[:, 128 * i : 128 * (i + 1)]
    copies[1].wait()
    copies[2].wait()


def factor_y_kernel(kappa, ay, by, qy, hy, edge):
    gy = lax.axis_index("gy")
    low_side = gy == 0
    end = jnp.where(low_side, COLS - 1, 0)
    start = COLS - 1 - end
    beside = jnp.where(low_side, COLS - 2, 1)
    cut = jnp.where(low_side, COLS - 1, 1)
    k = stand(kappa[...])
    row = lax.broadcasted_iota(jnp.int32, (256, 128), 0)
    lane = lax.broadcasted_iota(jnp.int32, (256, 128), 1)
    y = row // 128 * 512 + lane // 32 * 128 + row % 128
    face = (k + turn_lines(k, 1)) * 0.5
    low = jnp.where((y == 0) | (y == cut), 0.0, face)
    link = jnp.where(y == beside, jnp.where(low_side, turn_lines(face, -1), face), 0.0)
    ground = jnp.where(y == start, 1.0 + 0.5 * k, 1.0)

    def keep(index, up, down):
        ay[index] = up
        by[index] = down

    inverse, (profile,) = reduce_matrix(low, ground + link, [link], Y_STEPS, turn_lines, keep)
    qy[...] = jnp.where(y == end, 0.0, inverse)
    profile = lie(jnp.where(y == end, 1.0, profile))
    hy[...] = profile
    k = kappa[...]
    column = lax.broadcasted_iota(jnp.int32, (ALL, COLS), 1)
    total = jnp.sum(profile * jnp.where(column == start, 1.0 + 0.5 * k, 1.0), axis=1, keepdims=True)
    rim = jnp.sum(jnp.where(column == end, k, 0.0), axis=1, keepdims=True)
    wide = lax.broadcasted_iota(jnp.int32, (ALL, 128), 1)
    edge[...] = jnp.where(wide == 0, total, jnp.where(wide == 1, rim, 0.0))


def source_kernel(fields, fields_far, vertical, vertical_far, h1, h2, parts, after, source, keep, send):
    del after
    even = lax.axis_index("gx") % 2 == 0
    here = fields[...]
    v = vertical[...]
    s = here + (v + vertical_far[...]) * 0.5 * (fields_far[...] - here) - v * 0.5 * here
    source[...] = s
    elements = []
    for f in range(2):
        mine = slice(f * ROWS, (f + 1) * ROWS)
        first = dense(jnp.sum(h1[mine, :] * s[mine, :], axis=0, keepdims=True))
        last = dense(jnp.sum(h2[mine, :] * s[mine, :], axis=0, keepdims=True))
        elements.append((parts[0, f], parts[1, f], parts[2, f], first, last, parts[3, f], parts[4, f]))
    for n, (one, two) in enumerate(zip(*elements)):
        keep[n] = jnp.where(even, one, two)
        send[n] = jnp.where(even, two, one)


def local_x_kernel(source, ax, bx, qx, out):
    half = 512
    for f in range(2):
        mine = pl.ds(f * ROWS, ROWS)
        for c in range(COLS // half):
            cols = pl.ds(c * half, half)
            r = source[mine, cols]
            r = reduce_right(r, X_STEPS, turn_rows, lambda i: (ax[i, mine, cols], bx[i, mine, cols]))
            out[mine, cols] = r * qx[mine, cols]


def merge(one, two):
    g, sl, sr, rl, rr = one
    g2, sl2, sr2, rl2, rr2 = two
    s = sr + sl2
    r = rr + rl2
    inverse = 1.0 / (g + g2 + s)
    a = g * inverse
    b = g2 * inverse
    return (a * g2, sl + a * s, sr2 + b * s, rl + a * r, rr2 + b * r), (a, b, r * inverse)


def behind(face, two):
    g, s, sr, r, rr = two
    inverse = 1.0 / (face + g + s)
    a = face * inverse
    b = g * inverse
    return (a * g, a * s, sr + b * s, a * r, rr + b * r), (a, b, r * inverse)


def load(ref):
    return tuple(ref[n] for n in range(7))


def within(node, left, right):
    a, b, c = node
    return (a * left[0] + b * right[0], a * left[1] + b * right[1], a * left[2] + b * right[2] + c)


def join(first, second):
    tail, start = behind((first[6] + second[5]) * 0.5, second[:5])
    element, end = merge(first[:5], tail)
    return (*element, first[5], second[6]), (*end, *start)


def ordered(low, mine, other):
    first = [jnp.where(low, m, o) for m, o in zip(mine, other)]
    second = [jnp.where(low, o, m) for m, o in zip(mine, other)]
    return first, second


def join_kernel(bit, mine, other, both, rows):
    low = lax.axis_index("gx") // bit % 2 == 0
    element, nodes = join(*ordered(low, load(mine), load(other)))
    for n, value in enumerate(element):
        both[n] = value
    for n, value in enumerate(nodes):
        rows[n] = value


def above_kernel(first_up, second_up, both):
    two, one = ordered(lax.axis_index("gx") < 16, load(first_up), load(second_up))
    element, _ = join(one, two)
    for n, value in enumerate(element):
        both[n] = value


def half_kernel(mine, other, after, both, again):
    del after
    low = lax.axis_index("gx") // 16 % 2 == 0
    element, _ = join(*ordered(low, load(mine), load(other)))
    for n, value in enumerate(element):
        both[n] = value
    again[...] = mine[...]


def slab_kernel(chip, far1, far2, far3, middle, slab, nodes):
    y = lax.axis_index("gx") // 2 % 4
    arrived = [load(chip), load(far1), load(far2), load(far3)]
    chips = []
    for m in range(4):
        chosen = arrived[0]
        for shift in range(1, 4):
            here = (y + shift) % 4 == m
            chosen = [jnp.where(here, a, c) for a, c in zip(arrived[shift], chosen)]
        chips.append(chosen)
    element = chips[0][:5]
    inner, fronts = [], []
    for m in range(1, 4):
        tail, front = behind((chips[m - 1][6] + chips[m][5]) * 0.5, chips[m][:5])
        element, node = merge(element, tail)
        inner.append(node)
        fronts.append(front)
    for n, value in enumerate((*element, chips[0][5], chips[3][6])):
        slab[n] = value
    zero, one = jnp.zeros((8, 128), F32), jnp.ones((8, 128), F32)
    left = (one, zero, zero)
    lasts = [(zero, one, zero)]
    for node in inner[::-1]:
        lasts.append(within(node, left, lasts[-1]))
    lasts = lasts[::-1]
    firsts = [left] + [within(fronts[m - 1], lasts[m - 1], lasts[m]) for m in range(1, 4)]
    first, last = firsts[0], lasts[0]
    for m in range(1, 4):
        first = [jnp.where(y == m, new, old) for new, old in zip(firsts[m], first)]
        last = [jnp.where(y == m, new, old) for new, old in zip(lasts[m], last)]
    before = within(tuple(middle[n] for n in range(3)), first, last)
    second = within(tuple(middle[n] for n in range(3, 6)), before, last)
    for n, trio in enumerate((first, before, second, last)):
        for m in range(3):
            nodes[n, m] = trio[m]


def ends_kernel(pair, inner_low, half_down, inner_high, half_up, pair_rows, nodes, mine, other):
    gx = lax.axis_index("gx")
    z = gx // 8
    even = gx % 2 == 0
    lower = z < 4
    own = load(pair)
    inner = [jnp.where(lower, a, b) for a, b in zip(load(inner_low), load(inner_high))]
    one, two = ordered(z // 2 % 2 == 0, own, inner)
    below, above = load(half_down), load(half_up)
    chain = [
        [jnp.where(lower, a, b) for a, b in zip(one, below)],
        [jnp.where(lower, a, b) for a, b in zip(two, one)],
        [jnp.where(lower, a, b) for a, b in zip(above, two)],
    ]
    tails, fronts = [], []
    for k in range(3):
        face = chain[k][5] * 0.5 if k == 0 else (chain[k - 1][6] + chain[k][5]) * 0.5
        tail, front = behind(face, chain[k][:5])
        tails.append(tail)
        fronts.append(front)
    g, _, conduct, _, right = tails[0]
    conduct = conduct + g
    ratios, offsets = [], []
    for k in (1, 2):
        g, sl, sr, rl, rr = tails[k]
        conduct = conduct + sl
        right = right + rl
        inverse = 1.0 / (conduct + g)
        f = g * inverse
        ratios.append(f)
        offsets.append(right * inverse)
        conduct = sr + f * conduct
        right = rr + f * right
    last2 = right / (conduct + chain[2][6] * 0.5)
    last1 = ratios[1] * last2 + offsets[1]
    last0 = ratios[0] * last1 + offsets[0]
    lasts = (last0, last1, last2)
    firsts = []
    for k in range(3):
        a, b, c = fronts[k]
        firsts.append(b * lasts[k] + c if k == 0 else a * lasts[k - 1] + b * lasts[k] + c)
    place = z // 2 % 2 + jnp.where(lower, 0, 1)
    first, last = firsts[0], lasts[0]
    for k in (1, 2):
        first = jnp.where(place == k, firsts[k], first)
        last = jnp.where(place == k, lasts[k], last)
    end = pair_rows[0] * first + pair_rows[1] * last + pair_rows[2]
    start = pair_rows[3] * end + pair_rows[4] * last + pair_rows[5]
    left = z % 2 == 0
    first, last = jnp.where(left, first, start), jnp.where(left, end, last)
    row = [nodes[n, 0] * first + nodes[n, 1] * last + nodes[n, 2] for n in range(4)]
    for n in range(2):
        mine[n] = jnp.where(even, row[n], row[n + 2])
        other[n] = jnp.where(even, row[n + 2], row[n])


def section_kernel(mine, other, local, h1, h2, hy, edge, section, message):
    core = lax.axis_index("gx") % 2
    wide = lax.broadcasted_iota(jnp.int32, (8, 128), 1)
    for f in range(2):
        first = jnp.where(core == f, mine[0], other[0])
        last = jnp.where(core == f, mine[1], other[1])
        rows = slice(f * ROWS, (f + 1) * ROWS)
        s = local[rows, :] + h1[rows, :] * natural(first, ROWS) + h2[rows, :] * natural(last, ROWS)
        section[rows, :] = s
        total = jnp.sum(hy[rows, :] * s, axis=1, keepdims=True)
        for g in range(2):
            part = slice(f * ROWS + g * 8, f * ROWS + g * 8 + 8)
            message[part, :] = jnp.where(wide == 2, total[g * 8 : g * 8 + 8], edge[part, :])


def local_y_kernel(section, ay, by, qy, out):
    r = stand(section[...])
    r = reduce_right(r, Y_STEPS, turn_lines, lambda i: (ay[i], by[i]))
    out[...] = lie(r * qy[...])


def output_kernel(message, far, local, hy, out):
    e, k, r = (message[:, n : n + 1] for n in range(3))
    e2, k2, r2 = (far[:, n : n + 1] for n in range(3))
    c = (k + k2) * 0.5
    value = ((e2 + c) * r + c * r2) / (e * e2 + c * (e + e2))
    out[...] = local[...] + hy[...] * value


def call(kernel, outs, specs, flops=0, size=0, scratch=()):
    return pl.pallas_call(
        kernel,
        out_shape=outs,
        in_specs=specs,
        out_specs=jax.tree.map(lambda _: VMEM, outs),
        scratch_shapes=scratch,
        compiler_params=PARAMS,
        cost_estimate=pl.CostEstimate(flops=flops, bytes_accessed=size, transcendentals=0),
    )


CORES = [(i, i ^ 1) for i in range(64)]


def chips_on(shift):
    return [(i // 8 * 8 + (i + 2 * shift) % 8, i) for i in range(64)]


def slabs(pairs):
    return [(8 * a + i, 8 * b + i) for a, b in pairs for i in range(8)]


SLABS = slabs([(z, z ^ 1) for z in range(8)])
LOWER = slabs([(z, z ^ 2) for z in range(4)])
UPPER = slabs([(z, z ^ 2) for z in range(4, 8)])
UP_FIRST = slabs([(7, 0), (6, 1), (5, 2), (4, 3)])
UP_SECOND = slabs([(5, 0), (4, 1), (7, 2), (6, 3)])
DOWN = slabs([(0, 5), (1, 4), (2, 7), (3, 6)])


def local(fields, kappa, vertical):
    grid = (ALL, COLS)
    swap = [(0, 1), (1, 0)]
    fields_far = lax.ppermute(fields, "gz", swap)
    vertical_far = lax.ppermute(vertical, "gz", swap)
    full = shape(*grid)
    half = shape(7, 8, 128)
    standing = shape(256, 128)
    fields_here, vertical_here, kappa_here, ax, bx, qx, h1, h2, parts = call(
        factor_x_kernel,
        (full, full, full, shape(4, *grid), shape(4, *grid), full, full, full, shape(5, 2, 8, 128)),
        [HBM] * 3,
        flops=4_000_000,
        size=2_000_000,
        scratch=[pltpu.SemaphoreType.DMA((3,))],
    )(*(pltpu.with_memory_space_constraint(x.reshape(grid), pltpu.HBM) for x in (fields, vertical, kappa)))
    ay, by, qy, hy, edge = call(
        factor_y_kernel,
        (shape(10, 256, 128), shape(10, 256, 128), standing, full, shape(ALL, 128)),
        [VMEM],
        flops=20_000_000,
        size=4_000_000,
    )(kappa_here)
    source, keep, send = call(source_kernel, (full, half, half), [VMEM] * 8)(
        fields_here, fields_far.reshape(grid), vertical_here, vertical_far.reshape(grid),
        h1, h2, parts, edge,
    )
    got = lax.ppermute(send, "gx", CORES)
    local_x = call(local_x_kernel, full, [VMEM] * 4, flops=1_000_000, size=1_000_000)(source, ax, bx, qx)
    rows = shape(6, 8, 128)
    chip, middle = call(functools.partial(join_kernel, 1), (half, rows), [VMEM] * 2)(keep, got)
    far = [lax.ppermute(chip, "gx", chips_on(shift)) for shift in (2, 1, 3)]
    slab, nodes = call(slab_kernel, (half, shape(4, 3, 8, 128)), [VMEM] * 5)(
        chip, far[1], far[0], far[2], middle
    )
    got = lax.ppermute(slab, "gx", SLABS)
    pair, pair_rows = call(functools.partial(join_kernel, 8), (half, rows), [VMEM] * 2)(slab, got)
    first_up = lax.ppermute(pair, "gx", UP_FIRST)
    second_up = lax.ppermute(pair, "gx", UP_SECOND)
    inner_low = lax.ppermute(pair, "gx", LOWER)
    half_up = call(above_kernel, half, [VMEM] * 2)(first_up, second_up)
    lower, again = call(half_kernel, (half, half), [VMEM] * 3)(pair, inner_low, half_up)
    half_down = lax.ppermute(lower, "gx", DOWN)
    inner_high = lax.ppermute(again, "gx", UPPER)
    mine, other = call(
        ends_kernel, (shape(2, 8, 128), shape(2, 8, 128)), [VMEM] * 7
    )(pair, inner_low, half_down, inner_high, half_up, pair_rows, nodes)
    other = lax.ppermute(other, "gx", CORES)
    section, message = call(
        section_kernel, (full, shape(ALL, 128)), [VMEM] * 7
    )(mine, other, local_x, h1, h2, hy, edge)
    far = lax.ppermute(message, "gy", swap)
    local_y = call(local_y_kernel, full, [VMEM] * 4, flops=4_000_000, size=3_000_000)(section, ay, by, qy)
    out = call(output_kernel, full, [VMEM] * 4)(message, far, local_y, hy)
    return out.reshape(fields.shape)


def solution(mesh):
    spec = P(None, "gz", "gx", "gy")
    return jax.shard_map(
        local, mesh=mesh, in_specs=(spec, spec, spec), out_specs=spec, check_vma=False
    )
```

```python
import functools

import jax
import jax.numpy as jnp
from jax import lax
from jax.experimental import pallas as pl
from jax.experimental.pallas import tpu as pltpu
from jax.sharding import PartitionSpec as P

F32 = jnp.float32
ROWS = 16
COLS = 1024
ALL = 2 * ROWS
VMEM = pl.BlockSpec(memory_space=pltpu.VMEM)
HBM = pl.BlockSpec(memory_space=pltpu.HBM)
X_STEPS = (1, 2, 4, 8)
Y_STEPS = (1, 2, 4, 8, 16, 32, 64, 128, 256, 512)
PARAMS = pltpu.CompilerParams(vmem_limit_bytes=40 * 1024 * 1024)


def shape(*dims):
    return jax.ShapeDtypeStruct(dims, F32)


def turn(x, k, axis):
    n = x.shape[axis]
    k = k % n
    unit = 128 if axis == 1 else 8
    if k == 0:
        return x
    if k % unit == 0:
        low = lax.slice_in_dim(x, n - k, n, axis=axis)
        high = lax.slice_in_dim(x, 0, n - k, axis=axis)
        return jnp.concatenate([low, high], axis=axis)
    return pltpu.roll(x, k, axis)


def turn_lines(x, k):
    lanes = lax.broadcasted_iota(jnp.int32, (1, 128), 1)

    def blocks(pair, n):
        if n == 4:
            return pair[::-1]
        turned = [pltpu.roll(p, 32 * n % 128, 1) for p in pair]
        over = lanes < 32 * n if n > 0 else lanes >= 128 + 32 * n
        return [jnp.where(over, turned[1 - h], turned[h]) for h in range(2)]

    pair = [x[:128], x[128:]]
    size = abs(k)
    if size >= 128:
        pair = blocks(pair, 4 if size == 512 else k // 128)
    elif size >= 8:
        if k > 0:
            moved = blocks([p[128 - k :] for p in pair], 1)
            pair = [jnp.concatenate([m, p[: 128 - k]], axis=0) for m, p in zip(moved, pair)]
        else:
            moved = blocks([p[:size] for p in pair], -1)
            pair = [jnp.concatenate([p[size:], m], axis=0) for m, p in zip(moved, pair)]
    else:
        rows = lax.broadcasted_iota(jnp.int32, (8, 128), 0)
        turned = [pltpu.roll(p, k % 128, 0) for p in pair]
        if k > 0:
            ends = [t[:8] for t in turned]
            ends = [jnp.where(rows < k, m, e) for m, e in zip(blocks(ends, 1), ends)]
            pair = [jnp.concatenate([e, t[8:]], axis=0) for e, t in zip(ends, turned)]
        else:
            ends = [t[120:] for t in turned]
            ends = [jnp.where(rows >= 8 + k, m, e) for m, e in zip(blocks(ends, -1), ends)]
            pair = [jnp.concatenate([t[:120], e], axis=0) for e, t in zip(ends, turned)]
    return jnp.concatenate(pair, axis=0)


def stand(x):
    tiles = [x[:, 128 * j : 128 * (j + 1)] for j in range(8)]
    return jnp.concatenate(
        [jnp.concatenate(tiles[4 * h : 4 * h + 4], axis=0).T for h in range(2)], axis=0
    )


def lie(x):
    tiles = [x[128 * h : 128 * (h + 1)].T for h in range(2)]
    return jnp.concatenate(
        [tiles[h][ALL * b : ALL * (b + 1)] for h in range(2) for b in range(4)], axis=1
    )


def turn_rows(x, k):
    return turn(x, k, 0)


def reduce_matrix(low, excess, rights, steps, move, keep):
    for index, k in enumerate(steps):
        high = move(low, -k)
        inverse = 1.0 / (low + high + excess)
        up = high * inverse
        down = low * inverse
        keep(index, up, down)
        excess = excess + move(up * excess, k) + move(down * excess, -k)
        rights = [r + move(up * r, k) + move(down * r, -k) for r in rights]
        low = move(up * low, k)
    inverse = 1.0 / excess
    return inverse, [r * inverse for r in rights]


def reduce_right(right, steps, move, load):
    for index, k in enumerate(steps):
        up, down = load(index)
        right = right + move(up * right, k) + move(down * right, -k)
    return right


def dense(row):
    return jnp.concatenate([row[:, 128 * i : 128 * (i + 1)] for i in range(8)], axis=0)


def natural(tile, rows):
    return jnp.concatenate(
        [jnp.broadcast_to(tile[i : i + 1, :], (rows, 128)) for i in range(8)], axis=1
    )


def factor_x_kernel(
    fields_arg, vertical_arg, kappa_arg, fields, vertical, kappa, ax, bx, qx, h1, h2, parts, done
):
    pairs = ((kappa_arg, kappa), (fields_arg, fields), (vertical_arg, vertical))
    copies = [pltpu.make_async_copy(a, b, done.at[n]) for n, (a, b) in enumerate(pairs)]
    for copy in copies:
        copy.start()
    copies[0].wait()
    half = 512
    rows = lax.broadcasted_iota(jnp.int32, (ROWS, half), 0)
    for f in range(2):
        mine = pl.ds(f * ROWS, ROWS)
        for c in range(COLS // half):
            cols = pl.ds(c * half, half)
            k = kappa[mine, cols]
            face = (k + turn(k, 1, 0)) * 0.5
            low = jnp.where((rows >= 2) & (rows <= 14), face, 0.0)
            first = jnp.where(rows == 1, face, 0.0)
            last = jnp.where(rows == 14, turn(face, -1, 0), 0.0)

            def keep(index, a, b, mine=mine, cols=cols):
                ax[index, mine, cols] = a
                bx[index, mine, cols] = b

            inverse, (one, two) = reduce_matrix(
                low, 1.0 + first + last, [first, last], X_STEPS, turn_rows, keep
            )
            qx[mine, cols] = jnp.where((rows >= 1) & (rows <= 14), inverse, 0.0)
            one = jnp.where(rows == 0, 1.0, one)
            two = jnp.where(rows == ROWS - 1, 1.0, two)
            h1[mine, cols] = one
            h2[mine, cols] = two
            sums = (
                jnp.sum(first * two, axis=0, keepdims=True),
                jnp.sum(one, axis=0, keepdims=True),
                jnp.sum(two, axis=0, keepdims=True),
                k[:1],
                k[ROWS - 1 :],
            )
            for n, row in enumerate(sums):
                for i in range(half // 128):
                    parts[n, f, pl.ds(c * (half // 128) + i, 1), :] = row[:, 128 * i : 128 * (i + 1)]
    copies[1].wait()
    copies[2].wait()


def factor_y_kernel(kappa, ay, by, qy, hy, edge):
    gy = lax.axis_index("gy")
    low_side = gy == 0
    end = jnp.where(low_side, COLS - 1, 0)
    start = COLS - 1 - end
    beside = jnp.where(low_side, COLS - 2, 1)
    cut = jnp.where(low_side, COLS - 1, 1)
    k = stand(kappa[...])
    row = lax.broadcasted_iota(jnp.int32, (256, 128), 0)
    lane = lax.broadcasted_iota(jnp.int32, (256, 128), 1)
    y = row // 128 * 512 + lane // 32 * 128 + row % 128
    face = (k + turn_lines(k, 1)) * 0.5
    low = jnp.where((y == 0) | (y == cut), 0.0, face)
    link = jnp.where(y == beside, jnp.where(low_side, turn_lines(face, -1), face), 0.0)
    ground = jnp.where(y == start, 1.0 + 0.5 * k, 1.0)

    def keep(index, up, down):
        ay[index] = up
        by[index] = down

    inverse, (profile,) = reduce_matrix(low, ground + link, [link], Y_STEPS, turn_lines, keep)
    qy[...] = jnp.where(y == end, 0.0, inverse)
    profile = lie(jnp.where(y == end, 1.0, profile))
    hy[...] = profile
    k = kappa[...]
    column = lax.broadcasted_iota(jnp.int32, (ALL, COLS), 1)
    total = jnp.sum(profile * jnp.where(column == start, 1.0 + 0.5 * k, 1.0), axis=1, keepdims=True)
    rim = jnp.sum(jnp.where(column == end, k, 0.0), axis=1, keepdims=True)
    wide = lax.broadcasted_iota(jnp.int32, (ALL, 128), 1)
    edge[...] = jnp.where(wide == 0, total, jnp.where(wide == 1, rim, 0.0))


def source_kernel(fields, fields_far, vertical, vertical_far, h1, h2, parts, after, source, keep, send):
    del after
    even = lax.axis_index("gx") % 2 == 0
    here = fields[...]
    v = vertical[...]
    s = here + (v + vertical_far[...]) * 0.5 * (fields_far[...] - here) - v * 0.5 * here
    source[...] = s
    elements = []
    for f in range(2):
        mine = slice(f * ROWS, (f + 1) * ROWS)
        first = dense(jnp.sum(h1[mine, :] * s[mine, :], axis=0, keepdims=True))
        last = dense(jnp.sum(h2[mine, :] * s[mine, :], axis=0, keepdims=True))
        elements.append((parts[0, f], parts[1, f], parts[2, f], first, last, parts[3, f], parts[4, f]))
    for n, (one, two) in enumerate(zip(*elements)):
        keep[n] = jnp.where(even, one, two)
        send[n] = jnp.where(even, two, one)


def local_x_kernel(source, ax, bx, qx, out):
    half = 512
    for f in range(2):
        mine = pl.ds(f * ROWS, ROWS)
        for c in range(COLS // half):
            cols = pl.ds(c * half, half)
            r = source[mine, cols]
            r = reduce_right(r, X_STEPS, turn_rows, lambda i: (ax[i, mine, cols], bx[i, mine, cols]))
            out[mine, cols] = r * qx[mine, cols]


def merge(one, two):
    g, sl, sr, rl, rr = one
    g2, sl2, sr2, rl2, rr2 = two
    s = sr + sl2
    r = rr + rl2
    inverse = 1.0 / (g + g2 + s)
    a = g * inverse
    b = g2 * inverse
    return (a * g2, sl + a * s, sr2 + b * s, rl + a * r, rr2 + b * r), (a, b, r * inverse)


def behind(face, two):
    g, s, sr, r, rr = two
    inverse = 1.0 / (face + g + s)
    a = face * inverse
    b = g * inverse
    return (a * g, a * s, sr + b * s, a * r, rr + b * r), (a, b, r * inverse)


def load(ref):
    return tuple(ref[n] for n in range(7))


def within(node, left, right):
    a, b, c = node
    return (a * left[0] + b * right[0], a * left[1] + b * right[1], a * left[2] + b * right[2] + c)


def chip_kernel(keep, got, message, middle):
    even = lax.axis_index("gx") % 2 == 0
    mine, other = load(keep), load(got)
    first = [jnp.where(even, m, o) for m, o in zip(mine, other)]
    second = [jnp.where(even, o, m) for m, o in zip(mine, other)]
    tail, start = behind((first[6] + second[5]) * 0.5, second[:5])
    element, end = merge(first[:5], tail)
    for n, value in enumerate((*element, first[5], second[6])):
        for m in range(4):
            message[m, n] = value
    for n, value in enumerate((*end, *start)):
        middle[n] = value


def slab_kernel(got, middle, message, nodes):
    y = lax.axis_index("gx") // 2 % 4
    chips = [tuple(got[m, n] for n in range(7)) for m in range(4)]
    element = chips[0][:5]
    inner, fronts = [], []
    for m in range(1, 4):
        tail, front = behind((chips[m - 1][6] + chips[m][5]) * 0.5, chips[m][:5])
        element, node = merge(element, tail)
        inner.append(node)
        fronts.append(front)
    for n, value in enumerate((*element, chips[0][5], chips[3][6])):
        for j in range(8):
            message[j, n] = value
    zero, one = jnp.zeros((8, 128), F32), jnp.ones((8, 128), F32)
    left = (one, zero, zero)
    lasts = [(zero, one, zero)]
    for node in inner[::-1]:
        lasts.append(within(node, left, lasts[-1]))
    lasts = lasts[::-1]
    firsts = [left] + [within(fronts[m - 1], lasts[m - 1], lasts[m]) for m in range(1, 4)]
    first, last = firsts[0], lasts[0]
    for m in range(1, 4):
        first = [jnp.where(y == m, new, old) for new, old in zip(firsts[m], first)]
        last = [jnp.where(y == m, new, old) for new, old in zip(lasts[m], last)]
    before = within(tuple(middle[n] for n in range(3)), first, last)
    second = within(tuple(middle[n] for n in range(3, 6)), before, last)
    for n, trio in enumerate((first, before, second, last)):
        for m in range(3):
            nodes[n, m] = trio[m]


def ends_kernel(got, nodes, mine, other):
    gx = lax.axis_index("gx")
    slab = gx // 8
    even = gx % 2 == 0
    zero = jnp.zeros((8, 128), F32)
    slabs, fronts = [], []
    for z in range(8):
        face = got[z, 5] * 0.5 if z == 0 else (got[z - 1, 6] + got[z, 5]) * 0.5
        tail, front = behind(face, tuple(got[z, n] for n in range(5)))
        slabs.append(tail)
        fronts.append(front)
    g, _, conduct, _, right = slabs[0]
    conduct = conduct + g
    ratios, offsets = [], []
    for z in range(1, 8):
        g, sl, sr, rl, rr = slabs[z]
        conduct = conduct + sl
        right = right + rl
        inverse = 1.0 / (conduct + g)
        f = g * inverse
        ratios.append(f)
        offsets.append(right * inverse)
        conduct = sr + f * conduct
        right = rr + f * right
    value = right / (conduct + got[7, 6] * 0.5)
    values = [value]
    for k in range(6, -1, -1):
        value = ratios[k] * value + offsets[k]
        values.append(value)
    values = [zero] + values[::-1]
    first, last = zero, zero
    for z in range(8):
        a, b, c = fronts[z]
        first = jnp.where(slab == z, a * values[z] + b * values[z + 1] + c, first)
        last = jnp.where(slab == z, values[z + 1], last)
    row = [nodes[n, 0] * first + nodes[n, 1] * last + nodes[n, 2] for n in range(4)]
    for n in range(2):
        mine[n] = jnp.where(even, row[n], row[n + 2])
        other[n] = jnp.where(even, row[n + 2], row[n])


def section_kernel(mine, other, local, h1, h2, hy, edge, section, message):
    core = lax.axis_index("gx") % 2
    wide = lax.broadcasted_iota(jnp.int32, (8, 128), 1)
    for f in range(2):
        first = jnp.where(core == f, mine[0], other[0])
        last = jnp.where(core == f, mine[1], other[1])
        rows = slice(f * ROWS, (f + 1) * ROWS)
        s = local[rows, :] + h1[rows, :] * natural(first, ROWS) + h2[rows, :] * natural(last, ROWS)
        section[rows, :] = s
        total = jnp.sum(hy[rows, :] * s, axis=1, keepdims=True)
        for g in range(2):
            part = slice(f * ROWS + g * 8, f * ROWS + g * 8 + 8)
            message[part, :] = jnp.where(wide == 2, total[g * 8 : g * 8 + 8], edge[part, :])


def local_y_kernel(section, ay, by, qy, out):
    r = stand(section[...])
    r = reduce_right(r, Y_STEPS, turn_lines, lambda i: (ay[i], by[i]))
    out[...] = lie(r * qy[...])


def output_kernel(message, far, local, hy, out):
    e, k, r = (message[:, n : n + 1] for n in range(3))
    e2, k2, r2 = (far[:, n : n + 1] for n in range(3))
    c = (k + k2) * 0.5
    value = ((e2 + c) * r + c * r2) / (e * e2 + c * (e + e2))
    out[...] = local[...] + hy[...] * value


def call(kernel, outs, specs, flops=0, size=0, scratch=()):
    return pl.pallas_call(
        kernel,
        out_shape=outs,
        in_specs=specs,
        out_specs=jax.tree.map(lambda _: VMEM, outs),
        scratch_shapes=scratch,
        compiler_params=PARAMS,
        cost_estimate=pl.CostEstimate(flops=flops, bytes_accessed=size, transcendentals=0),
    )


SLAB_GROUPS = [[8 * b + a for b in range(8)] for a in range(8)]
CHIP_GROUPS = [[8 * z + 2 * y + c for y in range(4)] for z in range(8) for c in range(2)]
CORES = [(i, i ^ 1) for i in range(64)]


def local(fields, kappa, vertical):
    grid = (ALL, COLS)
    swap = [(0, 1), (1, 0)]
    fields_far = lax.ppermute(fields, "gz", swap)
    vertical_far = lax.ppermute(vertical, "gz", swap)
    full = shape(*grid)
    half = shape(7, 8, 128)
    standing = shape(256, 128)
    fields_here, vertical_here, kappa_here, ax, bx, qx, h1, h2, parts = call(
        factor_x_kernel,
        (full, full, full, shape(4, *grid), shape(4, *grid), full, full, full, shape(5, 2, 8, 128)),
        [HBM] * 3,
        flops=4_000_000,
        size=2_000_000,
        scratch=[pltpu.SemaphoreType.DMA((3,))],
    )(*(pltpu.with_memory_space_constraint(x.reshape(grid), pltpu.HBM) for x in (fields, vertical, kappa)))
    ay, by, qy, hy, edge = call(
        factor_y_kernel,
        (shape(10, 256, 128), shape(10, 256, 128), standing, full, shape(ALL, 128)),
        [VMEM],
        flops=20_000_000,
        size=4_000_000,
    )(kappa_here)
    source, keep, send = call(source_kernel, (full, half, half), [VMEM] * 8)(
        fields_here, fields_far.reshape(grid), vertical_here, vertical_far.reshape(grid),
        h1, h2, parts, edge,
    )
    got = lax.ppermute(send, "gx", CORES)
    local_x = call(local_x_kernel, full, [VMEM] * 4, flops=1_000_000, size=1_000_000)(source, ax, bx, qx)
    message, middle = call(
        chip_kernel, (shape(4, 7, 8, 128), shape(6, 8, 128)), [VMEM] * 2
    )(keep, got)
    got = lax.all_to_all(message, "gx", 0, 0, axis_index_groups=CHIP_GROUPS, tiled=True)
    message, nodes = call(
        slab_kernel, (shape(8, 7, 8, 128), shape(4, 3, 8, 128)), [VMEM] * 2
    )(got, middle)
    got = lax.all_to_all(message, "gx", 0, 0, axis_index_groups=SLAB_GROUPS, tiled=True)
    mine, other = call(
        ends_kernel, (shape(2, 8, 128), shape(2, 8, 128)), [VMEM, VMEM]
    )(got, nodes)
    other = lax.ppermute(other, "gx", CORES)
    section, message = call(
        section_kernel, (full, shape(ALL, 128)), [VMEM] * 7
    )(mine, other, local_x, h1, h2, hy, edge)
    far = lax.ppermute(message, "gy", swap)
    local_y = call(local_y_kernel, full, [VMEM] * 4, flops=4_000_000, size=3_000_000)(section, ay, by, qy)
    out = call(output_kernel, full, [VMEM] * 4)(message, far, local_y, hy)
    return out.reshape(fields.shape)


def solution(mesh):
    spec = P(None, "gz", "gx", "gy")
    return jax.shard_map(
        local, mesh=mesh, in_specs=(spec, spec, spec), out_specs=spec, check_vma=False
    )
```

```python
import functools

import jax
import jax.numpy as jnp
from jax import lax
from jax.experimental import pallas as pl
from jax.experimental.pallas import tpu as pltpu
from jax.sharding import PartitionSpec as P

F32 = jnp.float32
ROWS = 16
COLS = 1024
ALL = 2 * ROWS
VMEM = pl.BlockSpec(memory_space=pltpu.VMEM)
HBM = pl.BlockSpec(memory_space=pltpu.HBM)
X_STEPS = (1, 2, 4, 8)
Y_STEPS = (1, 2, 4, 8, 16, 32, 64, 128, 256, 512)
PARAMS = pltpu.CompilerParams(vmem_limit_bytes=40 * 1024 * 1024)


def shape(*dims):
    return jax.ShapeDtypeStruct(dims, F32)


def turn(x, k, axis):
    n = x.shape[axis]
    k = k % n
    unit = 128 if axis == 1 else 8
    if k == 0:
        return x
    if k % unit == 0:
        low = lax.slice_in_dim(x, n - k, n, axis=axis)
        high = lax.slice_in_dim(x, 0, n - k, axis=axis)
        return jnp.concatenate([low, high], axis=axis)
    return pltpu.roll(x, k, axis)


def turn_lines(x, k):
    lanes = lax.broadcasted_iota(jnp.int32, (1, 128), 1)

    def blocks(pair, n):
        if n == 4:
            return pair[::-1]
        turned = [pltpu.roll(p, 32 * n % 128, 1) for p in pair]
        over = lanes < 32 * n if n > 0 else lanes >= 128 + 32 * n
        return [jnp.where(over, turned[1 - h], turned[h]) for h in range(2)]

    pair = [x[:128], x[128:]]
    size = abs(k)
    if size >= 128:
        pair = blocks(pair, 4 if size == 512 else k // 128)
    elif size >= 8:
        if k > 0:
            moved = blocks([p[128 - k :] for p in pair], 1)
            pair = [jnp.concatenate([m, p[: 128 - k]], axis=0) for m, p in zip(moved, pair)]
        else:
            moved = blocks([p[:size] for p in pair], -1)
            pair = [jnp.concatenate([p[size:], m], axis=0) for m, p in zip(moved, pair)]
    else:
        rows = lax.broadcasted_iota(jnp.int32, (8, 128), 0)
        turned = [pltpu.roll(p, k % 128, 0) for p in pair]
        if k > 0:
            ends = [t[:8] for t in turned]
            ends = [jnp.where(rows < k, m, e) for m, e in zip(blocks(ends, 1), ends)]
            pair = [jnp.concatenate([e, t[8:]], axis=0) for e, t in zip(ends, turned)]
        else:
            ends = [t[120:] for t in turned]
            ends = [jnp.where(rows >= 8 + k, m, e) for m, e in zip(blocks(ends, -1), ends)]
            pair = [jnp.concatenate([t[:120], e], axis=0) for e, t in zip(ends, turned)]
    return jnp.concatenate(pair, axis=0)


def stand(x):
    tiles = [x[:, 128 * j : 128 * (j + 1)] for j in range(8)]
    return jnp.concatenate(
        [jnp.concatenate(tiles[4 * h : 4 * h + 4], axis=0).T for h in range(2)], axis=0
    )


def lie(x):
    tiles = [x[128 * h : 128 * (h + 1)].T for h in range(2)]
    return jnp.concatenate(
        [tiles[h][ALL * b : ALL * (b + 1)] for h in range(2) for b in range(4)], axis=1
    )


def turn_rows(x, k):
    return turn(x, k, 0)


def reduce_matrix(low, excess, rights, steps, move, keep):
    for index, k in enumerate(steps):
        high = move(low, -k)
        inverse = 1.0 / (low + high + excess)
        up = high * inverse
        down = low * inverse
        keep(index, up, down)
        excess = excess + move(up * excess, k) + move(down * excess, -k)
        rights = [r + move(up * r, k) + move(down * r, -k) for r in rights]
        low = move(up * low, k)
    inverse = 1.0 / excess
    return inverse, [r * inverse for r in rights]


def reduce_right(right, steps, move, load):
    for index, k in enumerate(steps):
        up, down = load(index)
        right = right + move(up * right, k) + move(down * right, -k)
    return right


def dense(row):
    return jnp.concatenate([row[:, 128 * i : 128 * (i + 1)] for i in range(8)], axis=0)


def natural(tile, rows):
    return jnp.concatenate(
        [jnp.broadcast_to(tile[i : i + 1, :], (rows, 128)) for i in range(8)], axis=1
    )


def factor_x_kernel(
    fields_arg, vertical_arg, kappa_arg, fields, vertical, kappa, ax, bx, qx, h1, h2, parts, done
):
    pairs = ((kappa_arg, kappa), (fields_arg, fields), (vertical_arg, vertical))
    copies = [pltpu.make_async_copy(a, b, done.at[n]) for n, (a, b) in enumerate(pairs)]
    for copy in copies:
        copy.start()
    copies[0].wait()
    half = 512
    rows = lax.broadcasted_iota(jnp.int32, (ROWS, half), 0)
    for f in range(2):
        mine = pl.ds(f * ROWS, ROWS)
        for c in range(COLS // half):
            cols = pl.ds(c * half, half)
            k = kappa[mine, cols]
            face = (k + turn(k, 1, 0)) * 0.5
            low = jnp.where((rows >= 2) & (rows <= 14), face, 0.0)
            first = jnp.where(rows == 1, face, 0.0)
            last = jnp.where(rows == 14, turn(face, -1, 0), 0.0)

            def keep(index, a, b, mine=mine, cols=cols):
                ax[index, mine, cols] = a
                bx[index, mine, cols] = b

            inverse, (one, two) = reduce_matrix(
                low, 1.0 + first + last, [first, last], X_STEPS, turn_rows, keep
            )
            qx[mine, cols] = jnp.where((rows >= 1) & (rows <= 14), inverse, 0.0)
            one = jnp.where(rows == 0, 1.0, one)
            two = jnp.where(rows == ROWS - 1, 1.0, two)
            h1[mine, cols] = one
            h2[mine, cols] = two
            sums = (
                jnp.sum(first * two, axis=0, keepdims=True),
                jnp.sum(one, axis=0, keepdims=True),
                jnp.sum(two, axis=0, keepdims=True),
                k[:1],
                k[ROWS - 1 :],
            )
            for n, row in enumerate(sums):
                for i in range(half // 128):
                    parts[n, f, pl.ds(c * (half // 128) + i, 1), :] = row[:, 128 * i : 128 * (i + 1)]
    copies[1].wait()
    copies[2].wait()


def factor_y_kernel(kappa, ay, by, qy, hy, edge):
    gy = lax.axis_index("gy")
    low_side = gy == 0
    end = jnp.where(low_side, COLS - 1, 0)
    start = COLS - 1 - end
    beside = jnp.where(low_side, COLS - 2, 1)
    cut = jnp.where(low_side, COLS - 1, 1)
    k = stand(kappa[...])
    row = lax.broadcasted_iota(jnp.int32, (256, 128), 0)
    lane = lax.broadcasted_iota(jnp.int32, (256, 128), 1)
    y = row // 128 * 512 + lane // 32 * 128 + row % 128
    face = (k + turn_lines(k, 1)) * 0.5
    low = jnp.where((y == 0) | (y == cut), 0.0, face)
    link = jnp.where(y == beside, jnp.where(low_side, turn_lines(face, -1), face), 0.0)
    ground = jnp.where(y == start, 1.0 + 0.5 * k, 1.0)

    def keep(index, up, down):
        ay[index] = up
        by[index] = down

    inverse, (profile,) = reduce_matrix(low, ground + link, [link], Y_STEPS, turn_lines, keep)
    qy[...] = jnp.where(y == end, 0.0, inverse)
    profile = lie(jnp.where(y == end, 1.0, profile))
    hy[...] = profile
    k = kappa[...]
    column = lax.broadcasted_iota(jnp.int32, (ALL, COLS), 1)
    total = jnp.sum(profile * jnp.where(column == start, 1.0 + 0.5 * k, 1.0), axis=1, keepdims=True)
    rim = jnp.sum(jnp.where(column == end, k, 0.0), axis=1, keepdims=True)
    wide = lax.broadcasted_iota(jnp.int32, (ALL, 128), 1)
    edge[...] = jnp.where(wide == 0, total, jnp.where(wide == 1, rim, 0.0))


def source_kernel(fields, fields_far, vertical, vertical_far, h1, h2, parts, after, source, keep, send):
    del after
    even = lax.axis_index("gx") % 2 == 0
    here = fields[...]
    v = vertical[...]
    s = here + (v + vertical_far[...]) * 0.5 * (fields_far[...] - here) - v * 0.5 * here
    source[...] = s
    elements = []
    for f in range(2):
        mine = slice(f * ROWS, (f + 1) * ROWS)
        first = dense(jnp.sum(h1[mine, :] * s[mine, :], axis=0, keepdims=True))
        last = dense(jnp.sum(h2[mine, :] * s[mine, :], axis=0, keepdims=True))
        elements.append((parts[0, f], parts[1, f], parts[2, f], first, last, parts[3, f], parts[4, f]))
    for n, (one, two) in enumerate(zip(*elements)):
        keep[n] = jnp.where(even, one, two)
        send[n] = jnp.where(even, two, one)


def local_x_kernel(source, ax, bx, qx, out):
    half = 512
    for f in range(2):
        mine = pl.ds(f * ROWS, ROWS)
        for c in range(COLS // half):
            cols = pl.ds(c * half, half)
            r = source[mine, cols]
            r = reduce_right(r, X_STEPS, turn_rows, lambda i: (ax[i, mine, cols], bx[i, mine, cols]))
            out[mine, cols] = r * qx[mine, cols]


def merge(one, two):
    g, sl, sr, rl, rr = one
    g2, sl2, sr2, rl2, rr2 = two
    s = sr + sl2
    r = rr + rl2
    inverse = 1.0 / (g + g2 + s)
    a = g * inverse
    b = g2 * inverse
    return (a * g2, sl + a * s, sr2 + b * s, rl + a * r, rr2 + b * r), (a, b, r * inverse)


def behind(face, two):
    g, s, sr, r, rr = two
    inverse = 1.0 / (face + g + s)
    a = face * inverse
    b = g * inverse
    return (a * g, a * s, sr + b * s, a * r, rr + b * r), (a, b, r * inverse)


def load(ref):
    return tuple(ref[n] for n in range(7))


def within(node, left, right):
    a, b, c = node
    return (a * left[0] + b * right[0], a * left[1] + b * right[1], a * left[2] + b * right[2] + c)


def chip_kernel(keep, got, chip, middle):
    even = lax.axis_index("gx") % 2 == 0
    mine, other = load(keep), load(got)
    first = [jnp.where(even, m, o) for m, o in zip(mine, other)]
    second = [jnp.where(even, o, m) for m, o in zip(mine, other)]
    tail, start = behind((first[6] + second[5]) * 0.5, second[:5])
    element, end = merge(first[:5], tail)
    for n, value in enumerate((*element, first[5], second[6])):
        chip[n] = value
    for n, value in enumerate((*end, *start)):
        middle[n] = value


def slab_kernel(chip, far1, far3, far2, middle, message, nodes):
    y = lax.axis_index("gx") // 2 % 4
    arrived = [load(chip), load(far1), load(far2), load(far3)]
    chips = []
    for m in range(4):
        chosen = arrived[0]
        for flip in range(1, 4):
            here = y ^ flip == m
            chosen = [jnp.where(here, a, c) for a, c in zip(arrived[flip], chosen)]
        chips.append(chosen)
    element = chips[0][:5]
    inner, fronts = [], []
    for m in range(1, 4):
        tail, front = behind((chips[m - 1][6] + chips[m][5]) * 0.5, chips[m][:5])
        element, node = merge(element, tail)
        inner.append(node)
        fronts.append(front)
    for n, value in enumerate((*element, chips[0][5], chips[3][6])):
        for j in range(8):
            message[j, n] = value
    zero, one = jnp.zeros((8, 128), F32), jnp.ones((8, 128), F32)
    left = (one, zero, zero)
    lasts = [(zero, one, zero)]
    for node in inner[::-1]:
        lasts.append(within(node, left, lasts[-1]))
    lasts = lasts[::-1]
    firsts = [left] + [within(fronts[m - 1], lasts[m - 1], lasts[m]) for m in range(1, 4)]
    first, last = firsts[0], lasts[0]
    for m in range(1, 4):
        first = [jnp.where(y == m, new, old) for new, old in zip(firsts[m], first)]
        last = [jnp.where(y == m, new, old) for new, old in zip(lasts[m], last)]
    before = within(tuple(middle[n] for n in range(3)), first, last)
    second = within(tuple(middle[n] for n in range(3, 6)), before, last)
    for n, trio in enumerate((first, before, second, last)):
        for m in range(3):
            nodes[n, m] = trio[m]


def ends_kernel(got, nodes, mine, other):
    gx = lax.axis_index("gx")
    slab = gx // 8
    even = gx % 2 == 0
    zero = jnp.zeros((8, 128), F32)
    slabs, fronts = [], []
    for z in range(8):
        face = got[z, 5] * 0.5 if z == 0 else (got[z - 1, 6] + got[z, 5]) * 0.5
        tail, front = behind(face, tuple(got[z, n] for n in range(5)))
        slabs.append(tail)
        fronts.append(front)
    g, _, conduct, _, right = slabs[0]
    conduct = conduct + g
    ratios, offsets = [], []
    for z in range(1, 8):
        g, sl, sr, rl, rr = slabs[z]
        conduct = conduct + sl
        right = right + rl
        inverse = 1.0 / (conduct + g)
        f = g * inverse
        ratios.append(f)
        offsets.append(right * inverse)
        conduct = sr + f * conduct
        right = rr + f * right
    value = right / (conduct + got[7, 6] * 0.5)
    values = [value]
    for k in range(6, -1, -1):
        value = ratios[k] * value + offsets[k]
        values.append(value)
    values = [zero] + values[::-1]
    first, last = zero, zero
    for z in range(8):
        a, b, c = fronts[z]
        first = jnp.where(slab == z, a * values[z] + b * values[z + 1] + c, first)
        last = jnp.where(slab == z, values[z + 1], last)
    row = [nodes[n, 0] * first + nodes[n, 1] * last + nodes[n, 2] for n in range(4)]
    for n in range(2):
        mine[n] = jnp.where(even, row[n], row[n + 2])
        other[n] = jnp.where(even, row[n + 2], row[n])


def section_kernel(mine, other, local, h1, h2, hy, edge, section, message):
    core = lax.axis_index("gx") % 2
    wide = lax.broadcasted_iota(jnp.int32, (8, 128), 1)
    for f in range(2):
        first = jnp.where(core == f, mine[0], other[0])
        last = jnp.where(core == f, mine[1], other[1])
        rows = slice(f * ROWS, (f + 1) * ROWS)
        s = local[rows, :] + h1[rows, :] * natural(first, ROWS) + h2[rows, :] * natural(last, ROWS)
        section[rows, :] = s
        total = jnp.sum(hy[rows, :] * s, axis=1, keepdims=True)
        for g in range(2):
            part = slice(f * ROWS + g * 8, f * ROWS + g * 8 + 8)
            message[part, :] = jnp.where(wide == 2, total[g * 8 : g * 8 + 8], edge[part, :])


def local_y_kernel(section, ay, by, qy, out):
    r = stand(section[...])
    r = reduce_right(r, Y_STEPS, turn_lines, lambda i: (ay[i], by[i]))
    out[...] = lie(r * qy[...])


def output_kernel(message, far, local, hy, out):
    e, k, r = (message[:, n : n + 1] for n in range(3))
    e2, k2, r2 = (far[:, n : n + 1] for n in range(3))
    c = (k + k2) * 0.5
    value = ((e2 + c) * r + c * r2) / (e * e2 + c * (e + e2))
    out[...] = local[...] + hy[...] * value


def call(kernel, outs, specs, flops=0, size=0, scratch=()):
    return pl.pallas_call(
        kernel,
        out_shape=outs,
        in_specs=specs,
        out_specs=jax.tree.map(lambda _: VMEM, outs),
        scratch_shapes=scratch,
        compiler_params=PARAMS,
        cost_estimate=pl.CostEstimate(flops=flops, bytes_accessed=size, transcendentals=0),
    )


SLAB_GROUPS = [[8 * b + a for b in range(8)] for a in range(8)]
CORES = [(i, i ^ 1) for i in range(64)]


def chips_across(flip):
    return [(i, i ^ 2 * flip) for i in range(64)]


def local(fields, kappa, vertical):
    grid = (ALL, COLS)
    swap = [(0, 1), (1, 0)]
    fields_far = lax.ppermute(fields, "gz", swap)
    vertical_far = lax.ppermute(vertical, "gz", swap)
    full = shape(*grid)
    half = shape(7, 8, 128)
    standing = shape(256, 128)
    fields_here, vertical_here, kappa_here, ax, bx, qx, h1, h2, parts = call(
        factor_x_kernel,
        (full, full, full, shape(4, *grid), shape(4, *grid), full, full, full, shape(5, 2, 8, 128)),
        [HBM] * 3,
        flops=4_000_000,
        size=2_000_000,
        scratch=[pltpu.SemaphoreType.DMA((3,))],
    )(*(pltpu.with_memory_space_constraint(x.reshape(grid), pltpu.HBM) for x in (fields, vertical, kappa)))
    ay, by, qy, hy, edge = call(
        factor_y_kernel,
        (shape(10, 256, 128), shape(10, 256, 128), standing, full, shape(ALL, 128)),
        [VMEM],
        flops=20_000_000,
        size=4_000_000,
    )(kappa_here)
    source, keep, send = call(source_kernel, (full, half, half), [VMEM] * 8)(
        fields_here, fields_far.reshape(grid), vertical_here, vertical_far.reshape(grid),
        h1, h2, parts, edge,
    )
    got = lax.ppermute(send, "gx", CORES)
    local_x = call(local_x_kernel, full, [VMEM] * 4, flops=1_000_000, size=1_000_000)(source, ax, bx, qx)
    chip, middle = call(chip_kernel, (half, shape(6, 8, 128)), [VMEM] * 2)(keep, got)
    far = [lax.ppermute(chip, "gx", chips_across(flip)) for flip in (1, 3, 2)]
    message, nodes = call(
        slab_kernel, (shape(8, 7, 8, 128), shape(4, 3, 8, 128)), [VMEM] * 5
    )(chip, *far, middle)
    got = lax.all_to_all(message, "gx", 0, 0, axis_index_groups=SLAB_GROUPS, tiled=True)
    mine, other = call(
        ends_kernel, (shape(2, 8, 128), shape(2, 8, 128)), [VMEM, VMEM]
    )(got, nodes)
    other = lax.ppermute(other, "gx", CORES)
    section, message = call(
        section_kernel, (full, shape(ALL, 128)), [VMEM] * 7
    )(mine, other, local_x, h1, h2, hy, edge)
    far = lax.ppermute(message, "gy", swap)
    local_y = call(local_y_kernel, full, [VMEM] * 4, flops=4_000_000, size=3_000_000)(section, ay, by, qy)
    out = call(output_kernel, full, [VMEM] * 4)(message, far, local_y, hy)
    return out.reshape(fields.shape)


def solution(mesh):
    spec = P(None, "gz", "gx", "gy")
    return jax.shard_map(
        local, mesh=mesh, in_specs=(spec, spec, spec), out_specs=spec, check_vma=False
    )
```

```python
import functools

import jax
import jax.numpy as jnp
from jax import lax
from jax.experimental import pallas as pl
from jax.experimental.pallas import tpu as pltpu
from jax.sharding import PartitionSpec as P

F32 = jnp.float32
ROWS = 16
COLS = 1024
ALL = 2 * ROWS
VMEM = pl.BlockSpec(memory_space=pltpu.VMEM)
HBM = pl.BlockSpec(memory_space=pltpu.HBM)
X_STEPS = (1, 2, 4, 8)
Y_STEPS = (1, 2, 4, 8, 16, 32, 64, 128, 256, 512)
PARAMS = pltpu.CompilerParams(vmem_limit_bytes=40 * 1024 * 1024)


def shape(*dims):
    return jax.ShapeDtypeStruct(dims, F32)


def turn(x, k, axis):
    n = x.shape[axis]
    k = k % n
    unit = 128 if axis == 1 else 8
    if k == 0:
        return x
    if k % unit == 0:
        low = lax.slice_in_dim(x, n - k, n, axis=axis)
        high = lax.slice_in_dim(x, 0, n - k, axis=axis)
        return jnp.concatenate([low, high], axis=axis)
    return pltpu.roll(x, k, axis)


def turn_lines(x, k):
    lanes = lax.broadcasted_iota(jnp.int32, (1, 128), 1)

    def blocks(pair, n):
        if n == 4:
            return pair[::-1]
        turned = [pltpu.roll(p, 32 * n % 128, 1) for p in pair]
        over = lanes < 32 * n if n > 0 else lanes >= 128 + 32 * n
        return [jnp.where(over, turned[1 - h], turned[h]) for h in range(2)]

    pair = [x[:128], x[128:]]
    size = abs(k)
    if size >= 128:
        pair = blocks(pair, 4 if size == 512 else k // 128)
    elif size >= 8:
        if k > 0:
            moved = blocks([p[128 - k :] for p in pair], 1)
            pair = [jnp.concatenate([m, p[: 128 - k]], axis=0) for m, p in zip(moved, pair)]
        else:
            moved = blocks([p[:size] for p in pair], -1)
            pair = [jnp.concatenate([p[size:], m], axis=0) for m, p in zip(moved, pair)]
    else:
        rows = lax.broadcasted_iota(jnp.int32, (8, 128), 0)
        turned = [pltpu.roll(p, k % 128, 0) for p in pair]
        if k > 0:
            ends = [t[:8] for t in turned]
            ends = [jnp.where(rows < k, m, e) for m, e in zip(blocks(ends, 1), ends)]
            pair = [jnp.concatenate([e, t[8:]], axis=0) for e, t in zip(ends, turned)]
        else:
            ends = [t[120:] for t in turned]
            ends = [jnp.where(rows >= 8 + k, m, e) for m, e in zip(blocks(ends, -1), ends)]
            pair = [jnp.concatenate([t[:120], e], axis=0) for e, t in zip(ends, turned)]
    return jnp.concatenate(pair, axis=0)


def stand(x):
    tiles = [x[:, 128 * j : 128 * (j + 1)] for j in range(8)]
    return jnp.concatenate(
        [jnp.concatenate(tiles[4 * h : 4 * h + 4], axis=0).T for h in range(2)], axis=0
    )


def lie(x):
    tiles = [x[128 * h : 128 * (h + 1)].T for h in range(2)]
    return jnp.concatenate(
        [tiles[h][ALL * b : ALL * (b + 1)] for h in range(2) for b in range(4)], axis=1
    )


def turn_rows(x, k):
    return turn(x, k, 0)


def reduce_matrix(low, excess, rights, steps, move, keep):
    for index, k in enumerate(steps):
        high = move(low, -k)
        inverse = 1.0 / (low + high + excess)
        up = high * inverse
        down = low * inverse
        keep(index, up, down)
        excess = excess + move(up * excess, k) + move(down * excess, -k)
        rights = [r + move(up * r, k) + move(down * r, -k) for r in rights]
        low = move(up * low, k)
    inverse = 1.0 / excess
    return inverse, [r * inverse for r in rights]


def reduce_right(right, steps, move, load):
    for index, k in enumerate(steps):
        up, down = load(index)
        right = right + move(up * right, k) + move(down * right, -k)
    return right


def dense(row):
    return jnp.concatenate([row[:, 128 * i : 128 * (i + 1)] for i in range(8)], axis=0)


def natural(tile, rows):
    return jnp.concatenate(
        [jnp.broadcast_to(tile[i : i + 1, :], (rows, 128)) for i in range(8)], axis=1
    )


def factor_x_kernel(
    fields_arg, vertical_arg, kappa_arg, fields, vertical, kappa, ax, bx, qx, h1, h2, parts, done
):
    pairs = ((kappa_arg, kappa), (fields_arg, fields), (vertical_arg, vertical))
    copies = [pltpu.make_async_copy(a, b, done.at[n]) for n, (a, b) in enumerate(pairs)]
    for copy in copies:
        copy.start()
    copies[0].wait()
    half = 512
    rows = lax.broadcasted_iota(jnp.int32, (ROWS, half), 0)
    for f in range(2):
        mine = pl.ds(f * ROWS, ROWS)
        for c in range(COLS // half):
            cols = pl.ds(c * half, half)
            k = kappa[mine, cols]
            face = (k + turn(k, 1, 0)) * 0.5
            low = jnp.where((rows >= 2) & (rows <= 14), face, 0.0)
            first = jnp.where(rows == 1, face, 0.0)
            last = jnp.where(rows == 14, turn(face, -1, 0), 0.0)

            def keep(index, a, b, mine=mine, cols=cols):
                ax[index, mine, cols] = a
                bx[index, mine, cols] = b

            inverse, (one, two) = reduce_matrix(
                low, 1.0 + first + last, [first, last], X_STEPS, turn_rows, keep
            )
            qx[mine, cols] = jnp.where((rows >= 1) & (rows <= 14), inverse, 0.0)
            one = jnp.where(rows == 0, 1.0, one)
            two = jnp.where(rows == ROWS - 1, 1.0, two)
            h1[mine, cols] = one
            h2[mine, cols] = two
            sums = (
                jnp.sum(first * two, axis=0, keepdims=True),
                jnp.sum(one, axis=0, keepdims=True),
                jnp.sum(two, axis=0, keepdims=True),
                k[:1],
                k[ROWS - 1 :],
            )
            for n, row in enumerate(sums):
                for i in range(half // 128):
                    parts[n, f, pl.ds(c * (half // 128) + i, 1), :] = row[:, 128 * i : 128 * (i + 1)]
    copies[1].wait()
    copies[2].wait()


def factor_y_kernel(kappa, ay, by, qy, hy, edge):
    gy = lax.axis_index("gy")
    low_side = gy == 0
    end = jnp.where(low_side, COLS - 1, 0)
    start = COLS - 1 - end
    beside = jnp.where(low_side, COLS - 2, 1)
    cut = jnp.where(low_side, COLS - 1, 1)
    k = stand(kappa[...])
    row = lax.broadcasted_iota(jnp.int32, (256, 128), 0)
    lane = lax.broadcasted_iota(jnp.int32, (256, 128), 1)
    y = row // 128 * 512 + lane // 32 * 128 + row % 128
    face = (k + turn_lines(k, 1)) * 0.5
    low = jnp.where((y == 0) | (y == cut), 0.0, face)
    link = jnp.where(y == beside, jnp.where(low_side, turn_lines(face, -1), face), 0.0)
    ground = jnp.where(y == start, 1.0 + 0.5 * k, 1.0)

    def keep(index, up, down):
        ay[index] = up
        by[index] = down

    inverse, (profile,) = reduce_matrix(low, ground + link, [link], Y_STEPS, turn_lines, keep)
    qy[...] = jnp.where(y == end, 0.0, inverse)
    profile = lie(jnp.where(y == end, 1.0, profile))
    hy[...] = profile
    k = kappa[...]
    column = lax.broadcasted_iota(jnp.int32, (ALL, COLS), 1)
    total = jnp.sum(profile * jnp.where(column == start, 1.0 + 0.5 * k, 1.0), axis=1, keepdims=True)
    rim = jnp.sum(jnp.where(column == end, k, 0.0), axis=1, keepdims=True)
    lane = lax.broadcasted_iota(jnp.int32, (8, 128), 1)
    tile = jnp.zeros((8, 128), F32)
    for g in range(ALL // 8):
        part = slice(8 * g, 8 * g + 8)
        tile = jnp.where(lane == 4 * g, total[part], jnp.where(lane == 4 * g + 1, rim[part], tile))
    edge[...] = tile


def source_kernel(fields, fields_far, vertical, vertical_far, h1, h2, parts, after, source, keep, send):
    del after
    even = lax.axis_index("gx") % 2 == 0
    here = fields[...]
    v = vertical[...]
    s = here + (v + vertical_far[...]) * 0.5 * (fields_far[...] - here) - v * 0.5 * here
    source[...] = s
    elements = []
    for f in range(2):
        mine = slice(f * ROWS, (f + 1) * ROWS)
        first = dense(jnp.sum(h1[mine, :] * s[mine, :], axis=0, keepdims=True))
        last = dense(jnp.sum(h2[mine, :] * s[mine, :], axis=0, keepdims=True))
        elements.append((parts[0, f], parts[1, f], parts[2, f], first, last, parts[3, f], parts[4, f]))
    for n, (one, two) in enumerate(zip(*elements)):
        keep[n] = jnp.where(even, one, two)
        send[n] = jnp.where(even, two, one)


def local_x_kernel(source, ax, bx, qx, out):
    half = 512
    for f in range(2):
        mine = pl.ds(f * ROWS, ROWS)
        for c in range(COLS // half):
            cols = pl.ds(c * half, half)
            r = source[mine, cols]
            r = reduce_right(r, X_STEPS, turn_rows, lambda i: (ax[i, mine, cols], bx[i, mine, cols]))
            out[mine, cols] = r * qx[mine, cols]


def merge(one, two):
    g, sl, sr, rl, rr = one
    g2, sl2, sr2, rl2, rr2 = two
    s = sr + sl2
    r = rr + rl2
    inverse = 1.0 / (g + g2 + s)
    a = g * inverse
    b = g2 * inverse
    return (a * g2, sl + a * s, sr2 + b * s, rl + a * r, rr2 + b * r), (a, b, r * inverse)


def behind(face, two):
    g, s, sr, r, rr = two
    inverse = 1.0 / (face + g + s)
    a = face * inverse
    b = g * inverse
    return (a * g, a * s, sr + b * s, a * r, rr + b * r), (a, b, r * inverse)


def load(ref):
    return tuple(ref[n] for n in range(7))


def within(node, left, right):
    a, b, c = node
    return (a * left[0] + b * right[0], a * left[1] + b * right[1], a * left[2] + b * right[2] + c)


def chip_kernel(keep, got, chip, middle):
    even = lax.axis_index("gx") % 2 == 0
    mine, other = load(keep), load(got)
    first = [jnp.where(even, m, o) for m, o in zip(mine, other)]
    second = [jnp.where(even, o, m) for m, o in zip(mine, other)]
    tail, start = behind((first[6] + second[5]) * 0.5, second[:5])
    element, end = merge(first[:5], tail)
    for n, value in enumerate((*element, first[5], second[6])):
        chip[n] = value
    for n, value in enumerate((*end, *start)):
        middle[n] = value


def slab_kernel(chip, far1, far3, far2, middle, message, nodes):
    y = lax.axis_index("gx") // 2 % 4
    arrived = [load(chip), load(far1), load(far2), load(far3)]
    chips = []
    for m in range(4):
        chosen = arrived[0]
        for flip in range(1, 4):
            here = y ^ flip == m
            chosen = [jnp.where(here, a, c) for a, c in zip(arrived[flip], chosen)]
        chips.append(chosen)
    element = chips[0][:5]
    inner, fronts = [], []
    for m in range(1, 4):
        tail, front = behind((chips[m - 1][6] + chips[m][5]) * 0.5, chips[m][:5])
        element, node = merge(element, tail)
        inner.append(node)
        fronts.append(front)
    for n, value in enumerate((*element, chips[0][5], chips[3][6])):
        for j in range(8):
            message[j, n] = value
    zero, one = jnp.zeros((8, 128), F32), jnp.ones((8, 128), F32)
    left = (one, zero, zero)
    lasts = [(zero, one, zero)]
    for node in inner[::-1]:
        lasts.append(within(node, left, lasts[-1]))
    lasts = lasts[::-1]
    firsts = [left] + [within(fronts[m - 1], lasts[m - 1], lasts[m]) for m in range(1, 4)]
    first, last = firsts[0], lasts[0]
    for m in range(1, 4):
        first = [jnp.where(y == m, new, old) for new, old in zip(firsts[m], first)]
        last = [jnp.where(y == m, new, old) for new, old in zip(lasts[m], last)]
    before = within(tuple(middle[n] for n in range(3)), first, last)
    second = within(tuple(middle[n] for n in range(3, 6)), before, last)
    for n, trio in enumerate((first, before, second, last)):
        for m in range(3):
            nodes[n, m] = trio[m]


def ends_kernel(got, nodes, mine, other):
    gx = lax.axis_index("gx")
    slab = gx // 8
    even = gx % 2 == 0
    zero = jnp.zeros((8, 128), F32)
    slabs, fronts = [], []
    for z in range(8):
        face = got[z, 5] * 0.5 if z == 0 else (got[z - 1, 6] + got[z, 5]) * 0.5
        tail, front = behind(face, tuple(got[z, n] for n in range(5)))
        slabs.append(tail)
        fronts.append(front)
    g, _, conduct, _, right = slabs[0]
    conduct = conduct + g
    ratios, offsets = [], []
    for z in range(1, 8):
        g, sl, sr, rl, rr = slabs[z]
        conduct = conduct + sl
        right = right + rl
        inverse = 1.0 / (conduct + g)
        f = g * inverse
        ratios.append(f)
        offsets.append(right * inverse)
        conduct = sr + f * conduct
        right = rr + f * right
    value = right / (conduct + got[7, 6] * 0.5)
    values = [value]
    for k in range(6, -1, -1):
        value = ratios[k] * value + offsets[k]
        values.append(value)
    values = [zero] + values[::-1]
    first, last = zero, zero
    for z in range(8):
        a, b, c = fronts[z]
        first = jnp.where(slab == z, a * values[z] + b * values[z + 1] + c, first)
        last = jnp.where(slab == z, values[z + 1], last)
    row = [nodes[n, 0] * first + nodes[n, 1] * last + nodes[n, 2] for n in range(4)]
    for n in range(2):
        mine[n] = jnp.where(even, row[n], row[n + 2])
        other[n] = jnp.where(even, row[n + 2], row[n])


def section_kernel(mine, other, local, h1, h2, hy, edge, section, message):
    core = lax.axis_index("gx") % 2
    lane = lax.broadcasted_iota(jnp.int32, (8, 128), 1)
    tile = edge[...]
    for f in range(2):
        first = jnp.where(core == f, mine[0], other[0])
        last = jnp.where(core == f, mine[1], other[1])
        rows = slice(f * ROWS, (f + 1) * ROWS)
        s = local[rows, :] + h1[rows, :] * natural(first, ROWS) + h2[rows, :] * natural(last, ROWS)
        section[rows, :] = s
        total = jnp.sum(hy[rows, :] * s, axis=1, keepdims=True)
        for g in range(2):
            tile = jnp.where(lane == 4 * (2 * f + g) + 2, total[8 * g : 8 * g + 8], tile)
    message[...] = tile


def local_y_kernel(section, ay, by, qy, out):
    r = stand(section[...])
    r = reduce_right(r, Y_STEPS, turn_lines, lambda i: (ay[i], by[i]))
    out[...] = lie(r * qy[...])


def output_kernel(message, far, local, hy, out):
    for g in range(ALL // 8):
        part = slice(8 * g, 8 * g + 8)
        e, k, r = (message[:, 4 * g + n : 4 * g + n + 1] for n in range(3))
        e2, k2, r2 = (far[:, 4 * g + n : 4 * g + n + 1] for n in range(3))
        c = (k + k2) * 0.5
        value = ((e2 + c) * r + c * r2) / (e * e2 + c * (e + e2))
        out[part, :] = local[part, :] + hy[part, :] * value


def call(kernel, outs, specs, flops=0, size=0, scratch=()):
    return pl.pallas_call(
        kernel,
        out_shape=outs,
        in_specs=specs,
        out_specs=jax.tree.map(lambda _: VMEM, outs),
        scratch_shapes=scratch,
        compiler_params=PARAMS,
        cost_estimate=pl.CostEstimate(flops=flops, bytes_accessed=size, transcendentals=0),
    )


SLAB_GROUPS = [[8 * b + a for b in range(8)] for a in range(8)]
CORES = [(i, i ^ 1) for i in range(64)]


def chips_across(flip):
    return [(i, i ^ 2 * flip) for i in range(64)]


def local(fields, kappa, vertical):
    grid = (ALL, COLS)
    swap = [(0, 1), (1, 0)]
    fields_far = lax.ppermute(fields, "gz", swap)
    vertical_far = lax.ppermute(vertical, "gz", swap)
    full = shape(*grid)
    half = shape(7, 8, 128)
    standing = shape(256, 128)
    fields_here, vertical_here, kappa_here, ax, bx, qx, h1, h2, parts = call(
        factor_x_kernel,
        (full, full, full, shape(4, *grid), shape(4, *grid), full, full, full, shape(5, 2, 8, 128)),
        [HBM] * 3,
        flops=4_000_000,
        size=2_000_000,
        scratch=[pltpu.SemaphoreType.DMA((3,))],
    )(*(pltpu.with_memory_space_constraint(x.reshape(grid), pltpu.HBM) for x in (fields, vertical, kappa)))
    ay, by, qy, hy, edge = call(
        factor_y_kernel,
        (shape(10, 256, 128), shape(10, 256, 128), standing, full, shape(8, 128)),
        [VMEM],
        flops=20_000_000,
        size=4_000_000,
    )(kappa_here)
    source, keep, send = call(source_kernel, (full, half, half), [VMEM] * 8)(
        fields_here, fields_far.reshape(grid), vertical_here, vertical_far.reshape(grid),
        h1, h2, parts, edge,
    )
    got = lax.ppermute(send, "gx", CORES)
    local_x = call(local_x_kernel, full, [VMEM] * 4, flops=1_000_000, size=1_000_000)(source, ax, bx, qx)
    chip, middle = call(chip_kernel, (half, shape(6, 8, 128)), [VMEM] * 2)(keep, got)
    far = [lax.ppermute(chip, "gx", chips_across(flip)) for flip in (1, 3, 2)]
    message, nodes = call(
        slab_kernel, (shape(8, 7, 8, 128), shape(4, 3, 8, 128)), [VMEM] * 5
    )(chip, *far, middle)
    got = lax.all_to_all(message, "gx", 0, 0, axis_index_groups=SLAB_GROUPS, tiled=True)
    mine, other = call(
        ends_kernel, (shape(2, 8, 128), shape(2, 8, 128)), [VMEM, VMEM]
    )(got, nodes)
    other = lax.ppermute(other, "gx", CORES)
    section, message = call(
        section_kernel, (full, shape(8, 128)), [VMEM] * 7
    )(mine, other, local_x, h1, h2, hy, edge)
    far = lax.ppermute(message, "gy", swap)
    local_y = call(local_y_kernel, full, [VMEM] * 4, flops=4_000_000, size=3_000_000)(section, ay, by, qy)
    out = call(output_kernel, full, [VMEM] * 4)(message, far, local_y, hy)
    return out.reshape(fields.shape)


def solution(mesh):
    spec = P(None, "gz", "gx", "gy")
    return jax.shard_map(
        local, mesh=mesh, in_specs=(spec, spec, spec), out_specs=spec, check_vma=False
    )
```

```python
import functools

import jax
import jax.numpy as jnp
from jax import lax
from jax.experimental import pallas as pl
from jax.experimental.pallas import tpu as pltpu
from jax.sharding import PartitionSpec as P

F32 = jnp.float32
ROWS = 16
COLS = 1024
ALL = 2 * ROWS
VMEM = pl.BlockSpec(memory_space=pltpu.VMEM)
HBM = pl.BlockSpec(memory_space=pltpu.HBM)
X_STEPS = (1, 2, 4, 8)
Y_STEPS = (1, 2, 4, 8, 16, 32, 64, 128, 256, 512)
PARAMS = pltpu.CompilerParams(vmem_limit_bytes=40 * 1024 * 1024)


def shape(*dims):
    return jax.ShapeDtypeStruct(dims, F32)


def turn(x, k, axis):
    n = x.shape[axis]
    k = k % n
    unit = 128 if axis == 1 else 8
    if k == 0:
        return x
    if k % unit == 0:
        low = lax.slice_in_dim(x, n - k, n, axis=axis)
        high = lax.slice_in_dim(x, 0, n - k, axis=axis)
        return jnp.concatenate([low, high], axis=axis)
    return pltpu.roll(x, k, axis)


def turn_lines(x, k):
    lanes = lax.broadcasted_iota(jnp.int32, (1, 128), 1)

    def blocks(pair, n):
        if n == 4:
            return pair[::-1]
        turned = [pltpu.roll(p, 32 * n % 128, 1) for p in pair]
        over = lanes < 32 * n if n > 0 else lanes >= 128 + 32 * n
        return [jnp.where(over, turned[1 - h], turned[h]) for h in range(2)]

    pair = [x[:128], x[128:]]
    size = abs(k)
    if size >= 128:
        pair = blocks(pair, 4 if size == 512 else k // 128)
    elif size >= 8:
        if k > 0:
            moved = blocks([p[128 - k :] for p in pair], 1)
            pair = [jnp.concatenate([m, p[: 128 - k]], axis=0) for m, p in zip(moved, pair)]
        else:
            moved = blocks([p[:size] for p in pair], -1)
            pair = [jnp.concatenate([p[size:], m], axis=0) for m, p in zip(moved, pair)]
    else:
        rows = lax.broadcasted_iota(jnp.int32, (8, 128), 0)
        turned = [pltpu.roll(p, k % 128, 0) for p in pair]
        if k > 0:
            ends = [t[:8] for t in turned]
            ends = [jnp.where(rows < k, m, e) for m, e in zip(blocks(ends, 1), ends)]
            pair = [jnp.concatenate([e, t[8:]], axis=0) for e, t in zip(ends, turned)]
        else:
            ends = [t[120:] for t in turned]
            ends = [jnp.where(rows >= 8 + k, m, e) for m, e in zip(blocks(ends, -1), ends)]
            pair = [jnp.concatenate([t[:120], e], axis=0) for e, t in zip(ends, turned)]
    return jnp.concatenate(pair, axis=0)


def stand(x):
    tiles = [x[:, 128 * j : 128 * (j + 1)] for j in range(8)]
    return jnp.concatenate(
        [jnp.concatenate(tiles[4 * h : 4 * h + 4], axis=0).T for h in range(2)], axis=0
    )


def lie(x):
    tiles = [x[128 * h : 128 * (h + 1)].T for h in range(2)]
    return jnp.concatenate(
        [tiles[h][ALL * b : ALL * (b + 1)] for h in range(2) for b in range(4)], axis=1
    )


def turn_rows(x, k):
    return turn(x, k, 0)


def reduce_matrix(low, excess, rights, steps, move, keep):
    for index, k in enumerate(steps):
        high = move(low, -k)
        inverse = 1.0 / (low + high + excess)
        up = high * inverse
        down = low * inverse
        keep(index, up, down)
        excess = excess + move(up * excess, k) + move(down * excess, -k)
        rights = [r + move(up * r, k) + move(down * r, -k) for r in rights]
        low = move(up * low, k)
    inverse = 1.0 / excess
    return inverse, [r * inverse for r in rights]


def reduce_right(right, steps, move, load):
    for index, k in enumerate(steps):
        up, down = load(index)
        right = right + move(up * right, k) + move(down * right, -k)
    return right


def dense(row):
    return jnp.concatenate([row[:, 128 * i : 128 * (i + 1)] for i in range(8)], axis=0)


def natural(tile, rows):
    return jnp.concatenate(
        [jnp.broadcast_to(tile[i : i + 1, :], (rows, 128)) for i in range(8)], axis=1
    )


def factor_x_kernel(
    fields_arg, vertical_arg, kappa_arg, fields, vertical, kappa, ax, bx, qx, h1, h2, parts, done
):
    pairs = ((kappa_arg, kappa), (fields_arg, fields), (vertical_arg, vertical))
    copies = [pltpu.make_async_copy(a, b, done.at[n]) for n, (a, b) in enumerate(pairs)]
    for copy in copies:
        copy.start()
    copies[0].wait()
    half = 512
    rows = lax.broadcasted_iota(jnp.int32, (ROWS, half), 0)
    for f in range(2):
        mine = pl.ds(f * ROWS, ROWS)
        for c in range(COLS // half):
            cols = pl.ds(c * half, half)
            k = kappa[mine, cols]
            face = (k + turn(k, 1, 0)) * 0.5
            low = jnp.where((rows >= 2) & (rows <= 14), face, 0.0)
            first = jnp.where(rows == 1, face, 0.0)
            last = jnp.where(rows == 14, turn(face, -1, 0), 0.0)

            def keep(index, a, b, mine=mine, cols=cols):
                ax[index, mine, cols] = a
                bx[index, mine, cols] = b

            inverse, (one, two) = reduce_matrix(
                low, 1.0 + first + last, [first, last], X_STEPS, turn_rows, keep
            )
            qx[mine, cols] = jnp.where((rows >= 1) & (rows <= 14), inverse, 0.0)
            one = jnp.where(rows == 0, 1.0, one)
            two = jnp.where(rows == ROWS - 1, 1.0, two)
            h1[mine, cols] = one
            h2[mine, cols] = two
            sums = (
                jnp.sum(first * two, axis=0, keepdims=True),
                jnp.sum(one, axis=0, keepdims=True),
                jnp.sum(two, axis=0, keepdims=True),
                k[:1],
                k[ROWS - 1 :],
            )
            for n, row in enumerate(sums):
                for i in range(half // 128):
                    parts[n, f, pl.ds(c * (half // 128) + i, 1), :] = row[:, 128 * i : 128 * (i + 1)]
    copies[1].wait()
    copies[2].wait()


def factor_y_kernel(kappa, ay, by, qy, hy, edge):
    gy = lax.axis_index("gy")
    low_side = gy == 0
    end = jnp.where(low_side, COLS - 1, 0)
    start = COLS - 1 - end
    beside = jnp.where(low_side, COLS - 2, 1)
    cut = jnp.where(low_side, COLS - 1, 1)
    k = stand(kappa[...])
    row = lax.broadcasted_iota(jnp.int32, (256, 128), 0)
    lane = lax.broadcasted_iota(jnp.int32, (256, 128), 1)
    y = row // 128 * 512 + lane // 32 * 128 + row % 128
    face = (k + turn_lines(k, 1)) * 0.5
    low = jnp.where((y == 0) | (y == cut), 0.0, face)
    link = jnp.where(y == beside, jnp.where(low_side, turn_lines(face, -1), face), 0.0)
    ground = jnp.where(y == start, 1.0 + 0.5 * k, 1.0)

    def keep(index, up, down):
        ay[index] = up
        by[index] = down

    inverse, (profile,) = reduce_matrix(low, ground + link, [link], Y_STEPS, turn_lines, keep)
    qy[...] = jnp.where(y == end, 0.0, inverse)
    profile = lie(jnp.where(y == end, 1.0, profile))
    hy[...] = profile
    k = kappa[...]
    column = lax.broadcasted_iota(jnp.int32, (ALL, COLS), 1)
    total = jnp.sum(profile * jnp.where(column == start, 1.0 + 0.5 * k, 1.0), axis=1, keepdims=True)
    rim = jnp.sum(jnp.where(column == end, k, 0.0), axis=1, keepdims=True)
    lane = lax.broadcasted_iota(jnp.int32, (8, 128), 1)
    tile = jnp.zeros((8, 128), F32)
    for g in range(ALL // 8):
        part = slice(8 * g, 8 * g + 8)
        tile = jnp.where(lane == 4 * g, total[part], jnp.where(lane == 4 * g + 1, rim[part], tile))
    edge[...] = tile


def source_kernel(fields, fields_far, vertical, vertical_far, h1, h2, parts, after, source, keep, send):
    del after
    even = lax.axis_index("gx") % 2 == 0
    here = fields[...]
    v = vertical[...]
    s = here + (v + vertical_far[...]) * 0.5 * (fields_far[...] - here) - v * 0.5 * here
    source[...] = s
    elements = []
    for f in range(2):
        mine = slice(f * ROWS, (f + 1) * ROWS)
        first = dense(jnp.sum(h1[mine, :] * s[mine, :], axis=0, keepdims=True))
        last = dense(jnp.sum(h2[mine, :] * s[mine, :], axis=0, keepdims=True))
        elements.append((parts[0, f], parts[1, f], parts[2, f], first, last, parts[3, f], parts[4, f]))
    for n, (one, two) in enumerate(zip(*elements)):
        keep[n] = jnp.where(even, one, two)
        send[n] = jnp.where(even, two, one)


def local_x_kernel(source, ax, bx, qx, out):
    half = 512
    for f in range(2):
        mine = pl.ds(f * ROWS, ROWS)
        for c in range(COLS // half):
            cols = pl.ds(c * half, half)
            r = source[mine, cols]
            r = reduce_right(r, X_STEPS, turn_rows, lambda i: (ax[i, mine, cols], bx[i, mine, cols]))
            out[mine, cols] = r * qx[mine, cols]


def merge(one, two):
    g, sl, sr, rl, rr = one
    g2, sl2, sr2, rl2, rr2 = two
    s = sr + sl2
    r = rr + rl2
    inverse = 1.0 / (g + g2 + s)
    a = g * inverse
    b = g2 * inverse
    return (a * g2, sl + a * s, sr2 + b * s, rl + a * r, rr2 + b * r), (a, b, r * inverse)


def behind(face, two):
    g, s, sr, r, rr = two
    inverse = 1.0 / (face + g + s)
    a = face * inverse
    b = g * inverse
    return (a * g, a * s, sr + b * s, a * r, rr + b * r), (a, b, r * inverse)


def load(ref):
    return tuple(ref[n] for n in range(7))


def within(node, left, right):
    a, b, c = node
    return (a * left[0] + b * right[0], a * left[1] + b * right[1], a * left[2] + b * right[2] + c)


def chip_kernel(keep, got, chip, middle):
    even = lax.axis_index("gx") % 2 == 0
    mine, other = load(keep), load(got)
    first = [jnp.where(even, m, o) for m, o in zip(mine, other)]
    second = [jnp.where(even, o, m) for m, o in zip(mine, other)]
    tail, start = behind((first[6] + second[5]) * 0.5, second[:5])
    element, end = merge(first[:5], tail)
    for n, value in enumerate((*element, first[5], second[6])):
        chip[n] = value
    for n, value in enumerate((*end, *start)):
        middle[n] = value


def slab_kernel(chip, far1, far3, far2, middle, message, nodes):
    y = lax.axis_index("gx") // 2 % 4
    arrived = [load(chip), load(far1), load(far2), load(far3)]
    chips = []
    for m in range(4):
        chosen = arrived[0]
        for flip in range(1, 4):
            here = y ^ flip == m
            chosen = [jnp.where(here, a, c) for a, c in zip(arrived[flip], chosen)]
        chips.append(chosen)
    element = chips[0][:5]
    inner, fronts = [], []
    for m in range(1, 4):
        tail, front = behind((chips[m - 1][6] + chips[m][5]) * 0.5, chips[m][:5])
        element, node = merge(element, tail)
        inner.append(node)
        fronts.append(front)
    for n, value in enumerate((*element, chips[0][5], chips[3][6])):
        for j in range(8):
            message[j, n] = value
    zero, one = jnp.zeros((8, 128), F32), jnp.ones((8, 128), F32)
    left = (one, zero, zero)
    lasts = [(zero, one, zero)]
    for node in inner[::-1]:
        lasts.append(within(node, left, lasts[-1]))
    lasts = lasts[::-1]
    firsts = [left] + [within(fronts[m - 1], lasts[m - 1], lasts[m]) for m in range(1, 4)]
    first, last = firsts[0], lasts[0]
    for m in range(1, 4):
        first = [jnp.where(y == m, new, old) for new, old in zip(firsts[m], first)]
        last = [jnp.where(y == m, new, old) for new, old in zip(lasts[m], last)]
    before = within(tuple(middle[n] for n in range(3)), first, last)
    second = within(tuple(middle[n] for n in range(3, 6)), before, last)
    for n, trio in enumerate((first, before, second, last)):
        for m in range(3):
            nodes[n, m] = trio[m]


def ends_kernel(got, nodes, mine, other):
    gx = lax.axis_index("gx")
    slab = gx // 8
    even = gx % 2 == 0
    zero = jnp.zeros((8, 128), F32)
    slabs, fronts = [], []
    for z in range(8):
        face = got[z, 5] * 0.5 if z == 0 else (got[z - 1, 6] + got[z, 5]) * 0.5
        tail, front = behind(face, tuple(got[z, n] for n in range(5)))
        slabs.append(tail)
        fronts.append(front)
    g, _, conduct, _, right = slabs[0]
    conduct = conduct + g
    ratios, offsets = [], []
    for z in range(1, 8):
        g, sl, sr, rl, rr = slabs[z]
        conduct = conduct + sl
        right = right + rl
        inverse = 1.0 / (conduct + g)
        f = g * inverse
        ratios.append(f)
        offsets.append(right * inverse)
        conduct = sr + f * conduct
        right = rr + f * right
    value = right / (conduct + got[7, 6] * 0.5)
    values = [value]
    for k in range(6, -1, -1):
        value = ratios[k] * value + offsets[k]
        values.append(value)
    values = [zero] + values[::-1]
    first, last = zero, zero
    for z in range(8):
        a, b, c = fronts[z]
        first = jnp.where(slab == z, a * values[z] + b * values[z + 1] + c, first)
        last = jnp.where(slab == z, values[z + 1], last)
    row = [nodes[n, 0] * first + nodes[n, 1] * last + nodes[n, 2] for n in range(4)]
    for n in range(2):
        mine[n] = jnp.where(even, row[n], row[n + 2])
        other[n] = jnp.where(even, row[n + 2], row[n])


def section_kernel(mine, other, local, h1, h2, hy, edge, section, message):
    core = lax.axis_index("gx") % 2
    lane = lax.broadcasted_iota(jnp.int32, (8, 128), 1)
    tile = edge[...]
    for f in range(2):
        first = jnp.where(core == f, mine[0], other[0])
        last = jnp.where(core == f, mine[1], other[1])
        rows = slice(f * ROWS, (f + 1) * ROWS)
        s = local[rows, :] + h1[rows, :] * natural(first, ROWS) + h2[rows, :] * natural(last, ROWS)
        section[rows, :] = s
        total = jnp.sum(hy[rows, :] * s, axis=1, keepdims=True)
        for g in range(2):
            tile = jnp.where(lane == 4 * (2 * f + g) + 2, total[8 * g : 8 * g + 8], tile)
    message[...] = tile


def local_y_kernel(section, ay, by, qy, out):
    r = stand(section[...])
    r = reduce_right(r, Y_STEPS, turn_lines, lambda i: (ay[i], by[i]))
    out[...] = lie(r * qy[...])


def output_kernel(message, far, local, hy, out, rows, done):
    copies = []
    for g in range(ALL // 8):
        part = pl.ds(8 * g, 8)
        e, k, r = (message[:, 4 * g + n : 4 * g + n + 1] for n in range(3))
        e2, k2, r2 = (far[:, 4 * g + n : 4 * g + n + 1] for n in range(3))
        c = (k + k2) * 0.5
        value = ((e2 + c) * r + c * r2) / (e * e2 + c * (e + e2))
        rows[part, :] = local[part, :] + hy[part, :] * value
        copies.append(pltpu.make_async_copy(rows.at[part], out.at[part], done.at[g]))
        copies[-1].start()
    for copy in copies:
        copy.wait()


def call(kernel, outs, specs, flops=0, size=0, scratch=()):
    return pl.pallas_call(
        kernel,
        out_shape=outs,
        in_specs=specs,
        out_specs=jax.tree.map(lambda _: VMEM, outs),
        scratch_shapes=scratch,
        compiler_params=PARAMS,
        cost_estimate=pl.CostEstimate(flops=flops, bytes_accessed=size, transcendentals=0),
    )


SLAB_GROUPS = [[8 * b + a for b in range(8)] for a in range(8)]
CORES = [(i, i ^ 1) for i in range(64)]


def chips_across(flip):
    return [(i, i ^ 2 * flip) for i in range(64)]


def local(fields, kappa, vertical):
    grid = (ALL, COLS)
    swap = [(0, 1), (1, 0)]
    fields_far = lax.ppermute(fields, "gz", swap)
    vertical_far = lax.ppermute(vertical, "gz", swap)
    full = shape(*grid)
    half = shape(7, 8, 128)
    standing = shape(256, 128)
    fields_here, vertical_here, kappa_here, ax, bx, qx, h1, h2, parts = call(
        factor_x_kernel,
        (full, full, full, shape(4, *grid), shape(4, *grid), full, full, full, shape(5, 2, 8, 128)),
        [HBM] * 3,
        flops=4_000_000,
        size=2_000_000,
        scratch=[pltpu.SemaphoreType.DMA((3,))],
    )(*(pltpu.with_memory_space_constraint(x.reshape(grid), pltpu.HBM) for x in (fields, vertical, kappa)))
    ay, by, qy, hy, edge = call(
        factor_y_kernel,
        (shape(10, 256, 128), shape(10, 256, 128), standing, full, shape(8, 128)),
        [VMEM],
        flops=20_000_000,
        size=4_000_000,
    )(kappa_here)
    source, keep, send = call(source_kernel, (full, half, half), [VMEM] * 8)(
        fields_here, fields_far.reshape(grid), vertical_here, vertical_far.reshape(grid),
        h1, h2, parts, edge,
    )
    got = lax.ppermute(send, "gx", CORES)
    local_x = call(local_x_kernel, full, [VMEM] * 4, flops=1_000_000, size=1_000_000)(source, ax, bx, qx)
    chip, middle = call(chip_kernel, (half, shape(6, 8, 128)), [VMEM] * 2)(keep, got)
    far = [lax.ppermute(chip, "gx", chips_across(flip)) for flip in (1, 3, 2)]
    message, nodes = call(
        slab_kernel, (shape(8, 7, 8, 128), shape(4, 3, 8, 128)), [VMEM] * 5
    )(chip, *far, middle)
    got = lax.all_to_all(message, "gx", 0, 0, axis_index_groups=SLAB_GROUPS, tiled=True)
    mine, other = call(
        ends_kernel, (shape(2, 8, 128), shape(2, 8, 128)), [VMEM, VMEM]
    )(got, nodes)
    other = lax.ppermute(other, "gx", CORES)
    section, message = call(
        section_kernel, (full, shape(8, 128)), [VMEM] * 7
    )(mine, other, local_x, h1, h2, hy, edge)
    far = lax.ppermute(message, "gy", swap)
    local_y = call(local_y_kernel, full, [VMEM] * 4, flops=4_000_000, size=3_000_000)(section, ay, by, qy)
    out = pl.pallas_call(
        output_kernel,
        out_shape=full,
        in_specs=[VMEM] * 4,
        out_specs=pl.BlockSpec(memory_space=pltpu.HBM),
        scratch_shapes=[pltpu.VMEM(grid, F32), pltpu.SemaphoreType.DMA((ALL // 8,))],
        compiler_params=PARAMS,
    )(message, far, local_y, hy)
    return out.reshape(fields.shape)


def solution(mesh):
    spec = P(None, "gz", "gx", "gy")
    return jax.shard_map(
        local, mesh=mesh, in_specs=(spec, spec, spec), out_specs=spec, check_vma=False
    )
```

```python
import functools

import jax
import jax.numpy as jnp
from jax import lax
from jax.experimental import pallas as pl
from jax.experimental.pallas import tpu as pltpu
from jax.sharding import PartitionSpec as P

F32 = jnp.float32
ROWS = 16
COLS = 1024
ALL = 2 * ROWS
VMEM = pl.BlockSpec(memory_space=pltpu.VMEM)
HBM = pl.BlockSpec(memory_space=pltpu.HBM)
X_STEPS = (1, 2, 4, 8, 16)
Y_STEPS = (1, 2, 4, 8, 16, 32, 64, 128, 256, 512)
PARAMS = pltpu.CompilerParams(vmem_limit_bytes=40 * 1024 * 1024)


def shape(*dims):
    return jax.ShapeDtypeStruct(dims, F32)


def turn(x, k, axis):
    n = x.shape[axis]
    k = k % n
    unit = 128 if axis == 1 else 8
    if k == 0:
        return x
    if k % unit == 0:
        low = lax.slice_in_dim(x, n - k, n, axis=axis)
        high = lax.slice_in_dim(x, 0, n - k, axis=axis)
        return jnp.concatenate([low, high], axis=axis)
    return pltpu.roll(x, k, axis)


def turn_lines(x, k):
    lanes = lax.broadcasted_iota(jnp.int32, (1, 128), 1)

    def blocks(pair, n):
        if n == 4:
            return pair[::-1]
        turned = [pltpu.roll(p, 32 * n % 128, 1) for p in pair]
        over = lanes < 32 * n if n > 0 else lanes >= 128 + 32 * n
        return [jnp.where(over, turned[1 - h], turned[h]) for h in range(2)]

    pair = [x[:128], x[128:]]
    size = abs(k)
    if size >= 128:
        pair = blocks(pair, 4 if size == 512 else k // 128)
    elif size >= 8:
        if k > 0:
            moved = blocks([p[128 - k :] for p in pair], 1)
            pair = [jnp.concatenate([m, p[: 128 - k]], axis=0) for m, p in zip(moved, pair)]
        else:
            moved = blocks([p[:size] for p in pair], -1)
            pair = [jnp.concatenate([p[size:], m], axis=0) for m, p in zip(moved, pair)]
    else:
        rows = lax.broadcasted_iota(jnp.int32, (8, 128), 0)
        turned = [pltpu.roll(p, k % 128, 0) for p in pair]
        if k > 0:
            ends = [t[:8] for t in turned]
            ends = [jnp.where(rows < k, m, e) for m, e in zip(blocks(ends, 1), ends)]
            pair = [jnp.concatenate([e, t[8:]], axis=0) for e, t in zip(ends, turned)]
        else:
            ends = [t[120:] for t in turned]
            ends = [jnp.where(rows >= 8 + k, m, e) for m, e in zip(blocks(ends, -1), ends)]
            pair = [jnp.concatenate([t[:120], e], axis=0) for e, t in zip(ends, turned)]
    return jnp.concatenate(pair, axis=0)


def stand(x):
    tiles = [x[:, 128 * j : 128 * (j + 1)] for j in range(8)]
    return jnp.concatenate(
        [jnp.concatenate(tiles[4 * h : 4 * h + 4], axis=0).T for h in range(2)], axis=0
    )


def lie(x):
    tiles = [x[128 * h : 128 * (h + 1)].T for h in range(2)]
    return jnp.concatenate(
        [tiles[h][ALL * b : ALL * (b + 1)] for h in range(2) for b in range(4)], axis=1
    )


def turn_rows(x, k):
    return turn(x, k, 0)


def reduce_matrix(low, excess, rights, steps, move, keep):
    for index, k in enumerate(steps):
        high = move(low, -k)
        inverse = 1.0 / (low + high + excess)
        up = high * inverse
        down = low * inverse
        keep(index, up, down)
        excess = excess + move(up * excess, k) + move(down * excess, -k)
        rights = [r + move(up * r, k) + move(down * r, -k) for r in rights]
        low = move(up * low, k)
    inverse = 1.0 / excess
    return inverse, [r * inverse for r in rights]


def reduce_right(right, steps, move, load):
    for index, k in enumerate(steps):
        up, down = load(index)
        right = right + move(up * right, k) + move(down * right, -k)
    return right


def dense(row):
    return jnp.concatenate([row[:, 128 * i : 128 * (i + 1)] for i in range(8)], axis=0)


def natural(tile, rows):
    return jnp.concatenate(
        [jnp.broadcast_to(tile[i : i + 1, :], (rows, 128)) for i in range(8)], axis=1
    )


def own(even, mine, other):
    return jnp.concatenate([jnp.where(even, mine, other), jnp.where(even, other, mine)], axis=0)


def input_kernel(fields, vertical, kappa, same, cross, swapped, kappa_own, done):
    core = lax.axis_index("gx") % 2
    other = 1 - core
    pairs = (
        (fields.at[core], same.at[0]),
        (vertical.at[core], same.at[1]),
        (fields.at[other], cross.at[0]),
        (vertical.at[other], cross.at[1]),
        (fields.at[other], swapped.at[0]),
        (vertical.at[other], swapped.at[1]),
        (kappa.at[other], swapped.at[2]),
        (kappa.at[core], kappa_own),
    )
    copies = [pltpu.make_async_copy(a, b, done.at[n]) for n, (a, b) in enumerate(pairs)]
    for copy in copies:
        copy.start()
    for copy in copies:
        copy.wait()


def factor_x_kernel(kappa_own, swapped, kappa, ax, bx, qx, h1, h2, parts):
    even = lax.axis_index("gx") % 2 == 0
    kappa[...] = own(even, kappa_own[...], swapped[2])
    width = 256
    rows = lax.broadcasted_iota(jnp.int32, (ALL, width), 0)
    inside = (rows >= 1) & (rows <= ALL - 2)
    for c in range(COLS // width):
        cols = pl.ds(c * width, width)
        k = kappa[:, cols]
        face = (k + turn(k, 1, 0)) * 0.5
        low = jnp.where((rows >= 2) & (rows <= ALL - 2), face, 0.0)
        first = jnp.where(rows == 1, face, 0.0)
        last = jnp.where(rows == ALL - 2, turn(face, -1, 0), 0.0)

        def keep(index, a, b, cols=cols):
            ax[index, :, cols] = a
            bx[index, :, cols] = b

        inverse, (one, two) = reduce_matrix(
            low, 1.0 + first + last, [first, last], X_STEPS, turn_rows, keep
        )
        qx[:, cols] = jnp.where(inside, inverse, 0.0)
        one = jnp.where(rows == 0, 1.0, jnp.where(inside, one, 0.0))
        two = jnp.where(rows == ALL - 1, 1.0, jnp.where(inside, two, 0.0))
        h1[:, cols] = one
        h2[:, cols] = two
        sums = (
            jnp.sum(first * two, axis=0, keepdims=True),
            jnp.sum(one, axis=0, keepdims=True),
            jnp.sum(two, axis=0, keepdims=True),
            k[:1],
            k[ALL - 1 :],
        )
        for n, row in enumerate(sums):
            for i in range(width // 128):
                parts[n, pl.ds(c * (width // 128) + i, 1), :] = row[:, 128 * i : 128 * (i + 1)]


def factor_y_kernel(kappa, ay, by, qy, hy, edge):
    gy = lax.axis_index("gy")
    low_side = gy == 0
    end = jnp.where(low_side, COLS - 1, 0)
    start = COLS - 1 - end
    beside = jnp.where(low_side, COLS - 2, 1)
    cut = jnp.where(low_side, COLS - 1, 1)
    k = stand(kappa[...])
    row = lax.broadcasted_iota(jnp.int32, (256, 128), 0)
    lane = lax.broadcasted_iota(jnp.int32, (256, 128), 1)
    y = row // 128 * 512 + lane // 32 * 128 + row % 128
    face = (k + turn_lines(k, 1)) * 0.5
    low = jnp.where((y == 0) | (y == cut), 0.0, face)
    link = jnp.where(y == beside, jnp.where(low_side, turn_lines(face, -1), face), 0.0)
    ground = jnp.where(y == start, 1.0 + 0.5 * k, 1.0)

    def keep(index, up, down):
        ay[index] = up
        by[index] = down

    inverse, (profile,) = reduce_matrix(low, ground + link, [link], Y_STEPS, turn_lines, keep)
    qy[...] = jnp.where(y == end, 0.0, inverse)
    profile = lie(jnp.where(y == end, 1.0, profile))
    hy[...] = profile
    k = kappa[...]
    column = lax.broadcasted_iota(jnp.int32, (ALL, COLS), 1)
    total = jnp.sum(profile * jnp.where(column == start, 1.0 + 0.5 * k, 1.0), axis=1, keepdims=True)
    rim = jnp.sum(jnp.where(column == end, k, 0.0), axis=1, keepdims=True)
    lane = lax.broadcasted_iota(jnp.int32, (8, 128), 1)
    tile = jnp.zeros((8, 128), F32)
    for g in range(ALL // 8):
        part = slice(8 * g, 8 * g + 8)
        tile = jnp.where(lane == 4 * g, total[part], jnp.where(lane == 4 * g + 1, rim[part], tile))
    edge[...] = tile


def source_kernel(same, swapped, far_same, far_cross, h1, h2, parts, after, source, chip):
    del after
    even = lax.axis_index("gx") % 2 == 0

    def flux(here, v, there, v_there):
        return here + (v + v_there) * 0.5 * (there - here) - v * 0.5 * here

    s = own(
        even,
        flux(same[0], same[1], far_same[0], far_same[1]),
        flux(swapped[0], swapped[1], far_cross[0], far_cross[1]),
    )
    source[...] = s
    first = dense(jnp.sum(h1[...] * s, axis=0, keepdims=True))
    last = dense(jnp.sum(h2[...] * s, axis=0, keepdims=True))
    for n, value in enumerate((parts[0], parts[1], parts[2], first, last, parts[3], parts[4])):
        chip[n] = value


def local_x_kernel(source, ax, bx, qx, out):
    width = 256
    for c in range(COLS // width):
        cols = pl.ds(c * width, width)
        r = reduce_right(
            source[:, cols], X_STEPS, turn_rows, lambda i: (ax[i, :, cols], bx[i, :, cols])
        )
        out[:, cols] = r * qx[:, cols]


def merge(one, two):
    g, sl, sr, rl, rr = one
    g2, sl2, sr2, rl2, rr2 = two
    s = sr + sl2
    r = rr + rl2
    inverse = 1.0 / (g + g2 + s)
    a = g * inverse
    b = g2 * inverse
    return (a * g2, sl + a * s, sr2 + b * s, rl + a * r, rr2 + b * r), (a, b, r * inverse)


def behind(face, two):
    g, s, sr, r, rr = two
    inverse = 1.0 / (face + g + s)
    a = face * inverse
    b = g * inverse
    return (a * g, a * s, sr + b * s, a * r, rr + b * r), (a, b, r * inverse)


def load(ref):
    return tuple(ref[n] for n in range(7))


def within(node, left, right):
    a, b, c = node
    return (a * left[0] + b * right[0], a * left[1] + b * right[1], a * left[2] + b * right[2] + c)


def slab_kernel(chip, far1, far3, far2, after, message, nodes):
    del after
    y = lax.axis_index("gx") // 2 % 4
    arrived = [load(chip), load(far1), load(far2), load(far3)]
    chips = []
    for m in range(4):
        chosen = arrived[0]
        for flip in range(1, 4):
            here = y ^ flip == m
            chosen = [jnp.where(here, a, c) for a, c in zip(arrived[flip], chosen)]
        chips.append(chosen)
    element = chips[0][:5]
    inner, fronts = [], []
    for m in range(1, 4):
        tail, front = behind((chips[m - 1][6] + chips[m][5]) * 0.5, chips[m][:5])
        element, node = merge(element, tail)
        inner.append(node)
        fronts.append(front)
    for n, value in enumerate((*element, chips[0][5], chips[3][6])):
        for j in range(8):
            message[j, n] = value
    zero, one = jnp.zeros((8, 128), F32), jnp.ones((8, 128), F32)
    left = (one, zero, zero)
    lasts = [(zero, one, zero)]
    for node in inner[::-1]:
        lasts.append(within(node, left, lasts[-1]))
    lasts = lasts[::-1]
    firsts = [left] + [within(fronts[m - 1], lasts[m - 1], lasts[m]) for m in range(1, 4)]
    first, last = firsts[0], lasts[0]
    for m in range(1, 4):
        first = [jnp.where(y == m, new, old) for new, old in zip(firsts[m], first)]
        last = [jnp.where(y == m, new, old) for new, old in zip(lasts[m], last)]
    for n, trio in enumerate((first, last)):
        for m in range(3):
            nodes[n, m] = trio[m]


def ends_kernel(got, nodes, ends):
    slab = lax.axis_index("gx") // 8
    zero = jnp.zeros((8, 128), F32)
    slabs, fronts = [], []
    for z in range(8):
        face = got[z, 5] * 0.5 if z == 0 else (got[z - 1, 6] + got[z, 5]) * 0.5
        tail, front = behind(face, tuple(got[z, n] for n in range(5)))
        slabs.append(tail)
        fronts.append(front)
    g, _, conduct, _, right = slabs[0]
    conduct = conduct + g
    ratios, offsets = [], []
    for z in range(1, 8):
        g, sl, sr, rl, rr = slabs[z]
        conduct = conduct + sl
        right = right + rl
        inverse = 1.0 / (conduct + g)
        f = g * inverse
        ratios.append(f)
        offsets.append(right * inverse)
        conduct = sr + f * conduct
        right = rr + f * right
    value = right / (conduct + got[7, 6] * 0.5)
    values = [value]
    for k in range(6, -1, -1):
        value = ratios[k] * value + offsets[k]
        values.append(value)
    values = [zero] + values[::-1]
    first, last = zero, zero
    for z in range(8):
        a, b, c = fronts[z]
        first = jnp.where(slab == z, a * values[z] + b * values[z + 1] + c, first)
        last = jnp.where(slab == z, values[z + 1], last)
    for n in range(2):
        ends[n] = nodes[n, 0] * first + nodes[n, 1] * last + nodes[n, 2]


def section_kernel(ends, local, h1, h2, hy, edge, section, message):
    lane = lax.broadcasted_iota(jnp.int32, (8, 128), 1)
    s = local[...] + h1[...] * natural(ends[0], ALL) + h2[...] * natural(ends[1], ALL)
    section[...] = s
    total = jnp.sum(hy[...] * s, axis=1, keepdims=True)
    tile = edge[...]
    for g in range(ALL // 8):
        tile = jnp.where(lane == 4 * g + 2, total[8 * g : 8 * g + 8], tile)
    message[...] = tile


def local_y_kernel(section, ay, by, qy, out):
    r = stand(section[...])
    r = reduce_right(r, Y_STEPS, turn_lines, lambda i: (ay[i], by[i]))
    out[...] = lie(r * qy[...])


def result_kernel(message, far, local, hy, mine, ship):
    even = lax.axis_index("gx") % 2 == 0
    parts = []
    for g in range(ALL // 8):
        part = slice(8 * g, 8 * g + 8)
        e, k, r = (message[:, 4 * g + n : 4 * g + n + 1] for n in range(3))
        e2, k2, r2 = (far[:, 4 * g + n : 4 * g + n + 1] for n in range(3))
        c = (k + k2) * 0.5
        value = ((e2 + c) * r + c * r2) / (e * e2 + c * (e + e2))
        parts.append(local[part, :] + hy[part, :] * value)
    for g in range(2):
        part = slice(8 * g, 8 * g + 8)
        mine[part, :] = jnp.where(even, parts[g], parts[2 + g])
        ship[part, :] = jnp.where(even, parts[2 + g], parts[g])


def output_kernel(mine, got, out):
    even = lax.axis_index("gx") % 2 == 0
    out[...] = own(even, mine[...], got[...])


def call(kernel, outs, specs, flops=0, size=0, scratch=()):
    return pl.pallas_call(
        kernel,
        out_shape=outs,
        in_specs=specs,
        out_specs=jax.tree.map(lambda _: VMEM, outs),
        scratch_shapes=scratch,
        compiler_params=PARAMS,
        cost_estimate=pl.CostEstimate(flops=flops, bytes_accessed=size, transcendentals=0),
    )


SLAB_GROUPS = [[8 * b + a for b in range(8)] for a in range(8)]
CORES = [(i, i ^ 1) for i in range(64)]


def chips_across(flip):
    return [(i, i ^ 2 * flip) for i in range(64)]


SAME = [(2 * i + z, 2 * i + 1 - z) for i in range(64) for z in range(2)]
CROSS = [(2 * i + z, 2 * (i ^ 1) + 1 - z) for i in range(64) for z in range(2)]


def local(fields, kappa, vertical):
    grid = (ALL, COLS)
    full = shape(*grid)
    tile = shape(8, 128)
    element = shape(7, 8, 128)
    two = shape(2, ROWS, COLS)
    three = shape(3, ROWS, COLS)
    same, cross, swapped, kappa_own = call(
        input_kernel,
        (two, two, three, shape(ROWS, COLS)),
        [HBM] * 3,
        flops=1_000_000,
        size=1_000_000,
        scratch=[pltpu.SemaphoreType.DMA((8,))],
    )(
        *(
            pltpu.with_memory_space_constraint(x.reshape(2, ROWS, COLS), pltpu.HBM)
            for x in (fields, vertical, kappa)
        )
    )
    far_same = lax.ppermute(same, ("gx", "gz"), SAME)
    far_cross = lax.ppermute(cross, ("gx", "gz"), CROSS)
    swapped = lax.ppermute(swapped, "gx", CORES)
    kappa_here, ax, bx, qx, h1, h2, parts = call(
        factor_x_kernel,
        (full, shape(5, *grid), shape(5, *grid), full, full, full, shape(5, 8, 128)),
        [VMEM] * 2,
        flops=4_000_000,
        size=2_000_000,
    )(kappa_own, swapped)
    ay, by, qy, hy, edge = call(
        factor_y_kernel,
        (shape(10, 256, 128), shape(10, 256, 128), shape(256, 128), full, tile),
        [VMEM],
        flops=20_000_000,
        size=4_000_000,
    )(kappa_here)
    source, chip = call(source_kernel, (full, element), [VMEM] * 8)(
        same, swapped, far_same, far_cross, h1, h2, parts, edge
    )
    local_x = call(local_x_kernel, full, [VMEM] * 4, flops=1_000_000, size=1_000_000)(source, ax, bx, qx)
    far = [lax.ppermute(chip, "gx", chips_across(flip)) for flip in (1, 3, 2)]
    message, nodes = call(
        slab_kernel, (shape(8, 7, 8, 128), shape(2, 3, 8, 128)), [VMEM] * 5
    )(chip, *far, local_x)
    got = lax.all_to_all(message, "gx", 0, 0, axis_index_groups=SLAB_GROUPS, tiled=True)
    ends = call(ends_kernel, shape(2, 8, 128), [VMEM] * 2)(got, nodes)
    section, message = call(section_kernel, (full, tile), [VMEM] * 6)(ends, local_x, h1, h2, hy, edge)
    far = lax.ppermute(message, "gy", [(0, 1), (1, 0)])
    local_y = call(local_y_kernel, full, [VMEM] * 4, flops=4_000_000, size=3_000_000)(section, ay, by, qy)
    rows = shape(ROWS, COLS)
    mine, ship = call(result_kernel, (rows, rows), [VMEM] * 4)(message, far, local_y, hy)
    got = lax.ppermute(ship, "gx", CORES)
    out = call(output_kernel, full, [VMEM] * 2)(mine, got)
    return out.reshape(fields.shape)


def solution(mesh):
    spec = P(None, "gz", "gx", "gy")
    return jax.shard_map(
        local, mesh=mesh, in_specs=(spec, spec, spec), out_specs=spec, check_vma=False
    )
```

```python
import functools

import jax
import jax.numpy as jnp
from jax import lax
from jax.experimental import pallas as pl
from jax.experimental.pallas import tpu as pltpu
from jax.sharding import PartitionSpec as P

F32 = jnp.float32
ROWS = 16
COLS = 1024
ALL = 2 * ROWS
VMEM = pl.BlockSpec(memory_space=pltpu.VMEM)
HBM = pl.BlockSpec(memory_space=pltpu.HBM)
X_STEPS = (1, 2, 4, 8)
Y_STEPS = (1, 2, 4, 8, 16, 32, 64, 128, 256, 512)
PARAMS = pltpu.CompilerParams(vmem_limit_bytes=40 * 1024 * 1024)


def shape(*dims):
    return jax.ShapeDtypeStruct(dims, F32)


def turn(x, k, axis):
    n = x.shape[axis]
    k = k % n
    unit = 128 if axis == 1 else 8
    if k == 0:
        return x
    if k % unit == 0:
        low = lax.slice_in_dim(x, n - k, n, axis=axis)
        high = lax.slice_in_dim(x, 0, n - k, axis=axis)
        return jnp.concatenate([low, high], axis=axis)
    return pltpu.roll(x, k, axis)


def turn_lines(x, k):
    lanes = lax.broadcasted_iota(jnp.int32, (1, 128), 1)

    def blocks(pair, n):
        if n == 4:
            return pair[::-1]
        turned = [pltpu.roll(p, 32 * n % 128, 1) for p in pair]
        over = lanes < 32 * n if n > 0 else lanes >= 128 + 32 * n
        return [jnp.where(over, turned[1 - h], turned[h]) for h in range(2)]

    pair = [x[:128], x[128:]]
    size = abs(k)
    if size >= 128:
        pair = blocks(pair, 4 if size == 512 else k // 128)
    elif size >= 8:
        if k > 0:
            moved = blocks([p[128 - k :] for p in pair], 1)
            pair = [jnp.concatenate([m, p[: 128 - k]], axis=0) for m, p in zip(moved, pair)]
        else:
            moved = blocks([p[:size] for p in pair], -1)
            pair = [jnp.concatenate([p[size:], m], axis=0) for m, p in zip(moved, pair)]
    else:
        rows = lax.broadcasted_iota(jnp.int32, (8, 128), 0)
        turned = [pltpu.roll(p, k % 128, 0) for p in pair]
        if k > 0:
            ends = [t[:8] for t in turned]
            ends = [jnp.where(rows < k, m, e) for m, e in zip(blocks(ends, 1), ends)]
            pair = [jnp.concatenate([e, t[8:]], axis=0) for e, t in zip(ends, turned)]
        else:
            ends = [t[120:] for t in turned]
            ends = [jnp.where(rows >= 8 + k, m, e) for m, e in zip(blocks(ends, -1), ends)]
            pair = [jnp.concatenate([t[:120], e], axis=0) for e, t in zip(ends, turned)]
    return jnp.concatenate(pair, axis=0)


def stand(x):
    tiles = [x[:, 128 * j : 128 * (j + 1)] for j in range(8)]
    return jnp.concatenate(
        [jnp.concatenate(tiles[4 * h : 4 * h + 4], axis=0).T for h in range(2)], axis=0
    )


def lie(x):
    tiles = [x[128 * h : 128 * (h + 1)].T for h in range(2)]
    return jnp.concatenate(
        [tiles[h][ALL * b : ALL * (b + 1)] for h in range(2) for b in range(4)], axis=1
    )


def turn_rows(x, k):
    return turn(x, k, 0)


def reduce_matrix(low, excess, rights, steps, move, keep):
    for index, k in enumerate(steps):
        high = move(low, -k)
        inverse = 1.0 / (low + high + excess)
        up = high * inverse
        down = low * inverse
        keep(index, up, down)
        excess = excess + move(up * excess, k) + move(down * excess, -k)
        rights = [r + move(up * r, k) + move(down * r, -k) for r in rights]
        low = move(up * low, k)
    inverse = 1.0 / excess
    return inverse, [r * inverse for r in rights]


def reduce_right(right, steps, move, load):
    for index, k in enumerate(steps):
        up, down = load(index)
        right = right + move(up * right, k) + move(down * right, -k)
    return right


def dense(row):
    return jnp.concatenate([row[:, 128 * i : 128 * (i + 1)] for i in range(8)], axis=0)


def natural(tile, rows):
    return jnp.concatenate(
        [jnp.broadcast_to(tile[i : i + 1, :], (rows, 128)) for i in range(8)], axis=1
    )


def factor_x_kernel(
    fields_arg, vertical_arg, kappa_arg, fields, vertical, kappa, ax, bx, qx, h1, h2, parts, done
):
    pairs = ((kappa_arg, kappa), (fields_arg, fields), (vertical_arg, vertical))
    copies = [pltpu.make_async_copy(a, b, done.at[n]) for n, (a, b) in enumerate(pairs)]
    for copy in copies:
        copy.start()
    copies[0].wait()
    half = 512
    rows = lax.broadcasted_iota(jnp.int32, (ROWS, half), 0)
    for f in range(2):
        mine = pl.ds(f * ROWS, ROWS)
        for c in range(COLS // half):
            cols = pl.ds(c * half, half)
            k = kappa[mine, cols]
            face = (k + turn(k, 1, 0)) * 0.5
            low = jnp.where((rows >= 2) & (rows <= 14), face, 0.0)
            first = jnp.where(rows == 1, face, 0.0)
            last = jnp.where(rows == 14, turn(face, -1, 0), 0.0)

            def keep(index, a, b, mine=mine, cols=cols):
                ax[index, mine, cols] = a
                bx[index, mine, cols] = b

            inverse, (one, two) = reduce_matrix(
                low, 1.0 + first + last, [first, last], X_STEPS, turn_rows, keep
            )
            qx[mine, cols] = jnp.where((rows >= 1) & (rows <= 14), inverse, 0.0)
            one = jnp.where(rows == 0, 1.0, one)
            two = jnp.where(rows == ROWS - 1, 1.0, two)
            h1[mine, cols] = one
            h2[mine, cols] = two
            sums = (
                jnp.sum(first * two, axis=0, keepdims=True),
                jnp.sum(one, axis=0, keepdims=True),
                jnp.sum(two, axis=0, keepdims=True),
                k[:1],
                k[ROWS - 1 :],
            )
            for n, row in enumerate(sums):
                for i in range(half // 128):
                    parts[n, f, pl.ds(c * (half // 128) + i, 1), :] = row[:, 128 * i : 128 * (i + 1)]
    copies[1].wait()
    copies[2].wait()


def factor_y_kernel(kappa, ay, by, qy, hy, edge):
    gy = lax.axis_index("gy")
    low_side = gy == 0
    end = jnp.where(low_side, COLS - 1, 0)
    start = COLS - 1 - end
    beside = jnp.where(low_side, COLS - 2, 1)
    cut = jnp.where(low_side, COLS - 1, 1)
    k = stand(kappa[...])
    row = lax.broadcasted_iota(jnp.int32, (256, 128), 0)
    lane = lax.broadcasted_iota(jnp.int32, (256, 128), 1)
    y = row // 128 * 512 + lane // 32 * 128 + row % 128
    face = (k + turn_lines(k, 1)) * 0.5
    low = jnp.where((y == 0) | (y == cut), 0.0, face)
    link = jnp.where(y == beside, jnp.where(low_side, turn_lines(face, -1), face), 0.0)
    ground = jnp.where(y == start, 1.0 + 0.5 * k, 1.0)

    def keep(index, up, down):
        ay[index] = up
        by[index] = down

    inverse, (profile,) = reduce_matrix(low, ground + link, [link], Y_STEPS, turn_lines, keep)
    qy[...] = jnp.where(y == end, 0.0, inverse)
    profile = lie(jnp.where(y == end, 1.0, profile))
    hy[...] = profile
    k = kappa[...]
    column = lax.broadcasted_iota(jnp.int32, (ALL, COLS), 1)
    total = jnp.sum(profile * jnp.where(column == start, 1.0 + 0.5 * k, 1.0), axis=1, keepdims=True)
    rim = jnp.sum(jnp.where(column == end, k, 0.0), axis=1, keepdims=True)
    lane = lax.broadcasted_iota(jnp.int32, (8, 128), 1)
    tile = jnp.zeros((8, 128), F32)
    for g in range(ALL // 8):
        part = slice(8 * g, 8 * g + 8)
        tile = jnp.where(lane == 4 * g, total[part], jnp.where(lane == 4 * g + 1, rim[part], tile))
    edge[...] = tile


def source_kernel(fields, fields_far, vertical, vertical_far, h1, h2, parts, after, source, elements):
    del after
    here = fields[...]
    v = vertical[...]
    s = here + (v + vertical_far[...]) * 0.5 * (fields_far[...] - here) - v * 0.5 * here
    source[...] = s
    for f in range(2):
        mine = slice(f * ROWS, (f + 1) * ROWS)
        first = dense(jnp.sum(h1[mine, :] * s[mine, :], axis=0, keepdims=True))
        last = dense(jnp.sum(h2[mine, :] * s[mine, :], axis=0, keepdims=True))
        element = (parts[0, f], parts[1, f], parts[2, f], first, last, parts[3, f], parts[4, f])
        for n, value in enumerate(element):
            elements[f, n] = value


def local_x_kernel(source, ax, bx, qx, out):
    half = 512
    for f in range(2):
        mine = pl.ds(f * ROWS, ROWS)
        for c in range(COLS // half):
            cols = pl.ds(c * half, half)
            r = source[mine, cols]
            r = reduce_right(r, X_STEPS, turn_rows, lambda i: (ax[i, mine, cols], bx[i, mine, cols]))
            out[mine, cols] = r * qx[mine, cols]


def merge(one, two):
    g, sl, sr, rl, rr = one
    g2, sl2, sr2, rl2, rr2 = two
    s = sr + sl2
    r = rr + rl2
    inverse = 1.0 / (g + g2 + s)
    a = g * inverse
    b = g2 * inverse
    return (a * g2, sl + a * s, sr2 + b * s, rl + a * r, rr2 + b * r), (a, b, r * inverse)


def behind(face, two):
    g, s, sr, r, rr = two
    inverse = 1.0 / (face + g + s)
    a = face * inverse
    b = g * inverse
    return (a * g, a * s, sr + b * s, a * r, rr + b * r), (a, b, r * inverse)


def load(ref, *field):
    return tuple(ref[(*field, n)] for n in range(7))


def within(node, left, right):
    a, b, c = node
    return (a * left[0] + b * right[0], a * left[1] + b * right[1], a * left[2] + b * right[2] + c)


def chip_kernel(mine, other, chips, chip, middle):
    even = lax.axis_index("gx") % 2 == 0
    fields = []
    for f in range(2):
        a, b = load(mine, f), load(other, f)
        first = [jnp.where(even, m, o) for m, o in zip(a, b)]
        second = [jnp.where(even, o, m) for m, o in zip(a, b)]
        tail, start = behind((first[6] + second[5]) * 0.5, second[:5])
        element, end = merge(first[:5], tail)
        fields.append(((*element, first[5], second[6]), (*end, *start)))
        for n, value in enumerate(fields[f][0]):
            chips[f, n] = value
    for out, (one, two) in zip((chip, middle), zip(*fields)):
        for n, (a, b) in enumerate(zip(one, two)):
            out[n] = jnp.where(even, a, b)


def pick_kernel(chips, keep, send):
    even = lax.axis_index("gx") % 2 == 0
    for n, (one, two) in enumerate(zip(load(chips, 0), load(chips, 1))):
        keep[n] = jnp.where(even, one, two)
        send[n] = jnp.where(even, two, one)


def slab_kernel(chip, far1, keep, got, middle, message, nodes):
    y = lax.axis_index("gx") // 2 % 4
    even = lax.axis_index("gx") % 2 == 0
    far2 = [jnp.where(even, g, k) for k, g in zip(load(keep), load(got))]
    far3 = [jnp.where(even, k, g) for k, g in zip(load(keep), load(got))]
    arrived = [load(chip), load(far1), far2, far3]
    chips = []
    for m in range(4):
        chosen = arrived[0]
        for flip in range(1, 4):
            here = y ^ flip == m
            chosen = [jnp.where(here, a, c) for a, c in zip(arrived[flip], chosen)]
        chips.append(chosen)
    element = chips[0][:5]
    inner, fronts = [], []
    for m in range(1, 4):
        tail, front = behind((chips[m - 1][6] + chips[m][5]) * 0.5, chips[m][:5])
        element, node = merge(element, tail)
        inner.append(node)
        fronts.append(front)
    for n, value in enumerate((*element, chips[0][5], chips[3][6])):
        for j in range(8):
            message[j, n] = value
    zero, one = jnp.zeros((8, 128), F32), jnp.ones((8, 128), F32)
    left = (one, zero, zero)
    lasts = [(zero, one, zero)]
    for node in inner[::-1]:
        lasts.append(within(node, left, lasts[-1]))
    lasts = lasts[::-1]
    firsts = [left] + [within(fronts[m - 1], lasts[m - 1], lasts[m]) for m in range(1, 4)]
    first, last = firsts[0], lasts[0]
    for m in range(1, 4):
        first = [jnp.where(y == m, new, old) for new, old in zip(firsts[m], first)]
        last = [jnp.where(y == m, new, old) for new, old in zip(lasts[m], last)]
    before = within(tuple(middle[n] for n in range(3)), first, last)
    second = within(tuple(middle[n] for n in range(3, 6)), before, last)
    for n, trio in enumerate((first, before, second, last)):
        for m in range(3):
            nodes[n, m] = trio[m]


def ends_kernel(got, nodes, mine, other):
    gx = lax.axis_index("gx")
    slab = gx // 8
    even = gx % 2 == 0
    zero = jnp.zeros((8, 128), F32)
    slabs, fronts = [], []
    for z in range(8):
        face = got[z, 5] * 0.5 if z == 0 else (got[z - 1, 6] + got[z, 5]) * 0.5
        tail, front = behind(face, tuple(got[z, n] for n in range(5)))
        slabs.append(tail)
        fronts.append(front)
    g, _, conduct, _, right = slabs[0]
    conduct = conduct + g
    ratios, offsets = [], []
    for z in range(1, 8):
        g, sl, sr, rl, rr = slabs[z]
        conduct = conduct + sl
        right = right + rl
        inverse = 1.0 / (conduct + g)
        f = g * inverse
        ratios.append(f)
        offsets.append(right * inverse)
        conduct = sr + f * conduct
        right = rr + f * right
    value = right / (conduct + got[7, 6] * 0.5)
    values = [value]
    for k in range(6, -1, -1):
        value = ratios[k] * value + offsets[k]
        values.append(value)
    values = [zero] + values[::-1]
    first, last = zero, zero
    for z in range(8):
        a, b, c = fronts[z]
        first = jnp.where(slab == z, a * values[z] + b * values[z + 1] + c, first)
        last = jnp.where(slab == z, values[z + 1], last)
    row = [nodes[n, 0] * first + nodes[n, 1] * last + nodes[n, 2] for n in range(4)]
    for n in range(2):
        mine[n] = jnp.where(even, row[n], row[n + 2])
        other[n] = jnp.where(even, row[n + 2], row[n])


def section_kernel(mine, other, local, h1, h2, hy, edge, section, message):
    core = lax.axis_index("gx") % 2
    lane = lax.broadcasted_iota(jnp.int32, (8, 128), 1)
    tile = edge[...]
    for f in range(2):
        first = jnp.where(core == f, mine[0], other[0])
        last = jnp.where(core == f, mine[1], other[1])
        rows = slice(f * ROWS, (f + 1) * ROWS)
        s = local[rows, :] + h1[rows, :] * natural(first, ROWS) + h2[rows, :] * natural(last, ROWS)
        section[rows, :] = s
        total = jnp.sum(hy[rows, :] * s, axis=1, keepdims=True)
        for g in range(2):
            tile = jnp.where(lane == 4 * (2 * f + g) + 2, total[8 * g : 8 * g + 8], tile)
    message[...] = tile


def local_y_kernel(section, ay, by, qy, out):
    r = stand(section[...])
    r = reduce_right(r, Y_STEPS, turn_lines, lambda i: (ay[i], by[i]))
    out[...] = lie(r * qy[...])


def output_kernel(message, far, local, hy, out):
    for g in range(ALL // 8):
        part = slice(8 * g, 8 * g + 8)
        e, k, r = (message[:, 4 * g + n : 4 * g + n + 1] for n in range(3))
        e2, k2, r2 = (far[:, 4 * g + n : 4 * g + n + 1] for n in range(3))
        c = (k + k2) * 0.5
        value = ((e2 + c) * r + c * r2) / (e * e2 + c * (e + e2))
        out[part, :] = local[part, :] + hy[part, :] * value


def call(kernel, outs, specs, flops=0, size=0, scratch=()):
    return pl.pallas_call(
        kernel,
        out_shape=outs,
        in_specs=specs,
        out_specs=jax.tree.map(lambda _: VMEM, outs),
        scratch_shapes=scratch,
        compiler_params=PARAMS,
        cost_estimate=pl.CostEstimate(flops=flops, bytes_accessed=size, transcendentals=0),
    )


SLAB_GROUPS = [[8 * b + a for b in range(8)] for a in range(8)]
CORES = [(i, i ^ 1) for i in range(64)]


CHIPS = [(i, i ^ (4 if i % 2 else 6)) for i in range(64)]
NEXT = [(i, i ^ 2) for i in range(64)]


def local(fields, kappa, vertical):
    grid = (ALL, COLS)
    swap = [(0, 1), (1, 0)]
    fields_far = lax.ppermute(fields, "gz", swap)
    vertical_far = lax.ppermute(vertical, "gz", swap)
    full = shape(*grid)
    half = shape(7, 8, 128)
    standing = shape(256, 128)
    fields_here, vertical_here, kappa_here, ax, bx, qx, h1, h2, parts = call(
        factor_x_kernel,
        (full, full, full, shape(4, *grid), shape(4, *grid), full, full, full, shape(5, 2, 8, 128)),
        [HBM] * 3,
        flops=4_000_000,
        size=2_000_000,
        scratch=[pltpu.SemaphoreType.DMA((3,))],
    )(*(pltpu.with_memory_space_constraint(x.reshape(grid), pltpu.HBM) for x in (fields, vertical, kappa)))
    ay, by, qy, hy, edge = call(
        factor_y_kernel,
        (shape(10, 256, 128), shape(10, 256, 128), standing, full, shape(8, 128)),
        [VMEM],
        flops=20_000_000,
        size=4_000_000,
    )(kappa_here)
    both = shape(2, 7, 8, 128)
    source, elements = call(source_kernel, (full, both), [VMEM] * 8)(
        fields_here, fields_far.reshape(grid), vertical_here, vertical_far.reshape(grid),
        h1, h2, parts, edge,
    )
    got = lax.ppermute(elements, "gx", CORES)
    local_x = call(local_x_kernel, full, [VMEM] * 4, flops=1_000_000, size=1_000_000)(source, ax, bx, qx)
    chips, chip, middle = call(chip_kernel, (both, half, shape(6, 8, 128)), [VMEM] * 2)(elements, got)
    far = lax.ppermute(chips, "gx", CHIPS)
    far1 = lax.ppermute(chip, "gx", NEXT)
    keep, send = call(pick_kernel, (half, half), [VMEM])(far)
    got = lax.ppermute(send, "gx", CORES)
    message, nodes = call(
        slab_kernel, (shape(8, 7, 8, 128), shape(4, 3, 8, 128)), [VMEM] * 5
    )(chip, far1, keep, got, middle)
    got = lax.all_to_all(message, "gx", 0, 0, axis_index_groups=SLAB_GROUPS, tiled=True)
    mine, other = call(
        ends_kernel, (shape(2, 8, 128), shape(2, 8, 128)), [VMEM, VMEM]
    )(got, nodes)
    other = lax.ppermute(other, "gx", CORES)
    section, message = call(
        section_kernel, (full, shape(8, 128)), [VMEM] * 7
    )(mine, other, local_x, h1, h2, hy, edge)
    far = lax.ppermute(message, "gy", swap)
    local_y = call(local_y_kernel, full, [VMEM] * 4, flops=4_000_000, size=3_000_000)(section, ay, by, qy)
    out = call(output_kernel, full, [VMEM] * 4)(message, far, local_y, hy)
    return out.reshape(fields.shape)


def solution(mesh):
    spec = P(None, "gz", "gx", "gy")
    return jax.shard_map(
        local, mesh=mesh, in_specs=(spec, spec, spec), out_specs=spec, check_vma=False
    )
```

```python
import functools

import jax
import jax.numpy as jnp
from jax import lax
from jax.experimental import pallas as pl
from jax.experimental.pallas import tpu as pltpu
from jax.sharding import PartitionSpec as P

F32 = jnp.float32
ROWS = 16
COLS = 1024
ALL = 2 * ROWS
VMEM = pl.BlockSpec(memory_space=pltpu.VMEM)
HBM = pl.BlockSpec(memory_space=pltpu.HBM)
X_STEPS = (1, 2, 4, 8)
Y_STEPS = (1, 2, 4, 8, 16, 32, 64, 128, 256, 512)
PARAMS = pltpu.CompilerParams(vmem_limit_bytes=40 * 1024 * 1024)


def shape(*dims):
    return jax.ShapeDtypeStruct(dims, F32)


def turn(x, k, axis):
    n = x.shape[axis]
    k = k % n
    unit = 128 if axis == 1 else 8
    if k == 0:
        return x
    if k % unit == 0:
        low = lax.slice_in_dim(x, n - k, n, axis=axis)
        high = lax.slice_in_dim(x, 0, n - k, axis=axis)
        return jnp.concatenate([low, high], axis=axis)
    return pltpu.roll(x, k, axis)


def turn_lines(x, k):
    lanes = lax.broadcasted_iota(jnp.int32, (1, 128), 1)

    def blocks(pair, n):
        if n == 4:
            return pair[::-1]
        turned = [pltpu.roll(p, 32 * n % 128, 1) for p in pair]
        over = lanes < 32 * n if n > 0 else lanes >= 128 + 32 * n
        return [jnp.where(over, turned[1 - h], turned[h]) for h in range(2)]

    pair = [x[:128], x[128:]]
    size = abs(k)
    if size >= 128:
        pair = blocks(pair, 4 if size == 512 else k // 128)
    elif size >= 8:
        if k > 0:
            moved = blocks([p[128 - k :] for p in pair], 1)
            pair = [jnp.concatenate([m, p[: 128 - k]], axis=0) for m, p in zip(moved, pair)]
        else:
            moved = blocks([p[:size] for p in pair], -1)
            pair = [jnp.concatenate([p[size:], m], axis=0) for m, p in zip(moved, pair)]
    else:
        rows = lax.broadcasted_iota(jnp.int32, (8, 128), 0)
        turned = [pltpu.roll(p, k % 128, 0) for p in pair]
        if k > 0:
            ends = [t[:8] for t in turned]
            ends = [jnp.where(rows < k, m, e) for m, e in zip(blocks(ends, 1), ends)]
            pair = [jnp.concatenate([e, t[8:]], axis=0) for e, t in zip(ends, turned)]
        else:
            ends = [t[120:] for t in turned]
            ends = [jnp.where(rows >= 8 + k, m, e) for m, e in zip(blocks(ends, -1), ends)]
            pair = [jnp.concatenate([t[:120], e], axis=0) for e, t in zip(ends, turned)]
    return jnp.concatenate(pair, axis=0)


def stand(x):
    tiles = [x[:, 128 * j : 128 * (j + 1)] for j in range(8)]
    return jnp.concatenate(
        [jnp.concatenate(tiles[4 * h : 4 * h + 4], axis=0).T for h in range(2)], axis=0
    )


def lie(x):
    tiles = [x[128 * h : 128 * (h + 1)].T for h in range(2)]
    return jnp.concatenate(
        [tiles[h][ALL * b : ALL * (b + 1)] for h in range(2) for b in range(4)], axis=1
    )


def turn_rows(x, k):
    return turn(x, k, 0)


def reduce_matrix(low, excess, rights, steps, move, keep):
    for index, k in enumerate(steps):
        high = move(low, -k)
        inverse = 1.0 / (low + high + excess)
        up = high * inverse
        down = low * inverse
        keep(index, up, down)
        excess = excess + move(up * excess, k) + move(down * excess, -k)
        rights = [r + move(up * r, k) + move(down * r, -k) for r in rights]
        low = move(up * low, k)
    inverse = 1.0 / excess
    return inverse, [r * inverse for r in rights]


def reduce_right(right, steps, move, load):
    for index, k in enumerate(steps):
        up, down = load(index)
        right = right + move(up * right, k) + move(down * right, -k)
    return right


def dense(row):
    return jnp.concatenate([row[:, 128 * i : 128 * (i + 1)] for i in range(8)], axis=0)


def natural(tile, rows):
    return jnp.concatenate(
        [jnp.broadcast_to(tile[i : i + 1, :], (rows, 128)) for i in range(8)], axis=1
    )


def input_kernel(fields_arg, vertical_arg, kappa_arg, fields, vertical, kappa, rim, done):
    pairs = ((kappa_arg, kappa), (fields_arg, fields), (vertical_arg, vertical))
    copies = [pltpu.make_async_copy(a, b, done.at[n]) for n, (a, b) in enumerate(pairs)]
    for copy in copies:
        copy.start()
    copies[0].wait()
    for f in range(2):
        rim[f] = dense(kappa[f * ROWS + ROWS - 1 : f * ROWS + ROWS, :])
    copies[1].wait()
    copies[2].wait()


def factor_x_kernel(kappa, ax, bx, qx, h1, h2, parts):
    half = 512
    rows = lax.broadcasted_iota(jnp.int32, (ROWS, half), 0)
    for f in range(2):
        mine = pl.ds(f * ROWS, ROWS)
        for c in range(COLS // half):
            cols = pl.ds(c * half, half)
            k = kappa[mine, cols]
            face = (k + turn(k, 1, 0)) * 0.5
            low = jnp.where((rows >= 2) & (rows <= 14), face, 0.0)
            first = jnp.where(rows == 1, face, 0.0)
            last = jnp.where(rows == 14, turn(face, -1, 0), 0.0)

            def keep(index, a, b, mine=mine, cols=cols):
                ax[index, mine, cols] = a
                bx[index, mine, cols] = b

            inverse, (one, two) = reduce_matrix(
                low, 1.0 + first + last, [first, last], X_STEPS, turn_rows, keep
            )
            qx[mine, cols] = jnp.where((rows >= 1) & (rows <= 14), inverse, 0.0)
            one = jnp.where(rows == 0, 1.0, one)
            two = jnp.where(rows == ROWS - 1, 1.0, two)
            h1[mine, cols] = one
            h2[mine, cols] = two
            sums = (
                jnp.sum(first * two, axis=0, keepdims=True),
                jnp.sum(one, axis=0, keepdims=True),
                jnp.sum(two, axis=0, keepdims=True),
                k[:1],
                k[ROWS - 1 :],
            )
            for n, row in enumerate(sums):
                for i in range(half // 128):
                    parts[n, f, pl.ds(c * (half // 128) + i, 1), :] = row[:, 128 * i : 128 * (i + 1)]


def factor_y_kernel(kappa, after, ay, by, qy, hy, edge):
    del after
    gy = lax.axis_index("gy")
    low_side = gy == 0
    end = jnp.where(low_side, COLS - 1, 0)
    start = COLS - 1 - end
    beside = jnp.where(low_side, COLS - 2, 1)
    cut = jnp.where(low_side, COLS - 1, 1)
    k = stand(kappa[...])
    row = lax.broadcasted_iota(jnp.int32, (256, 128), 0)
    lane = lax.broadcasted_iota(jnp.int32, (256, 128), 1)
    y = row // 128 * 512 + lane // 32 * 128 + row % 128
    face = (k + turn_lines(k, 1)) * 0.5
    low = jnp.where((y == 0) | (y == cut), 0.0, face)
    link = jnp.where(y == beside, jnp.where(low_side, turn_lines(face, -1), face), 0.0)
    ground = jnp.where(y == start, 1.0 + 0.5 * k, 1.0)

    def keep(index, up, down):
        ay[index] = up
        by[index] = down

    inverse, (profile,) = reduce_matrix(low, ground + link, [link], Y_STEPS, turn_lines, keep)
    qy[...] = jnp.where(y == end, 0.0, inverse)
    profile = lie(jnp.where(y == end, 1.0, profile))
    hy[...] = profile
    k = kappa[...]
    column = lax.broadcasted_iota(jnp.int32, (ALL, COLS), 1)
    total = jnp.sum(profile * jnp.where(column == start, 1.0 + 0.5 * k, 1.0), axis=1, keepdims=True)
    rim = jnp.sum(jnp.where(column == end, k, 0.0), axis=1, keepdims=True)
    lane = lax.broadcasted_iota(jnp.int32, (8, 128), 1)
    tile = jnp.zeros((8, 128), F32)
    for g in range(ALL // 8):
        part = slice(8 * g, 8 * g + 8)
        tile = jnp.where(lane == 4 * g, total[part], jnp.where(lane == 4 * g + 1, rim[part], tile))
    edge[...] = tile


def source_kernel(fields, fields_far, vertical, vertical_far, h1, h2, parts, prev, source, elements):
    here = fields[...]
    v = vertical[...]
    s = here + (v + vertical_far[...]) * 0.5 * (fields_far[...] - here) - v * 0.5 * here
    source[...] = s
    for f in range(2):
        mine = slice(f * ROWS, (f + 1) * ROWS)
        first = dense(jnp.sum(h1[mine, :] * s[mine, :], axis=0, keepdims=True))
        last = dense(jnp.sum(h2[mine, :] * s[mine, :], axis=0, keepdims=True))
        element = (parts[0, f], parts[1, f], parts[2, f], first, last, parts[3, f], parts[4, f], prev[f])
        for n, value in enumerate(element):
            elements[f, n] = value


def local_x_kernel(source, ax, bx, qx, out):
    half = 512
    for f in range(2):
        mine = pl.ds(f * ROWS, ROWS)
        for c in range(COLS // half):
            cols = pl.ds(c * half, half)
            r = source[mine, cols]
            r = reduce_right(r, X_STEPS, turn_rows, lambda i: (ax[i, mine, cols], bx[i, mine, cols]))
            out[mine, cols] = r * qx[mine, cols]


def merge(one, two):
    g, sl, sr, rl, rr = one
    g2, sl2, sr2, rl2, rr2 = two
    s = sr + sl2
    r = rr + rl2
    inverse = 1.0 / (g + g2 + s)
    a = g * inverse
    b = g2 * inverse
    return (a * g2, sl + a * s, sr2 + b * s, rl + a * r, rr2 + b * r), (a, b, r * inverse)


def behind(face, two):
    g, s, sr, r, rr = two
    inverse = 1.0 / (face + g + s)
    a = face * inverse
    b = g * inverse
    return (a * g, a * s, sr + b * s, a * r, rr + b * r), (a, b, r * inverse)


def load(ref, *field):
    return tuple(ref[(*field, n)] for n in range(8))


def within(node, left, right):
    a, b, c = node
    return (a * left[0] + b * right[0], a * left[1] + b * right[1], a * left[2] + b * right[2] + c)


def chip_kernel(mine, other, chips, chip, middle):
    even = lax.axis_index("gx") % 2 == 0
    fields = []
    for f in range(2):
        a, b = load(mine, f), load(other, f)
        first = [jnp.where(even, m, o) for m, o in zip(a, b)]
        second = [jnp.where(even, o, m) for m, o in zip(a, b)]
        tail, start = behind((first[6] + second[5]) * 0.5, second[:5])
        element, end = merge(first[:5], tail)
        fields.append(((*element, first[5], *second[6:]), (*end, *start)))
        for n, value in enumerate(fields[f][0]):
            chips[f, n] = value
    for out, (one, two) in zip((chip, middle), zip(*fields)):
        for n, (a, b) in enumerate(zip(one, two)):
            out[n] = jnp.where(even, a, b)


def pick_kernel(chips, after, keep, send):
    del after
    even = lax.axis_index("gx") % 2 == 0
    for n, (one, two) in enumerate(zip(load(chips, 0), load(chips, 1))):
        keep[n] = jnp.where(even, one, two)
        send[n] = jnp.where(even, two, one)


def slab_kernel(chip, far1, keep, got, middle, message, nodes):
    y = lax.axis_index("gx") // 2 % 4
    even = lax.axis_index("gx") % 2 == 0
    far2 = [jnp.where(even, g, k) for k, g in zip(load(keep), load(got))]
    far3 = [jnp.where(even, k, g) for k, g in zip(load(keep), load(got))]
    arrived = [load(chip), load(far1), far2, far3]
    chips = []
    for m in range(4):
        chosen = arrived[0]
        for flip in range(1, 4):
            here = y ^ flip == m
            chosen = [jnp.where(here, a, c) for a, c in zip(arrived[flip], chosen)]
        chips.append(chosen)
    slab = lax.axis_index("gx") // 8
    before = jnp.where(slab == 0, 0.0, chips[3][7])
    element, inner, fronts = None, [], []
    for m in range(4):
        face = ((before if m == 0 else chips[m - 1][6]) + chips[m][5]) * 0.5
        tail, front = behind(face, chips[m][:5])
        fronts.append(front)
        if m == 0:
            element = tail
        else:
            element, node = merge(element, tail)
            inner.append(node)
    g, sl, sr, rl, rr = element
    sr = jnp.where(slab == 7, sr + chips[3][6] * 0.5, sr)
    for n, value in enumerate((g, sl, sr, rl, rr)):
        for j in range(8):
            message[j, n] = value
    zero, one = jnp.zeros((8, 128), F32), jnp.ones((8, 128), F32)
    left = (one, zero, zero)
    lasts = [(zero, one, zero)]
    for node in inner[::-1]:
        lasts.append(within(node, left, lasts[-1]))
    lasts = [left] + lasts[::-1]
    firsts = [within(fronts[m], lasts[m], lasts[m + 1]) for m in range(4)]
    lasts = lasts[1:]
    first, last = firsts[0], lasts[0]
    for m in range(1, 4):
        first = [jnp.where(y == m, new, old) for new, old in zip(firsts[m], first)]
        last = [jnp.where(y == m, new, old) for new, old in zip(lasts[m], last)]
    before = within(tuple(middle[n] for n in range(3)), first, last)
    second = within(tuple(middle[n] for n in range(3, 6)), before, last)
    for n, trio in enumerate((first, before, second, last)):
        for m in range(3):
            nodes[n, m] = trio[m]


def ends_kernel(got, nodes, mine, other):
    gx = lax.axis_index("gx")
    slab = gx // 8
    even = gx % 2 == 0
    zero = jnp.zeros((8, 128), F32)
    conduct = got[0, 0] + got[0, 2]
    right = got[0, 4]
    ratios, offsets = [], []
    for z in range(1, 8):
        g, sl, sr, rl, rr = (got[z, n] for n in range(5))
        conduct = conduct + sl
        right = right + rl
        inverse = 1.0 / (conduct + g)
        f = g * inverse
        ratios.append(f)
        offsets.append(right * inverse)
        conduct = sr + f * conduct
        right = rr + f * right
    value = right / conduct
    values = [value]
    for k in range(6, -1, -1):
        value = ratios[k] * value + offsets[k]
        values.append(value)
    values = [zero] + values[::-1]
    first, last = zero, zero
    for z in range(8):
        first = jnp.where(slab == z, values[z], first)
        last = jnp.where(slab == z, values[z + 1], last)
    row = [nodes[n, 0] * first + nodes[n, 1] * last + nodes[n, 2] for n in range(4)]
    for n in range(2):
        mine[n] = jnp.where(even, row[n], row[n + 2])
        other[n] = jnp.where(even, row[n + 2], row[n])


def section_kernel(mine, other, local, h1, h2, hy, edge, section, message):
    core = lax.axis_index("gx") % 2
    lane = lax.broadcasted_iota(jnp.int32, (8, 128), 1)
    tile = edge[...]
    for f in range(2):
        first = jnp.where(core == f, mine[0], other[0])
        last = jnp.where(core == f, mine[1], other[1])
        rows = slice(f * ROWS, (f + 1) * ROWS)
        s = local[rows, :] + h1[rows, :] * natural(first, ROWS) + h2[rows, :] * natural(last, ROWS)
        section[rows, :] = s
        total = jnp.sum(hy[rows, :] * s, axis=1, keepdims=True)
        for g in range(2):
            tile = jnp.where(lane == 4 * (2 * f + g) + 2, total[8 * g : 8 * g + 8], tile)
    message[...] = tile


def local_y_kernel(section, ay, by, qy, out):
    r = stand(section[...])
    r = reduce_right(r, Y_STEPS, turn_lines, lambda i: (ay[i], by[i]))
    out[...] = lie(r * qy[...])


def output_kernel(message, far, local, hy, out):
    for g in range(ALL // 8):
        part = slice(8 * g, 8 * g + 8)
        e, k, r = (message[:, 4 * g + n : 4 * g + n + 1] for n in range(3))
        e2, k2, r2 = (far[:, 4 * g + n : 4 * g + n + 1] for n in range(3))
        c = (k + k2) * 0.5
        value = ((e2 + c) * r + c * r2) / (e * e2 + c * (e + e2))
        out[part, :] = local[part, :] + hy[part, :] * value


def call(kernel, outs, specs, flops=0, size=0, scratch=()):
    return pl.pallas_call(
        kernel,
        out_shape=outs,
        in_specs=specs,
        out_specs=jax.tree.map(lambda _: VMEM, outs),
        scratch_shapes=scratch,
        compiler_params=PARAMS,
        cost_estimate=pl.CostEstimate(flops=flops, bytes_accessed=size, transcendentals=0),
    )


SLAB_GROUPS = [[8 * b + a for b in range(8)] for a in range(8)]
CORES = [(i, i ^ 1) for i in range(64)]


CHIPS = [(i, i ^ (4 if i % 2 else 6)) for i in range(64)]
NEXT = [(i, i ^ 2) for i in range(64)]


def local(fields, kappa, vertical):
    grid = (ALL, COLS)
    swap = [(0, 1), (1, 0)]
    fields_far = lax.ppermute(fields, "gz", swap)
    vertical_far = lax.ppermute(vertical, "gz", swap)
    full = shape(*grid)
    half = shape(8, 8, 128)
    standing = shape(256, 128)
    fields_here, vertical_here, kappa_here, rim = call(
        input_kernel,
        (full, full, full, shape(2, 8, 128)),
        [HBM] * 3,
        flops=1_000_000,
        size=1_000_000,
        scratch=[pltpu.SemaphoreType.DMA((3,))],
    )(*(pltpu.with_memory_space_constraint(x.reshape(grid), pltpu.HBM) for x in (fields, vertical, kappa)))
    prev = lax.ppermute(rim, "gx", [(i, (i + 8) % 64) for i in range(64)])
    ax, bx, qx, h1, h2, parts = call(
        factor_x_kernel,
        (shape(4, *grid), shape(4, *grid), full, full, full, shape(5, 2, 8, 128)),
        [VMEM],
        flops=4_000_000,
        size=2_000_000,
    )(kappa_here)
    both = shape(2, 8, 8, 128)
    source, elements = call(source_kernel, (full, both), [VMEM] * 8)(
        fields_here, fields_far.reshape(grid), vertical_here, vertical_far.reshape(grid),
        h1, h2, parts, prev,
    )
    got = lax.ppermute(elements, "gx", CORES)
    local_x = call(local_x_kernel, full, [VMEM] * 4, flops=1_000_000, size=1_000_000)(source, ax, bx, qx)
    chips, chip, middle = call(chip_kernel, (both, half, shape(6, 8, 128)), [VMEM] * 2)(elements, got)
    far = lax.ppermute(chips, "gx", CHIPS)
    far1 = lax.ppermute(chip, "gx", NEXT)
    ay, by, qy, hy, edge = call(
        factor_y_kernel,
        (shape(10, 256, 128), shape(10, 256, 128), standing, full, shape(8, 128)),
        [VMEM] * 2,
        flops=20_000_000,
        size=4_000_000,
    )(kappa_here, chip)
    keep, send = call(pick_kernel, (half, half), [VMEM] * 2)(far, edge)
    got = lax.ppermute(send, "gx", CORES)
    message, nodes = call(
        slab_kernel, (shape(8, 5, 8, 128), shape(4, 3, 8, 128)), [VMEM] * 5
    )(chip, far1, keep, got, middle)
    got = lax.all_to_all(message, "gx", 0, 0, axis_index_groups=SLAB_GROUPS, tiled=True)
    mine, other = call(
        ends_kernel, (shape(2, 8, 128), shape(2, 8, 128)), [VMEM, VMEM]
    )(got, nodes)
    other = lax.ppermute(other, "gx", CORES)
    section, message = call(
        section_kernel, (full, shape(8, 128)), [VMEM] * 7
    )(mine, other, local_x, h1, h2, hy, edge)
    far = lax.ppermute(message, "gy", swap)
    local_y = call(local_y_kernel, full, [VMEM] * 4, flops=4_000_000, size=3_000_000)(section, ay, by, qy)
    out = call(output_kernel, full, [VMEM] * 4)(message, far, local_y, hy)
    return out.reshape(fields.shape)


def solution(mesh):
    spec = P(None, "gz", "gx", "gy")
    return jax.shard_map(
        local, mesh=mesh, in_specs=(spec, spec, spec), out_specs=spec, check_vma=False
    )
```

```python
import functools

import jax
import jax.numpy as jnp
from jax import lax
from jax.experimental import pallas as pl
from jax.experimental.pallas import tpu as pltpu
from jax.sharding import PartitionSpec as P

F32 = jnp.float32
ROWS = 16
COLS = 1024
ALL = 2 * ROWS
VMEM = pl.BlockSpec(memory_space=pltpu.VMEM)
HBM = pl.BlockSpec(memory_space=pltpu.HBM)
X_STEPS = (1, 2, 4, 8)
Y_STEPS = (1, 2, 4, 8, 16, 32, 64, 128, 256, 512)
PARAMS = pltpu.CompilerParams(vmem_limit_bytes=40 * 1024 * 1024)


def shape(*dims):
    return jax.ShapeDtypeStruct(dims, F32)


def turn(x, k, axis):
    n = x.shape[axis]
    k = k % n
    unit = 128 if axis == 1 else 8
    if k == 0:
        return x
    if k % unit == 0:
        low = lax.slice_in_dim(x, n - k, n, axis=axis)
        high = lax.slice_in_dim(x, 0, n - k, axis=axis)
        return jnp.concatenate([low, high], axis=axis)
    return pltpu.roll(x, k, axis)


def turn_lines(x, k):
    lanes = lax.broadcasted_iota(jnp.int32, (1, 128), 1)

    def blocks(pair, n):
        if n == 4:
            return pair[::-1]
        turned = [pltpu.roll(p, 32 * n % 128, 1) for p in pair]
        over = lanes < 32 * n if n > 0 else lanes >= 128 + 32 * n
        return [jnp.where(over, turned[1 - h], turned[h]) for h in range(2)]

    pair = [x[:128], x[128:]]
    size = abs(k)
    if size >= 128:
        pair = blocks(pair, 4 if size == 512 else k // 128)
    elif size >= 8:
        if k > 0:
            moved = blocks([p[128 - k :] for p in pair], 1)
            pair = [jnp.concatenate([m, p[: 128 - k]], axis=0) for m, p in zip(moved, pair)]
        else:
            moved = blocks([p[:size] for p in pair], -1)
            pair = [jnp.concatenate([p[size:], m], axis=0) for m, p in zip(moved, pair)]
    else:
        rows = lax.broadcasted_iota(jnp.int32, (8, 128), 0)
        turned = [pltpu.roll(p, k % 128, 0) for p in pair]
        if k > 0:
            ends = [t[:8] for t in turned]
            ends = [jnp.where(rows < k, m, e) for m, e in zip(blocks(ends, 1), ends)]
            pair = [jnp.concatenate([e, t[8:]], axis=0) for e, t in zip(ends, turned)]
        else:
            ends = [t[120:] for t in turned]
            ends = [jnp.where(rows >= 8 + k, m, e) for m, e in zip(blocks(ends, -1), ends)]
            pair = [jnp.concatenate([t[:120], e], axis=0) for e, t in zip(ends, turned)]
    return jnp.concatenate(pair, axis=0)


def stand(x):
    tiles = [x[:, 128 * j : 128 * (j + 1)] for j in range(8)]
    return jnp.concatenate(
        [jnp.concatenate(tiles[4 * h : 4 * h + 4], axis=0).T for h in range(2)], axis=0
    )


def lie(x):
    tiles = [x[128 * h : 128 * (h + 1)].T for h in range(2)]
    return jnp.concatenate(
        [tiles[h][ALL * b : ALL * (b + 1)] for h in range(2) for b in range(4)], axis=1
    )


def turn_rows(x, k):
    return turn(x, k, 0)


def reduce_matrix(low, excess, rights, steps, move, keep):
    for index, k in enumerate(steps):
        high = move(low, -k)
        inverse = 1.0 / (low + high + excess)
        up = high * inverse
        down = low * inverse
        keep(index, up, down)
        excess = excess + move(up * excess, k) + move(down * excess, -k)
        rights = [r + move(up * r, k) + move(down * r, -k) for r in rights]
        low = move(up * low, k)
    inverse = 1.0 / excess
    return inverse, [r * inverse for r in rights]


def reduce_right(right, steps, move, load):
    for index, k in enumerate(steps):
        up, down = load(index)
        right = right + move(up * right, k) + move(down * right, -k)
    return right


def dense(row):
    return jnp.concatenate([row[:, 128 * i : 128 * (i + 1)] for i in range(8)], axis=0)


def natural(tile, rows):
    return jnp.concatenate(
        [jnp.broadcast_to(tile[i : i + 1, :], (rows, 128)) for i in range(8)], axis=1
    )


def input_kernel(fields_arg, vertical_arg, kappa_arg, fields, vertical, kappa, rim, done):
    pairs = ((kappa_arg, kappa), (fields_arg, fields), (vertical_arg, vertical))
    copies = [pltpu.make_async_copy(a, b, done.at[n]) for n, (a, b) in enumerate(pairs)]
    for copy in copies:
        copy.start()
    copies[0].wait()
    for f in range(2):
        rim[f] = dense(kappa[f * ROWS + ROWS - 1 : f * ROWS + ROWS, :])
    copies[1].wait()
    copies[2].wait()


def factor_x_kernel(kappa, ax, bx, qx, h1, h2, parts):
    half = 512
    rows = lax.broadcasted_iota(jnp.int32, (ROWS, half), 0)
    for f in range(2):
        mine = pl.ds(f * ROWS, ROWS)
        for c in range(COLS // half):
            cols = pl.ds(c * half, half)
            k = kappa[mine, cols]
            face = (k + turn(k, 1, 0)) * 0.5
            low = jnp.where((rows >= 2) & (rows <= 14), face, 0.0)
            first = jnp.where(rows == 1, face, 0.0)
            last = jnp.where(rows == 14, turn(face, -1, 0), 0.0)

            def keep(index, a, b, mine=mine, cols=cols):
                ax[index, mine, cols] = a
                bx[index, mine, cols] = b

            inverse, (one, two) = reduce_matrix(
                low, 1.0 + first + last, [first, last], X_STEPS, turn_rows, keep
            )
            qx[mine, cols] = jnp.where((rows >= 1) & (rows <= 14), inverse, 0.0)
            one = jnp.where(rows == 0, 1.0, one)
            two = jnp.where(rows == ROWS - 1, 1.0, two)
            h1[mine, cols] = one
            h2[mine, cols] = two
            sums = (
                jnp.sum(first * two, axis=0, keepdims=True),
                jnp.sum(one, axis=0, keepdims=True),
                jnp.sum(two, axis=0, keepdims=True),
                k[:1],
                k[ROWS - 1 :],
            )
            for n, row in enumerate(sums):
                for i in range(half // 128):
                    parts[n, f, pl.ds(c * (half // 128) + i, 1), :] = row[:, 128 * i : 128 * (i + 1)]


def factor_y_kernel(kappa, ay, by, qy, hy, edge):
    gy = lax.axis_index("gy")
    low_side = gy == 0
    end = jnp.where(low_side, COLS - 1, 0)
    start = COLS - 1 - end
    beside = jnp.where(low_side, COLS - 2, 1)
    cut = jnp.where(low_side, COLS - 1, 1)
    k = stand(kappa[...])
    row = lax.broadcasted_iota(jnp.int32, (256, 128), 0)
    lane = lax.broadcasted_iota(jnp.int32, (256, 128), 1)
    y = row // 128 * 512 + lane // 32 * 128 + row % 128
    face = (k + turn_lines(k, 1)) * 0.5
    low = jnp.where((y == 0) | (y == cut), 0.0, face)
    link = jnp.where(y == beside, jnp.where(low_side, turn_lines(face, -1), face), 0.0)
    ground = jnp.where(y == start, 1.0 + 0.5 * k, 1.0)

    def keep(index, up, down):
        ay[index] = up
        by[index] = down

    inverse, (profile,) = reduce_matrix(low, ground + link, [link], Y_STEPS, turn_lines, keep)
    qy[...] = jnp.where(y == end, 0.0, inverse)
    profile = lie(jnp.where(y == end, 1.0, profile))
    hy[...] = profile
    k = kappa[...]
    column = lax.broadcasted_iota(jnp.int32, (ALL, COLS), 1)
    total = jnp.sum(profile * jnp.where(column == start, 1.0 + 0.5 * k, 1.0), axis=1, keepdims=True)
    rim = jnp.sum(jnp.where(column == end, k, 0.0), axis=1, keepdims=True)
    lane = lax.broadcasted_iota(jnp.int32, (8, 128), 1)
    tile = jnp.zeros((8, 128), F32)
    for g in range(ALL // 8):
        part = slice(8 * g, 8 * g + 8)
        tile = jnp.where(lane == 4 * g, total[part], jnp.where(lane == 4 * g + 1, rim[part], tile))
    edge[...] = tile


def source_kernel(fields, fields_far, vertical, vertical_far, h1, h2, parts, prev, after, source, elements):
    del after
    here = fields[...]
    v = vertical[...]
    s = here + (v + vertical_far[...]) * 0.5 * (fields_far[...] - here) - v * 0.5 * here
    source[...] = s
    for f in range(2):
        mine = slice(f * ROWS, (f + 1) * ROWS)
        first = dense(jnp.sum(h1[mine, :] * s[mine, :], axis=0, keepdims=True))
        last = dense(jnp.sum(h2[mine, :] * s[mine, :], axis=0, keepdims=True))
        element = (parts[0, f], parts[1, f], parts[2, f], first, last, parts[3, f], parts[4, f], prev[f])
        for n, value in enumerate(element):
            elements[f, n] = value


def local_x_kernel(source, ax, bx, qx, out):
    half = 512
    for f in range(2):
        mine = pl.ds(f * ROWS, ROWS)
        for c in range(COLS // half):
            cols = pl.ds(c * half, half)
            r = source[mine, cols]
            r = reduce_right(r, X_STEPS, turn_rows, lambda i: (ax[i, mine, cols], bx[i, mine, cols]))
            out[mine, cols] = r * qx[mine, cols]


def merge(one, two):
    g, sl, sr, rl, rr = one
    g2, sl2, sr2, rl2, rr2 = two
    s = sr + sl2
    r = rr + rl2
    inverse = 1.0 / (g + g2 + s)
    a = g * inverse
    b = g2 * inverse
    return (a * g2, sl + a * s, sr2 + b * s, rl + a * r, rr2 + b * r), (a, b, r * inverse)


def behind(face, two):
    g, s, sr, r, rr = two
    inverse = 1.0 / (face + g + s)
    a = face * inverse
    b = g * inverse
    return (a * g, a * s, sr + b * s, a * r, rr + b * r), (a, b, r * inverse)


def load(ref, *field):
    return tuple(ref[(*field, n)] for n in range(8))


def within(node, left, right):
    a, b, c = node
    return (a * left[0] + b * right[0], a * left[1] + b * right[1], a * left[2] + b * right[2] + c)


def chip_kernel(mine, other, chips, chip, middle):
    even = lax.axis_index("gx") % 2 == 0
    fields = []
    for f in range(2):
        a, b = load(mine, f), load(other, f)
        first = [jnp.where(even, m, o) for m, o in zip(a, b)]
        second = [jnp.where(even, o, m) for m, o in zip(a, b)]
        tail, start = behind((first[6] + second[5]) * 0.5, second[:5])
        element, end = merge(first[:5], tail)
        fields.append(((*element, first[5], *second[6:]), (*end, *start)))
        for n, value in enumerate(fields[f][0]):
            chips[f, n] = value
    for out, (one, two) in zip((chip, middle), zip(*fields)):
        for n, (a, b) in enumerate(zip(one, two)):
            out[n] = jnp.where(even, a, b)


def pick_kernel(chips, keep, send):
    even = lax.axis_index("gx") % 2 == 0
    for n, (one, two) in enumerate(zip(load(chips, 0), load(chips, 1))):
        keep[n] = jnp.where(even, one, two)
        send[n] = jnp.where(even, two, one)


def slab_kernel(chip, far1, keep, got, middle, message, nodes):
    y = lax.axis_index("gx") // 2 % 4
    even = lax.axis_index("gx") % 2 == 0
    far2 = [jnp.where(even, g, k) for k, g in zip(load(keep), load(got))]
    far3 = [jnp.where(even, k, g) for k, g in zip(load(keep), load(got))]
    arrived = [load(chip), load(far1), far2, far3]
    chips = []
    for m in range(4):
        chosen = arrived[0]
        for flip in range(1, 4):
            here = y ^ flip == m
            chosen = [jnp.where(here, a, c) for a, c in zip(arrived[flip], chosen)]
        chips.append(chosen)
    slab = lax.axis_index("gx") // 8
    before = jnp.where(slab == 0, 0.0, chips[3][7])
    element, inner, fronts = None, [], []
    for m in range(4):
        face = ((before if m == 0 else chips[m - 1][6]) + chips[m][5]) * 0.5
        tail, front = behind(face, chips[m][:5])
        fronts.append(front)
        if m == 0:
            element = tail
        else:
            element, node = merge(element, tail)
            inner.append(node)
    g, sl, sr, rl, rr = element
    sr = jnp.where(slab == 7, sr + chips[3][6] * 0.5, sr)
    for n, value in enumerate((g, sl, sr, rl, rr)):
        for j in range(8):
            message[j, n] = value
    zero, one = jnp.zeros((8, 128), F32), jnp.ones((8, 128), F32)
    left = (one, zero, zero)
    lasts = [(zero, one, zero)]
    for node in inner[::-1]:
        lasts.append(within(node, left, lasts[-1]))
    lasts = [left] + lasts[::-1]
    firsts = [within(fronts[m], lasts[m], lasts[m + 1]) for m in range(4)]
    lasts = lasts[1:]
    first, last = firsts[0], lasts[0]
    for m in range(1, 4):
        first = [jnp.where(y == m, new, old) for new, old in zip(firsts[m], first)]
        last = [jnp.where(y == m, new, old) for new, old in zip(lasts[m], last)]
    before = within(tuple(middle[n] for n in range(3)), first, last)
    second = within(tuple(middle[n] for n in range(3, 6)), before, last)
    for n, trio in enumerate((first, before, second, last)):
        for m in range(3):
            nodes[n, m] = trio[m]


def ends_kernel(got, nodes, mine, other):
    gx = lax.axis_index("gx")
    slab = gx // 8
    even = gx % 2 == 0
    zero = jnp.zeros((8, 128), F32)
    conduct = got[0, 0] + got[0, 2]
    right = got[0, 4]
    ratios, offsets = [], []
    for z in range(1, 8):
        g, sl, sr, rl, rr = (got[z, n] for n in range(5))
        conduct = conduct + sl
        right = right + rl
        inverse = 1.0 / (conduct + g)
        f = g * inverse
        ratios.append(f)
        offsets.append(right * inverse)
        conduct = sr + f * conduct
        right = rr + f * right
    value = right / conduct
    values = [value]
    for k in range(6, -1, -1):
        value = ratios[k] * value + offsets[k]
        values.append(value)
    values = [zero] + values[::-1]
    first, last = zero, zero
    for z in range(8):
        first = jnp.where(slab == z, values[z], first)
        last = jnp.where(slab == z, values[z + 1], last)
    row = [nodes[n, 0] * first + nodes[n, 1] * last + nodes[n, 2] for n in range(4)]
    for n in range(2):
        mine[n] = jnp.where(even, row[n], row[n + 2])
        other[n] = jnp.where(even, row[n + 2], row[n])


def section_kernel(mine, other, local, h1, h2, hy, edge, section, message):
    core = lax.axis_index("gx") % 2
    lane = lax.broadcasted_iota(jnp.int32, (8, 128), 1)
    tile = edge[...]
    for f in range(2):
        first = jnp.where(core == f, mine[0], other[0])
        last = jnp.where(core == f, mine[1], other[1])
        rows = slice(f * ROWS, (f + 1) * ROWS)
        s = local[rows, :] + h1[rows, :] * natural(first, ROWS) + h2[rows, :] * natural(last, ROWS)
        section[rows, :] = s
        total = jnp.sum(hy[rows, :] * s, axis=1, keepdims=True)
        for g in range(2):
            tile = jnp.where(lane == 4 * (2 * f + g) + 2, total[8 * g : 8 * g + 8], tile)
    message[...] = tile


def local_y_kernel(section, ay, by, qy, out):
    r = stand(section[...])
    r = reduce_right(r, Y_STEPS, turn_lines, lambda i: (ay[i], by[i]))
    out[...] = lie(r * qy[...])


def output_kernel(message, far, local, hy, out):
    for g in range(ALL // 8):
        part = slice(8 * g, 8 * g + 8)
        e, k, r = (message[:, 4 * g + n : 4 * g + n + 1] for n in range(3))
        e2, k2, r2 = (far[:, 4 * g + n : 4 * g + n + 1] for n in range(3))
        c = (k + k2) * 0.5
        value = ((e2 + c) * r + c * r2) / (e * e2 + c * (e + e2))
        out[part, :] = local[part, :] + hy[part, :] * value


def call(kernel, outs, specs, flops=0, size=0, scratch=()):
    return pl.pallas_call(
        kernel,
        out_shape=outs,
        in_specs=specs,
        out_specs=jax.tree.map(lambda _: VMEM, outs),
        scratch_shapes=scratch,
        compiler_params=PARAMS,
        cost_estimate=pl.CostEstimate(flops=flops, bytes_accessed=size, transcendentals=0),
    )


SLAB_GROUPS = [[8 * b + a for b in range(8)] for a in range(8)]
CORES = [(i, i ^ 1) for i in range(64)]


CHIPS = [(i, i ^ (4 if i % 2 else 6)) for i in range(64)]
NEXT = [(i, i ^ 2) for i in range(64)]


def local(fields, kappa, vertical):
    grid = (ALL, COLS)
    swap = [(0, 1), (1, 0)]
    fields_far = lax.ppermute(fields, "gz", swap)
    vertical_far = lax.ppermute(vertical, "gz", swap)
    full = shape(*grid)
    half = shape(8, 8, 128)
    standing = shape(256, 128)
    fields_here, vertical_here, kappa_here, rim = call(
        input_kernel,
        (full, full, full, shape(2, 8, 128)),
        [HBM] * 3,
        flops=1_000_000,
        size=1_000_000,
        scratch=[pltpu.SemaphoreType.DMA((3,))],
    )(*(pltpu.with_memory_space_constraint(x.reshape(grid), pltpu.HBM) for x in (fields, vertical, kappa)))
    prev = lax.ppermute(rim, "gx", [(i, (i + 8) % 64) for i in range(64)])
    ax, bx, qx, h1, h2, parts = call(
        factor_x_kernel,
        (shape(4, *grid), shape(4, *grid), full, full, full, shape(5, 2, 8, 128)),
        [VMEM],
        flops=4_000_000,
        size=2_000_000,
    )(kappa_here)
    ay, by, qy, hy, edge = call(
        factor_y_kernel,
        (shape(10, 256, 128), shape(10, 256, 128), standing, full, shape(8, 128)),
        [VMEM],
        flops=20_000_000,
        size=4_000_000,
    )(kappa_here)
    both = shape(2, 8, 8, 128)
    source, elements = call(source_kernel, (full, both), [VMEM] * 9)(
        fields_here, fields_far.reshape(grid), vertical_here, vertical_far.reshape(grid),
        h1, h2, parts, prev, edge,
    )
    got = lax.ppermute(elements, "gx", CORES)
    local_x = call(local_x_kernel, full, [VMEM] * 4, flops=1_000_000, size=1_000_000)(source, ax, bx, qx)
    chips, chip, middle = call(chip_kernel, (both, half, shape(6, 8, 128)), [VMEM] * 2)(elements, got)
    far = lax.ppermute(chips, "gx", CHIPS)
    far1 = lax.ppermute(chip, "gx", NEXT)
    keep, send = call(pick_kernel, (half, half), [VMEM])(far)
    got = lax.ppermute(send, "gx", CORES)
    message, nodes = call(
        slab_kernel, (shape(8, 5, 8, 128), shape(4, 3, 8, 128)), [VMEM] * 5
    )(chip, far1, keep, got, middle)
    got = lax.all_to_all(message, "gx", 0, 0, axis_index_groups=SLAB_GROUPS, tiled=True)
    mine, other = call(
        ends_kernel, (shape(2, 8, 128), shape(2, 8, 128)), [VMEM, VMEM]
    )(got, nodes)
    other = lax.ppermute(other, "gx", CORES)
    section, message = call(
        section_kernel, (full, shape(8, 128)), [VMEM] * 7
    )(mine, other, local_x, h1, h2, hy, edge)
    far = lax.ppermute(message, "gy", swap)
    local_y = call(local_y_kernel, full, [VMEM] * 4, flops=4_000_000, size=3_000_000)(section, ay, by, qy)
    out = call(output_kernel, full, [VMEM] * 4)(message, far, local_y, hy)
    return out.reshape(fields.shape)


def solution(mesh):
    spec = P(None, "gz", "gx", "gy")
    return jax.shard_map(
        local, mesh=mesh, in_specs=(spec, spec, spec), out_specs=spec, check_vma=False
    )
```

```python
import functools

import jax
import jax.numpy as jnp
from jax import lax
from jax.experimental import pallas as pl
from jax.experimental.pallas import tpu as pltpu
from jax.sharding import PartitionSpec as P

F32 = jnp.float32
ROWS = 16
COLS = 1024
ALL = 2 * ROWS
VMEM = pl.BlockSpec(memory_space=pltpu.VMEM)
HBM = pl.BlockSpec(memory_space=pltpu.HBM)
X_STEPS = (1, 2, 4, 8)
Y_STEPS = (1, 2, 4, 8, 16, 32, 64, 128, 256, 512)
PARAMS = pltpu.CompilerParams(vmem_limit_bytes=40 * 1024 * 1024)


def shape(*dims):
    return jax.ShapeDtypeStruct(dims, F32)


def turn(x, k, axis):
    n = x.shape[axis]
    k = k % n
    unit = 128 if axis == 1 else 8
    if k == 0:
        return x
    if k % unit == 0:
        low = lax.slice_in_dim(x, n - k, n, axis=axis)
        high = lax.slice_in_dim(x, 0, n - k, axis=axis)
        return jnp.concatenate([low, high], axis=axis)
    return pltpu.roll(x, k, axis)


def turn_lines(x, k):
    lanes = lax.broadcasted_iota(jnp.int32, (1, 128), 1)

    def blocks(pair, n):
        if n == 4:
            return pair[::-1]
        turned = [pltpu.roll(p, 32 * n % 128, 1) for p in pair]
        over = lanes < 32 * n if n > 0 else lanes >= 128 + 32 * n
        return [jnp.where(over, turned[1 - h], turned[h]) for h in range(2)]

    pair = [x[:128], x[128:]]
    size = abs(k)
    if size >= 128:
        pair = blocks(pair, 4 if size == 512 else k // 128)
    elif size >= 8:
        if k > 0:
            moved = blocks([p[128 - k :] for p in pair], 1)
            pair = [jnp.concatenate([m, p[: 128 - k]], axis=0) for m, p in zip(moved, pair)]
        else:
            moved = blocks([p[:size] for p in pair], -1)
            pair = [jnp.concatenate([p[size:], m], axis=0) for m, p in zip(moved, pair)]
    else:
        rows = lax.broadcasted_iota(jnp.int32, (8, 128), 0)
        turned = [pltpu.roll(p, k % 128, 0) for p in pair]
        if k > 0:
            ends = [t[:8] for t in turned]
            ends = [jnp.where(rows < k, m, e) for m, e in zip(blocks(ends, 1), ends)]
            pair = [jnp.concatenate([e, t[8:]], axis=0) for e, t in zip(ends, turned)]
        else:
            ends = [t[120:] for t in turned]
            ends = [jnp.where(rows >= 8 + k, m, e) for m, e in zip(blocks(ends, -1), ends)]
            pair = [jnp.concatenate([t[:120], e], axis=0) for e, t in zip(ends, turned)]
    return jnp.concatenate(pair, axis=0)


def stand(x):
    tiles = [x[:, 128 * j : 128 * (j + 1)] for j in range(8)]
    return jnp.concatenate(
        [jnp.concatenate(tiles[4 * h : 4 * h + 4], axis=0).T for h in range(2)], axis=0
    )


def lie(x):
    tiles = [x[128 * h : 128 * (h + 1)].T for h in range(2)]
    return jnp.concatenate(
        [tiles[h][ALL * b : ALL * (b + 1)] for h in range(2) for b in range(4)], axis=1
    )


def turn_rows(x, k):
    return turn(x, k, 0)


def reduce_matrix(low, excess, rights, steps, move, keep):
    for index, k in enumerate(steps):
        high = move(low, -k)
        inverse = 1.0 / (low + high + excess)
        up = high * inverse
        down = low * inverse
        keep(index, up, down)
        excess = excess + move(up * excess, k) + move(down * excess, -k)
        rights = [r + move(up * r, k) + move(down * r, -k) for r in rights]
        low = move(up * low, k)
    inverse = 1.0 / excess
    return inverse, [r * inverse for r in rights]


def reduce_right(right, steps, move, load):
    for index, k in enumerate(steps):
        up, down = load(index)
        right = right + move(up * right, k) + move(down * right, -k)
    return right


def dense(row):
    return jnp.concatenate([row[:, 128 * i : 128 * (i + 1)] for i in range(8)], axis=0)


def natural(tile, rows):
    return jnp.concatenate(
        [jnp.broadcast_to(tile[i : i + 1, :], (rows, 128)) for i in range(8)], axis=1
    )


def input_kernel(fields_arg, vertical_arg, kappa_arg, fields, vertical, kappa, rim, done):
    pairs = ((kappa_arg, kappa), (fields_arg, fields), (vertical_arg, vertical))
    copies = [pltpu.make_async_copy(a, b, done.at[n]) for n, (a, b) in enumerate(pairs)]
    for copy in copies:
        copy.start()
    copies[0].wait()
    for f in range(2):
        rim[f] = dense(kappa[f * ROWS + ROWS - 1 : f * ROWS + ROWS, :])
    copies[1].wait()
    copies[2].wait()


def factor_x_kernel(kappa, ax, bx, qx, h1, h2, parts):
    half = 512
    rows = lax.broadcasted_iota(jnp.int32, (ROWS, half), 0)
    for f in range(2):
        mine = pl.ds(f * ROWS, ROWS)
        for c in range(COLS // half):
            cols = pl.ds(c * half, half)
            k = kappa[mine, cols]
            face = (k + turn(k, 1, 0)) * 0.5
            low = jnp.where((rows >= 2) & (rows <= 14), face, 0.0)
            first = jnp.where(rows == 1, face, 0.0)
            last = jnp.where(rows == 14, turn(face, -1, 0), 0.0)

            def keep(index, a, b, mine=mine, cols=cols):
                ax[index, mine, cols] = a
                bx[index, mine, cols] = b

            inverse, (one, two) = reduce_matrix(
                low, 1.0 + first + last, [first, last], X_STEPS, turn_rows, keep
            )
            qx[mine, cols] = jnp.where((rows >= 1) & (rows <= 14), inverse, 0.0)
            one = jnp.where(rows == 0, 1.0, one)
            two = jnp.where(rows == ROWS - 1, 1.0, two)
            h1[mine, cols] = one
            h2[mine, cols] = two
            sums = (
                jnp.sum(first * two, axis=0, keepdims=True),
                jnp.sum(one, axis=0, keepdims=True),
                jnp.sum(two, axis=0, keepdims=True),
                k[:1],
                k[ROWS - 1 :],
            )
            for n, row in enumerate(sums):
                for i in range(half // 128):
                    parts[n, f, pl.ds(c * (half // 128) + i, 1), :] = row[:, 128 * i : 128 * (i + 1)]


def factor_y_kernel(kappa, ay, by, qy, hy, edge):
    gy = lax.axis_index("gy")
    low_side = gy == 0
    end = jnp.where(low_side, COLS - 1, 0)
    start = COLS - 1 - end
    beside = jnp.where(low_side, COLS - 2, 1)
    cut = jnp.where(low_side, COLS - 1, 1)
    k = stand(kappa[...])
    row = lax.broadcasted_iota(jnp.int32, (256, 128), 0)
    lane = lax.broadcasted_iota(jnp.int32, (256, 128), 1)
    y = row // 128 * 512 + lane // 32 * 128 + row % 128
    face = (k + turn_lines(k, 1)) * 0.5
    low = jnp.where((y == 0) | (y == cut), 0.0, face)
    link = jnp.where(y == beside, jnp.where(low_side, turn_lines(face, -1), face), 0.0)
    ground = jnp.where(y == start, 1.0 + 0.5 * k, 1.0)

    def keep(index, up, down):
        ay[index] = up
        by[index] = down

    inverse, (profile,) = reduce_matrix(low, ground + link, [link], Y_STEPS, turn_lines, keep)
    qy[...] = jnp.where(y == end, 0.0, inverse)
    profile = lie(jnp.where(y == end, 1.0, profile))
    hy[...] = profile
    k = kappa[...]
    column = lax.broadcasted_iota(jnp.int32, (ALL, COLS), 1)
    total = jnp.sum(profile * jnp.where(column == start, 1.0 + 0.5 * k, 1.0), axis=1, keepdims=True)
    rim = jnp.sum(jnp.where(column == end, k, 0.0), axis=1, keepdims=True)
    lane = lax.broadcasted_iota(jnp.int32, (8, 128), 1)
    tile = jnp.zeros((8, 128), F32)
    for g in range(ALL // 8):
        part = slice(8 * g, 8 * g + 8)
        tile = jnp.where(lane == 4 * g, total[part], jnp.where(lane == 4 * g + 1, rim[part], tile))
    edge[...] = tile


def source_kernel(fields, fields_far, vertical, vertical_far, h1, h2, parts, prev, after, source, elements):
    del after
    here = fields[...]
    v = vertical[...]
    s = here + (v + vertical_far[...]) * 0.5 * (fields_far[...] - here) - v * 0.5 * here
    source[...] = s
    for f in range(2):
        mine = slice(f * ROWS, (f + 1) * ROWS)
        first = dense(jnp.sum(h1[mine, :] * s[mine, :], axis=0, keepdims=True))
        last = dense(jnp.sum(h2[mine, :] * s[mine, :], axis=0, keepdims=True))
        element = (parts[0, f], parts[1, f], parts[2, f], first, last, parts[3, f], parts[4, f], prev[f])
        for n, value in enumerate(element):
            elements[f, n] = value


def fill(tile, totals):
    lane = lax.broadcasted_iota(jnp.int32, (8, 128), 1)
    for g in range(ALL // 8):
        tile = jnp.where(lane == 4 * g + 2, totals[8 * g : 8 * g + 8], tile)
    return tile


def weights_kernel(h1, h2, hy, after, weights):
    del after
    weights[0] = hy[...] * h1[...]
    weights[1] = hy[...] * h2[...]


def local_x_kernel(source, ax, bx, qx, hy, edge, out, tile):
    half = 512
    for f in range(2):
        mine = pl.ds(f * ROWS, ROWS)
        for c in range(COLS // half):
            cols = pl.ds(c * half, half)
            r = source[mine, cols]
            r = reduce_right(r, X_STEPS, turn_rows, lambda i: (ax[i, mine, cols], bx[i, mine, cols]))
            out[mine, cols] = r * qx[mine, cols]
    tile[...] = fill(edge[...], jnp.sum(hy[...] * out[...], axis=1, keepdims=True))


def merge(one, two):
    g, sl, sr, rl, rr = one
    g2, sl2, sr2, rl2, rr2 = two
    s = sr + sl2
    r = rr + rl2
    inverse = 1.0 / (g + g2 + s)
    a = g * inverse
    b = g2 * inverse
    return (a * g2, sl + a * s, sr2 + b * s, rl + a * r, rr2 + b * r), (a, b, r * inverse)


def behind(face, two):
    g, s, sr, r, rr = two
    inverse = 1.0 / (face + g + s)
    a = face * inverse
    b = g * inverse
    return (a * g, a * s, sr + b * s, a * r, rr + b * r), (a, b, r * inverse)


def load(ref, *field):
    return tuple(ref[(*field, n)] for n in range(8))


def within(node, left, right):
    a, b, c = node
    return (a * left[0] + b * right[0], a * left[1] + b * right[1], a * left[2] + b * right[2] + c)


def chip_kernel(mine, other, chips, chip, middle):
    even = lax.axis_index("gx") % 2 == 0
    fields = []
    for f in range(2):
        a, b = load(mine, f), load(other, f)
        first = [jnp.where(even, m, o) for m, o in zip(a, b)]
        second = [jnp.where(even, o, m) for m, o in zip(a, b)]
        tail, start = behind((first[6] + second[5]) * 0.5, second[:5])
        element, end = merge(first[:5], tail)
        fields.append(((*element, first[5], *second[6:]), (*end, *start)))
        for n, value in enumerate(fields[f][0]):
            chips[f, n] = value
    for out, (one, two) in zip((chip, middle), zip(*fields)):
        for n, (a, b) in enumerate(zip(one, two)):
            out[n] = jnp.where(even, a, b)


def pick_kernel(chips, keep, send):
    even = lax.axis_index("gx") % 2 == 0
    for n, (one, two) in enumerate(zip(load(chips, 0), load(chips, 1))):
        keep[n] = jnp.where(even, one, two)
        send[n] = jnp.where(even, two, one)


def slab_kernel(chip, far1, keep, got, middle, tile, weights, message, nodes):
    del tile, weights
    y = lax.axis_index("gx") // 2 % 4
    even = lax.axis_index("gx") % 2 == 0
    far2 = [jnp.where(even, g, k) for k, g in zip(load(keep), load(got))]
    far3 = [jnp.where(even, k, g) for k, g in zip(load(keep), load(got))]
    arrived = [load(chip), load(far1), far2, far3]
    chips = []
    for m in range(4):
        chosen = arrived[0]
        for flip in range(1, 4):
            here = y ^ flip == m
            chosen = [jnp.where(here, a, c) for a, c in zip(arrived[flip], chosen)]
        chips.append(chosen)
    slab = lax.axis_index("gx") // 8
    before = jnp.where(slab == 0, 0.0, chips[3][7])
    element, inner, fronts = None, [], []
    for m in range(4):
        face = ((before if m == 0 else chips[m - 1][6]) + chips[m][5]) * 0.5
        tail, front = behind(face, chips[m][:5])
        fronts.append(front)
        if m == 0:
            element = tail
        else:
            element, node = merge(element, tail)
            inner.append(node)
    g, sl, sr, rl, rr = element
    sr = jnp.where(slab == 7, sr + chips[3][6] * 0.5, sr)
    for n, value in enumerate((g, sl, sr, rl, rr)):
        for j in range(8):
            message[j, n] = value
    zero, one = jnp.zeros((8, 128), F32), jnp.ones((8, 128), F32)
    left = (one, zero, zero)
    lasts = [(zero, one, zero)]
    for node in inner[::-1]:
        lasts.append(within(node, left, lasts[-1]))
    lasts = [left] + lasts[::-1]
    firsts = [within(fronts[m], lasts[m], lasts[m + 1]) for m in range(4)]
    lasts = lasts[1:]
    first, last = firsts[0], lasts[0]
    for m in range(1, 4):
        first = [jnp.where(y == m, new, old) for new, old in zip(firsts[m], first)]
        last = [jnp.where(y == m, new, old) for new, old in zip(lasts[m], last)]
    before = within(tuple(middle[n] for n in range(3)), first, last)
    second = within(tuple(middle[n] for n in range(3, 6)), before, last)
    for n, trio in enumerate((first, before, second, last)):
        for m in range(3):
            nodes[n, m] = trio[m]


def ends_kernel(got, nodes, tile, rows):
    slab = lax.axis_index("gx") // 8
    zero = jnp.zeros((8, 128), F32)
    conduct = got[0, 0] + got[0, 2]
    right = got[0, 4]
    ratios, offsets = [], []
    for z in range(1, 8):
        g, sl, sr, rl, rr = (got[z, n] for n in range(5))
        conduct = conduct + sl
        right = right + rl
        inverse = 1.0 / (conduct + g)
        f = g * inverse
        ratios.append(f)
        offsets.append(right * inverse)
        conduct = sr + f * conduct
        right = rr + f * right
    value = right / conduct
    values = [value]
    for k in range(6, -1, -1):
        value = ratios[k] * value + offsets[k]
        values.append(value)
    values = [zero] + values[::-1]
    first, last = zero, zero
    for z in range(8):
        first = jnp.where(slab == z, values[z], first)
        last = jnp.where(slab == z, values[z + 1], last)
    for n in range(4):
        rows[n] = nodes[n, 0] * first + nodes[n, 1] * last + nodes[n, 2]
    rows[4] = tile[...]


def ends_of(low, mine, other, f):
    here = lax.axis_index("gx") % 2 == f
    row = [jnp.where(here, mine[n], other[n]) for n in range(4)]
    return jnp.where(low, row[0], row[2]), jnp.where(low, row[1], row[3])


def message_kernel(mine, other, weights, message):
    low = lax.axis_index("gx") % 2 == 1
    totals = []
    for f in range(2):
        first, last = ends_of(low, mine, other, f)
        rows = slice(f * ROWS, (f + 1) * ROWS)
        s = weights[0, rows, :] * natural(first, ROWS) + weights[1, rows, :] * natural(last, ROWS)
        totals.append(jnp.sum(s, axis=1, keepdims=True))
    totals = jnp.concatenate(totals, axis=0)
    tile = other[4]
    message[...] = tile + fill(jnp.zeros((8, 128), F32), totals)


def section_kernel(mine, other, local, h1, h2, hy, edge, section, message):
    low = lax.axis_index("gx") % 2 == 0
    totals = []
    for f in range(2):
        first, last = ends_of(low, mine, other, f)
        rows = slice(f * ROWS, (f + 1) * ROWS)
        s = local[rows, :] + h1[rows, :] * natural(first, ROWS) + h2[rows, :] * natural(last, ROWS)
        section[rows, :] = s
        totals.append(jnp.sum(hy[rows, :] * s, axis=1, keepdims=True))
    message[...] = fill(edge[...], jnp.concatenate(totals, axis=0))


def local_y_kernel(section, ay, by, qy, out):
    r = stand(section[...])
    r = reduce_right(r, Y_STEPS, turn_lines, lambda i: (ay[i], by[i]))
    out[...] = lie(r * qy[...])


def output_kernel(message, far, local, hy, out):
    for g in range(ALL // 8):
        part = slice(8 * g, 8 * g + 8)
        e, k, r = (message[:, 4 * g + n : 4 * g + n + 1] for n in range(3))
        e2, k2, r2 = (far[:, 4 * g + n : 4 * g + n + 1] for n in range(3))
        c = (k + k2) * 0.5
        value = ((e2 + c) * r + c * r2) / (e * e2 + c * (e + e2))
        out[part, :] = local[part, :] + hy[part, :] * value


def call(kernel, outs, specs, flops=0, size=0, scratch=()):
    return pl.pallas_call(
        kernel,
        out_shape=outs,
        in_specs=specs,
        out_specs=jax.tree.map(lambda _: VMEM, outs),
        scratch_shapes=scratch,
        compiler_params=PARAMS,
        cost_estimate=pl.CostEstimate(flops=flops, bytes_accessed=size, transcendentals=0),
    )


SLAB_GROUPS = [[8 * b + a for b in range(8)] for a in range(8)]
CORES = [(i, i ^ 1) for i in range(64)]


CHIPS = [(i, i ^ (4 if i % 2 else 6)) for i in range(64)]
ACROSS = [(2 * i + y, 2 * (i ^ 1) + 1 - y) for i in range(64) for y in range(2)]
NEXT = [(i, i ^ 2) for i in range(64)]


def local(fields, kappa, vertical):
    grid = (ALL, COLS)
    swap = [(0, 1), (1, 0)]
    fields_far = lax.ppermute(fields, "gz", swap)
    vertical_far = lax.ppermute(vertical, "gz", swap)
    full = shape(*grid)
    half = shape(8, 8, 128)
    standing = shape(256, 128)
    fields_here, vertical_here, kappa_here, rim = call(
        input_kernel,
        (full, full, full, shape(2, 8, 128)),
        [HBM] * 3,
        flops=1_000_000,
        size=1_000_000,
        scratch=[pltpu.SemaphoreType.DMA((3,))],
    )(*(pltpu.with_memory_space_constraint(x.reshape(grid), pltpu.HBM) for x in (fields, vertical, kappa)))
    prev = lax.ppermute(rim, "gx", [(i, (i + 8) % 64) for i in range(64)])
    ax, bx, qx, h1, h2, parts = call(
        factor_x_kernel,
        (shape(4, *grid), shape(4, *grid), full, full, full, shape(5, 2, 8, 128)),
        [VMEM],
        flops=4_000_000,
        size=2_000_000,
    )(kappa_here)
    ay, by, qy, hy, edge = call(
        factor_y_kernel,
        (shape(10, 256, 128), shape(10, 256, 128), standing, full, shape(8, 128)),
        [VMEM],
        flops=20_000_000,
        size=4_000_000,
    )(kappa_here)
    both = shape(2, 8, 8, 128)
    source, elements = call(source_kernel, (full, both), [VMEM] * 9)(
        fields_here, fields_far.reshape(grid), vertical_here, vertical_far.reshape(grid),
        h1, h2, parts, prev, edge,
    )
    got = lax.ppermute(elements, "gx", CORES)
    local_x, tile = call(
        local_x_kernel, (full, shape(8, 128)), [VMEM] * 6, flops=1_000_000, size=1_000_000
    )(source, ax, bx, qx, hy, edge)
    chips, chip, middle = call(chip_kernel, (both, half, shape(6, 8, 128)), [VMEM] * 2)(elements, got)
    far = lax.ppermute(chips, "gx", CHIPS)
    weights = call(weights_kernel, shape(2, *grid), [VMEM] * 4)(h1, h2, hy, chip)
    weights = lax.ppermute(weights, "gx", CORES)
    far1 = lax.ppermute(chip, "gx", NEXT)
    keep, send = call(pick_kernel, (half, half), [VMEM])(far)
    got = lax.ppermute(send, "gx", CORES)
    message, nodes = call(
        slab_kernel, (shape(8, 5, 8, 128), shape(4, 3, 8, 128)), [VMEM] * 7
    )(chip, far1, keep, got, middle, tile, weights)
    got = lax.all_to_all(message, "gx", 0, 0, axis_index_groups=SLAB_GROUPS, tiled=True)
    mine = call(ends_kernel, shape(5, 8, 128), [VMEM] * 3)(got, nodes, tile)
    other = lax.ppermute(mine, "gx", CORES)
    message = call(message_kernel, shape(8, 128), [VMEM] * 3)(mine, other, weights)
    far = lax.ppermute(message, ("gx", "gy"), ACROSS)
    section, message = call(
        section_kernel, (full, shape(8, 128)), [VMEM] * 7, flops=1_000_000, size=1_000_000
    )(mine, other, local_x, h1, h2, hy, edge)
    local_y = call(local_y_kernel, full, [VMEM] * 4, flops=4_000_000, size=3_000_000)(section, ay, by, qy)
    out = call(output_kernel, full, [VMEM] * 4)(message, far, local_y, hy)
    return out.reshape(fields.shape)


def solution(mesh):
    spec = P(None, "gz", "gx", "gy")
    return jax.shard_map(
        local, mesh=mesh, in_specs=(spec, spec, spec), out_specs=spec, check_vma=False
    )
```

```python
import functools

import jax
import jax.numpy as jnp
from jax import lax
from jax.experimental import pallas as pl
from jax.experimental.pallas import tpu as pltpu
from jax.sharding import PartitionSpec as P

F32 = jnp.float32
ROWS = 16
COLS = 1024
ALL = 2 * ROWS
VMEM = pl.BlockSpec(memory_space=pltpu.VMEM)
HBM = pl.BlockSpec(memory_space=pltpu.HBM)
X_STEPS = (1, 2, 4, 8)
Y_STEPS = (1, 2, 4, 8, 16, 32, 64, 128, 256, 512)
PARAMS = pltpu.CompilerParams(vmem_limit_bytes=40 * 1024 * 1024)


def shape(*dims):
    return jax.ShapeDtypeStruct(dims, F32)


def turn(x, k, axis):
    n = x.shape[axis]
    k = k % n
    unit = 128 if axis == 1 else 8
    if k == 0:
        return x
    if k % unit == 0:
        low = lax.slice_in_dim(x, n - k, n, axis=axis)
        high = lax.slice_in_dim(x, 0, n - k, axis=axis)
        return jnp.concatenate([low, high], axis=axis)
    return pltpu.roll(x, k, axis)


def turn_lines(x, k):
    lanes = lax.broadcasted_iota(jnp.int32, (1, 128), 1)

    def blocks(pair, n):
        if n == 4:
            return pair[::-1]
        turned = [pltpu.roll(p, 32 * n % 128, 1) for p in pair]
        over = lanes < 32 * n if n > 0 else lanes >= 128 + 32 * n
        return [jnp.where(over, turned[1 - h], turned[h]) for h in range(2)]

    pair = [x[:128], x[128:]]
    size = abs(k)
    if size >= 128:
        pair = blocks(pair, 4 if size == 512 else k // 128)
    elif size >= 8:
        if k > 0:
            moved = blocks([p[128 - k :] for p in pair], 1)
            pair = [jnp.concatenate([m, p[: 128 - k]], axis=0) for m, p in zip(moved, pair)]
        else:
            moved = blocks([p[:size] for p in pair], -1)
            pair = [jnp.concatenate([p[size:], m], axis=0) for m, p in zip(moved, pair)]
    else:
        rows = lax.broadcasted_iota(jnp.int32, (8, 128), 0)
        turned = [pltpu.roll(p, k % 128, 0) for p in pair]
        if k > 0:
            ends = [t[:8] for t in turned]
            ends = [jnp.where(rows < k, m, e) for m, e in zip(blocks(ends, 1), ends)]
            pair = [jnp.concatenate([e, t[8:]], axis=0) for e, t in zip(ends, turned)]
        else:
            ends = [t[120:] for t in turned]
            ends = [jnp.where(rows >= 8 + k, m, e) for m, e in zip(blocks(ends, -1), ends)]
            pair = [jnp.concatenate([t[:120], e], axis=0) for e, t in zip(ends, turned)]
    return jnp.concatenate(pair, axis=0)


def stand(x):
    tiles = [x[:, 128 * j : 128 * (j + 1)] for j in range(8)]
    return jnp.concatenate(
        [jnp.concatenate(tiles[4 * h : 4 * h + 4], axis=0).T for h in range(2)], axis=0
    )


def lie(x):
    tiles = [x[128 * h : 128 * (h + 1)].T for h in range(2)]
    return jnp.concatenate(
        [tiles[h][ALL * b : ALL * (b + 1)] for h in range(2) for b in range(4)], axis=1
    )


def turn_rows(x, k):
    return turn(x, k, 0)


def reduce_matrix(low, excess, rights, steps, move, keep):
    for index, k in enumerate(steps):
        high = move(low, -k)
        inverse = 1.0 / (low + high + excess)
        up = high * inverse
        down = low * inverse
        keep(index, up, down)
        excess = excess + move(up * excess, k) + move(down * excess, -k)
        rights = [r + move(up * r, k) + move(down * r, -k) for r in rights]
        low = move(up * low, k)
    inverse = 1.0 / excess
    return inverse, [r * inverse for r in rights]


def reduce_right(right, steps, move, load):
    for index, k in enumerate(steps):
        up, down = load(index)
        right = right + move(up * right, k) + move(down * right, -k)
    return right


def dense(row):
    return jnp.concatenate([row[:, 128 * i : 128 * (i + 1)] for i in range(8)], axis=0)


def natural(tile, rows):
    return jnp.concatenate(
        [jnp.broadcast_to(tile[i : i + 1, :], (rows, 128)) for i in range(8)], axis=1
    )


def input_kernel(fields_arg, vertical_arg, kappa_arg, fields, vertical, kappa, rim, done):
    pairs = ((kappa_arg, kappa), (fields_arg, fields), (vertical_arg, vertical))
    copies = [pltpu.make_async_copy(a, b, done.at[n]) for n, (a, b) in enumerate(pairs)]
    for copy in copies:
        copy.start()
    copies[0].wait()
    for f in range(2):
        rim[f] = dense(kappa[f * ROWS + ROWS - 1 : f * ROWS + ROWS, :])
    copies[1].wait()
    copies[2].wait()


def factor_x_kernel(kappa, ax, bx, qx, h1, h2, parts):
    half = 512
    rows = lax.broadcasted_iota(jnp.int32, (ROWS, half), 0)
    for f in range(2):
        mine = pl.ds(f * ROWS, ROWS)
        for c in range(COLS // half):
            cols = pl.ds(c * half, half)
            k = kappa[mine, cols]
            face = (k + turn(k, 1, 0)) * 0.5
            low = jnp.where((rows >= 2) & (rows <= 14), face, 0.0)
            first = jnp.where(rows == 1, face, 0.0)
            last = jnp.where(rows == 14, turn(face, -1, 0), 0.0)

            def keep(index, a, b, mine=mine, cols=cols):
                ax[index, mine, cols] = a
                bx[index, mine, cols] = b

            inverse, (one, two) = reduce_matrix(
                low, 1.0 + first + last, [first, last], X_STEPS, turn_rows, keep
            )
            qx[mine, cols] = jnp.where((rows >= 1) & (rows <= 14), inverse, 0.0)
            one = jnp.where(rows == 0, 1.0, one)
            two = jnp.where(rows == ROWS - 1, 1.0, two)
            h1[mine, cols] = one
            h2[mine, cols] = two
            sums = (
                jnp.sum(first * two, axis=0, keepdims=True),
                jnp.sum(one, axis=0, keepdims=True),
                jnp.sum(two, axis=0, keepdims=True),
                k[:1],
                k[ROWS - 1 :],
            )
            for n, row in enumerate(sums):
                for i in range(half // 128):
                    parts[n, f, pl.ds(c * (half // 128) + i, 1), :] = row[:, 128 * i : 128 * (i + 1)]


def factor_y_kernel(kappa, after, ay, by, qy, hy, edge):
    del after
    gy = lax.axis_index("gy")
    low_side = gy == 0
    end = jnp.where(low_side, COLS - 1, 0)
    start = COLS - 1 - end
    beside = jnp.where(low_side, COLS - 2, 1)
    cut = jnp.where(low_side, COLS - 1, 1)
    k = stand(kappa[...])
    row = lax.broadcasted_iota(jnp.int32, (256, 128), 0)
    lane = lax.broadcasted_iota(jnp.int32, (256, 128), 1)
    y = row // 128 * 512 + lane // 32 * 128 + row % 128
    face = (k + turn_lines(k, 1)) * 0.5
    low = jnp.where((y == 0) | (y == cut), 0.0, face)
    link = jnp.where(y == beside, jnp.where(low_side, turn_lines(face, -1), face), 0.0)
    ground = jnp.where(y == start, 1.0 + 0.5 * k, 1.0)

    def keep(index, up, down):
        ay[index] = up
        by[index] = down

    inverse, (profile,) = reduce_matrix(low, ground + link, [link], Y_STEPS, turn_lines, keep)
    qy[...] = jnp.where(y == end, 0.0, inverse)
    profile = lie(jnp.where(y == end, 1.0, profile))
    hy[...] = profile
    k = kappa[...]
    column = lax.broadcasted_iota(jnp.int32, (ALL, COLS), 1)
    total = jnp.sum(profile * jnp.where(column == start, 1.0 + 0.5 * k, 1.0), axis=1, keepdims=True)
    rim = jnp.sum(jnp.where(column == end, k, 0.0), axis=1, keepdims=True)
    lane = lax.broadcasted_iota(jnp.int32, (8, 128), 1)
    tile = jnp.zeros((8, 128), F32)
    for g in range(ALL // 8):
        part = slice(8 * g, 8 * g + 8)
        tile = jnp.where(lane == 4 * g, total[part], jnp.where(lane == 4 * g + 1, rim[part], tile))
    edge[...] = tile


def source_kernel(fields, fields_far, vertical, vertical_far, h1, h2, parts, prev, source, elements):
    gx = lax.axis_index("gx")
    here = fields[...]
    v = vertical[...]
    s = here + (v + vertical_far[...]) * 0.5 * (fields_far[...] - here) - v * 0.5 * here
    source[...] = s
    for f in range(2):
        mine = slice(f * ROWS, (f + 1) * ROWS)
        first = dense(jnp.sum(h1[mine, :] * s[mine, :], axis=0, keepdims=True))
        last = dense(jnp.sum(h2[mine, :] * s[mine, :], axis=0, keepdims=True))
        rim = parts[4, f]
        s_last = jnp.where(gx == 63, parts[2, f] + rim * 0.5, parts[2, f])
        rim = jnp.where(gx % 8 == 7, jnp.where(gx == 7, 0.0, prev[f]), rim)
        element = (parts[0, f], parts[1, f], s_last, first, last, parts[3, f], rim)
        for n, value in enumerate(element):
            elements[f, n] = value


def local_x_kernel(source, ax, bx, qx, out):
    half = 512
    for f in range(2):
        mine = pl.ds(f * ROWS, ROWS)
        for c in range(COLS // half):
            cols = pl.ds(c * half, half)
            r = source[mine, cols]
            r = reduce_right(r, X_STEPS, turn_rows, lambda i: (ax[i, mine, cols], bx[i, mine, cols]))
            out[mine, cols] = r * qx[mine, cols]


def merge(one, two):
    g, sl, sr, rl, rr = one
    g2, sl2, sr2, rl2, rr2 = two
    s = sr + sl2
    r = rr + rl2
    inverse = 1.0 / (g + g2 + s)
    a = g * inverse
    b = g2 * inverse
    return (a * g2, sl + a * s, sr2 + b * s, rl + a * r, rr2 + b * r), (a, b, r * inverse)


def behind(face, two):
    g, s, sr, r, rr = two
    inverse = 1.0 / (face + g + s)
    a = face * inverse
    b = g * inverse
    return (a * g, a * s, sr + b * s, a * r, rr + b * r), (a, b, r * inverse)


def load(ref, *field):
    return tuple(ref[(*field, n)] for n in range(7))


def within(node, left, right):
    a, b, c = node
    return (a * left[0] + b * right[0], a * left[1] + b * right[1], a * left[2] + b * right[2] + c)


def chip_kernel(mine, other, chips, chip, middle):
    even = lax.axis_index("gx") % 2 == 0
    fields = []
    for f in range(2):
        a, b = load(mine, f), load(other, f)
        first = [jnp.where(even, m, o) for m, o in zip(a, b)]
        second = [jnp.where(even, o, m) for m, o in zip(a, b)]
        tail, start = behind((first[6] + second[5]) * 0.5, second[:5])
        element, end = merge(first[:5], tail)
        fields.append(((*element, first[5], second[6]), (*end, *start)))
        for n, value in enumerate(fields[f][0]):
            chips[f, n] = value
    for out, (one, two) in zip((chip, middle), zip(*fields)):
        for n, (a, b) in enumerate(zip(one, two)):
            out[n] = jnp.where(even, a, b)


def pick_kernel(chips, after, keep, send):
    del after
    even = lax.axis_index("gx") % 2 == 0
    for n, (one, two) in enumerate(zip(load(chips, 0), load(chips, 1))):
        keep[n] = jnp.where(even, one, two)
        send[n] = jnp.where(even, two, one)


def slab_kernel(chip, far1, keep, got, middle, message, nodes):
    y = lax.axis_index("gx") // 2 % 4
    even = lax.axis_index("gx") % 2 == 0
    far2 = [jnp.where(even, g, k) for k, g in zip(load(keep), load(got))]
    far3 = [jnp.where(even, k, g) for k, g in zip(load(keep), load(got))]
    arrived = [load(chip), load(far1), far2, far3]
    chips = []
    for m in range(4):
        chosen = arrived[0]
        for flip in range(1, 4):
            here = y ^ flip == m
            chosen = [jnp.where(here, a, c) for a, c in zip(arrived[flip], chosen)]
        chips.append(chosen)
    element, inner, fronts = None, [], []
    for m in range(4):
        face = (chips[m - 1][6] + chips[m][5]) * 0.5
        tail, front = behind(face, chips[m][:5])
        fronts.append(front)
        if m == 0:
            element = tail
        else:
            element, node = merge(element, tail)
            inner.append(node)
    for n, value in enumerate(element):
        for j in range(8):
            message[j, n] = value
    zero, one = jnp.zeros((8, 128), F32), jnp.ones((8, 128), F32)
    left = (one, zero, zero)
    lasts = [(zero, one, zero)]
    for node in inner[::-1]:
        lasts.append(within(node, left, lasts[-1]))
    lasts = [left] + lasts[::-1]
    firsts = [within(fronts[m], lasts[m], lasts[m + 1]) for m in range(4)]
    lasts = lasts[1:]
    first, last = firsts[0], lasts[0]
    for m in range(1, 4):
        first = [jnp.where(y == m, new, old) for new, old in zip(firsts[m], first)]
        last = [jnp.where(y == m, new, old) for new, old in zip(lasts[m], last)]
    before = within(tuple(middle[n] for n in range(3)), first, last)
    second = within(tuple(middle[n] for n in range(3, 6)), before, last)
    for n, trio in enumerate((first, before, second, last)):
        for m in range(3):
            nodes[n, m] = trio[m]


def ends_kernel(got, nodes, mine, other):
    gx = lax.axis_index("gx")
    slab = gx // 8
    even = gx % 2 == 0
    zero = jnp.zeros((8, 128), F32)
    conduct = got[0, 0] + got[0, 2]
    right = got[0, 4]
    ratios, offsets = [], []
    for z in range(1, 8):
        g, sl, sr, rl, rr = (got[z, n] for n in range(5))
        conduct = conduct + sl
        right = right + rl
        inverse = 1.0 / (conduct + g)
        f = g * inverse
        ratios.append(f)
        offsets.append(right * inverse)
        conduct = sr + f * conduct
        right = rr + f * right
    value = right / conduct
    values = [value]
    for k in range(6, -1, -1):
        value = ratios[k] * value + offsets[k]
        values.append(value)
    values = [zero] + values[::-1]
    first, last = zero, zero
    for z in range(8):
        first = jnp.where(slab == z, values[z], first)
        last = jnp.where(slab == z, values[z + 1], last)
    row = [nodes[n, 0] * first + nodes[n, 1] * last + nodes[n, 2] for n in range(4)]
    for n in range(2):
        mine[n] = jnp.where(even, row[n], row[n + 2])
        other[n] = jnp.where(even, row[n + 2], row[n])


def section_kernel(mine, other, local, h1, h2, hy, edge, section, message):
    core = lax.axis_index("gx") % 2
    lane = lax.broadcasted_iota(jnp.int32, (8, 128), 1)
    tile = edge[...]
    for f in range(2):
        first = jnp.where(core == f, mine[0], other[0])
        last = jnp.where(core == f, mine[1], other[1])
        rows = slice(f * ROWS, (f + 1) * ROWS)
        s = local[rows, :] + h1[rows, :] * natural(first, ROWS) + h2[rows, :] * natural(last, ROWS)
        section[rows, :] = s
        total = jnp.sum(hy[rows, :] * s, axis=1, keepdims=True)
        for g in range(2):
            tile = jnp.where(lane == 4 * (2 * f + g) + 2, total[8 * g : 8 * g + 8], tile)
    message[...] = tile


def local_y_kernel(section, ay, by, qy, out):
    r = stand(section[...])
    r = reduce_right(r, Y_STEPS, turn_lines, lambda i: (ay[i], by[i]))
    out[...] = lie(r * qy[...])


def output_kernel(message, far, local, hy, out):
    for g in range(ALL // 8):
        part = slice(8 * g, 8 * g + 8)
        e, k, r = (message[:, 4 * g + n : 4 * g + n + 1] for n in range(3))
        e2, k2, r2 = (far[:, 4 * g + n : 4 * g + n + 1] for n in range(3))
        c = (k + k2) * 0.5
        value = ((e2 + c) * r + c * r2) / (e * e2 + c * (e + e2))
        out[part, :] = local[part, :] + hy[part, :] * value


def call(kernel, outs, specs, flops=0, size=0, scratch=()):
    return pl.pallas_call(
        kernel,
        out_shape=outs,
        in_specs=specs,
        out_specs=jax.tree.map(lambda _: VMEM, outs),
        scratch_shapes=scratch,
        compiler_params=PARAMS,
        cost_estimate=pl.CostEstimate(flops=flops, bytes_accessed=size, transcendentals=0),
    )


SLAB_GROUPS = [[8 * b + a for b in range(8)] for a in range(8)]
CORES = [(i, i ^ 1) for i in range(64)]


CHIPS = [(i, i ^ (4 if i % 2 else 6)) for i in range(64)]
NEXT = [(i, i ^ 2) for i in range(64)]


def local(fields, kappa, vertical):
    grid = (ALL, COLS)
    swap = [(0, 1), (1, 0)]
    fields_far = lax.ppermute(fields, "gz", swap)
    vertical_far = lax.ppermute(vertical, "gz", swap)
    full = shape(*grid)
    half = shape(7, 8, 128)
    standing = shape(256, 128)
    fields_here, vertical_here, kappa_here, rim = call(
        input_kernel,
        (full, full, full, shape(2, 8, 128)),
        [HBM] * 3,
        flops=1_000_000,
        size=1_000_000,
        scratch=[pltpu.SemaphoreType.DMA((3,))],
    )(*(pltpu.with_memory_space_constraint(x.reshape(grid), pltpu.HBM) for x in (fields, vertical, kappa)))
    prev = lax.ppermute(rim, "gx", [(i, (i + 8) % 64) for i in range(64)])
    ax, bx, qx, h1, h2, parts = call(
        factor_x_kernel,
        (shape(4, *grid), shape(4, *grid), full, full, full, shape(5, 2, 8, 128)),
        [VMEM],
        flops=4_000_000,
        size=2_000_000,
    )(kappa_here)
    both = shape(2, 7, 8, 128)
    source, elements = call(source_kernel, (full, both), [VMEM] * 8)(
        fields_here, fields_far.reshape(grid), vertical_here, vertical_far.reshape(grid),
        h1, h2, parts, prev,
    )
    got = lax.ppermute(elements, "gx", CORES)
    local_x = call(local_x_kernel, full, [VMEM] * 4, flops=1_000_000, size=1_000_000)(source, ax, bx, qx)
    chips, chip, middle = call(chip_kernel, (both, half, shape(6, 8, 128)), [VMEM] * 2)(elements, got)
    far = lax.ppermute(chips, "gx", CHIPS)
    far1 = lax.ppermute(chip, "gx", NEXT)
    ay, by, qy, hy, edge = call(
        factor_y_kernel,
        (shape(10, 256, 128), shape(10, 256, 128), standing, full, shape(8, 128)),
        [VMEM] * 2,
        flops=20_000_000,
        size=4_000_000,
    )(kappa_here, chip)
    keep, send = call(pick_kernel, (half, half), [VMEM] * 2)(far, edge)
    got = lax.ppermute(send, "gx", CORES)
    message, nodes = call(
        slab_kernel, (shape(8, 5, 8, 128), shape(4, 3, 8, 128)), [VMEM] * 5
    )(chip, far1, keep, got, middle)
    got = lax.all_to_all(message, "gx", 0, 0, axis_index_groups=SLAB_GROUPS, tiled=True)
    mine, other = call(
        ends_kernel, (shape(2, 8, 128), shape(2, 8, 128)), [VMEM, VMEM]
    )(got, nodes)
    other = lax.ppermute(other, "gx", CORES)
    section, message = call(
        section_kernel, (full, shape(8, 128)), [VMEM] * 7
    )(mine, other, local_x, h1, h2, hy, edge)
    far = lax.ppermute(message, "gy", swap)
    local_y = call(local_y_kernel, full, [VMEM] * 4, flops=4_000_000, size=3_000_000)(section, ay, by, qy)
    out = call(output_kernel, full, [VMEM] * 4)(message, far, local_y, hy)
    return out.reshape(fields.shape)


def solution(mesh):
    spec = P(None, "gz", "gx", "gy")
    return jax.shard_map(
        local, mesh=mesh, in_specs=(spec, spec, spec), out_specs=spec, check_vma=False
    )
```

```python
import functools

import jax
import jax.numpy as jnp
from jax import lax
from jax.experimental import pallas as pl
from jax.experimental.pallas import tpu as pltpu
from jax.sharding import PartitionSpec as P

F32 = jnp.float32
ROWS = 16
COLS = 1024
ALL = 2 * ROWS
VMEM = pl.BlockSpec(memory_space=pltpu.VMEM)
HBM = pl.BlockSpec(memory_space=pltpu.HBM)
X_STEPS = (1, 2, 4, 8)
Y_STEPS = (1, 2, 4, 8, 16, 32, 64, 128, 256, 512)
PARAMS = pltpu.CompilerParams(vmem_limit_bytes=40 * 1024 * 1024)


def shape(*dims):
    return jax.ShapeDtypeStruct(dims, F32)


def turn(x, k, axis):
    n = x.shape[axis]
    k = k % n
    unit = 128 if axis == 1 else 8
    if k == 0:
        return x
    if k % unit == 0:
        low = lax.slice_in_dim(x, n - k, n, axis=axis)
        high = lax.slice_in_dim(x, 0, n - k, axis=axis)
        return jnp.concatenate([low, high], axis=axis)
    return pltpu.roll(x, k, axis)


def turn_lines(x, k):
    lanes = lax.broadcasted_iota(jnp.int32, (1, 128), 1)

    def blocks(pair, n):
        if n == 4:
            return pair[::-1]
        turned = [pltpu.roll(p, 32 * n % 128, 1) for p in pair]
        over = lanes < 32 * n if n > 0 else lanes >= 128 + 32 * n
        return [jnp.where(over, turned[1 - h], turned[h]) for h in range(2)]

    pair = [x[:128], x[128:]]
    size = abs(k)
    if size >= 128:
        pair = blocks(pair, 4 if size == 512 else k // 128)
    elif size >= 8:
        if k > 0:
            moved = blocks([p[128 - k :] for p in pair], 1)
            pair = [jnp.concatenate([m, p[: 128 - k]], axis=0) for m, p in zip(moved, pair)]
        else:
            moved = blocks([p[:size] for p in pair], -1)
            pair = [jnp.concatenate([p[size:], m], axis=0) for m, p in zip(moved, pair)]
    else:
        rows = lax.broadcasted_iota(jnp.int32, (8, 128), 0)
        turned = [pltpu.roll(p, k % 128, 0) for p in pair]
        if k > 0:
            ends = [t[:8] for t in turned]
            ends = [jnp.where(rows < k, m, e) for m, e in zip(blocks(ends, 1), ends)]
            pair = [jnp.concatenate([e, t[8:]], axis=0) for e, t in zip(ends, turned)]
        else:
            ends = [t[120:] for t in turned]
            ends = [jnp.where(rows >= 8 + k, m, e) for m, e in zip(blocks(ends, -1), ends)]
            pair = [jnp.concatenate([t[:120], e], axis=0) for e, t in zip(ends, turned)]
    return jnp.concatenate(pair, axis=0)


def stand(x):
    tiles = [x[:, 128 * j : 128 * (j + 1)] for j in range(8)]
    return jnp.concatenate(
        [jnp.concatenate(tiles[4 * h : 4 * h + 4], axis=0).T for h in range(2)], axis=0
    )


def lie(x):
    tiles = [x[128 * h : 128 * (h + 1)].T for h in range(2)]
    return jnp.concatenate(
        [tiles[h][ALL * b : ALL * (b + 1)] for h in range(2) for b in range(4)], axis=1
    )


def turn_rows(x, k):
    return turn(x, k, 0)


def reduce_matrix(low, excess, rights, steps, move, keep):
    for index, k in enumerate(steps):
        high = move(low, -k)
        inverse = 1.0 / (low + high + excess)
        up = high * inverse
        down = low * inverse
        keep(index, up, down)
        excess = excess + move(up * excess, k) + move(down * excess, -k)
        rights = [r + move(up * r, k) + move(down * r, -k) for r in rights]
        low = move(up * low, k)
    inverse = 1.0 / excess
    return inverse, [r * inverse for r in rights]


def reduce_right(right, steps, move, load):
    for index, k in enumerate(steps):
        up, down = load(index)
        right = right + move(up * right, k) + move(down * right, -k)
    return right


def dense(row):
    return jnp.concatenate([row[:, 128 * i : 128 * (i + 1)] for i in range(8)], axis=0)


def natural(tile, rows):
    return jnp.concatenate(
        [jnp.broadcast_to(tile[i : i + 1, :], (rows, 128)) for i in range(8)], axis=1
    )


def input_kernel(fields_arg, vertical_arg, kappa_arg, fields, vertical, kappa, rim, done):
    pairs = ((kappa_arg, kappa), (fields_arg, fields), (vertical_arg, vertical))
    copies = [pltpu.make_async_copy(a, b, done.at[n]) for n, (a, b) in enumerate(pairs)]
    for copy in copies:
        copy.start()
    copies[0].wait()
    for f in range(2):
        rim[f] = dense(kappa[f * ROWS + ROWS - 1 : f * ROWS + ROWS, :])
    copies[1].wait()
    copies[2].wait()


def factor_x_kernel(kappa, ax, bx, qx, h1, h2, parts):
    half = 512
    rows = lax.broadcasted_iota(jnp.int32, (ROWS, half), 0)
    for f in range(2):
        mine = pl.ds(f * ROWS, ROWS)
        for c in range(COLS // half):
            cols = pl.ds(c * half, half)
            k = kappa[mine, cols]
            face = (k + turn(k, 1, 0)) * 0.5
            low = jnp.where((rows >= 2) & (rows <= 14), face, 0.0)
            first = jnp.where(rows == 1, face, 0.0)
            last = jnp.where(rows == 14, turn(face, -1, 0), 0.0)

            def keep(index, a, b, mine=mine, cols=cols):
                ax[index, mine, cols] = a
                bx[index, mine, cols] = b

            inverse, (one, two) = reduce_matrix(
                low, 1.0 + first + last, [first, last], X_STEPS, turn_rows, keep
            )
            qx[mine, cols] = jnp.where((rows >= 1) & (rows <= 14), inverse, 0.0)
            one = jnp.where(rows == 0, 1.0, one)
            two = jnp.where(rows == ROWS - 1, 1.0, two)
            h1[mine, cols] = one
            h2[mine, cols] = two
            sums = (
                jnp.sum(first * two, axis=0, keepdims=True),
                jnp.sum(one, axis=0, keepdims=True),
                jnp.sum(two, axis=0, keepdims=True),
                k[:1],
                k[ROWS - 1 :],
            )
            for n, row in enumerate(sums):
                for i in range(half // 128):
                    parts[n, f, pl.ds(c * (half // 128) + i, 1), :] = row[:, 128 * i : 128 * (i + 1)]


def factor_y(kappa, ay, by, qy, hy, edge):
    gy = lax.axis_index("gy")
    low_side = gy == 0
    end = jnp.where(low_side, COLS - 1, 0)
    start = COLS - 1 - end
    beside = jnp.where(low_side, COLS - 2, 1)
    cut = jnp.where(low_side, COLS - 1, 1)
    k = stand(kappa[...])
    row = lax.broadcasted_iota(jnp.int32, (256, 128), 0)
    lane = lax.broadcasted_iota(jnp.int32, (256, 128), 1)
    y = row // 128 * 512 + lane // 32 * 128 + row % 128
    face = (k + turn_lines(k, 1)) * 0.5
    low = jnp.where((y == 0) | (y == cut), 0.0, face)
    link = jnp.where(y == beside, jnp.where(low_side, turn_lines(face, -1), face), 0.0)
    ground = jnp.where(y == start, 1.0 + 0.5 * k, 1.0)

    def keep(index, up, down):
        ay[index] = up
        by[index] = down

    inverse, (profile,) = reduce_matrix(low, ground + link, [link], Y_STEPS, turn_lines, keep)
    qy[...] = jnp.where(y == end, 0.0, inverse)
    profile = lie(jnp.where(y == end, 1.0, profile))
    hy[...] = profile
    k = kappa[...]
    column = lax.broadcasted_iota(jnp.int32, (ALL, COLS), 1)
    total = jnp.sum(profile * jnp.where(column == start, 1.0 + 0.5 * k, 1.0), axis=1, keepdims=True)
    rim = jnp.sum(jnp.where(column == end, k, 0.0), axis=1, keepdims=True)
    lane = lax.broadcasted_iota(jnp.int32, (8, 128), 1)
    tile = jnp.zeros((8, 128), F32)
    for g in range(ALL // 8):
        part = slice(8 * g, 8 * g + 8)
        tile = jnp.where(lane == 4 * g, total[part], jnp.where(lane == 4 * g + 1, rim[part], tile))
    edge[...] = tile


def factor_y_kernel(kappa, after, *outs):
    del after

    @pl.when(lax.axis_index("gx") % 2 == 0)
    def _():
        factor_y(kappa, *outs)


def factor_y_late_kernel(kappa, after, after_too, *refs):
    del after, after_too

    @pl.when(lax.axis_index("gx") % 2 == 1)
    def _():
        factor_y(kappa, *refs[5:])


def source_kernel(fields, fields_far, vertical, vertical_far, h1, h2, parts, prev, source, elements):
    gx = lax.axis_index("gx")
    here = fields[...]
    v = vertical[...]
    s = here + (v + vertical_far[...]) * 0.5 * (fields_far[...] - here) - v * 0.5 * here
    source[...] = s
    for f in range(2):
        mine = slice(f * ROWS, (f + 1) * ROWS)
        first = dense(jnp.sum(h1[mine, :] * s[mine, :], axis=0, keepdims=True))
        last = dense(jnp.sum(h2[mine, :] * s[mine, :], axis=0, keepdims=True))
        rim = parts[4, f]
        s_last = jnp.where(gx == 63, parts[2, f] + rim * 0.5, parts[2, f])
        rim = jnp.where(gx % 8 == 7, jnp.where(gx == 7, 0.0, prev[f]), rim)
        element = (parts[0, f], parts[1, f], s_last, first, last, parts[3, f], rim)
        for n, value in enumerate(element):
            elements[f, n] = value


def local_x_kernel(source, ax, bx, qx, out):
    half = 512
    for f in range(2):
        mine = pl.ds(f * ROWS, ROWS)
        for c in range(COLS // half):
            cols = pl.ds(c * half, half)
            r = source[mine, cols]
            r = reduce_right(r, X_STEPS, turn_rows, lambda i: (ax[i, mine, cols], bx[i, mine, cols]))
            out[mine, cols] = r * qx[mine, cols]


def merge(one, two):
    g, sl, sr, rl, rr = one
    g2, sl2, sr2, rl2, rr2 = two
    s = sr + sl2
    r = rr + rl2
    inverse = 1.0 / (g + g2 + s)
    a = g * inverse
    b = g2 * inverse
    return (a * g2, sl + a * s, sr2 + b * s, rl + a * r, rr2 + b * r), (a, b, r * inverse)


def behind(face, two):
    g, s, sr, r, rr = two
    inverse = 1.0 / (face + g + s)
    a = face * inverse
    b = g * inverse
    return (a * g, a * s, sr + b * s, a * r, rr + b * r), (a, b, r * inverse)


def load(ref, *field):
    return tuple(ref[(*field, n)] for n in range(7))


def within(node, left, right):
    a, b, c = node
    return (a * left[0] + b * right[0], a * left[1] + b * right[1], a * left[2] + b * right[2] + c)


def chip_kernel(mine, other, chips, chip, middle):
    even = lax.axis_index("gx") % 2 == 0
    fields = []
    for f in range(2):
        a, b = load(mine, f), load(other, f)
        first = [jnp.where(even, m, o) for m, o in zip(a, b)]
        second = [jnp.where(even, o, m) for m, o in zip(a, b)]
        tail, start = behind((first[6] + second[5]) * 0.5, second[:5])
        element, end = merge(first[:5], tail)
        fields.append(((*element, first[5], second[6]), (*end, *start)))
        for n, value in enumerate(fields[f][0]):
            chips[f, n] = value
    for out, (one, two) in zip((chip, middle), zip(*fields)):
        for n, (a, b) in enumerate(zip(one, two)):
            out[n] = jnp.where(even, a, b)


def pick_kernel(chips, after, keep, send):
    del after
    even = lax.axis_index("gx") % 2 == 0
    for n, (one, two) in enumerate(zip(load(chips, 0), load(chips, 1))):
        keep[n] = jnp.where(even, one, two)
        send[n] = jnp.where(even, two, one)


def slab_kernel(chip, far1, keep, got, middle, after, message, nodes):
    del after
    y = lax.axis_index("gx") // 2 % 4
    even = lax.axis_index("gx") % 2 == 0
    far2 = [jnp.where(even, g, k) for k, g in zip(load(keep), load(got))]
    far3 = [jnp.where(even, k, g) for k, g in zip(load(keep), load(got))]
    arrived = [load(chip), load(far1), far2, far3]
    chips = []
    for m in range(4):
        chosen = arrived[0]
        for flip in range(1, 4):
            here = y ^ flip == m
            chosen = [jnp.where(here, a, c) for a, c in zip(arrived[flip], chosen)]
        chips.append(chosen)
    element, inner, fronts = None, [], []
    for m in range(4):
        face = (chips[m - 1][6] + chips[m][5]) * 0.5
        tail, front = behind(face, chips[m][:5])
        fronts.append(front)
        if m == 0:
            element = tail
        else:
            element, node = merge(element, tail)
            inner.append(node)
    for n, value in enumerate(element):
        for j in range(8):
            message[j, n] = value
    zero, one = jnp.zeros((8, 128), F32), jnp.ones((8, 128), F32)
    left = (one, zero, zero)
    lasts = [(zero, one, zero)]
    for node in inner[::-1]:
        lasts.append(within(node, left, lasts[-1]))
    lasts = [left] + lasts[::-1]
    firsts = [within(fronts[m], lasts[m], lasts[m + 1]) for m in range(4)]
    lasts = lasts[1:]
    first, last = firsts[0], lasts[0]
    for m in range(1, 4):
        first = [jnp.where(y == m, new, old) for new, old in zip(firsts[m], first)]
        last = [jnp.where(y == m, new, old) for new, old in zip(lasts[m], last)]
    before = within(tuple(middle[n] for n in range(3)), first, last)
    second = within(tuple(middle[n] for n in range(3, 6)), before, last)
    for n, trio in enumerate((first, before, second, last)):
        for m in range(3):
            nodes[n, m] = trio[m]


def ends_kernel(got, nodes, mine, other):
    gx = lax.axis_index("gx")
    slab = gx // 8
    even = gx % 2 == 0
    zero = jnp.zeros((8, 128), F32)
    conduct = got[0, 0] + got[0, 2]
    right = got[0, 4]
    ratios, offsets = [], []
    for z in range(1, 8):
        g, sl, sr, rl, rr = (got[z, n] for n in range(5))
        conduct = conduct + sl
        right = right + rl
        inverse = 1.0 / (conduct + g)
        f = g * inverse
        ratios.append(f)
        offsets.append(right * inverse)
        conduct = sr + f * conduct
        right = rr + f * right
    value = right / conduct
    values = [value]
    for k in range(6, -1, -1):
        value = ratios[k] * value + offsets[k]
        values.append(value)
    values = [zero] + values[::-1]
    first, last = zero, zero
    for z in range(8):
        first = jnp.where(slab == z, values[z], first)
        last = jnp.where(slab == z, values[z + 1], last)
    row = [nodes[n, 0] * first + nodes[n, 1] * last + nodes[n, 2] for n in range(4)]
    for n in range(2):
        mine[n] = jnp.where(even, row[n], row[n + 2])
        other[n] = jnp.where(even, row[n + 2], row[n])


def section_kernel(mine, other, local, h1, h2, hy, edge, section, message):
    core = lax.axis_index("gx") % 2
    lane = lax.broadcasted_iota(jnp.int32, (8, 128), 1)
    tile = edge[...]
    for f in range(2):
        first = jnp.where(core == f, mine[0], other[0])
        last = jnp.where(core == f, mine[1], other[1])
        rows = slice(f * ROWS, (f + 1) * ROWS)
        s = local[rows, :] + h1[rows, :] * natural(first, ROWS) + h2[rows, :] * natural(last, ROWS)
        section[rows, :] = s
        total = jnp.sum(hy[rows, :] * s, axis=1, keepdims=True)
        for g in range(2):
            tile = jnp.where(lane == 4 * (2 * f + g) + 2, total[8 * g : 8 * g + 8], tile)
    message[...] = tile


def local_y_kernel(section, ay, by, qy, out):
    r = stand(section[...])
    r = reduce_right(r, Y_STEPS, turn_lines, lambda i: (ay[i], by[i]))
    out[...] = lie(r * qy[...])


def output_kernel(message, far, local, hy, out):
    for g in range(ALL // 8):
        part = slice(8 * g, 8 * g + 8)
        e, k, r = (message[:, 4 * g + n : 4 * g + n + 1] for n in range(3))
        e2, k2, r2 = (far[:, 4 * g + n : 4 * g + n + 1] for n in range(3))
        c = (k + k2) * 0.5
        value = ((e2 + c) * r + c * r2) / (e * e2 + c * (e + e2))
        out[part, :] = local[part, :] + hy[part, :] * value


def call(kernel, outs, specs, flops=0, size=0, scratch=()):
    return pl.pallas_call(
        kernel,
        out_shape=outs,
        in_specs=specs,
        out_specs=jax.tree.map(lambda _: VMEM, outs),
        scratch_shapes=scratch,
        compiler_params=PARAMS,
        cost_estimate=pl.CostEstimate(flops=flops, bytes_accessed=size, transcendentals=0),
    )


SLAB_GROUPS = [[8 * b + a for b in range(8)] for a in range(8)]
CORES = [(i, i ^ 1) for i in range(64)]


CHIPS = [(i, i ^ (4 if i % 2 else 6)) for i in range(64)]
NEXT = [(i, i ^ 2) for i in range(64)]


def local(fields, kappa, vertical):
    grid = (ALL, COLS)
    swap = [(0, 1), (1, 0)]
    fields_far = lax.ppermute(fields, "gz", swap)
    vertical_far = lax.ppermute(vertical, "gz", swap)
    full = shape(*grid)
    half = shape(7, 8, 128)
    standing = shape(256, 128)
    fields_here, vertical_here, kappa_here, rim = call(
        input_kernel,
        (full, full, full, shape(2, 8, 128)),
        [HBM] * 3,
        flops=1_000_000,
        size=1_000_000,
        scratch=[pltpu.SemaphoreType.DMA((3,))],
    )(*(pltpu.with_memory_space_constraint(x.reshape(grid), pltpu.HBM) for x in (fields, vertical, kappa)))
    prev = lax.ppermute(rim, "gx", [(i, (i + 8) % 64) for i in range(64)])
    ax, bx, qx, h1, h2, parts = call(
        factor_x_kernel,
        (shape(4, *grid), shape(4, *grid), full, full, full, shape(5, 2, 8, 128)),
        [VMEM],
        flops=4_000_000,
        size=2_000_000,
    )(kappa_here)
    both = shape(2, 7, 8, 128)
    source, elements = call(source_kernel, (full, both), [VMEM] * 8)(
        fields_here, fields_far.reshape(grid), vertical_here, vertical_far.reshape(grid),
        h1, h2, parts, prev,
    )
    got = lax.ppermute(elements, "gx", CORES)
    local_x = call(local_x_kernel, full, [VMEM] * 4, flops=1_000_000, size=1_000_000)(source, ax, bx, qx)
    chips, chip, middle = call(chip_kernel, (both, half, shape(6, 8, 128)), [VMEM] * 2)(elements, got)
    far = lax.ppermute(chips, "gx", CHIPS)
    far1 = lax.ppermute(chip, "gx", NEXT)
    lines = (shape(10, 256, 128), shape(10, 256, 128), standing, full, shape(8, 128))
    factors = call(factor_y_kernel, lines, [VMEM] * 2, flops=20_000_000, size=4_000_000)(kappa_here, chip)
    keep, send = call(pick_kernel, (half, half), [VMEM] * 2)(far, factors[4])
    got = lax.ppermute(send, "gx", CORES)
    ay, by, qy, hy, edge = pl.pallas_call(
        factor_y_late_kernel,
        out_shape=lines,
        in_specs=[VMEM] * 8,
        out_specs=(VMEM,) * 5,
        input_output_aliases={3 + n: n for n in range(5)},
        compiler_params=PARAMS,
        cost_estimate=pl.CostEstimate(flops=20_000_000, bytes_accessed=4_000_000, transcendentals=0),
    )(kappa_here, got, far1, *factors)
    message, nodes = call(
        slab_kernel, (shape(8, 5, 8, 128), shape(4, 3, 8, 128)), [VMEM] * 6
    )(chip, far1, keep, got, middle, edge)
    got = lax.all_to_all(message, "gx", 0, 0, axis_index_groups=SLAB_GROUPS, tiled=True)
    mine, other = call(
        ends_kernel, (shape(2, 8, 128), shape(2, 8, 128)), [VMEM, VMEM]
    )(got, nodes)
    other = lax.ppermute(other, "gx", CORES)
    section, message = call(
        section_kernel, (full, shape(8, 128)), [VMEM] * 7
    )(mine, other, local_x, h1, h2, hy, edge)
    far = lax.ppermute(message, "gy", swap)
    local_y = call(local_y_kernel, full, [VMEM] * 4, flops=4_000_000, size=3_000_000)(section, ay, by, qy)
    out = call(output_kernel, full, [VMEM] * 4)(message, far, local_y, hy)
    return out.reshape(fields.shape)


def solution(mesh):
    spec = P(None, "gz", "gx", "gy")
    return jax.shard_map(
        local, mesh=mesh, in_specs=(spec, spec, spec), out_specs=spec, check_vma=False
    )
```

```python
import functools

import jax
import jax.numpy as jnp
from jax import lax
from jax.experimental import pallas as pl
from jax.experimental.pallas import tpu as pltpu
from jax.sharding import PartitionSpec as P

F32 = jnp.float32
ROWS = 16
COLS = 1024
ALL = 2 * ROWS
VMEM = pl.BlockSpec(memory_space=pltpu.VMEM)
HBM = pl.BlockSpec(memory_space=pltpu.HBM)
X_STEPS = (1, 2, 4, 8)
Y_STEPS = (1, 2, 4, 8, 16, 32, 64, 128, 256, 512)
PARAMS = pltpu.CompilerParams(vmem_limit_bytes=40 * 1024 * 1024)


def shape(*dims):
    return jax.ShapeDtypeStruct(dims, F32)


def turn(x, k, axis):
    n = x.shape[axis]
    k = k % n
    unit = 128 if axis == 1 else 8
    if k == 0:
        return x
    if k % unit == 0:
        low = lax.slice_in_dim(x, n - k, n, axis=axis)
        high = lax.slice_in_dim(x, 0, n - k, axis=axis)
        return jnp.concatenate([low, high], axis=axis)
    return pltpu.roll(x, k, axis)


def turn_lines(x, k):
    lanes = lax.broadcasted_iota(jnp.int32, (1, 128), 1)

    def blocks(pair, n):
        if n == 4:
            return pair[::-1]
        turned = [pltpu.roll(p, 32 * n % 128, 1) for p in pair]
        over = lanes < 32 * n if n > 0 else lanes >= 128 + 32 * n
        return [jnp.where(over, turned[1 - h], turned[h]) for h in range(2)]

    pair = [x[:128], x[128:]]
    size = abs(k)
    if size >= 128:
        pair = blocks(pair, 4 if size == 512 else k // 128)
    elif size >= 8:
        if k > 0:
            moved = blocks([p[128 - k :] for p in pair], 1)
            pair = [jnp.concatenate([m, p[: 128 - k]], axis=0) for m, p in zip(moved, pair)]
        else:
            moved = blocks([p[:size] for p in pair], -1)
            pair = [jnp.concatenate([p[size:], m], axis=0) for m, p in zip(moved, pair)]
    else:
        rows = lax.broadcasted_iota(jnp.int32, (8, 128), 0)
        turned = [pltpu.roll(p, k % 128, 0) for p in pair]
        if k > 0:
            ends = [t[:8] for t in turned]
            ends = [jnp.where(rows < k, m, e) for m, e in zip(blocks(ends, 1), ends)]
            pair = [jnp.concatenate([e, t[8:]], axis=0) for e, t in zip(ends, turned)]
        else:
            ends = [t[120:] for t in turned]
            ends = [jnp.where(rows >= 8 + k, m, e) for m, e in zip(blocks(ends, -1), ends)]
            pair = [jnp.concatenate([t[:120], e], axis=0) for e, t in zip(ends, turned)]
    return jnp.concatenate(pair, axis=0)


def stand(x):
    tiles = [x[:, 128 * j : 128 * (j + 1)] for j in range(8)]
    return jnp.concatenate(
        [jnp.concatenate(tiles[4 * h : 4 * h + 4], axis=0).T for h in range(2)], axis=0
    )


def lie(x):
    tiles = [x[128 * h : 128 * (h + 1)].T for h in range(2)]
    return jnp.concatenate(
        [tiles[h][ALL * b : ALL * (b + 1)] for h in range(2) for b in range(4)], axis=1
    )


def turn_rows(x, k):
    return turn(x, k, 0)


def reduce_matrix(low, excess, rights, steps, move, keep):
    for index, k in enumerate(steps):
        high = move(low, -k)
        inverse = 1.0 / (low + high + excess)
        up = high * inverse
        down = low * inverse
        keep(index, up, down)
        excess = excess + move(up * excess, k) + move(down * excess, -k)
        rights = [r + move(up * r, k) + move(down * r, -k) for r in rights]
        low = move(up * low, k)
    inverse = 1.0 / excess
    return inverse, [r * inverse for r in rights]


def reduce_right(right, steps, move, load):
    for index, k in enumerate(steps):
        up, down = load(index)
        right = right + move(up * right, k) + move(down * right, -k)
    return right


def dense(row):
    return jnp.concatenate([row[:, 128 * i : 128 * (i + 1)] for i in range(8)], axis=0)


def natural(tile, rows):
    return jnp.concatenate(
        [jnp.broadcast_to(tile[i : i + 1, :], (rows, 128)) for i in range(8)], axis=1
    )


def input_kernel(fields_arg, vertical_arg, kappa_arg, fields, vertical, kappa, rim, done):
    pairs = ((kappa_arg, kappa), (fields_arg, fields), (vertical_arg, vertical))
    copies = [pltpu.make_async_copy(a, b, done.at[n]) for n, (a, b) in enumerate(pairs)]
    for copy in copies:
        copy.start()
    copies[0].wait()
    for f in range(2):
        rim[f] = dense(kappa[f * ROWS + ROWS - 1 : f * ROWS + ROWS, :])
    copies[1].wait()
    copies[2].wait()


def factor_x_kernel(kappa, ax, bx, qx, h1, h2, parts):
    half = 512
    rows = lax.broadcasted_iota(jnp.int32, (ROWS, half), 0)
    for f in range(2):
        mine = pl.ds(f * ROWS, ROWS)
        for c in range(COLS // half):
            cols = pl.ds(c * half, half)
            k = kappa[mine, cols]
            face = (k + turn(k, 1, 0)) * 0.5
            low = jnp.where((rows >= 2) & (rows <= 14), face, 0.0)
            first = jnp.where(rows == 1, face, 0.0)
            last = jnp.where(rows == 14, turn(face, -1, 0), 0.0)

            def keep(index, a, b, mine=mine, cols=cols):
                ax[index, mine, cols] = a
                bx[index, mine, cols] = b

            inverse, (one, two) = reduce_matrix(
                low, 1.0 + first + last, [first, last], X_STEPS, turn_rows, keep
            )
            qx[mine, cols] = jnp.where((rows >= 1) & (rows <= 14), inverse, 0.0)
            one = jnp.where(rows == 0, 1.0, one)
            two = jnp.where(rows == ROWS - 1, 1.0, two)
            h1[mine, cols] = one
            h2[mine, cols] = two
            sums = (
                jnp.sum(first * two, axis=0, keepdims=True),
                jnp.sum(one, axis=0, keepdims=True),
                jnp.sum(two, axis=0, keepdims=True),
                k[:1],
                k[ROWS - 1 :],
            )
            for n, row in enumerate(sums):
                for i in range(half // 128):
                    parts[n, f, pl.ds(c * (half // 128) + i, 1), :] = row[:, 128 * i : 128 * (i + 1)]


def factor_y_kernel(kappa, after, ay, by, qy, hy, edge):
    del after
    gy = lax.axis_index("gy")
    low_side = gy == 0
    end = jnp.where(low_side, COLS - 1, 0)
    start = COLS - 1 - end
    beside = jnp.where(low_side, COLS - 2, 1)
    cut = jnp.where(low_side, COLS - 1, 1)
    k = stand(kappa[...])
    row = lax.broadcasted_iota(jnp.int32, (256, 128), 0)
    lane = lax.broadcasted_iota(jnp.int32, (256, 128), 1)
    y = row // 128 * 512 + lane // 32 * 128 + row % 128
    face = (k + turn_lines(k, 1)) * 0.5
    low = jnp.where((y == 0) | (y == cut), 0.0, face)
    link = jnp.where(y == beside, jnp.where(low_side, turn_lines(face, -1), face), 0.0)
    ground = jnp.where(y == start, 1.0 + 0.5 * k, 1.0)

    def keep(index, up, down):
        ay[index] = up
        by[index] = down

    inverse, (profile,) = reduce_matrix(low, ground + link, [link], Y_STEPS, turn_lines, keep)
    qy[...] = jnp.where(y == end, 0.0, inverse)
    profile = lie(jnp.where(y == end, 1.0, profile))
    hy[...] = profile
    k = kappa[...]
    column = lax.broadcasted_iota(jnp.int32, (ALL, COLS), 1)
    total = jnp.sum(profile * jnp.where(column == start, 1.0 + 0.5 * k, 1.0), axis=1, keepdims=True)
    rim = jnp.sum(jnp.where(column == end, k, 0.0), axis=1, keepdims=True)
    lane = lax.broadcasted_iota(jnp.int32, (8, 128), 1)
    tile = jnp.zeros((8, 128), F32)
    for g in range(ALL // 8):
        part = slice(8 * g, 8 * g + 8)
        tile = jnp.where(lane == 4 * g, total[part], jnp.where(lane == 4 * g + 1, rim[part], tile))
    edge[...] = tile


def source_kernel(fields, fields_far, vertical, vertical_far, h1, h2, parts, prev, source, elements):
    gx = lax.axis_index("gx")
    here = fields[...]
    v = vertical[...]
    s = here + (v + vertical_far[...]) * 0.5 * (fields_far[...] - here) - v * 0.5 * here
    source[...] = s
    for f in range(2):
        mine = slice(f * ROWS, (f + 1) * ROWS)
        first = dense(jnp.sum(h1[mine, :] * s[mine, :], axis=0, keepdims=True))
        last = dense(jnp.sum(h2[mine, :] * s[mine, :], axis=0, keepdims=True))
        rim = parts[4, f]
        s_last = jnp.where(gx == 63, parts[2, f] + rim * 0.5, parts[2, f])
        rim = jnp.where(gx % 8 == 7, jnp.where(gx == 7, 0.0, prev[f]), rim)
        element = (parts[0, f], parts[1, f], s_last, first, last, parts[3, f], rim)
        for n, value in enumerate(element):
            elements[f, n] = value


def local_x_kernel(source, ax, bx, qx, out):
    half = 512
    for f in range(2):
        mine = pl.ds(f * ROWS, ROWS)
        for c in range(COLS // half):
            cols = pl.ds(c * half, half)
            r = source[mine, cols]
            r = reduce_right(r, X_STEPS, turn_rows, lambda i: (ax[i, mine, cols], bx[i, mine, cols]))
            out[mine, cols] = r * qx[mine, cols]


def merge(one, two):
    g, sl, sr, rl, rr = one
    g2, sl2, sr2, rl2, rr2 = two
    s = sr + sl2
    r = rr + rl2
    inverse = 1.0 / (g + g2 + s)
    a = g * inverse
    b = g2 * inverse
    return (a * g2, sl + a * s, sr2 + b * s, rl + a * r, rr2 + b * r), (a, b, r * inverse)


def behind(face, two):
    g, s, sr, r, rr = two
    inverse = 1.0 / (face + g + s)
    a = face * inverse
    b = g * inverse
    return (a * g, a * s, sr + b * s, a * r, rr + b * r), (a, b, r * inverse)


def load(ref, *field):
    return tuple(ref[(*field, n)] for n in range(7))


def within(node, left, right):
    a, b, c = node
    return (a * left[0] + b * right[0], a * left[1] + b * right[1], a * left[2] + b * right[2] + c)


def chip_kernel(mine, other, chips, chip, middle):
    even = lax.axis_index("gx") % 2 == 0
    fields = []
    for f in range(2):
        a, b = load(mine, f), load(other, f)
        first = [jnp.where(even, m, o) for m, o in zip(a, b)]
        second = [jnp.where(even, o, m) for m, o in zip(a, b)]
        tail, start = behind((first[6] + second[5]) * 0.5, second[:5])
        element, end = merge(first[:5], tail)
        fields.append(((*element, first[5], second[6]), (*end, *start)))
        for n, value in enumerate(fields[f][0]):
            chips[f, n] = value
    for out, (one, two) in zip((chip, middle), zip(*fields)):
        for n, (a, b) in enumerate(zip(one, two)):
            out[n] = jnp.where(even, a, b)


def pick_kernel(chips, after, keep, send):
    del after
    even = lax.axis_index("gx") % 2 == 0
    for n, (one, two) in enumerate(zip(load(chips, 0), load(chips, 1))):
        keep[n] = jnp.where(even, one, two)
        send[n] = jnp.where(even, two, one)


def slab_kernel(chip, far1, keep, got, middle, message, nodes):
    y = lax.axis_index("gx") // 2 % 4
    even = lax.axis_index("gx") % 2 == 0
    far2 = [jnp.where(even, k, g) for k, g in zip(load(keep), load(got))]
    far3 = [jnp.where(even, g, k) for k, g in zip(load(keep), load(got))]
    arrived = [load(chip), load(far1), far2, far3]
    chips = []
    for m in range(4):
        chosen = arrived[0]
        for flip in range(1, 4):
            here = y ^ flip == m
            chosen = [jnp.where(here, a, c) for a, c in zip(arrived[flip], chosen)]
        chips.append(chosen)
    element, inner, fronts = None, [], []
    for m in range(4):
        face = (chips[m - 1][6] + chips[m][5]) * 0.5
        tail, front = behind(face, chips[m][:5])
        fronts.append(front)
        if m == 0:
            element = tail
        else:
            element, node = merge(element, tail)
            inner.append(node)
    for n, value in enumerate(element):
        for j in range(8):
            message[j, n] = value
    zero, one = jnp.zeros((8, 128), F32), jnp.ones((8, 128), F32)
    left = (one, zero, zero)
    lasts = [(zero, one, zero)]
    for node in inner[::-1]:
        lasts.append(within(node, left, lasts[-1]))
    lasts = [left] + lasts[::-1]
    firsts = [within(fronts[m], lasts[m], lasts[m + 1]) for m in range(4)]
    lasts = lasts[1:]
    first, last = firsts[0], lasts[0]
    for m in range(1, 4):
        first = [jnp.where(y == m, new, old) for new, old in zip(firsts[m], first)]
        last = [jnp.where(y == m, new, old) for new, old in zip(lasts[m], last)]
    before = within(tuple(middle[n] for n in range(3)), first, last)
    second = within(tuple(middle[n] for n in range(3, 6)), before, last)
    for n, trio in enumerate((first, before, second, last)):
        for m in range(3):
            nodes[n, m] = trio[m]


def ends_kernel(got, nodes, mine, other):
    gx = lax.axis_index("gx")
    slab = gx // 8
    even = gx % 2 == 0
    zero = jnp.zeros((8, 128), F32)
    conduct = got[0, 0] + got[0, 2]
    right = got[0, 4]
    ratios, offsets = [], []
    for z in range(1, 8):
        g, sl, sr, rl, rr = (got[z, n] for n in range(5))
        conduct = conduct + sl
        right = right + rl
        inverse = 1.0 / (conduct + g)
        f = g * inverse
        ratios.append(f)
        offsets.append(right * inverse)
        conduct = sr + f * conduct
        right = rr + f * right
    value = right / conduct
    values = [value]
    for k in range(6, -1, -1):
        value = ratios[k] * value + offsets[k]
        values.append(value)
    values = [zero] + values[::-1]
    first, last = zero, zero
    for z in range(8):
        first = jnp.where(slab == z, values[z], first)
        last = jnp.where(slab == z, values[z + 1], last)
    row = [nodes[n, 0] * first + nodes[n, 1] * last + nodes[n, 2] for n in range(4)]
    for n in range(2):
        mine[n] = jnp.where(even, row[n], row[n + 2])
        other[n] = jnp.where(even, row[n + 2], row[n])


def section_kernel(mine, other, local, h1, h2, hy, edge, section, message):
    core = lax.axis_index("gx") % 2
    lane = lax.broadcasted_iota(jnp.int32, (8, 128), 1)
    tile = edge[...]
    for f in range(2):
        first = jnp.where(core == f, mine[0], other[0])
        last = jnp.where(core == f, mine[1], other[1])
        rows = slice(f * ROWS, (f + 1) * ROWS)
        s = local[rows, :] + h1[rows, :] * natural(first, ROWS) + h2[rows, :] * natural(last, ROWS)
        section[rows, :] = s
        total = jnp.sum(hy[rows, :] * s, axis=1, keepdims=True)
        for g in range(2):
            tile = jnp.where(lane == 4 * (2 * f + g) + 2, total[8 * g : 8 * g + 8], tile)
    message[...] = tile


def local_y_kernel(section, ay, by, qy, out):
    r = stand(section[...])
    r = reduce_right(r, Y_STEPS, turn_lines, lambda i: (ay[i], by[i]))
    out[...] = lie(r * qy[...])


def output_kernel(message, far, local, hy, out):
    for g in range(ALL // 8):
        part = slice(8 * g, 8 * g + 8)
        e, k, r = (message[:, 4 * g + n : 4 * g + n + 1] for n in range(3))
        e2, k2, r2 = (far[:, 4 * g + n : 4 * g + n + 1] for n in range(3))
        c = (k + k2) * 0.5
        value = ((e2 + c) * r + c * r2) / (e * e2 + c * (e + e2))
        out[part, :] = local[part, :] + hy[part, :] * value


def call(kernel, outs, specs, flops=0, size=0, scratch=()):
    return pl.pallas_call(
        kernel,
        out_shape=outs,
        in_specs=specs,
        out_specs=jax.tree.map(lambda _: VMEM, outs),
        scratch_shapes=scratch,
        compiler_params=PARAMS,
        cost_estimate=pl.CostEstimate(flops=flops, bytes_accessed=size, transcendentals=0),
    )


SLAB_GROUPS = [[8 * b + a for b in range(8)] for a in range(8)]
CORES = [(i, i ^ 1) for i in range(64)]


CHIPS = [(i, i ^ (5 if i % 2 else 7)) for i in range(64)]
NEXT = [(i, i ^ 2) for i in range(64)]


def local(fields, kappa, vertical):
    grid = (ALL, COLS)
    swap = [(0, 1), (1, 0)]
    fields_far = lax.ppermute(fields, "gz", swap)
    vertical_far = lax.ppermute(vertical, "gz", swap)
    full = shape(*grid)
    half = shape(7, 8, 128)
    standing = shape(256, 128)
    fields_here, vertical_here, kappa_here, rim = call(
        input_kernel,
        (full, full, full, shape(2, 8, 128)),
        [HBM] * 3,
        flops=1_000_000,
        size=1_000_000,
        scratch=[pltpu.SemaphoreType.DMA((3,))],
    )(*(pltpu.with_memory_space_constraint(x.reshape(grid), pltpu.HBM) for x in (fields, vertical, kappa)))
    prev = lax.ppermute(rim, "gx", [(i, (i + 8) % 64) for i in range(64)])
    ax, bx, qx, h1, h2, parts = call(
        factor_x_kernel,
        (shape(4, *grid), shape(4, *grid), full, full, full, shape(5, 2, 8, 128)),
        [VMEM],
        flops=4_000_000,
        size=2_000_000,
    )(kappa_here)
    both = shape(2, 7, 8, 128)
    source, elements = call(source_kernel, (full, both), [VMEM] * 8)(
        fields_here, fields_far.reshape(grid), vertical_here, vertical_far.reshape(grid),
        h1, h2, parts, prev,
    )
    got = lax.ppermute(elements, "gx", CORES)
    local_x = call(local_x_kernel, full, [VMEM] * 4, flops=1_000_000, size=1_000_000)(source, ax, bx, qx)
    chips, chip, middle = call(chip_kernel, (both, half, shape(6, 8, 128)), [VMEM] * 2)(elements, got)
    far = lax.ppermute(chips, "gx", CHIPS)
    far1 = lax.ppermute(chip, "gx", NEXT)
    ay, by, qy, hy, edge = call(
        factor_y_kernel,
        (shape(10, 256, 128), shape(10, 256, 128), standing, full, shape(8, 128)),
        [VMEM] * 2,
        flops=20_000_000,
        size=4_000_000,
    )(kappa_here, chip)
    keep, send = call(pick_kernel, (half, half), [VMEM] * 2)(far, edge)
    got = lax.ppermute(send, "gx", CORES)
    message, nodes = call(
        slab_kernel, (shape(8, 5, 8, 128), shape(4, 3, 8, 128)), [VMEM] * 5
    )(chip, far1, keep, got, middle)
    got = lax.all_to_all(message, "gx", 0, 0, axis_index_groups=SLAB_GROUPS, tiled=True)
    mine, other = call(
        ends_kernel, (shape(2, 8, 128), shape(2, 8, 128)), [VMEM, VMEM]
    )(got, nodes)
    other = lax.ppermute(other, "gx", CORES)
    section, message = call(
        section_kernel, (full, shape(8, 128)), [VMEM] * 7
    )(mine, other, local_x, h1, h2, hy, edge)
    far = lax.ppermute(message, "gy", swap)
    local_y = call(local_y_kernel, full, [VMEM] * 4, flops=4_000_000, size=3_000_000)(section, ay, by, qy)
    out = call(output_kernel, full, [VMEM] * 4)(message, far, local_y, hy)
    return out.reshape(fields.shape)


def solution(mesh):
    spec = P(None, "gz", "gx", "gy")
    return jax.shard_map(
        local, mesh=mesh, in_specs=(spec, spec, spec), out_specs=spec, check_vma=False
    )
```

```python
import functools

import jax
import jax.numpy as jnp
from jax import lax
from jax.experimental import pallas as pl
from jax.experimental.pallas import tpu as pltpu
from jax.sharding import PartitionSpec as P

F32 = jnp.float32
ROWS = 16
COLS = 1024
ALL = 2 * ROWS
VMEM = pl.BlockSpec(memory_space=pltpu.VMEM)
HBM = pl.BlockSpec(memory_space=pltpu.HBM)
X_STEPS = (1, 2, 4, 8)
Y_STEPS = (1, 2, 4, 8, 16, 32, 64, 128, 256, 512)
PARAMS = pltpu.CompilerParams(vmem_limit_bytes=40 * 1024 * 1024)


def shape(*dims):
    return jax.ShapeDtypeStruct(dims, F32)


def turn(x, k, axis):
    n = x.shape[axis]
    k = k % n
    unit = 128 if axis == 1 else 8
    if k == 0:
        return x
    if k % unit == 0:
        low = lax.slice_in_dim(x, n - k, n, axis=axis)
        high = lax.slice_in_dim(x, 0, n - k, axis=axis)
        return jnp.concatenate([low, high], axis=axis)
    return pltpu.roll(x, k, axis)


def turn_lines(x, k):
    lanes = lax.broadcasted_iota(jnp.int32, (1, 128), 1)

    def blocks(pair, n):
        if n == 4:
            return pair[::-1]
        turned = [pltpu.roll(p, 32 * n % 128, 1) for p in pair]
        over = lanes < 32 * n if n > 0 else lanes >= 128 + 32 * n
        return [jnp.where(over, turned[1 - h], turned[h]) for h in range(2)]

    pair = [x[:128], x[128:]]
    size = abs(k)
    if size >= 128:
        pair = blocks(pair, 4 if size == 512 else k // 128)
    elif size >= 8:
        if k > 0:
            moved = blocks([p[128 - k :] for p in pair], 1)
            pair = [jnp.concatenate([m, p[: 128 - k]], axis=0) for m, p in zip(moved, pair)]
        else:
            moved = blocks([p[:size] for p in pair], -1)
            pair = [jnp.concatenate([p[size:], m], axis=0) for m, p in zip(moved, pair)]
    else:
        rows = lax.broadcasted_iota(jnp.int32, (8, 128), 0)
        turned = [pltpu.roll(p, k % 128, 0) for p in pair]
        if k > 0:
            ends = [t[:8] for t in turned]
            ends = [jnp.where(rows < k, m, e) for m, e in zip(blocks(ends, 1), ends)]
            pair = [jnp.concatenate([e, t[8:]], axis=0) for e, t in zip(ends, turned)]
        else:
            ends = [t[120:] for t in turned]
            ends = [jnp.where(rows >= 8 + k, m, e) for m, e in zip(blocks(ends, -1), ends)]
            pair = [jnp.concatenate([t[:120], e], axis=0) for e, t in zip(ends, turned)]
    return jnp.concatenate(pair, axis=0)


def stand(x):
    tiles = [x[:, 128 * j : 128 * (j + 1)] for j in range(8)]
    return jnp.concatenate(
        [jnp.concatenate(tiles[4 * h : 4 * h + 4], axis=0).T for h in range(2)], axis=0
    )


def lie(x):
    tiles = [x[128 * h : 128 * (h + 1)].T for h in range(2)]
    return jnp.concatenate(
        [tiles[h][ALL * b : ALL * (b + 1)] for h in range(2) for b in range(4)], axis=1
    )


def turn_rows(x, k):
    return turn(x, k, 0)


def reduce_matrix(low, excess, rights, steps, move, keep):
    for index, k in enumerate(steps):
        high = move(low, -k)
        inverse = 1.0 / (low + high + excess)
        up = high * inverse
        down = low * inverse
        keep(index, up, down)
        excess = excess + move(up * excess, k) + move(down * excess, -k)
        rights = [r + move(up * r, k) + move(down * r, -k) for r in rights]
        low = move(up * low, k)
    inverse = 1.0 / excess
    return inverse, [r * inverse for r in rights]


def reduce_right(right, steps, move, load):
    for index, k in enumerate(steps):
        up, down = load(index)
        right = right + move(up * right, k) + move(down * right, -k)
    return right


def dense(row):
    return jnp.concatenate([row[:, 128 * i : 128 * (i + 1)] for i in range(8)], axis=0)


def natural(tile, rows):
    return jnp.concatenate(
        [jnp.broadcast_to(tile[i : i + 1, :], (rows, 128)) for i in range(8)], axis=1
    )


def input_kernel(fields_arg, vertical_arg, kappa_arg, fields, vertical, kappa, rim, done):
    pairs = ((kappa_arg, kappa), (fields_arg, fields), (vertical_arg, vertical))
    copies = [pltpu.make_async_copy(a, b, done.at[n]) for n, (a, b) in enumerate(pairs)]
    for copy in copies:
        copy.start()
    copies[0].wait()
    for f in range(2):
        rim[f] = dense(kappa[f * ROWS + ROWS - 1 : f * ROWS + ROWS, :])
    copies[1].wait()
    copies[2].wait()


def factor_x_kernel(kappa, ax, bx, qx, h1, h2, parts):
    half = 512
    rows = lax.broadcasted_iota(jnp.int32, (ROWS, half), 0)
    for f in range(2):
        mine = pl.ds(f * ROWS, ROWS)
        for c in range(COLS // half):
            cols = pl.ds(c * half, half)
            k = kappa[mine, cols]
            face = (k + turn(k, 1, 0)) * 0.5
            low = jnp.where((rows >= 2) & (rows <= 14), face, 0.0)
            first = jnp.where(rows == 1, face, 0.0)
            last = jnp.where(rows == 14, turn(face, -1, 0), 0.0)

            def keep(index, a, b, mine=mine, cols=cols):
                ax[index, mine, cols] = a
                bx[index, mine, cols] = b

            inverse, (one, two) = reduce_matrix(
                low, 1.0 + first + last, [first, last], X_STEPS, turn_rows, keep
            )
            qx[mine, cols] = jnp.where((rows >= 1) & (rows <= 14), inverse, 0.0)
            one = jnp.where(rows == 0, 1.0, one)
            two = jnp.where(rows == ROWS - 1, 1.0, two)
            h1[mine, cols] = one
            h2[mine, cols] = two
            sums = (
                jnp.sum(first * two, axis=0, keepdims=True),
                jnp.sum(one, axis=0, keepdims=True),
                jnp.sum(two, axis=0, keepdims=True),
                k[:1],
                k[ROWS - 1 :],
            )
            for n, row in enumerate(sums):
                for i in range(half // 128):
                    parts[n, f, pl.ds(c * (half // 128) + i, 1), :] = row[:, 128 * i : 128 * (i + 1)]


def factor_y_kernel(kappa, ay, by, qy, hy, edge):
    gy = lax.axis_index("gy")
    low_side = gy == 0
    end = jnp.where(low_side, COLS - 1, 0)
    start = COLS - 1 - end
    beside = jnp.where(low_side, COLS - 2, 1)
    cut = jnp.where(low_side, COLS - 1, 1)
    k = stand(kappa[...])
    row = lax.broadcasted_iota(jnp.int32, (256, 128), 0)
    lane = lax.broadcasted_iota(jnp.int32, (256, 128), 1)
    y = row // 128 * 512 + lane // 32 * 128 + row % 128
    face = (k + turn_lines(k, 1)) * 0.5
    low = jnp.where((y == 0) | (y == cut), 0.0, face)
    link = jnp.where(y == beside, jnp.where(low_side, turn_lines(face, -1), face), 0.0)
    ground = jnp.where(y == start, 1.0 + 0.5 * k, 1.0)

    def keep(index, up, down):
        ay[index] = up
        by[index] = down

    inverse, (profile,) = reduce_matrix(low, ground + link, [link], Y_STEPS, turn_lines, keep)
    qy[...] = jnp.where(y == end, 0.0, inverse)
    profile = lie(jnp.where(y == end, 1.0, profile))
    hy[...] = profile
    k = kappa[...]
    column = lax.broadcasted_iota(jnp.int32, (ALL, COLS), 1)
    total = jnp.sum(profile * jnp.where(column == start, 1.0 + 0.5 * k, 1.0), axis=1, keepdims=True)
    rim = jnp.sum(jnp.where(column == end, k, 0.0), axis=1, keepdims=True)
    lane = lax.broadcasted_iota(jnp.int32, (8, 128), 1)
    tile = jnp.zeros((8, 128), F32)
    for g in range(ALL // 8):
        part = slice(8 * g, 8 * g + 8)
        tile = jnp.where(lane == 4 * g, total[part], jnp.where(lane == 4 * g + 1, rim[part], tile))
    edge[...] = tile


def source_kernel(fields, fields_far, vertical, vertical_far, h1, h2, parts, prev, after, source, elements):
    del after
    gx = lax.axis_index("gx")
    here = fields[...]
    v = vertical[...]
    s = here + (v + vertical_far[...]) * 0.5 * (fields_far[...] - here) - v * 0.5 * here
    source[...] = s
    for f in range(2):
        mine = slice(f * ROWS, (f + 1) * ROWS)
        first = dense(jnp.sum(h1[mine, :] * s[mine, :], axis=0, keepdims=True))
        last = dense(jnp.sum(h2[mine, :] * s[mine, :], axis=0, keepdims=True))
        rim = parts[4, f]
        s_last = jnp.where(gx == 63, parts[2, f] + rim * 0.5, parts[2, f])
        rim = jnp.where(gx % 8 == 7, jnp.where(gx == 7, 0.0, prev[f]), rim)
        element = (parts[0, f], parts[1, f], s_last, first, last, parts[3, f], rim)
        for n, value in enumerate(element):
            elements[f, n] = value


def local_x_kernel(source, ax, bx, qx, out):
    half = 512
    for f in range(2):
        mine = pl.ds(f * ROWS, ROWS)
        for c in range(COLS // half):
            cols = pl.ds(c * half, half)
            r = source[mine, cols]
            r = reduce_right(r, X_STEPS, turn_rows, lambda i: (ax[i, mine, cols], bx[i, mine, cols]))
            out[mine, cols] = r * qx[mine, cols]


def merge(one, two):
    g, sl, sr, rl, rr = one
    g2, sl2, sr2, rl2, rr2 = two
    s = sr + sl2
    r = rr + rl2
    inverse = 1.0 / (g + g2 + s)
    a = g * inverse
    b = g2 * inverse
    return (a * g2, sl + a * s, sr2 + b * s, rl + a * r, rr2 + b * r), (a, b, r * inverse)


def behind(face, two):
    g, s, sr, r, rr = two
    inverse = 1.0 / (face + g + s)
    a = face * inverse
    b = g * inverse
    return (a * g, a * s, sr + b * s, a * r, rr + b * r), (a, b, r * inverse)


def load(ref, *field):
    return tuple(ref[(*field, n)] for n in range(7))


def within(node, left, right):
    a, b, c = node
    return (a * left[0] + b * right[0], a * left[1] + b * right[1], a * left[2] + b * right[2] + c)


def chip_kernel(mine, other, chips, chip, middle):
    even = lax.axis_index("gx") % 2 == 0
    fields = []
    for f in range(2):
        a, b = load(mine, f), load(other, f)
        first = [jnp.where(even, m, o) for m, o in zip(a, b)]
        second = [jnp.where(even, o, m) for m, o in zip(a, b)]
        tail, start = behind((first[6] + second[5]) * 0.5, second[:5])
        element, end = merge(first[:5], tail)
        fields.append(((*element, first[5], second[6]), (*end, *start)))
        for n, value in enumerate(fields[f][0]):
            chips[f, n] = value
    for out, (one, two) in zip((chip, middle), zip(*fields)):
        for n, (a, b) in enumerate(zip(one, two)):
            out[n] = jnp.where(even, a, b)


def pick_kernel(chips, keep, send):
    even = lax.axis_index("gx") % 2 == 0
    for n, (one, two) in enumerate(zip(load(chips, 0), load(chips, 1))):
        keep[n] = jnp.where(even, one, two)
        send[n] = jnp.where(even, two, one)


def slab_kernel(chip, far1, keep, got, middle, message, nodes):
    y = lax.axis_index("gx") // 2 % 4
    even = lax.axis_index("gx") % 2 == 0
    far2 = [jnp.where(even, k, g) for k, g in zip(load(keep), load(got))]
    far3 = [jnp.where(even, g, k) for k, g in zip(load(keep), load(got))]
    arrived = [load(chip), load(far1), far2, far3]
    chips = []
    for m in range(4):
        chosen = arrived[0]
        for flip in range(1, 4):
            here = y ^ flip == m
            chosen = [jnp.where(here, a, c) for a, c in zip(arrived[flip], chosen)]
        chips.append(chosen)
    element, inner, fronts = None, [], []
    for m in range(4):
        face = (chips[m - 1][6] + chips[m][5]) * 0.5
        tail, front = behind(face, chips[m][:5])
        fronts.append(front)
        if m == 0:
            element = tail
        else:
            element, node = merge(element, tail)
            inner.append(node)
    for n, value in enumerate(element):
        for j in range(8):
            message[j, n] = value
    zero, one = jnp.zeros((8, 128), F32), jnp.ones((8, 128), F32)
    left = (one, zero, zero)
    lasts = [(zero, one, zero)]
    for node in inner[::-1]:
        lasts.append(within(node, left, lasts[-1]))
    lasts = [left] + lasts[::-1]
    firsts = [within(fronts[m], lasts[m], lasts[m + 1]) for m in range(4)]
    lasts = lasts[1:]
    first, last = firsts[0], lasts[0]
    for m in range(1, 4):
        first = [jnp.where(y == m, new, old) for new, old in zip(firsts[m], first)]
        last = [jnp.where(y == m, new, old) for new, old in zip(lasts[m], last)]
    before = within(tuple(middle[n] for n in range(3)), first, last)
    second = within(tuple(middle[n] for n in range(3, 6)), before, last)
    for n, trio in enumerate((first, before, second, last)):
        for m in range(3):
            nodes[n, m] = trio[m]


def ends_kernel(got, nodes, mine, other):
    gx = lax.axis_index("gx")
    slab = gx // 8
    even = gx % 2 == 0
    zero = jnp.zeros((8, 128), F32)
    conduct = got[0, 0] + got[0, 2]
    right = got[0, 4]
    ratios, offsets = [], []
    for z in range(1, 8):
        g, sl, sr, rl, rr = (got[z, n] for n in range(5))
        conduct = conduct + sl
        right = right + rl
        inverse = 1.0 / (conduct + g)
        f = g * inverse
        ratios.append(f)
        offsets.append(right * inverse)
        conduct = sr + f * conduct
        right = rr + f * right
    value = right / conduct
    values = [value]
    for k in range(6, -1, -1):
        value = ratios[k] * value + offsets[k]
        values.append(value)
    values = [zero] + values[::-1]
    first, last = zero, zero
    for z in range(8):
        first = jnp.where(slab == z, values[z], first)
        last = jnp.where(slab == z, values[z + 1], last)
    row = [nodes[n, 0] * first + nodes[n, 1] * last + nodes[n, 2] for n in range(4)]
    for n in range(2):
        mine[n] = jnp.where(even, row[n], row[n + 2])
        other[n] = jnp.where(even, row[n + 2], row[n])


def section_kernel(mine, other, local, h1, h2, hy, edge, section, message):
    core = lax.axis_index("gx") % 2
    lane = lax.broadcasted_iota(jnp.int32, (8, 128), 1)
    tile = edge[...]
    for f in range(2):
        first = jnp.where(core == f, mine[0], other[0])
        last = jnp.where(core == f, mine[1], other[1])
        rows = slice(f * ROWS, (f + 1) * ROWS)
        s = local[rows, :] + h1[rows, :] * natural(first, ROWS) + h2[rows, :] * natural(last, ROWS)
        section[rows, :] = s
        total = jnp.sum(hy[rows, :] * s, axis=1, keepdims=True)
        for g in range(2):
            tile = jnp.where(lane == 4 * (2 * f + g) + 2, total[8 * g : 8 * g + 8], tile)
    message[...] = tile


def local_y_kernel(section, ay, by, qy, out):
    r = stand(section[...])
    r = reduce_right(r, Y_STEPS, turn_lines, lambda i: (ay[i], by[i]))
    out[...] = lie(r * qy[...])


def output_kernel(message, far, local, hy, out):
    for g in range(ALL // 8):
        part = slice(8 * g, 8 * g + 8)
        e, k, r = (message[:, 4 * g + n : 4 * g + n + 1] for n in range(3))
        e2, k2, r2 = (far[:, 4 * g + n : 4 * g + n + 1] for n in range(3))
        c = (k + k2) * 0.5
        value = ((e2 + c) * r + c * r2) / (e * e2 + c * (e + e2))
        out[part, :] = local[part, :] + hy[part, :] * value


def call(kernel, outs, specs, flops=0, size=0, scratch=()):
    return pl.pallas_call(
        kernel,
        out_shape=outs,
        in_specs=specs,
        out_specs=jax.tree.map(lambda _: VMEM, outs),
        scratch_shapes=scratch,
        compiler_params=PARAMS,
        cost_estimate=pl.CostEstimate(flops=flops, bytes_accessed=size, transcendentals=0),
    )


SLAB_GROUPS = [[8 * b + a for b in range(8)] for a in range(8)]
CORES = [(i, i ^ 1) for i in range(64)]


CHIPS = [(i, i ^ (5 if i % 2 else 7)) for i in range(64)]
NEXT = [(i, i ^ 2) for i in range(64)]


def local(fields, kappa, vertical):
    grid = (ALL, COLS)
    swap = [(0, 1), (1, 0)]
    fields_far = lax.ppermute(fields, "gz", swap)
    vertical_far = lax.ppermute(vertical, "gz", swap)
    full = shape(*grid)
    half = shape(7, 8, 128)
    standing = shape(256, 128)
    fields_here, vertical_here, kappa_here, rim = call(
        input_kernel,
        (full, full, full, shape(2, 8, 128)),
        [HBM] * 3,
        flops=1_000_000,
        size=1_000_000,
        scratch=[pltpu.SemaphoreType.DMA((3,))],
    )(*(pltpu.with_memory_space_constraint(x.reshape(grid), pltpu.HBM) for x in (fields, vertical, kappa)))
    prev = lax.ppermute(rim, "gx", [(i, (i + 8) % 64) for i in range(64)])
    ax, bx, qx, h1, h2, parts = call(
        factor_x_kernel,
        (shape(4, *grid), shape(4, *grid), full, full, full, shape(5, 2, 8, 128)),
        [VMEM],
        flops=4_000_000,
        size=2_000_000,
    )(kappa_here)
    ay, by, qy, hy, edge = call(
        factor_y_kernel,
        (shape(10, 256, 128), shape(10, 256, 128), standing, full, shape(8, 128)),
        [VMEM],
        flops=20_000_000,
        size=4_000_000,
    )(kappa_here)
    both = shape(2, 7, 8, 128)
    source, elements = call(source_kernel, (full, both), [VMEM] * 9)(
        fields_here, fields_far.reshape(grid), vertical_here, vertical_far.reshape(grid),
        h1, h2, parts, prev, edge,
    )
    got = lax.ppermute(elements, "gx", CORES)
    local_x = call(local_x_kernel, full, [VMEM] * 4, flops=1_000_000, size=1_000_000)(source, ax, bx, qx)
    chips, chip, middle = call(chip_kernel, (both, half, shape(6, 8, 128)), [VMEM] * 2)(elements, got)
    far = lax.ppermute(chips, "gx", CHIPS)
    far1 = lax.ppermute(chip, "gx", NEXT)
    keep, send = call(pick_kernel, (half, half), [VMEM])(far)
    got = lax.ppermute(send, "gx", CORES)
    message, nodes = call(
        slab_kernel, (shape(8, 5, 8, 128), shape(4, 3, 8, 128)), [VMEM] * 5
    )(chip, far1, keep, got, middle)
    got = lax.all_to_all(message, "gx", 0, 0, axis_index_groups=SLAB_GROUPS, tiled=True)
    mine, other = call(
        ends_kernel, (shape(2, 8, 128), shape(2, 8, 128)), [VMEM, VMEM]
    )(got, nodes)
    other = lax.ppermute(other, "gx", CORES)
    section, message = call(
        section_kernel, (full, shape(8, 128)), [VMEM] * 7
    )(mine, other, local_x, h1, h2, hy, edge)
    far = lax.ppermute(message, "gy", swap)
    local_y = call(local_y_kernel, full, [VMEM] * 4, flops=4_000_000, size=3_000_000)(section, ay, by, qy)
    out = call(output_kernel, full, [VMEM] * 4)(message, far, local_y, hy)
    return out.reshape(fields.shape)


def solution(mesh):
    spec = P(None, "gz", "gx", "gy")
    return jax.shard_map(
        local, mesh=mesh, in_specs=(spec, spec, spec), out_specs=spec, check_vma=False
    )
```

```python
import functools

import jax
import jax.numpy as jnp
from jax import lax
from jax.experimental import pallas as pl
from jax.experimental.pallas import tpu as pltpu
from jax.sharding import PartitionSpec as P

F32 = jnp.float32
ROWS = 16
COLS = 1024
ALL = 2 * ROWS
VMEM = pl.BlockSpec(memory_space=pltpu.VMEM)
HBM = pl.BlockSpec(memory_space=pltpu.HBM)
X_STEPS = (1, 2, 4, 8)
Y_STEPS = (1, 2, 4, 8, 16, 32, 64, 128, 256, 512)
PARAMS = pltpu.CompilerParams(vmem_limit_bytes=40 * 1024 * 1024)


def shape(*dims):
    return jax.ShapeDtypeStruct(dims, F32)


def turn(x, k, axis):
    n = x.shape[axis]
    k = k % n
    unit = 128 if axis == 1 else 8
    if k == 0:
        return x
    if k % unit == 0:
        low = lax.slice_in_dim(x, n - k, n, axis=axis)
        high = lax.slice_in_dim(x, 0, n - k, axis=axis)
        return jnp.concatenate([low, high], axis=axis)
    return pltpu.roll(x, k, axis)


def turn_lines(x, k):
    lanes = lax.broadcasted_iota(jnp.int32, (1, 128), 1)

    def blocks(pair, n):
        if n == 4:
            return pair[::-1]
        turned = [pltpu.roll(p, 32 * n % 128, 1) for p in pair]
        over = lanes < 32 * n if n > 0 else lanes >= 128 + 32 * n
        return [jnp.where(over, turned[1 - h], turned[h]) for h in range(2)]

    pair = [x[:128], x[128:]]
    size = abs(k)
    if size >= 128:
        pair = blocks(pair, 4 if size == 512 else k // 128)
    elif size >= 8:
        if k > 0:
            moved = blocks([p[128 - k :] for p in pair], 1)
            pair = [jnp.concatenate([m, p[: 128 - k]], axis=0) for m, p in zip(moved, pair)]
        else:
            moved = blocks([p[:size] for p in pair], -1)
            pair = [jnp.concatenate([p[size:], m], axis=0) for m, p in zip(moved, pair)]
    else:
        rows = lax.broadcasted_iota(jnp.int32, (8, 128), 0)
        turned = [pltpu.roll(p, k % 128, 0) for p in pair]
        if k > 0:
            ends = [t[:8] for t in turned]
            ends = [jnp.where(rows < k, m, e) for m, e in zip(blocks(ends, 1), ends)]
            pair = [jnp.concatenate([e, t[8:]], axis=0) for e, t in zip(ends, turned)]
        else:
            ends = [t[120:] for t in turned]
            ends = [jnp.where(rows >= 8 + k, m, e) for m, e in zip(blocks(ends, -1), ends)]
            pair = [jnp.concatenate([t[:120], e], axis=0) for e, t in zip(ends, turned)]
    return jnp.concatenate(pair, axis=0)


def stand(x):
    tiles = [x[:, 128 * j : 128 * (j + 1)] for j in range(8)]
    return jnp.concatenate(
        [jnp.concatenate(tiles[4 * h : 4 * h + 4], axis=0).T for h in range(2)], axis=0
    )


def lie(x):
    tiles = [x[128 * h : 128 * (h + 1)].T for h in range(2)]
    return jnp.concatenate(
        [tiles[h][ALL * b : ALL * (b + 1)] for h in range(2) for b in range(4)], axis=1
    )


def turn_rows(x, k):
    return turn(x, k, 0)


def reduce_matrix(low, excess, rights, steps, move, keep):
    for index, k in enumerate(steps):
        high = move(low, -k)
        inverse = 1.0 / (low + high + excess)
        up = high * inverse
        down = low * inverse
        keep(index, up, down)
        excess = excess + move(up * excess, k) + move(down * excess, -k)
        rights = [r + move(up * r, k) + move(down * r, -k) for r in rights]
        low = move(up * low, k)
    inverse = 1.0 / excess
    return inverse, [r * inverse for r in rights]


def reduce_right(right, steps, move, load):
    for index, k in enumerate(steps):
        up, down = load(index)
        right = right + move(up * right, k) + move(down * right, -k)
    return right


def dense(row):
    return jnp.concatenate([row[:, 128 * i : 128 * (i + 1)] for i in range(8)], axis=0)


def natural(tile, rows):
    return jnp.concatenate(
        [jnp.broadcast_to(tile[i : i + 1, :], (rows, 128)) for i in range(8)], axis=1
    )


def input_kernel(fields_arg, vertical_arg, kappa_arg, fields, vertical, kappa, rim, done):
    pairs = ((kappa_arg, kappa), (fields_arg, fields), (vertical_arg, vertical))
    copies = [pltpu.make_async_copy(a, b, done.at[n]) for n, (a, b) in enumerate(pairs)]
    for copy in copies:
        copy.start()
    copies[0].wait()
    for f in range(2):
        rim[f] = dense(kappa[f * ROWS + ROWS - 1 : f * ROWS + ROWS, :])
    copies[1].wait()
    copies[2].wait()


def factor_x_kernel(kappa, ax, bx, qx, h1, h2, parts):
    half = 512
    rows = lax.broadcasted_iota(jnp.int32, (ROWS, half), 0)
    for f in range(2):
        mine = pl.ds(f * ROWS, ROWS)
        for c in range(COLS // half):
            cols = pl.ds(c * half, half)
            k = kappa[mine, cols]
            face = (k + turn(k, 1, 0)) * 0.5
            low = jnp.where((rows >= 2) & (rows <= 14), face, 0.0)
            first = jnp.where(rows == 1, face, 0.0)
            last = jnp.where(rows == 14, turn(face, -1, 0), 0.0)

            def keep(index, a, b, mine=mine, cols=cols):
                ax[index, mine, cols] = a
                bx[index, mine, cols] = b

            inverse, (one, two) = reduce_matrix(
                low, 1.0 + first + last, [first, last], X_STEPS, turn_rows, keep
            )
            qx[mine, cols] = jnp.where((rows >= 1) & (rows <= 14), inverse, 0.0)
            one = jnp.where(rows == 0, 1.0, one)
            two = jnp.where(rows == ROWS - 1, 1.0, two)
            h1[mine, cols] = one
            h2[mine, cols] = two
            sums = (
                jnp.sum(first * two, axis=0, keepdims=True),
                jnp.sum(one, axis=0, keepdims=True),
                jnp.sum(two, axis=0, keepdims=True),
                k[:1],
                k[ROWS - 1 :],
            )
            for n, row in enumerate(sums):
                for i in range(half // 128):
                    parts[n, f, pl.ds(c * (half // 128) + i, 1), :] = row[:, 128 * i : 128 * (i + 1)]


def factor_y_kernel(kappa, ay, by, qy, hy, edge):
    gy = lax.axis_index("gy")
    low_side = gy == 0
    end = jnp.where(low_side, COLS - 1, 0)
    start = COLS - 1 - end
    beside = jnp.where(low_side, COLS - 2, 1)
    cut = jnp.where(low_side, COLS - 1, 1)
    k = stand(kappa[...])
    row = lax.broadcasted_iota(jnp.int32, (256, 128), 0)
    lane = lax.broadcasted_iota(jnp.int32, (256, 128), 1)
    y = row // 128 * 512 + lane // 32 * 128 + row % 128
    face = (k + turn_lines(k, 1)) * 0.5
    low = jnp.where((y == 0) | (y == cut), 0.0, face)
    link = jnp.where(y == beside, jnp.where(low_side, turn_lines(face, -1), face), 0.0)
    ground = jnp.where(y == start, 1.0 + 0.5 * k, 1.0)

    def keep(index, up, down):
        ay[index] = up
        by[index] = down

    inverse, (profile,) = reduce_matrix(low, ground + link, [link], Y_STEPS, turn_lines, keep)
    qy[...] = jnp.where(y == end, 0.0, inverse)
    profile = lie(jnp.where(y == end, 1.0, profile))
    hy[...] = profile
    k = kappa[...]
    column = lax.broadcasted_iota(jnp.int32, (ALL, COLS), 1)
    total = jnp.sum(profile * jnp.where(column == start, 1.0 + 0.5 * k, 1.0), axis=1, keepdims=True)
    rim = jnp.sum(jnp.where(column == end, k, 0.0), axis=1, keepdims=True)
    lane = lax.broadcasted_iota(jnp.int32, (8, 128), 1)
    tile = jnp.zeros((8, 128), F32)
    for g in range(ALL // 8):
        part = slice(8 * g, 8 * g + 8)
        tile = jnp.where(lane == 4 * g, total[part], jnp.where(lane == 4 * g + 1, rim[part], tile))
    edge[...] = tile


def source_kernel(fields, fields_far, vertical, vertical_far, h1, h2, parts, prev, after, source, elements):
    del after
    gx = lax.axis_index("gx")
    here = fields[...]
    v = vertical[...]
    s = here + (v + vertical_far[...]) * 0.5 * (fields_far[...] - here) - v * 0.5 * here
    source[...] = s
    for f in range(2):
        mine = slice(f * ROWS, (f + 1) * ROWS)
        first = dense(jnp.sum(h1[mine, :] * s[mine, :], axis=0, keepdims=True))
        last = dense(jnp.sum(h2[mine, :] * s[mine, :], axis=0, keepdims=True))
        rim = parts[4, f]
        s_last = jnp.where(gx == 63, parts[2, f] + rim * 0.5, parts[2, f])
        rim = jnp.where(gx % 8 == 7, jnp.where(gx == 7, 0.0, prev[f]), rim)
        element = (parts[0, f], parts[1, f], s_last, first, last, parts[3, f], rim)
        for n, value in enumerate(element):
            elements[f, n] = value


def local_x_kernel(source, ax, bx, qx, out):
    half = 512
    for f in range(2):
        mine = pl.ds(f * ROWS, ROWS)
        for c in range(COLS // half):
            cols = pl.ds(c * half, half)
            r = source[mine, cols]
            r = reduce_right(r, X_STEPS, turn_rows, lambda i: (ax[i, mine, cols], bx[i, mine, cols]))
            out[mine, cols] = r * qx[mine, cols]


def merge(one, two):
    g, sl, sr, rl, rr = one
    g2, sl2, sr2, rl2, rr2 = two
    s = sr + sl2
    r = rr + rl2
    inverse = 1.0 / (g + g2 + s)
    a = g * inverse
    b = g2 * inverse
    return (a * g2, sl + a * s, sr2 + b * s, rl + a * r, rr2 + b * r), (a, b, r * inverse)


def behind(face, two):
    g, s, sr, r, rr = two
    inverse = 1.0 / (face + g + s)
    a = face * inverse
    b = g * inverse
    return (a * g, a * s, sr + b * s, a * r, rr + b * r), (a, b, r * inverse)


def load(ref, *field):
    return tuple(ref[(*field, n)] for n in range(7))


def within(node, left, right):
    a, b, c = node
    return (a * left[0] + b * right[0], a * left[1] + b * right[1], a * left[2] + b * right[2] + c)


def chip_kernel(mine, other, chips, chip, middle):
    even = lax.axis_index("gx") % 2 == 0
    fields = []
    for f in range(2):
        a, b = load(mine, f), load(other, f)
        first = [jnp.where(even, m, o) for m, o in zip(a, b)]
        second = [jnp.where(even, o, m) for m, o in zip(a, b)]
        tail, start = behind((first[6] + second[5]) * 0.5, second[:5])
        element, end = merge(first[:5], tail)
        fields.append(((*element, first[5], second[6]), (*end, *start)))
        for n, value in enumerate(fields[f][0]):
            chips[f, n] = value
    for out, (one, two) in zip((chip, middle), zip(*fields)):
        for n, (a, b) in enumerate(zip(one, two)):
            out[n] = jnp.where(even, a, b)


def pick_kernel(chips, keep, send):
    even = lax.axis_index("gx") % 2 == 0
    for n, (one, two) in enumerate(zip(load(chips, 0), load(chips, 1))):
        keep[n] = jnp.where(even, one, two)
        send[n] = jnp.where(even, two, one)


def slab_kernel(chip, far1, keep, got, middle, message, nodes):
    y = lax.axis_index("gx") // 2 % 4
    even = lax.axis_index("gx") % 2 == 0
    far2 = [jnp.where(even, g, k) for k, g in zip(load(keep), load(got))]
    far3 = [jnp.where(even, k, g) for k, g in zip(load(keep), load(got))]
    arrived = [load(chip), load(far1), far2, far3]
    chips = []
    for m in range(4):
        chosen = arrived[0]
        for flip in range(1, 4):
            here = y ^ flip == m
            chosen = [jnp.where(here, a, c) for a, c in zip(arrived[flip], chosen)]
        chips.append(chosen)
    element, inner, fronts = None, [], []
    for m in range(4):
        face = (chips[m - 1][6] + chips[m][5]) * 0.5
        tail, front = behind(face, chips[m][:5])
        fronts.append(front)
        if m == 0:
            element = tail
        else:
            element, node = merge(element, tail)
            inner.append(node)
    for n, value in enumerate(element):
        for j in range(8):
            message[j, n] = value
    zero, one = jnp.zeros((8, 128), F32), jnp.ones((8, 128), F32)
    left = (one, zero, zero)
    lasts = [(zero, one, zero)]
    for node in inner[::-1]:
        lasts.append(within(node, left, lasts[-1]))
    lasts = [left] + lasts[::-1]
    firsts = [within(fronts[m], lasts[m], lasts[m + 1]) for m in range(4)]
    lasts = lasts[1:]
    first, last = firsts[0], lasts[0]
    for m in range(1, 4):
        first = [jnp.where(y == m, new, old) for new, old in zip(firsts[m], first)]
        last = [jnp.where(y == m, new, old) for new, old in zip(lasts[m], last)]
    before = within(tuple(middle[n] for n in range(3)), first, last)
    second = within(tuple(middle[n] for n in range(3, 6)), before, last)
    for n, trio in enumerate((first, before, second, last)):
        for m in range(3):
            nodes[n, m] = trio[m]


def ends_kernel(got, nodes, mine, other):
    gx = lax.axis_index("gx")
    slab = gx // 8
    even = gx % 2 == 0
    zero = jnp.zeros((8, 128), F32)
    conduct = got[0, 0] + got[0, 2]
    right = got[0, 4]
    ratios, offsets = [], []
    for z in range(1, 8):
        g, sl, sr, rl, rr = (got[z, n] for n in range(5))
        conduct = conduct + sl
        right = right + rl
        inverse = 1.0 / (conduct + g)
        f = g * inverse
        ratios.append(f)
        offsets.append(right * inverse)
        conduct = sr + f * conduct
        right = rr + f * right
    value = right / conduct
    values = [value]
    for k in range(6, -1, -1):
        value = ratios[k] * value + offsets[k]
        values.append(value)
    values = [zero] + values[::-1]
    first, last = zero, zero
    for z in range(8):
        first = jnp.where(slab == z, values[z], first)
        last = jnp.where(slab == z, values[z + 1], last)
    row = [nodes[n, 0] * first + nodes[n, 1] * last + nodes[n, 2] for n in range(4)]
    for n in range(2):
        mine[n] = jnp.where(even, row[n], row[n + 2])
        other[n] = jnp.where(even, row[n + 2], row[n])


def section_kernel(mine, other, local, h1, h2, hy, edge, section, message):
    core = lax.axis_index("gx") % 2
    lane = lax.broadcasted_iota(jnp.int32, (8, 128), 1)
    tile = edge[...]
    for f in range(2):
        first = jnp.where(core == f, mine[0], other[0])
        last = jnp.where(core == f, mine[1], other[1])
        rows = slice(f * ROWS, (f + 1) * ROWS)
        s = local[rows, :] + h1[rows, :] * natural(first, ROWS) + h2[rows, :] * natural(last, ROWS)
        section[rows, :] = s
        total = jnp.sum(hy[rows, :] * s, axis=1, keepdims=True)
        for g in range(2):
            tile = jnp.where(lane == 4 * (2 * f + g) + 2, total[8 * g : 8 * g + 8], tile)
    message[...] = tile


def local_y_kernel(section, ay, by, qy, out):
    r = stand(section[...])
    r = reduce_right(r, Y_STEPS, turn_lines, lambda i: (ay[i], by[i]))
    out[...] = lie(r * qy[...])


def output_kernel(message, far, local, hy, out):
    for g in range(ALL // 8):
        part = slice(8 * g, 8 * g + 8)
        e, k, r = (message[:, 4 * g + n : 4 * g + n + 1] for n in range(3))
        e2, k2, r2 = (far[:, 4 * g + n : 4 * g + n + 1] for n in range(3))
        c = (k + k2) * 0.5
        value = ((e2 + c) * r + c * r2) / (e * e2 + c * (e + e2))
        out[part, :] = local[part, :] + hy[part, :] * value


def call(kernel, outs, specs, flops=0, size=0, scratch=()):
    return pl.pallas_call(
        kernel,
        out_shape=outs,
        in_specs=specs,
        out_specs=jax.tree.map(lambda _: VMEM, outs),
        scratch_shapes=scratch,
        compiler_params=PARAMS,
        cost_estimate=pl.CostEstimate(flops=flops, bytes_accessed=size, transcendentals=0),
    )


SLAB_GROUPS = [[8 * b + a for b in range(8)] for a in range(8)]
CORES = [(i, i ^ 1) for i in range(64)]


CHIPS = [(i, i ^ (7 if i % 2 else 5)) for i in range(64)]
NEXT = [(i, i ^ 2) for i in range(64)]


def local(fields, kappa, vertical):
    grid = (ALL, COLS)
    swap = [(0, 1), (1, 0)]
    fields_far = lax.ppermute(fields, "gz", swap)
    vertical_far = lax.ppermute(vertical, "gz", swap)
    full = shape(*grid)
    half = shape(7, 8, 128)
    standing = shape(256, 128)
    fields_here, vertical_here, kappa_here, rim = call(
        input_kernel,
        (full, full, full, shape(2, 8, 128)),
        [HBM] * 3,
        flops=1_000_000,
        size=1_000_000,
        scratch=[pltpu.SemaphoreType.DMA((3,))],
    )(*(pltpu.with_memory_space_constraint(x.reshape(grid), pltpu.HBM) for x in (fields, vertical, kappa)))
    prev = lax.ppermute(rim, "gx", [(i, (i + 8) % 64) for i in range(64)])
    ax, bx, qx, h1, h2, parts = call(
        factor_x_kernel,
        (shape(4, *grid), shape(4, *grid), full, full, full, shape(5, 2, 8, 128)),
        [VMEM],
        flops=4_000_000,
        size=2_000_000,
    )(kappa_here)
    ay, by, qy, hy, edge = call(
        factor_y_kernel,
        (shape(10, 256, 128), shape(10, 256, 128), standing, full, shape(8, 128)),
        [VMEM],
        flops=20_000_000,
        size=4_000_000,
    )(kappa_here)
    both = shape(2, 7, 8, 128)
    source, elements = call(source_kernel, (full, both), [VMEM] * 9)(
        fields_here, fields_far.reshape(grid), vertical_here, vertical_far.reshape(grid),
        h1, h2, parts, prev, edge,
    )
    got = lax.ppermute(elements, "gx", CORES)
    local_x = call(local_x_kernel, full, [VMEM] * 4, flops=1_000_000, size=1_000_000)(source, ax, bx, qx)
    chips, chip, middle = call(chip_kernel, (both, half, shape(6, 8, 128)), [VMEM] * 2)(elements, got)
    far = lax.ppermute(chips, "gx", CHIPS)
    far1 = lax.ppermute(chip, "gx", NEXT)
    keep, send = call(pick_kernel, (half, half), [VMEM])(far)
    got = lax.ppermute(send, "gx", CORES)
    message, nodes = call(
        slab_kernel, (shape(8, 5, 8, 128), shape(4, 3, 8, 128)), [VMEM] * 5
    )(chip, far1, keep, got, middle)
    got = lax.all_to_all(message, "gx", 0, 0, axis_index_groups=SLAB_GROUPS, tiled=True)
    mine, other = call(
        ends_kernel, (shape(2, 8, 128), shape(2, 8, 128)), [VMEM, VMEM]
    )(got, nodes)
    other = lax.ppermute(other, "gx", CORES)
    section, message = call(
        section_kernel, (full, shape(8, 128)), [VMEM] * 7
    )(mine, other, local_x, h1, h2, hy, edge)
    far = lax.ppermute(message, "gy", swap)
    local_y = call(local_y_kernel, full, [VMEM] * 4, flops=4_000_000, size=3_000_000)(section, ay, by, qy)
    out = call(output_kernel, full, [VMEM] * 4)(message, far, local_y, hy)
    return out.reshape(fields.shape)


def solution(mesh):
    spec = P(None, "gz", "gx", "gy")
    return jax.shard_map(
        local, mesh=mesh, in_specs=(spec, spec, spec), out_specs=spec, check_vma=False
    )
```

```python
import functools

import jax
import jax.numpy as jnp
from jax import lax
from jax.experimental import pallas as pl
from jax.experimental.pallas import tpu as pltpu
from jax.sharding import PartitionSpec as P

F32 = jnp.float32
ROWS = 16
COLS = 1024
ALL = 2 * ROWS
VMEM = pl.BlockSpec(memory_space=pltpu.VMEM)
HBM = pl.BlockSpec(memory_space=pltpu.HBM)
X_STEPS = (1, 2, 4, 8)
Y_STEPS = (1, 2, 4, 8, 16, 32, 64, 128, 256, 512)
PARAMS = pltpu.CompilerParams(vmem_limit_bytes=40 * 1024 * 1024)


def shape(*dims):
    return jax.ShapeDtypeStruct(dims, F32)


def turn(x, k, axis):
    n = x.shape[axis]
    k = k % n
    unit = 128 if axis == 1 else 8
    if k == 0:
        return x
    if k % unit == 0:
        low = lax.slice_in_dim(x, n - k, n, axis=axis)
        high = lax.slice_in_dim(x, 0, n - k, axis=axis)
        return jnp.concatenate([low, high], axis=axis)
    return pltpu.roll(x, k, axis)


def turn_lines(x, k):
    lanes = lax.broadcasted_iota(jnp.int32, (1, 128), 1)

    def blocks(pair, n):
        if n == 4:
            return pair[::-1]
        turned = [pltpu.roll(p, 32 * n % 128, 1) for p in pair]
        over = lanes < 32 * n if n > 0 else lanes >= 128 + 32 * n
        return [jnp.where(over, turned[1 - h], turned[h]) for h in range(2)]

    pair = [x[:128], x[128:]]
    size = abs(k)
    if size >= 128:
        pair = blocks(pair, 4 if size == 512 else k // 128)
    elif size >= 8:
        if k > 0:
            moved = blocks([p[128 - k :] for p in pair], 1)
            pair = [jnp.concatenate([m, p[: 128 - k]], axis=0) for m, p in zip(moved, pair)]
        else:
            moved = blocks([p[:size] for p in pair], -1)
            pair = [jnp.concatenate([p[size:], m], axis=0) for m, p in zip(moved, pair)]
    else:
        rows = lax.broadcasted_iota(jnp.int32, (8, 128), 0)
        turned = [pltpu.roll(p, k % 128, 0) for p in pair]
        if k > 0:
            ends = [t[:8] for t in turned]
            ends = [jnp.where(rows < k, m, e) for m, e in zip(blocks(ends, 1), ends)]
            pair = [jnp.concatenate([e, t[8:]], axis=0) for e, t in zip(ends, turned)]
        else:
            ends = [t[120:] for t in turned]
            ends = [jnp.where(rows >= 8 + k, m, e) for m, e in zip(blocks(ends, -1), ends)]
            pair = [jnp.concatenate([t[:120], e], axis=0) for e, t in zip(ends, turned)]
    return jnp.concatenate(pair, axis=0)


def stand(x):
    tiles = [x[:, 128 * j : 128 * (j + 1)] for j in range(8)]
    return jnp.concatenate(
        [jnp.concatenate(tiles[4 * h : 4 * h + 4], axis=0).T for h in range(2)], axis=0
    )


def lie(x):
    tiles = [x[128 * h : 128 * (h + 1)].T for h in range(2)]
    return jnp.concatenate(
        [tiles[h][ALL * b : ALL * (b + 1)] for h in range(2) for b in range(4)], axis=1
    )


def turn_rows(x, k):
    return turn(x, k, 0)


def reduce_matrix(low, excess, rights, steps, move, keep):
    for index, k in enumerate(steps):
        high = move(low, -k)
        inverse = 1.0 / (low + high + excess)
        up = high * inverse
        down = low * inverse
        keep(index, up, down)
        excess = excess + move(up * excess, k) + move(down * excess, -k)
        rights = [r + move(up * r, k) + move(down * r, -k) for r in rights]
        low = move(up * low, k)
    inverse = 1.0 / excess
    return inverse, [r * inverse for r in rights]


def reduce_right(right, steps, move, load):
    for index, k in enumerate(steps):
        up, down = load(index)
        right = right + move(up * right, k) + move(down * right, -k)
    return right


def dense(row):
    return jnp.concatenate([row[:, 128 * i : 128 * (i + 1)] for i in range(8)], axis=0)


def natural(tile, rows):
    return jnp.concatenate(
        [jnp.broadcast_to(tile[i : i + 1, :], (rows, 128)) for i in range(8)], axis=1
    )


def input_kernel(fields_arg, vertical_arg, kappa_arg, fields, vertical, kappa, rim, done):
    pairs = ((kappa_arg, kappa), (fields_arg, fields), (vertical_arg, vertical))
    copies = [pltpu.make_async_copy(a, b, done.at[n]) for n, (a, b) in enumerate(pairs)]
    for copy in copies:
        copy.start()
    copies[0].wait()
    for f in range(2):
        rim[f] = dense(kappa[f * ROWS + ROWS - 1 : f * ROWS + ROWS, :])
    copies[1].wait()
    copies[2].wait()


def factor_x_kernel(kappa, ax, bx, qx, h1, h2, parts):
    half = 512
    rows = lax.broadcasted_iota(jnp.int32, (ROWS, half), 0)
    for f in range(2):
        mine = pl.ds(f * ROWS, ROWS)
        for c in range(COLS // half):
            cols = pl.ds(c * half, half)
            k = kappa[mine, cols]
            face = (k + turn(k, 1, 0)) * 0.5
            low = jnp.where((rows >= 2) & (rows <= 14), face, 0.0)
            first = jnp.where(rows == 1, face, 0.0)
            last = jnp.where(rows == 14, turn(face, -1, 0), 0.0)

            def keep(index, a, b, mine=mine, cols=cols):
                ax[index, mine, cols] = a
                bx[index, mine, cols] = b

            inverse, (one, two) = reduce_matrix(
                low, 1.0 + first + last, [first, last], X_STEPS, turn_rows, keep
            )
            qx[mine, cols] = jnp.where((rows >= 1) & (rows <= 14), inverse, 0.0)
            one = jnp.where(rows == 0, 1.0, one)
            two = jnp.where(rows == ROWS - 1, 1.0, two)
            h1[mine, cols] = one
            h2[mine, cols] = two
            sums = (
                jnp.sum(first * two, axis=0, keepdims=True),
                jnp.sum(one, axis=0, keepdims=True),
                jnp.sum(two, axis=0, keepdims=True),
                k[:1],
                k[ROWS - 1 :],
            )
            for n, row in enumerate(sums):
                for i in range(half // 128):
                    parts[n, f, pl.ds(c * (half // 128) + i, 1), :] = row[:, 128 * i : 128 * (i + 1)]


def factor_y_kernel(kappa, ay, by, qy, hy, edge):
    gy = lax.axis_index("gy")
    low_side = gy == 0
    end = jnp.where(low_side, COLS - 1, 0)
    start = COLS - 1 - end
    beside = jnp.where(low_side, COLS - 2, 1)
    cut = jnp.where(low_side, COLS - 1, 1)
    k = stand(kappa[...])
    row = lax.broadcasted_iota(jnp.int32, (256, 128), 0)
    lane = lax.broadcasted_iota(jnp.int32, (256, 128), 1)
    y = row // 128 * 512 + lane // 32 * 128 + row % 128
    face = (k + turn_lines(k, 1)) * 0.5
    low = jnp.where((y == 0) | (y == cut), 0.0, face)
    link = jnp.where(y == beside, jnp.where(low_side, turn_lines(face, -1), face), 0.0)
    ground = jnp.where(y == start, 1.0 + 0.5 * k, 1.0)

    def keep(index, up, down):
        ay[index] = up
        by[index] = down

    inverse, (profile,) = reduce_matrix(low, ground + link, [link], Y_STEPS, turn_lines, keep)
    qy[...] = jnp.where(y == end, 0.0, inverse)
    profile = lie(jnp.where(y == end, 1.0, profile))
    hy[...] = profile
    k = kappa[...]
    column = lax.broadcasted_iota(jnp.int32, (ALL, COLS), 1)
    total = jnp.sum(profile * jnp.where(column == start, 1.0 + 0.5 * k, 1.0), axis=1, keepdims=True)
    rim = jnp.sum(jnp.where(column == end, k, 0.0), axis=1, keepdims=True)
    lane = lax.broadcasted_iota(jnp.int32, (8, 128), 1)
    tile = jnp.zeros((8, 128), F32)
    for g in range(ALL // 8):
        part = slice(8 * g, 8 * g + 8)
        tile = jnp.where(lane == 4 * g, total[part], jnp.where(lane == 4 * g + 1, rim[part], tile))
    edge[...] = tile


def source_kernel(fields, fields_far, vertical, vertical_far, h1, h2, parts, prev, after, source, elements):
    del after
    gx = lax.axis_index("gx")
    here = fields[...]
    v = vertical[...]
    s = here + (v + vertical_far[...]) * 0.5 * (fields_far[...] - here) - v * 0.5 * here
    source[...] = s
    for f in range(2):
        mine = slice(f * ROWS, (f + 1) * ROWS)
        first = dense(jnp.sum(h1[mine, :] * s[mine, :], axis=0, keepdims=True))
        last = dense(jnp.sum(h2[mine, :] * s[mine, :], axis=0, keepdims=True))
        rim = parts[4, f]
        s_last = jnp.where(gx == 63, parts[2, f] + rim * 0.5, parts[2, f])
        rim = jnp.where(gx % 8 == 7, jnp.where(gx == 7, 0.0, prev[f]), rim)
        element = (parts[0, f], parts[1, f], s_last, first, last, parts[3, f], rim)
        for n, value in enumerate(element):
            elements[f, n] = value


def local_x_kernel(source, ax, bx, qx, out):
    half = 512
    for f in range(2):
        mine = pl.ds(f * ROWS, ROWS)
        for c in range(COLS // half):
            cols = pl.ds(c * half, half)
            r = source[mine, cols]
            r = reduce_right(r, X_STEPS, turn_rows, lambda i: (ax[i, mine, cols], bx[i, mine, cols]))
            out[mine, cols] = r * qx[mine, cols]


def merge(one, two):
    g, sl, sr, rl, rr = one
    g2, sl2, sr2, rl2, rr2 = two
    s = sr + sl2
    r = rr + rl2
    inverse = 1.0 / (g + g2 + s)
    a = g * inverse
    b = g2 * inverse
    return (a * g2, sl + a * s, sr2 + b * s, rl + a * r, rr2 + b * r), (a, b, r * inverse)


def behind(face, two):
    g, s, sr, r, rr = two
    inverse = 1.0 / (face + g + s)
    a = face * inverse
    b = g * inverse
    return (a * g, a * s, sr + b * s, a * r, rr + b * r), (a, b, r * inverse)


def load(ref, *field):
    return tuple(ref[(*field, n)] for n in range(7))


def within(node, left, right):
    a, b, c = node
    return (a * left[0] + b * right[0], a * left[1] + b * right[1], a * left[2] + b * right[2] + c)


def chip_kernel(mine, other, chips, chip, middle):
    even = lax.axis_index("gx") % 2 == 0
    fields = []
    for f in range(2):
        a, b = load(mine, f), load(other, f)
        first = [jnp.where(even, m, o) for m, o in zip(a, b)]
        second = [jnp.where(even, o, m) for m, o in zip(a, b)]
        tail, start = behind((first[6] + second[5]) * 0.5, second[:5])
        element, end = merge(first[:5], tail)
        fields.append(((*element, first[5], second[6]), (*end, *start)))
        for n, value in enumerate(fields[f][0]):
            chips[f, n] = value
    for out, (one, two) in zip((chip, middle), zip(*fields)):
        for n, (a, b) in enumerate(zip(one, two)):
            out[n] = jnp.where(even, a, b)


def pick_kernel(chips, keep, send):
    even = lax.axis_index("gx") % 2 == 0
    for n, (one, two) in enumerate(zip(load(chips, 0), load(chips, 1))):
        keep[n] = jnp.where(even, one, two)
        send[n] = jnp.where(even, two, one)


def slab_kernel(chip, far1, keep, got, middle, after, message, nodes):
    del after
    y = lax.axis_index("gx") // 2 % 4
    even = lax.axis_index("gx") % 2 == 0
    far2 = [jnp.where(even, k, g) for k, g in zip(load(keep), load(got))]
    far3 = [jnp.where(even, g, k) for k, g in zip(load(keep), load(got))]
    arrived = [load(chip), load(far1), far2, far3]
    chips = []
    for m in range(4):
        chosen = arrived[0]
        for flip in range(1, 4):
            here = y ^ flip == m
            chosen = [jnp.where(here, a, c) for a, c in zip(arrived[flip], chosen)]
        chips.append(chosen)
    element, inner, fronts = None, [], []
    for m in range(4):
        face = (chips[m - 1][6] + chips[m][5]) * 0.5
        tail, front = behind(face, chips[m][:5])
        fronts.append(front)
        if m == 0:
            element = tail
        else:
            element, node = merge(element, tail)
            inner.append(node)
    for n, value in enumerate(element):
        for j in range(8):
            message[j, n] = value
    zero, one = jnp.zeros((8, 128), F32), jnp.ones((8, 128), F32)
    left = (one, zero, zero)
    lasts = [(zero, one, zero)]
    for node in inner[::-1]:
        lasts.append(within(node, left, lasts[-1]))
    lasts = [left] + lasts[::-1]
    firsts = [within(fronts[m], lasts[m], lasts[m + 1]) for m in range(4)]
    lasts = lasts[1:]
    first, last = firsts[0], lasts[0]
    for m in range(1, 4):
        first = [jnp.where(y == m, new, old) for new, old in zip(firsts[m], first)]
        last = [jnp.where(y == m, new, old) for new, old in zip(lasts[m], last)]
    before = within(tuple(middle[n] for n in range(3)), first, last)
    second = within(tuple(middle[n] for n in range(3, 6)), before, last)
    for n, trio in enumerate((first, before, second, last)):
        for m in range(3):
            nodes[n, m] = trio[m]


def ends_kernel(got, nodes, mine, other):
    gx = lax.axis_index("gx")
    slab = gx // 8
    even = gx % 2 == 0
    zero = jnp.zeros((8, 128), F32)
    conduct = got[0, 0] + got[0, 2]
    right = got[0, 4]
    ratios, offsets = [], []
    for z in range(1, 8):
        g, sl, sr, rl, rr = (got[z, n] for n in range(5))
        conduct = conduct + sl
        right = right + rl
        inverse = 1.0 / (conduct + g)
        f = g * inverse
        ratios.append(f)
        offsets.append(right * inverse)
        conduct = sr + f * conduct
        right = rr + f * right
    value = right / conduct
    values = [value]
    for k in range(6, -1, -1):
        value = ratios[k] * value + offsets[k]
        values.append(value)
    values = [zero] + values[::-1]
    first, last = zero, zero
    for z in range(8):
        first = jnp.where(slab == z, values[z], first)
        last = jnp.where(slab == z, values[z + 1], last)
    row = [nodes[n, 0] * first + nodes[n, 1] * last + nodes[n, 2] for n in range(4)]
    for n in range(2):
        mine[n] = jnp.where(even, row[n], row[n + 2])
        other[n] = jnp.where(even, row[n + 2], row[n])


def section_kernel(mine, other, local, h1, h2, hy, edge, section, message):
    core = lax.axis_index("gx") % 2
    lane = lax.broadcasted_iota(jnp.int32, (8, 128), 1)
    tile = edge[...]
    for f in range(2):
        first = jnp.where(core == f, mine[0], other[0])
        last = jnp.where(core == f, mine[1], other[1])
        rows = slice(f * ROWS, (f + 1) * ROWS)
        s = local[rows, :] + h1[rows, :] * natural(first, ROWS) + h2[rows, :] * natural(last, ROWS)
        section[rows, :] = s
        total = jnp.sum(hy[rows, :] * s, axis=1, keepdims=True)
        for g in range(2):
            tile = jnp.where(lane == 4 * (2 * f + g) + 2, total[8 * g : 8 * g + 8], tile)
    message[...] = tile


def local_y_kernel(section, ay, by, qy, out):
    r = stand(section[...])
    r = reduce_right(r, Y_STEPS, turn_lines, lambda i: (ay[i], by[i]))
    out[...] = lie(r * qy[...])


def output_kernel(message, far, local, hy, out):
    for g in range(ALL // 8):
        part = slice(8 * g, 8 * g + 8)
        e, k, r = (message[:, 4 * g + n : 4 * g + n + 1] for n in range(3))
        e2, k2, r2 = (far[:, 4 * g + n : 4 * g + n + 1] for n in range(3))
        c = (k + k2) * 0.5
        value = ((e2 + c) * r + c * r2) / (e * e2 + c * (e + e2))
        out[part, :] = local[part, :] + hy[part, :] * value


def call(kernel, outs, specs, flops=0, size=0, scratch=()):
    return pl.pallas_call(
        kernel,
        out_shape=outs,
        in_specs=specs,
        out_specs=jax.tree.map(lambda _: VMEM, outs),
        scratch_shapes=scratch,
        compiler_params=PARAMS,
        cost_estimate=pl.CostEstimate(flops=flops, bytes_accessed=size, transcendentals=0),
    )


SLAB_GROUPS = [[8 * b + a for b in range(8)] for a in range(8)]
CORES = [(i, i ^ 1) for i in range(64)]


CHIPS = [(i, i ^ (5 if i % 2 else 7)) for i in range(64)]
NEXT = [(i, i ^ 2) for i in range(64)]


def local(fields, kappa, vertical):
    grid = (ALL, COLS)
    swap = [(0, 1), (1, 0)]
    fields_far = lax.ppermute(fields, "gz", swap)
    vertical_far = lax.ppermute(vertical, "gz", swap)
    full = shape(*grid)
    half = shape(7, 8, 128)
    standing = shape(256, 128)
    fields_here, vertical_here, kappa_here, rim = call(
        input_kernel,
        (full, full, full, shape(2, 8, 128)),
        [HBM] * 3,
        flops=1_000_000,
        size=1_000_000,
        scratch=[pltpu.SemaphoreType.DMA((3,))],
    )(*(pltpu.with_memory_space_constraint(x.reshape(grid), pltpu.HBM) for x in (fields, vertical, kappa)))
    prev = lax.ppermute(rim, "gx", [(i, (i + 8) % 64) for i in range(64)])
    ax, bx, qx, h1, h2, parts = call(
        factor_x_kernel,
        (shape(4, *grid), shape(4, *grid), full, full, full, shape(5, 2, 8, 128)),
        [VMEM],
        flops=4_000_000,
        size=2_000_000,
    )(kappa_here)
    ay, by, qy, hy, edge = call(
        factor_y_kernel,
        (shape(10, 256, 128), shape(10, 256, 128), standing, full, shape(8, 128)),
        [VMEM],
        flops=20_000_000,
        size=4_000_000,
    )(kappa_here)
    both = shape(2, 7, 8, 128)
    source, elements = call(source_kernel, (full, both), [VMEM] * 9)(
        fields_here, fields_far.reshape(grid), vertical_here, vertical_far.reshape(grid),
        h1, h2, parts, prev, edge,
    )
    got = lax.ppermute(elements, "gx", CORES)
    local_x = call(local_x_kernel, full, [VMEM] * 4, flops=1_000_000, size=1_000_000)(source, ax, bx, qx)
    chips, chip, middle = call(chip_kernel, (both, half, shape(6, 8, 128)), [VMEM] * 2)(elements, got)
    far = lax.ppermute(chips, "gx", CHIPS)
    far1 = lax.ppermute(chip, "gx", NEXT)
    keep, send = call(pick_kernel, (half, half), [VMEM])(far)
    got = lax.ppermute(send, "gx", CORES)
    message, nodes = call(
        slab_kernel, (shape(8, 5, 8, 128), shape(4, 3, 8, 128)), [VMEM] * 6
    )(chip, far1, keep, got, middle, local_x)
    got = lax.all_to_all(message, "gx", 0, 0, axis_index_groups=SLAB_GROUPS, tiled=True)
    mine, other = call(
        ends_kernel, (shape(2, 8, 128), shape(2, 8, 128)), [VMEM, VMEM]
    )(got, nodes)
    other = lax.ppermute(other, "gx", CORES)
    section, message = call(
        section_kernel, (full, shape(8, 128)), [VMEM] * 7
    )(mine, other, local_x, h1, h2, hy, edge)
    far = lax.ppermute(message, "gy", swap)
    local_y = call(local_y_kernel, full, [VMEM] * 4, flops=4_000_000, size=3_000_000)(section, ay, by, qy)
    out = call(output_kernel, full, [VMEM] * 4)(message, far, local_y, hy)
    return out.reshape(fields.shape)


def solution(mesh):
    spec = P(None, "gz", "gx", "gy")
    return jax.shard_map(
        local, mesh=mesh, in_specs=(spec, spec, spec), out_specs=spec, check_vma=False
    )
```
